32 devices in a mesh: seq: 8 (over z, core), head: 4 (over y, x).
Axes of the slice: x: 2, y: 2, z: 4, core: 2. Of those that a mesh axis runs over, the one named last changes fastest.
Arguments:
- tokens: bfloat16 [4096, 2048], P(('seq', 'head')), may hold values from -6 to 6
- cotangent: bfloat16 [4096, 2048], P(('seq', 'head')), may hold values from -6 to 6
- arrange: int32 [8, 512], P('seq'), may hold values from 0 to 511, each once within a row
- doc_lengths: int32 [8, 3], P('seq'), may hold values from 1 to 409, 512 in all within a row
- routes: int32 [4096, 4], P(('seq', 'head')), may hold values from 0 to 7, all different within a row; in each aligned block of 128 rows (0 to 127, 128 to 255, ...) at most 96 rows name the same one
- norm1_gain: bfloat16 [2048], replicated, may hold values from 0.5 to 1.5
- qkv_weight: bfloat16 [2048, 16, 384], P('seq', 'head'), may hold values from -0.125 to 0.125
- qkv_bias: bfloat16 [16, 384], replicated, may hold values from -0.29882812 to 0.29882812
- out_weight: bfloat16 [2048, 2048], P('head', 'seq'), may hold values from -1.5 to 1.5
- norm2_gain: bfloat16 [2048], replicated, may hold values from 0.5 to 1.5
- router_weight: bfloat16 [2048, 8], replicated, may hold values from -0.0625 to 0.0625
- shared_gate_vec: bfloat16 [2048], replicated, may hold values from -0.125 to 0.125
- shared_gate_up: bfloat16 [2048, 2, 5632], P('seq', None, 'head'), may hold values from -0.125 to 0.125
- shared_down: bfloat16 [5632, 2048], P('head', 'seq'), may hold values from -0.15625 to 0.15625
- expert_gate_up: bfloat16 [8, 2048, 2816], P('seq', 'head'), may hold values from -0.125 to 0.125
- expert_down: bfloat16 [8, 1408, 2048], P('seq', None, 'head'), may hold values from -0.875 to 0.875
Outputs:
- mixed: bfloat16 [4096, 2048], P(('seq', 'head'))
- input_grad: float32 [4096, 2048], P(('seq', 'head'))
- norm1_gain_grad: float32 [2048], replicated
- qkv_weight_grad: float32 [2048, 16, 384], P('seq', 'head')
- qkv_bias_grad: float32 [16, 384], replicated
- out_weight_grad: float32 [2048, 2048], P('head', 'seq')
- norm2_gain_grad: float32 [2048], replicated
- router_weight_grad: float32 [2048, 8], replicated
- shared_gate_vec_grad: float32 [2048], replicated
- shared_gate_up_grad: float32 [2048, 2, 5632], P('seq', None, 'head')
- shared_down_grad: float32 [5632, 2048], P('head', 'seq')
- expert_gate_up_grad: float32 [8, 2048, 2816], P('seq', 'head')
- expert_down_grad: float32 [8, 1408, 2048], P('seq', None, 'head')
The draws below stay inside these ranges and needn't reach their ends.
Inputs may be any that keep to these rules, and one draw needn't show every extreme that they name: `arrange`: row g lists each token of group g once: entry p is the token (counted within the group) that stands at arranged place p. `doc_lengths`: each row sums to 512, and its largest entry is 409. `routes`: each row names 4 different experts. In the 128 rows of one device no expert is named more than 96 times, and some device and expert reach 96.
All inputs are finite; a program needn't handle non-finite values.
Results may differ from the reference program's by a relative error of at most 0.018.
Values may be sent and summed in bfloat16 or wider, within the bound.
A program may use at most 384 MiB of HBM per device.

```python
import math
import jax
import jax.numpy as jnp
import numpy as np
from jax import lax

D = 2048
H = 16
HD = 128
FF = 1408
FFS = 5632
TOPK = 4
DOCS = 3
TOK_DEV = 128
EXPERTS = 8
GROUP_TOK = 512
GROUPS = 8
TOKENS = 4096
CAP = 96
LONGEST = 409
N_SEQ = 8
N_HEAD = 4


def shard_levels(own_key, extent, cuts, smallest, high):
    def one(dim, blocks):
        steps = jax.random.uniform(jax.random.fold_in(jax.random.fold_in(own_key, 6), dim), (blocks,), jnp.float32, smallest / len(cuts), high / len(cuts))
        return jnp.repeat(jnp.exp(steps), extent[dim] // blocks).reshape((-1,) + (1,) * (len(extent) - dim - 1))

    gain = one(*cuts[0])
    for cut in cuts[1:]:
        gain = gain * one(*cut)
    return gain


def profile(amount, total, reach, skew):
    weights = [(1 << 20) // math.isqrt(standing ** skew) + 1 for standing in range(2, amount + 1)]
    rest, counts = total - reach - (amount - 1), [1] * (amount - 1)
    while rest > 0:
        movable = [i for i in range(amount - 1) if counts[i] < reach]
        pool, remaining = sum([weights[i] for i in movable]), rest
        for i in movable:
            extra = min(reach - counts[i], max(1, remaining * weights[i] // pool), rest)
            counts[i] = counts[i] + extra
            rest = rest - extra
    return np.array([reach] + counts)


def uneven_parts(own_key, count, total, reach, slope):
    if count == 2:
        one = jax.random.randint(own_key, (), max(1, total - reach), min(reach, total - 1) + 1)
        return jnp.stack([one, total - one])
    lengths = jnp.asarray(profile(count, total, reach, slope), jnp.int32)
    pairs = (count - 1) // 2
    source_of, sink = lengths[1:1 + 2 * pairs:2], lengths[2:2 + 2 * pairs:2]
    room = jnp.minimum(source_of - 1, reach - sink)
    shifted = jax.random.randint(jax.random.fold_in(own_key, 1), (pairs,), 0, 1 << 20) % (room + 1)
    lengths = lengths.at[1:1 + 2 * pairs:2].set(source_of - shifted).at[2:2 + 2 * pairs:2].set(sink + shifted)
    return lengths[jax.random.permutation(jax.random.fold_in(own_key, 2), count)]


def assign_block(key, own, number, rows, number_of, top, most, slope):
    sequence = jax.random.permutation(key, number_of)
    heavy_load, ordinary = shares(number_of, rows * top, most, slope, True), shares(number_of, rows * top, most, slope, False)
    places = jnp.arange(number_of)

    def named(tallies, rotation):
        used = int((tallies > 0).sum())
        fixed = max(1, used // 4)
        shifted = fixed + (places - fixed + rotation * (used - fixed)) % max(1, number_of - fixed)
        return jnp.zeros((number_of,), jnp.int32).at[sequence[jnp.where(places < fixed, places, shifted)]].set(jnp.asarray(tallies, jnp.int32))

    tallies = jnp.where(number % 4 == 0, named(heavy_load, number // 4), named(ordinary, number - number // 4 - 1))
    mixed = jax.random.permutation(jax.random.fold_in(own, 3), number_of)
    giver, sink = mixed[0:number_of // 2 * 2:2], mixed[1:number_of // 2 * 2:2]
    slack = jnp.minimum(tallies[giver] - 1, most - tallies[sink]) // 2
    slack = jnp.where((giver == sequence[0]) | (sink == sequence[0]) | (tallies[sink] == 0), 0, jnp.maximum(slack, 0))
    shifted = jax.random.randint(jax.random.fold_in(own, 4), (number_of // 2,), 0, 1 << 20) % (slack + 1)
    tallies = tallies.at[giver].add(-shifted).at[sink].add(shifted)
    labels = jnp.searchsorted(jnp.cumsum(tallies), jnp.arange(rows * top), side="right").astype(jnp.int32)
    listing = labels.reshape(top, rows).T
    listing = listing[jax.random.permutation(jax.random.fold_in(own, 1), rows)]
    rotation = jax.random.randint(jax.random.fold_in(own, 2), (rows, 1), 0, top)
    return jnp.take_along_axis(listing, (jnp.arange(top)[None, :] + rotation) % top, axis=1)


def shares(count, total, reach, skew, full):
    portions = [(1 << 20) // math.isqrt(rank ** skew) + 1 for rank in range(1, count + 1)]
    largest = reach if full else min(reach, max(-(-total // count), total * portions[0] // sum(portions)))
    least = 1 if total - largest >= count - 1 else 0
    holding, rest = [largest] + [least] * (count - 1), total - largest - least * (count - 1)
    while rest > 0:
        candidates = [i for i in range(1, count) if holding[i] < largest] or [i for i in range(1, count) if holding[i] < reach]
        whole, left = sum([portions[i] for i in candidates]), rest
        for i in candidates:
            extra = min(reach - holding[i], max(1, left * portions[i] // whole), rest)
            holding[i] = holding[i] + extra
            rest = rest - extra
    return np.array(holding)


def centred(stream_key, shape, deviation, most, split=(), held_as=jnp.bfloat16):
    values = deviation * jax.random.normal(stream_key, shape, jnp.float32)
    if split:
        values = values * shard_levels(stream_key, shape, split, -0.22, 0.18)
    return jnp.clip(values, -most, most).astype(held_as)


def setup_inputs(seed: int = 0) -> dict:
    key_list = jax.random.split(jax.random.key(seed), 17)
    tokens = centred(key_list[0], (TOKENS, D), 1.0, 6.0, ((0, 32),))
    cotangent = centred(key_list[1], (TOKENS, D), 1.0, 6.0, ((0, 32),))
    arrange = jax.vmap(lambda own: jax.random.permutation(own, GROUP_TOK))(jax.random.split(key_list[2], GROUPS)).reshape((GROUPS, GROUP_TOK)).astype(jnp.int32)
    doc_lengths = jax.vmap(lambda own: uneven_parts(own, DOCS, GROUP_TOK, LONGEST, 2))(jax.random.split(key_list[3], GROUPS)).reshape((GROUPS, DOCS)).astype(jnp.int32)
    routes_keys = jax.random.split(jax.random.fold_in(key_list[4], 1), TOKENS // TOK_DEV)
    routes_turns = jax.random.permutation(jax.random.fold_in(key_list[4], 3), TOKENS // TOK_DEV)
    routes = jax.vmap(lambda own, number: assign_block(jax.random.fold_in(key_list[4], 2), own, number, TOK_DEV, EXPERTS, TOPK, CAP, 2))(routes_keys, routes_turns).reshape((TOKENS, TOPK))
    norm1_gain = jnp.clip(1.0 + 0.1 * jax.random.normal(key_list[5], (D,), jnp.float32), 0.5, 1.5).astype(jnp.bfloat16)
    qkv_weight = centred(key_list[6], (D, H, 3 * HD), D ** -0.5, 0.125, ((0, 8), (1, 4)))
    qkv_bias = centred(key_list[7], (H, 3 * HD), 0.05, 0.29882812)
    out_weight = centred(key_list[8], (D, D), (D // 128) ** -0.5, 1.5, ((0, 4), (1, 8)))
    norm2_gain = jnp.clip(1.0 + 0.1 * jax.random.normal(key_list[9], (D,), jnp.float32), 0.5, 1.5).astype(jnp.bfloat16)
    router_weight = centred(key_list[10], (D, EXPERTS), (4 * D) ** -0.5, 0.0625)
    shared_gate_vec = centred(key_list[11], (D,), D ** -0.5, 0.125)
    shared_gate_up = centred(key_list[12], (D, 2, FFS), D ** -0.5, 0.125, ((0, 8), (2, 4)))
    shared_down = centred(key_list[13], (FFS, D), (FFS // 4) ** -0.5, 0.15625, ((0, 4), (1, 8)))
    expert_gate_up = centred(key_list[14], (EXPERTS, D, 2 * FF), D ** -0.5, 0.125, ((0, 8), (1, 4)))
    expert_down = centred(key_list[15], (EXPERTS, FF, D), (FF // 32) ** -0.5, 0.875, ((0, 8), (2, 4)))
    return dict(tokens=tokens, cotangent=cotangent, arrange=arrange, doc_lengths=doc_lengths, routes=routes, norm1_gain=norm1_gain, qkv_weight=qkv_weight, qkv_bias=qkv_bias, out_weight=out_weight, norm2_gain=norm2_gain, router_weight=router_weight, shared_gate_vec=shared_gate_vec, shared_gate_up=shared_gate_up, shared_down=shared_down, expert_gate_up=expert_gate_up, expert_down=expert_down)


EPS = 1e-06
THETA = 1000000.0
NEGATIVE = -1e+30

@jax.custom_vjp
def low(v):
    return lax.optimization_barrier(v.astype(jnp.bfloat16)).astype(jnp.float32)

@jax.custom_vjp
def low_back(v):
    return v

def low_keep(v):
    return (low(v), None)

def low_pass(kept, grad):
    return (grad,)

def back_keep(v):
    return (v, None)

def back_low(kept, grad):
    return (low(grad),)
low.defvjp(low_keep, low_pass)
low_back.defvjp(back_keep, back_low)

def matmul_exact(left, right):
    return jnp.dot(left, right, precision=lax.Precision.HIGHEST)

def rms_scale(values):
    return lax.rsqrt(lax.optimization_barrier(jnp.mean(values * values, axis=-1, keepdims=True)) + EPS)

def rope_tables(position):
    half = HD // 2
    exponent = jnp.arange(half, dtype=jnp.float32) * (2.0 / HD)
    frequency = THETA ** (-exponent)
    angle = position[:, None] * frequency[None, :]
    return (jnp.cos(angle), jnp.sin(angle))

def rotate(values, cosine, sine):
    half = HD // 2
    first = values[..., :half]
    second = values[..., half:]
    cosine = cosine[:, None, :]
    sine = sine[:, None, :]
    return jnp.concatenate([first * cosine - second * sine, second * cosine + first * sine], axis=-1)

def layout_of(arrange_row, length_row, group_tok):
    counter = jnp.arange(group_tok, dtype=jnp.int32)
    place = jnp.zeros((group_tok,), jnp.int32).at[arrange_row].set(counter)
    ends = jnp.cumsum(length_row, dtype=jnp.int32)
    starts = ends - length_row
    doc_index = lax.optimization_barrier(jnp.sum((place[:, None] >= ends[None, :]).astype(jnp.int32), axis=1, dtype=jnp.int32))
    picked = doc_index[:, None] == jnp.arange(length_row.shape[0], dtype=jnp.int32)[None, :]
    start_of = lax.optimization_barrier(jnp.sum(jnp.where(picked, starts[None, :], 0), axis=1, dtype=jnp.int32))
    return (place, doc_index, place - start_of)

def head_attention(queries, keys_here, values_here, allowed):
    scores = low_back(matmul_exact(queries, keys_here.T) * HD ** (-0.5))
    scores = jnp.where(allowed, scores, NEGATIVE)
    largest = lax.optimization_barrier(jnp.max(scores, axis=1, keepdims=True))
    weights = jnp.exp(scores - largest)
    probs = weights / lax.optimization_barrier(jnp.sum(weights, axis=1, keepdims=True))
    return matmul_exact(low(probs), values_here)

def reference(tokens, cotangent, arrange, doc_lengths, routes, norm1_gain, qkv_weight, qkv_bias, out_weight, norm2_gain, router_weight, shared_gate_vec, shared_gate_up, shared_down, expert_gate_up, expert_down):
    devices_all = N_SEQ * N_HEAD
    place, doc_index, position = jax.vmap(lambda row_a, row_b: layout_of(row_a, row_b, GROUP_TOK))(arrange, doc_lengths)
    cosine, sine = rope_tables(position.reshape(TOKENS).astype(jnp.float32))
    cosine = cosine.reshape(GROUPS, GROUP_TOK, HD // 2)
    sine = sine.reshape(GROUPS, GROUP_TOK, HD // 2)
    rows_dev = TOK_DEV * TOPK
    flat_routes = routes.reshape(devices_all, rows_dev)
    onehot = (flat_routes[:, :, None] == jnp.arange(EXPERTS, dtype=jnp.int32)[None, None, :]).astype(jnp.int32)
    slot = lax.optimization_barrier(jnp.sum(jnp.cumsum(onehot, axis=1, dtype=jnp.int32) * onehot, axis=2, dtype=jnp.int32)) - 1
    column = jnp.arange(devices_all, dtype=jnp.int32)[:, None] * CAP + slot
    entry = jnp.arange(TOKENS * TOPK, dtype=jnp.int32).reshape(devices_all, rows_dev)
    table = jnp.full((EXPERTS, devices_all * CAP), TOKENS * TOPK, jnp.int32).at[flat_routes, column].set(entry)

    def forward(stream, gain_first, qkv_mat, qkv_shift, out_mat, gain_second, router_mat, share_vector, share_upper, share_lower, expert_upper, expert_lower):

        def front(item):
            rows_in, place_g, doc_g, cos_g, sin_g = item
            normed = low(rows_in * rms_scale(rows_in) * gain_first)
            linear = low_back(matmul_exact(normed, qkv_mat.reshape(D, 3 * D)) + qkv_shift.reshape(3 * D))
            parts = linear.reshape(GROUP_TOK, H, 3, HD)
            roped = jnp.stack([rotate(parts[:, :, 0], cos_g, sin_g), rotate(parts[:, :, 1], cos_g, sin_g), parts[:, :, 2]], axis=2)
            ready = low(low_back(roped))
            allowed = (doc_g[:, None] == doc_g[None, :]) & (place_g[None, :] <= place_g[:, None])
            per_head = jnp.transpose(ready, (1, 2, 0, 3))
            attended = lax.map(jax.checkpoint(lambda triple: head_attention(triple[0], triple[1], triple[2], allowed)), per_head)
            merged = low(low_back(jnp.transpose(attended, (1, 0, 2)).reshape(GROUP_TOK, D)))
            return rows_in + low_back(matmul_exact(merged, out_mat))
        middle = lax.map(jax.checkpoint(front), (stream.reshape(GROUPS, GROUP_TOK, D), place, doc_index, cosine, sine)).reshape(TOKENS, D)
        second = low(middle * rms_scale(middle) * gain_second)
        probs = jax.nn.softmax(matmul_exact(second, router_mat), axis=-1)
        gates = jnp.take_along_axis(probs, routes, axis=1)
        second_pad = jnp.concatenate([second, jnp.zeros((1, D), jnp.float32)], axis=0)
        gate_pad = jnp.concatenate([gates.reshape(-1), jnp.zeros((1,), jnp.float32)], axis=0)

        def expert_step(total, item):
            rows, upper, lower = item
            token_ids = rows // TOPK
            inputs = low_back(second_pad[token_ids])
            gate_up = low_back(matmul_exact(inputs, upper))
            hidden = low(jax.nn.silu(gate_up[:, :FF]) * gate_up[:, FF:])
            result = low(low_back(matmul_exact(hidden, lower)))
            return (total.at[token_ids].add(gate_pad[rows][:, None] * result), None)
        routed_pad, unused = lax.scan(jax.checkpoint(expert_step), jnp.zeros((TOKENS + 1, D), jnp.float32), (table, expert_upper, expert_lower))
        routed = routed_pad[:TOKENS]
        share_wide = share_upper.reshape(D, 2 * FFS)

        def shared_block(rows_in):
            gate_up = low_back(matmul_exact(rows_in, share_wide))
            hidden = low(jax.nn.silu(gate_up[:, :FFS]) * gate_up[:, FFS:])
            return low_back(matmul_exact(hidden, share_lower))
        share_out = lax.map(jax.checkpoint(shared_block), second.reshape(GROUPS, GROUP_TOK, D)).reshape(TOKENS, D)
        share_gate = jax.nn.sigmoid(matmul_exact(second, share_vector))
        return middle + routed + share_gate[:, None] * share_out
    floats = (tokens.astype(jnp.float32), norm1_gain.astype(jnp.float32), qkv_weight.astype(jnp.float32), qkv_bias.astype(jnp.float32), out_weight.astype(jnp.float32), norm2_gain.astype(jnp.float32), router_weight.astype(jnp.float32), shared_gate_vec.astype(jnp.float32), shared_gate_up.astype(jnp.float32), shared_down.astype(jnp.float32), expert_gate_up.astype(jnp.float32), expert_down.astype(jnp.float32))
    mixed, pullback = jax.vjp(forward, *floats)
    grads = pullback(cotangent.astype(jnp.float32))
    return (mixed.astype(jnp.bfloat16), grads[0], grads[1], grads[2], grads[3], grads[4], grads[5], grads[6], grads[7], grads[8], grads[9], grads[10], grads[11])
```

```python
import jax
import jax.numpy as jnp
from jax import lax
from jax.sharding import PartitionSpec as P

HD = 128
EPS = 1e-06
THETA = 1000000.0
NEGATIVE = -1e30
LANES = 128
bf16 = jnp.bfloat16
f32 = jnp.float32


def rms_scale(values):
    return lax.rsqrt(jnp.mean(values * values, axis=-1, keepdims=True) + EPS)


def rope_tables(position):
    half = HD // 2
    exponent = jnp.arange(half, dtype=f32) * (2.0 / HD)
    frequency = THETA ** (-exponent)
    angle = position[:, None] * frequency[None, :]
    return (jnp.cos(angle), jnp.sin(angle))


def layout_of(arrange_row, length_row, group_tok):
    counter = jnp.arange(group_tok, dtype=jnp.int32)
    place = jnp.sum(
        jnp.where(arrange_row[None, :] == counter[:, None], counter[None, :], 0),
        axis=1,
        dtype=jnp.int32,
    )
    ends = jnp.cumsum(length_row, dtype=jnp.int32)
    starts = ends - length_row
    doc_index = jnp.sum(
        (place[:, None] >= ends[None, :]).astype(jnp.int32), axis=1, dtype=jnp.int32
    )
    picked = doc_index[:, None] == jnp.arange(length_row.shape[0], dtype=jnp.int32)[None, :]
    start_of = jnp.sum(jnp.where(picked, starts[None, :], 0), axis=1, dtype=jnp.int32)
    return (place, doc_index, place - start_of)


def dot(left, right, left_dim, right_dim):
    return lax.dot_general(
        left, right, (((left_dim,), (right_dim,)), ((), ())), preferred_element_type=f32
    )


def heads_dot(left, right, left_dim, right_dim):
    return lax.dot_general(
        left, right, (((left_dim,), (right_dim,)), ((0,), (0,))), preferred_element_type=f32
    )


def swap(block, axis, bit):
    size = lax.axis_size(axis)
    return lax.ppermute(block, axis, [(i, i ^ bit) for i in range(size)])


def bits_of(size):
    bits = []
    bit = 1
    while bit < size:
        bits.append(bit)
        bit *= 2
    return bits


def spread(block, order):
    found = {0: block}
    for bit in order:
        for near in sorted(found):
            found[near ^ bit] = swap(found[near], "head", bit)
    return found


def collect(parts, order):
    parts = dict(parts)
    for bit in reversed(order):
        for far in sorted((r for r in parts if r & bit), reverse=True):
            parts[far ^ bit] = parts[far ^ bit] + swap(parts.pop(far), "head", bit)
    return parts[0]


def group_gather(block):
    order = bits_of(lax.axis_size("head"))
    half = block.shape[0] // 2
    upper = spread(block[:half], order)
    lower = spread(block[half:], order[::-1])
    return jnp.concatenate([piece for r in sorted(upper) for piece in (upper[r], lower[r])], axis=0)


def group_scatter(block):
    n_head = lax.axis_size("head")
    order = bits_of(n_head)
    rows = block.shape[0] // n_head
    half = rows // 2
    upper = {r: block[r * rows : r * rows + half] for r in range(n_head)}
    lower = {r: block[r * rows + half : (r + 1) * rows] for r in range(n_head)}
    return jnp.concatenate([collect(upper, order), collect(lower, order[::-1])], axis=0)


def token_gather(block):
    order = bits_of(lax.axis_size("head"))
    column = lax.all_gather(block, "seq", axis=0, tiled=True)
    share = column.shape[0] // 2
    half = share // 2
    core = lax.rem(lax.axis_index("seq"), 2)
    own = lax.dynamic_slice_in_dim(column, core * share, share, 0)
    upper = spread(own[:half], order)
    lower = spread(own[half:], order[::-1])
    chunks = [column]
    for r in range(1, lax.axis_size("head")):
        pair = jnp.concatenate([upper[r], lower[r]], axis=0)
        chunks.append(jnp.concatenate([pair, swap(pair, "seq", 1)], axis=0))
    return chunks


def token_scatter(chunks):
    order = bits_of(lax.axis_size("head"))
    column = chunks[0]
    share = column.shape[0] // 2
    half = share // 2
    core = lax.rem(lax.axis_index("seq"), 2)
    own = lax.dynamic_slice_in_dim(column, core * share, share, 0)
    upper = {0: own[:half]}
    lower = {0: own[half:]}
    for r in range(1, len(chunks)):
        pair = chunks[r][:share] + swap(chunks[r][share:], "seq", 1)
        upper[r] = pair[:half]
        lower[r] = pair[half:]
    total = jnp.concatenate([collect(upper, order), collect(lower, order[::-1])], axis=0)
    column = lax.dynamic_update_slice_in_dim(column, total, core * share, 0)
    return lax.psum_scatter(column, "seq", scatter_dimension=0, tiled=True)


def total_over_all(values):
    for axis in ("head", "seq"):
        for bit in bits_of(lax.axis_size(axis)):
            values = values + swap(values, axis, bit)
    return values


def rotate(values, cosine, sine):
    half = HD // 2
    first = values[..., :half]
    second = values[..., half:]
    return jnp.concatenate(
        [first * cosine - second * sine, second * cosine + first * sine], axis=-1
    )


def unrotate(grads, cosine, sine):
    return rotate(grads, cosine, -sine)


def shards(
    tokens,
    cotangent,
    arrange,
    doc_lengths,
    routes,
    norm1_gain,
    qkv_weight,
    qkv_bias,
    out_weight,
    norm2_gain,
    router_weight,
    shared_gate_vec,
    shared_gate_up,
    shared_down,
    expert_gate_up,
    expert_down,
):
    highest = lax.Precision.HIGHEST
    tok_rows, width = tokens.shape
    n_seq = lax.axis_size("seq")
    n_head = lax.axis_size("head")
    seq = lax.axis_index("seq")
    head = lax.axis_index("head")
    group_tok = tok_rows * n_head
    heads_here = qkv_weight.shape[1]
    n_exp = router_weight.shape[1]
    hidden_all = expert_down.shape[1]
    exp_units = hidden_all // n_head
    share_all = shared_down.shape[0]
    share_units = share_all // n_seq
    units = exp_units + share_units
    unit_cols = -(-(units + n_exp + 1) // LANES) * LANES
    scale = HD ** (-0.5)

    qkv_full = lax.all_gather(qkv_weight.reshape(-1, heads_here * 3 * HD), "seq", axis=0, tiled=True)
    out_full = lax.all_gather(out_weight, "seq", axis=0)
    out_full = jnp.transpose(out_full, (1, 0, 2)).reshape(out_weight.shape[0], width)

    upper_e = expert_gate_up[0].reshape(-1, 2, n_head, exp_units)
    upper_e = lax.all_to_all(jnp.transpose(upper_e, (2, 0, 1, 3)), "head", split_axis=0, concat_axis=0)
    upper_e = upper_e.reshape(width, 2, exp_units)
    lower_e = lax.all_to_all(
        expert_down[0].reshape(n_head, exp_units, -1), "head", split_axis=0, concat_axis=0
    )
    lower_e = jnp.transpose(lower_e, (1, 0, 2)).reshape(exp_units, width)
    upper_s = shared_gate_up.reshape(-1, 2, n_seq, share_units)
    upper_s = lax.all_to_all(jnp.transpose(upper_s, (2, 0, 1, 3)), "seq", split_axis=0, concat_axis=0)
    upper_s = upper_s.reshape(width, 2, share_units)
    lower_s = lax.all_to_all(
        shared_down.reshape(n_seq, share_units, -1), "seq", split_axis=0, concat_axis=0
    )
    lower_s = jnp.transpose(lower_s, (1, 0, 2)).reshape(share_units, width)
    gate_cols = jnp.concatenate([router_weight, shared_gate_vec[:, None]], axis=1)
    spare = unit_cols - units - n_exp - 1
    upper = jnp.concatenate(
        [
            upper_e[:, 0],
            upper_s[:, 0],
            gate_cols,
            jnp.zeros((width, spare), bf16),
            upper_e[:, 1],
            upper_s[:, 1],
            jnp.zeros((width, unit_cols - units), bf16),
        ],
        axis=1,
    )
    lower = jnp.concatenate([lower_e, lower_s, jnp.zeros((unit_cols - units, width), bf16)], axis=0)

    place, doc_index, position = layout_of(arrange[0], doc_lengths[0], group_tok)
    blocks = jnp.bitwise_xor(head, jnp.arange(n_head, dtype=jnp.int32))
    table = jnp.stack([place, doc_index, position]).reshape(3, n_head, tok_rows)
    place, doc_index, position = jnp.take(table, blocks, axis=1).reshape(3, group_tok)
    allowed = (doc_index[:, None] == doc_index[None, :]) & (place[None, :] <= place[:, None])
    cosine, sine = rope_tables(position.astype(f32))

    stream = tokens.astype(f32)
    gain_first = norm1_gain.astype(f32)
    scale_first = rms_scale(stream)
    normed_first = stream * scale_first
    first_group = group_gather((normed_first * gain_first).astype(bf16))

    bias_here = lax.dynamic_slice_in_dim(qkv_bias, head * heads_here, heads_here, 0)
    linear = dot(first_group, qkv_full, 1, 0) + bias_here.astype(f32).reshape(-1)
    linear = jnp.transpose(linear.reshape(group_tok, heads_here, 3, HD), (2, 1, 0, 3))
    queries = rotate(linear[0], cosine, sine).astype(bf16)
    keys = rotate(linear[1], cosine, sine).astype(bf16)
    values = linear[2].astype(bf16)
    scores = jnp.where(allowed, heads_dot(queries, keys, 2, 2) * scale, NEGATIVE)
    largest = jnp.max(scores, axis=2, keepdims=True)
    weights = jnp.exp(scores - largest)
    probs_low = (weights / jnp.sum(weights, axis=2, keepdims=True)).astype(bf16)
    attended = heads_dot(probs_low, values, 2, 1).astype(bf16)
    merged = jnp.transpose(attended, (1, 0, 2)).reshape(group_tok, heads_here * HD)
    attn_out = group_scatter(dot(merged, out_full, 1, 0).astype(bf16))
    middle = stream + attn_out.astype(f32)
    gain_second = norm2_gain.astype(f32)
    scale_second = rms_scale(middle)
    normed_second = middle * scale_second
    lowered_second = (normed_second * gain_second).astype(bf16)

    expert_ids = jnp.arange(n_exp, dtype=jnp.int32)
    chosen = jnp.any(routes[:, :, None] == expert_ids[None, None, :], axis=1)
    marks = jnp.concatenate(
        [chosen.astype(bf16), jnp.zeros((tok_rows, LANES - n_exp), bf16)], axis=1
    )
    grad_chunks = token_gather(jnp.concatenate([cotangent, marks], axis=1))
    second_chunks = token_gather(lowered_second)

    lane = jnp.arange(unit_cols, dtype=jnp.int32)
    own_expert = (expert_ids == seq).astype(f32)
    ext_lane = jnp.arange(LANES, dtype=jnp.int32)
    out_chunks = []
    back_chunks = []
    grad_upper = 0.0
    grad_lower = 0.0
    for second, grad_ext in zip(second_chunks, grad_chunks):
        grad = grad_ext[:, :width]
        gate_up = dot(second, upper, 1, 0)
        probs = jax.nn.softmax(gate_up[:, units : units + n_exp], axis=-1)
        share_gate = jax.nn.sigmoid(gate_up[:, units + n_exp])
        mark = jnp.sum(grad_ext[:, width : width + n_exp].astype(f32) * own_expert, axis=1)
        gate_here = jnp.sum(probs * own_expert, axis=1) * mark
        factor = jnp.where(lane[None, :] < exp_units, gate_here[:, None], share_gate[:, None])
        gate_part = gate_up[:, :unit_cols]
        up_part = gate_up[:, unit_cols:]
        sigma = jax.nn.sigmoid(gate_part)
        silu = gate_part * sigma
        hidden = silu * up_part
        scaled = (hidden * factor).astype(bf16)
        grad_raw = dot(grad, lower, 1, 1)
        both = hidden * grad_raw
        grad_gate = jnp.sum(jnp.where(lane[None, :] < exp_units, both, 0.0), axis=1) * mark
        grad_share = jnp.sum(jnp.where(lane[None, :] >= exp_units, both, 0.0), axis=1)
        grad_hidden = grad_raw * factor
        grad_gate_up = jnp.concatenate(
            [
                grad_hidden * up_part * (sigma * (1.0 + gate_part * (1.0 - sigma))),
                grad_hidden * silu,
            ],
            axis=1,
        ).astype(bf16)
        back = dot(grad_gate_up, upper, 1, 1).astype(bf16)
        extra = jnp.where(
            ext_lane[None, :] == seq,
            grad_gate[:, None],
            jnp.where(ext_lane[None, :] == n_exp, grad_share[:, None], 0.0),
        )
        back_chunks.append(jnp.concatenate([back, extra.astype(bf16)], axis=1))
        out_chunks.append(dot(scaled, lower, 1, 0).astype(bf16))
        grad_upper = grad_upper + dot(second, grad_gate_up, 0, 0)
        grad_lower = grad_lower + dot(scaled, grad, 0, 0)

    back_own = token_scatter(back_chunks).astype(f32)
    out_own = token_scatter(out_chunks).astype(f32)
    mixed = (middle + out_own).astype(bf16)

    logits = jnp.dot(lowered_second, gate_cols, preferred_element_type=f32)
    probs = jax.nn.softmax(logits[:, :n_exp], axis=-1)
    share_gate = jax.nn.sigmoid(logits[:, n_exp:])
    grad_probs = back_own[:, width : width + n_exp]
    grad_logits = probs * (grad_probs - jnp.sum(probs * grad_probs, axis=1, keepdims=True))
    grad_gate_logit = (
        back_own[:, width + n_exp : width + n_exp + 1] * share_gate * (1.0 - share_gate)
    )
    small = jnp.concatenate([grad_logits, grad_gate_logit], axis=1)
    grad_second = back_own[:, :width] + jnp.dot(
        small, gate_cols.astype(f32).T, precision=highest
    )
    grad_gate_cols = jnp.dot(small.T, lowered_second.astype(f32), precision=highest)
    grad_gain_second = jnp.sum(grad_second * normed_second, axis=0)
    grad_normed = grad_second * gain_second
    grad_middle = cotangent.astype(f32) + scale_second * (
        grad_normed - normed_second * jnp.mean(grad_normed * normed_second, axis=1, keepdims=True)
    )
    totals_second = total_over_all(
        jnp.concatenate([grad_gate_cols, grad_gain_second[None, :]], axis=0)
    )

    grad_attn = group_gather(grad_middle.astype(bf16))
    grad_merged = dot(grad_attn, out_full, 1, 1).astype(bf16)
    grad_heads = jnp.transpose(grad_merged.reshape(group_tok, heads_here, HD), (1, 0, 2))
    probs_full = weights / jnp.sum(weights, axis=2, keepdims=True)
    grad_values = heads_dot(probs_low, grad_heads, 1, 1)
    grad_attn_probs = heads_dot(grad_heads, values, 2, 2)
    centre = jnp.sum(probs_full * grad_attn_probs, axis=2, keepdims=True)
    grad_scores = (probs_full * (grad_attn_probs - centre)).astype(bf16)
    grad_queries = (heads_dot(grad_scores, keys, 2, 1) * scale).astype(bf16).astype(f32)
    grad_keys = (heads_dot(grad_scores, queries, 1, 1) * scale).astype(bf16).astype(f32)
    grad_linear = jnp.stack(
        [
            unrotate(grad_queries, cosine, sine).astype(bf16),
            unrotate(grad_keys, cosine, sine).astype(bf16),
            grad_values.astype(bf16),
        ],
        axis=0,
    )
    grad_linear = jnp.transpose(grad_linear, (2, 1, 0, 3)).reshape(group_tok, heads_here * 3 * HD)
    grad_first = group_scatter(dot(grad_linear, qkv_full, 1, 1).astype(bf16)).astype(f32)
    grad_qkv = lax.psum_scatter(
        dot(first_group, grad_linear, 0, 0).astype(bf16), "seq", scatter_dimension=0, tiled=True
    )
    grad_out = dot(merged, grad_attn, 0, 0).astype(bf16)
    grad_out = jnp.transpose(grad_out.reshape(-1, n_seq, width // n_seq), (1, 0, 2))
    grad_out = lax.psum_scatter(grad_out, "seq", scatter_dimension=0, tiled=False)
    grad_bias_here = jnp.sum(grad_linear.astype(f32), axis=0).reshape(heads_here, 3 * HD)
    grad_bias = lax.dynamic_update_slice_in_dim(
        jnp.zeros(qkv_bias.shape, f32), grad_bias_here, head * heads_here, 0
    )
    grad_gain_first = jnp.sum(grad_first * normed_first, axis=0)
    grad_normed_first = grad_first * gain_first
    input_grad = grad_middle + scale_first * (
        grad_normed_first
        - normed_first * jnp.mean(grad_normed_first * normed_first, axis=1, keepdims=True)
    )
    totals_first = total_over_all(
        jnp.concatenate([grad_gain_first, grad_bias.reshape(-1)]).reshape(-1, LANES)
    ).reshape(-1)

    grad_upper = grad_upper.astype(bf16).reshape(width, 2, unit_cols)
    grad_lower = grad_lower.astype(bf16)
    send = grad_upper[:, :, :exp_units].reshape(n_head, width // n_head, 2, exp_units)
    send = lax.all_to_all(send, "head", split_axis=0, concat_axis=0)
    grad_upper_e = jnp.transpose(send, (1, 2, 0, 3)).reshape(1, width // n_head, 2 * hidden_all)
    send = jnp.transpose(
        grad_lower[:exp_units].reshape(exp_units, n_head, width // n_head), (1, 0, 2)
    )
    grad_lower_e = lax.all_to_all(send, "head", split_axis=0, concat_axis=0).reshape(
        1, hidden_all, width // n_head
    )
    send = grad_upper[:, :, exp_units:units].reshape(n_seq, width // n_seq, 2, share_units)
    send = lax.all_to_all(send, "seq", split_axis=0, concat_axis=0)
    grad_upper_s = jnp.transpose(send, (1, 2, 0, 3)).reshape(width // n_seq, 2, share_all)
    send = jnp.transpose(
        grad_lower[exp_units:units].reshape(share_units, n_seq, width // n_seq), (1, 0, 2)
    )
    grad_lower_s = lax.all_to_all(send, "seq", split_axis=0, concat_axis=0).reshape(
        share_all, width // n_seq
    )
    return (
        mixed,
        input_grad,
        totals_first[:width],
        grad_qkv.astype(f32).reshape(qkv_weight.shape),
        totals_first[width:].reshape(qkv_bias.shape),
        grad_out.astype(f32),
        totals_second[n_exp + 1],
        totals_second[:n_exp].T,
        totals_second[n_exp],
        grad_upper_s.astype(f32),
        grad_lower_s.astype(f32),
        grad_upper_e.astype(f32),
        grad_lower_e.astype(f32),
    )


def solution(mesh):
    return jax.shard_map(
        shards,
        mesh=mesh,
        in_specs=(
            P(("seq", "head"), None),
            P(("seq", "head"), None),
            P("seq", None),
            P("seq", None),
            P(("seq", "head"), None),
            P(),
            P("seq", "head", None),
            P(),
            P("head", "seq"),
            P(),
            P(),
            P(),
            P("seq", None, "head"),
            P("head", "seq"),
            P("seq", "head", None),
            P("seq", None, "head"),
        ),
        out_specs=(
            P(("seq", "head"), None),
            P(("seq", "head"), None),
            P(),
            P("seq", "head", None),
            P(),
            P("head", "seq"),
            P(),
            P(),
            P(),
            P("seq", None, "head"),
            P("head", "seq"),
            P("seq", "head", None),
            P("seq", None, "head"),
        ),
        check_vma=False,
    )
```

```python
import functools

import jax
import jax.numpy as jnp
from jax import lax
from jax.experimental import pallas as pl
from jax.experimental.pallas import tpu as pltpu
from jax.sharding import PartitionSpec as P

HD = 128
EPS = 1e-06
THETA = 1000000.0
NEGATIVE = -1e30
LANES = 128
TILE = 256
VMEM_BYTES = 60 * 1024 * 1024
bf16 = jnp.bfloat16
f32 = jnp.float32


def rms_scale(values):
    return lax.rsqrt(jnp.mean(values * values, axis=-1, keepdims=True) + EPS)


def rope_tables(position):
    half = HD // 2
    exponent = jnp.arange(half, dtype=f32) * (2.0 / HD)
    frequency = THETA ** (-exponent)
    angle = position[:, None] * frequency[None, :]
    return (jnp.cos(angle), jnp.sin(angle))


def layout_of(arrange_row, length_row, group_tok):
    counter = jnp.arange(group_tok, dtype=jnp.int32)
    place = jnp.sum(
        jnp.where(arrange_row[None, :] == counter[:, None], counter[None, :], 0),
        axis=1,
        dtype=jnp.int32,
    )
    ends = jnp.cumsum(length_row, dtype=jnp.int32)
    starts = ends - length_row
    doc_index = jnp.sum(
        (place[:, None] >= ends[None, :]).astype(jnp.int32), axis=1, dtype=jnp.int32
    )
    picked = doc_index[:, None] == jnp.arange(length_row.shape[0], dtype=jnp.int32)[None, :]
    start_of = jnp.sum(jnp.where(picked, starts[None, :], 0), axis=1, dtype=jnp.int32)
    return (place, doc_index, place - start_of)


def dot(left, right, left_dim, right_dim):
    return lax.dot_general(
        left, right, (((left_dim,), (right_dim,)), ((), ())), preferred_element_type=f32
    )


def swap(block, axis, bit):
    size = lax.axis_size(axis)
    return lax.ppermute(block, axis, [(i, i ^ bit) for i in range(size)])


def bits_of(size):
    bits = []
    bit = 1
    while bit < size:
        bits.append(bit)
        bit *= 2
    return bits


def spread(block, order):
    found = {0: block}
    for bit in order:
        for near in sorted(found):
            found[near ^ bit] = swap(found[near], "head", bit)
    return found


def collect(parts, order):
    parts = dict(parts)
    for bit in reversed(order):
        for far in sorted((r for r in parts if r & bit), reverse=True):
            parts[far ^ bit] = parts[far ^ bit] + swap(parts.pop(far), "head", bit)
    return parts[0]


def group_gather(block):
    order = bits_of(lax.axis_size("head"))
    half = block.shape[0] // 2
    upper = spread(block[:half], order)
    lower = spread(block[half:], order[::-1])
    return jnp.concatenate([piece for r in sorted(upper) for piece in (upper[r], lower[r])], axis=0)


def group_scatter(block):
    n_head = lax.axis_size("head")
    order = bits_of(n_head)
    rows = block.shape[0] // n_head
    half = rows // 2
    upper = {r: block[r * rows : r * rows + half] for r in range(n_head)}
    lower = {r: block[r * rows + half : (r + 1) * rows] for r in range(n_head)}
    return jnp.concatenate([collect(upper, order), collect(lower, order[::-1])], axis=0)


def mesh_part():
    return lax.axis_index("head") // 2


def token_bits():
    return bits_of(lax.axis_size("head"))[1:]


def token_gather(block):
    order = token_bits()
    column = lax.all_gather(block, "seq", axis=0, tiled=True)
    share = column.shape[0] // 2
    half = share // 2
    core = lax.rem(lax.axis_index("seq"), 2)
    own = lax.dynamic_slice_in_dim(column, core * share, share, 0)
    upper = spread(own[:half], order)
    lower = spread(own[half:], order[::-1])
    chunks = [column]
    for r in sorted(upper)[1:]:
        for piece in (upper[r], lower[r]):
            chunks.append(jnp.concatenate([piece, swap(piece, "seq", 1)], axis=0))
    return chunks


def token_scatter(chunks):
    order = token_bits()
    column = chunks[0]
    share = column.shape[0] // 2
    half = share // 2
    core = lax.rem(lax.axis_index("seq"), 2)
    own = lax.dynamic_slice_in_dim(column, core * share, share, 0)
    sides = [{0: own[:half]}, {0: own[half:]}]
    for i, chunk in enumerate(chunks[1:]):
        sides[i % 2][2 * (i // 2 + 1)] = chunk[:half] + swap(chunk[half:], "seq", 1)
    total = jnp.concatenate([collect(sides[0], order), collect(sides[1], order[::-1])], axis=0)
    column = lax.dynamic_update_slice_in_dim(column, total, core * share, 0)
    return lax.psum_scatter(column, "seq", scatter_dimension=0, tiled=True)


def total_over_all(values):
    for axis in ("head", "seq"):
        for bit in bits_of(lax.axis_size(axis)):
            values = values + swap(values, axis, bit)
    return values


def turn(values, cosine, sine):
    return values * cosine + pltpu.roll(values, HD // 2, 1) * sine


def mask_of(layout_col, layout_row):
    doc_col, place_col = layout_col[:, 0:1], layout_col[:, 1:2]
    doc_row, place_row = layout_row[0:1, :], layout_row[1:2, :]
    return jnp.where((doc_col == doc_row) & (place_row <= place_col), 0.0, NEGATIVE)


def attend_kernel(
    first, weight, wout, bias, cosine, sine, layout_col, layout_row,
    qkv, merged, log_total, partial, mask,
):
    n = pl.program_id(0)
    heads = pl.num_programs(0)
    scale = HD ** (-0.5)

    @pl.when(n == 0)
    def _():
        mask[...] = mask_of(layout_col[...], layout_row[...])

    linear = dot(first[...], weight[...], 1, 0) + bias[0]
    cos, sin = cosine[...], sine[...]
    queries = turn(linear[:, :HD], cos, sin).astype(bf16)
    keys = turn(linear[:, HD : 2 * HD], cos, sin).astype(bf16)
    values = linear[:, 2 * HD :].astype(bf16)
    qkv[:, :HD] = queries
    qkv[:, HD : 2 * HD] = keys
    qkv[:, 2 * HD :] = values
    scores = dot(queries, keys, 1, 1) * scale + mask[...]
    largest = jnp.max(scores, axis=1, keepdims=True)
    weights = jnp.exp(scores - largest)
    total = jnp.sum(weights, axis=1, keepdims=True)
    probs = (weights / total).astype(bf16)
    output = dot(probs, values, 1, 0).astype(bf16)
    merged[:, pl.ds(pl.multiple_of(n * HD, HD), HD)] = output
    log_total[0] = jnp.broadcast_to(largest + jnp.log(total), log_total.shape[1:])

    @pl.when(n == heads - 1)
    def _():
        size = weight.shape[0] // lax.axis_size("seq")
        for s in range(partial.shape[1] // size):
            acc = jnp.zeros((partial.shape[0], size), f32)
            for k in range(wout.shape[1] // size):
                acc += dot(
                    merged[:, k * size : (k + 1) * size],
                    wout[s * size : (s + 1) * size, k * size : (k + 1) * size],
                    1,
                    0,
                )
            partial[:, s * size : (s + 1) * size] = acc.astype(bf16)


def attend(first, gathered, bias, cosine, sine, layout_col, layout_row):
    rows, width = first.shape
    heads = bias.shape[0]
    step = 3 * HD
    wide = heads * HD

    def whole(shape):
        return pl.BlockSpec(shape, lambda n: (0,) * len(shape))

    return pl.pallas_call(
        attend_kernel,
        grid=(heads,),
        in_specs=[
            whole((rows, width)),
            pl.BlockSpec((width, step), lambda n: (0, n)),
            pl.BlockSpec((width, wide), lambda n: (0, 3)),
            pl.BlockSpec((1, 1, step), lambda n: (n, 0, 0)),
            whole((rows, HD)),
            whole((rows, HD)),
            whole((rows, 2)),
            whole((2, rows)),
        ],
        out_specs=[
            pl.BlockSpec((rows, step), lambda n: (0, n)),
            whole((rows, wide)),
            pl.BlockSpec((1, rows, LANES), lambda n: (n, 0, 0)),
            whole((rows, width)),
        ],
        out_shape=[
            jax.ShapeDtypeStruct((rows, heads * step), bf16),
            jax.ShapeDtypeStruct((rows, wide), bf16),
            jax.ShapeDtypeStruct((heads, rows, LANES), f32),
            jax.ShapeDtypeStruct((rows, width), bf16),
        ],
        scratch_shapes=[pltpu.VMEM((rows, rows), f32)],
        compiler_params=pltpu.CompilerParams(vmem_limit_bytes=VMEM_BYTES),
        cost_estimate=pl.CostEstimate(
            flops=2 * rows * width * 4 * wide, bytes_accessed=8 * width * wide, transcendentals=0
        ),
        name="attend",
    )(first, gathered, gathered, bias, cosine, sine, layout_col, layout_row)


def attend_back_kernel(
    grad, first, weight, wout, qkv, merged, log_total, cosine, sine, layout_col, layout_row,
    grad_first, grad_weight, grad_bias, mask, grad_merged, acc,
):
    n = pl.program_id(0)
    heads = pl.num_programs(0)
    scale = HD ** (-0.5)
    blocks, _, size = grad_weight.shape
    wide = wout.shape[1]

    @pl.when(n == 0)
    def _():
        mask[...] = mask_of(layout_col[...], layout_row[...])
        acc[...] = jnp.zeros_like(acc)
        for k in range(wide // size):
            total = jnp.zeros((grad.shape[0], size), f32)
            for s in range(blocks):
                total += dot(
                    grad[:, s * size : (s + 1) * size],
                    wout[s * size : (s + 1) * size, k * size : (k + 1) * size],
                    1,
                    1,
                )
            grad_merged[:, k * size : (k + 1) * size] = total.astype(bf16)
        for s in range(blocks):
            grad_weight[s, 3 * wide :, :] = dot(
                merged[...], grad[:, s * size : (s + 1) * size], 0, 0
            ).astype(bf16)

    cos, sin = cosine[...], -sine[...]
    queries, keys, values = qkv[:, :HD], qkv[:, HD : 2 * HD], qkv[:, 2 * HD :]
    grad_out = grad_merged[:, pl.ds(pl.multiple_of(n * HD, HD), HD)]
    scores = dot(queries, keys, 1, 1) * scale + mask[...]
    probs = jnp.exp(scores - log_total[0][:, 0:1])
    grad_values = dot(probs.astype(bf16), grad_out, 0, 0).astype(bf16)
    grad_probs = dot(grad_out, values, 1, 1)
    centre = jnp.sum(probs * grad_probs, axis=1, keepdims=True)
    grad_scores = (probs * (grad_probs - centre)).astype(bf16)
    grad_queries = (dot(grad_scores, keys, 1, 0) * scale).astype(bf16).astype(f32)
    grad_keys = (dot(grad_scores, queries, 0, 0) * scale).astype(bf16).astype(f32)
    grad_linear = jnp.concatenate(
        [turn(grad_queries, cos, sin).astype(bf16), turn(grad_keys, cos, sin).astype(bf16), grad_values],
        axis=1,
    )
    grad_bias[0] = jnp.sum(grad_linear.astype(f32), axis=0, keepdims=True)
    acc[...] += dot(grad_linear, weight[...], 1, 1)
    step = 3 * HD
    for s in range(blocks):
        grad_weight[s, pl.ds(pl.multiple_of(n * step, HD), step), :] = dot(
            grad_linear, first[:, s * size : (s + 1) * size], 0, 0
        ).astype(bf16)

    @pl.when(n == heads - 1)
    def _():
        grad_first[...] = acc[...].astype(bf16)


def attend_back(grad, first, gathered, qkv, merged, log_total, cosine, sine, layout_col, layout_row):
    rows, width = first.shape
    heads = log_total.shape[0]
    step = 3 * HD
    wide = heads * HD
    n_seq = lax.axis_size("seq")
    size = width // n_seq

    def whole(shape):
        return pl.BlockSpec(shape, lambda n: (0,) * len(shape))

    return pl.pallas_call(
        attend_back_kernel,
        grid=(heads,),
        in_specs=[
            whole((rows, width)),
            whole((rows, width)),
            pl.BlockSpec((width, step), lambda n: (0, n)),
            pl.BlockSpec((width, wide), lambda n: (0, 3)),
            pl.BlockSpec((rows, step), lambda n: (0, n)),
            whole((rows, wide)),
            pl.BlockSpec((1, rows, LANES), lambda n: (n, 0, 0)),
            whole((rows, HD)),
            whole((rows, HD)),
            whole((rows, 2)),
            whole((2, rows)),
        ],
        out_specs=[
            whole((rows, width)),
            whole((n_seq, 4 * wide, size)),
            pl.BlockSpec((1, 1, step), lambda n: (n, 0, 0)),
        ],
        out_shape=[
            jax.ShapeDtypeStruct((rows, width), bf16),
            jax.ShapeDtypeStruct((n_seq, 4 * wide, size), bf16),
            jax.ShapeDtypeStruct((heads, 1, step), f32),
        ],
        scratch_shapes=[
            pltpu.VMEM((rows, rows), f32),
            pltpu.VMEM((rows, wide), bf16),
            pltpu.VMEM((rows, width), f32),
        ],
        compiler_params=pltpu.CompilerParams(vmem_limit_bytes=VMEM_BYTES),
        cost_estimate=pl.CostEstimate(
            flops=4 * rows * width * 4 * wide, bytes_accessed=16 * width * wide, transcendentals=0
        ),
        name="attend_back",
    )(grad, first, gathered, gathered, qkv, merged, log_total, cosine, sine, layout_col, layout_row)


def pack_kernel(exp_units, share_units, at, *refs):
    experts, shares = refs[:-5], refs[-5:-3]
    rest, full, sems = refs[-3:]
    head = at[0]
    copies = []
    for r, block in enumerate(experts):
        size = block.shape[2]
        start = pl.multiple_of(jnp.bitwise_xor(head, r) * size, size)
        copies.append(
            pltpu.make_async_copy(
                block, full.at[:, pl.ds(0, exp_units), pl.ds(start, size)], sems.at[len(copies)]
            )
        )
    for r, block in enumerate(shares):
        size = block.shape[3]
        for s in range(block.shape[0]):
            copies.append(
                pltpu.make_async_copy(
                    block.at[s],
                    full.at[:, pl.ds(exp_units + r * share_units, share_units), pl.ds(s * size, size)],
                    sems.at[len(copies)],
                )
            )
    base = exp_units + 2 * share_units
    copies.append(
        pltpu.make_async_copy(rest, full.at[:, pl.ds(base, rest.shape[1]), :], sems.at[len(copies)])
    )
    for copy in copies:
        copy.start()
    for copy in copies:
        copy.wait()


def pack(at, experts, shares, rest, unit_rows):
    exp_units, share_units = experts[0].shape[1], shares[0].shape[2]
    count = len(experts) + 2 * shares[0].shape[0] + 1
    anywhere = pl.BlockSpec(memory_space=pl.ANY)
    return pl.pallas_call(
        functools.partial(pack_kernel, exp_units, share_units),
        in_specs=[pl.BlockSpec(memory_space=pltpu.SMEM)] + [anywhere] * (len(experts) + 3),
        out_specs=anywhere,
        out_shape=jax.ShapeDtypeStruct((3, unit_rows, rest.shape[2]), bf16),
        scratch_shapes=[pltpu.SemaphoreType.DMA((count,))],
        compiler_params=pltpu.CompilerParams(vmem_limit_bytes=1 << 20),
        cost_estimate=pl.CostEstimate(
            flops=0, bytes_accessed=12 * unit_rows * rest.shape[2], transcendentals=0
        ),
        name="pack",
    )(at, *experts, *shares, rest)


def mix_kernel(
    exp_units, base, n_exp, at, second, grad_ext, w_hbm, back, scaled, grad_gate_up, w, sems
):
    i = pl.program_id(0)
    copies = [pltpu.make_async_copy(w_hbm.at[m], w.at[m], sems.at[m]) for m in range(3)]
    seq = at[1]
    rows, width = second.shape
    unit_rows = w.shape[1]

    @pl.when(i == 0)
    def _():
        for copy in copies:
            copy.start()
        copies[0].wait()

    x = second[...]
    gate = dot(x, w[0], 1, 1)

    @pl.when(i == 0)
    def _():
        copies[1].wait()

    up = dot(x, w[1], 1, 1)

    @pl.when(i == 0)
    def _():
        copies[2].wait()

    raw = dot(grad_ext[:, :width], w[2], 1, 1)

    block = base // LANES * LANES
    logits = gate[:, block : block + LANES]
    lane = lax.broadcasted_iota(jnp.int32, (rows, LANES), 1)
    from_base = lane - (base - block)
    is_logit = (from_base >= 0) & (from_base < n_exp)
    largest = jnp.max(jnp.where(is_logit, logits, NEGATIVE), axis=1, keepdims=True)
    powers = jnp.where(is_logit, jnp.exp(jnp.where(is_logit, logits - largest, 0.0)), 0.0)
    chosen = jnp.sum(jnp.where(from_base == seq, powers, 0.0), axis=1, keepdims=True)
    marks = grad_ext[:, width:].astype(f32)
    mark = jnp.sum(jnp.where(lane == seq, marks, 0.0), axis=1, keepdims=True)
    gate_here = mark * chosen / jnp.sum(powers, axis=1, keepdims=True)
    share_gate = jax.nn.sigmoid(
        jnp.sum(jnp.where(from_base == n_exp, logits, 0.0), axis=1, keepdims=True)
    )
    unit = lax.broadcasted_iota(jnp.int32, (rows, unit_rows), 1)
    is_expert = unit < exp_units
    factor = jnp.where(is_expert, gate_here, share_gate)
    sigma = jax.nn.sigmoid(gate)
    silu = gate * sigma
    hidden = silu * up
    scaled[...] = (hidden * factor).astype(bf16)
    both = hidden * raw
    all_sum = jnp.sum(both, axis=1, keepdims=True)
    exp_sum = jnp.sum(jnp.where(is_expert, both, 0.0), axis=1, keepdims=True)
    grad_hidden = raw * factor
    grad_gate = (grad_hidden * up * (sigma + silu * (1.0 - sigma))).astype(bf16)
    grad_up = (grad_hidden * silu).astype(bf16)
    grad_gate_up[0] = grad_gate
    grad_gate_up[1] = grad_up
    back[:, :width] = (dot(grad_gate, w[0], 1, 0) + dot(grad_up, w[1], 1, 0)).astype(bf16)
    back[:, width:] = jnp.where(
        lane == seq, exp_sum * mark, jnp.where(lane == n_exp, all_sum - exp_sum, 0.0)
    ).astype(bf16)


def mix(at, second, grad_ext, full, exp_units, base, n_exp):
    rows, width = second.shape
    unit_rows = full.shape[1]
    wide = grad_ext.shape[1]
    flops = 10 * rows * width * unit_rows
    return pl.pallas_call(
        functools.partial(mix_kernel, exp_units, base, n_exp),
        grid=(rows // TILE,),
        in_specs=[
            pl.BlockSpec(memory_space=pltpu.SMEM),
            pl.BlockSpec((TILE, width), lambda i: (i, 0)),
            pl.BlockSpec((TILE, wide), lambda i: (i, 0)),
            pl.BlockSpec(memory_space=pl.ANY),
        ],
        out_specs=[
            pl.BlockSpec((TILE, wide), lambda i: (i, 0)),
            pl.BlockSpec((TILE, unit_rows), lambda i: (i, 0)),
            pl.BlockSpec((2, TILE, unit_rows), lambda i: (0, i, 0)),
        ],
        out_shape=[
            jax.ShapeDtypeStruct((rows, wide), bf16),
            jax.ShapeDtypeStruct((rows, unit_rows), bf16),
            jax.ShapeDtypeStruct((2, rows, unit_rows), bf16),
        ],
        scratch_shapes=[
            pltpu.VMEM((3, unit_rows, width), bf16),
            pltpu.SemaphoreType.DMA((3,)),
        ],
        compiler_params=pltpu.CompilerParams(vmem_limit_bytes=VMEM_BYTES),
        cost_estimate=pl.CostEstimate(
            flops=flops, bytes_accessed=6 * unit_rows * width + 8 * rows * width, transcendentals=0
        ),
        name="mix",
    )(at, second, grad_ext, full)


def after(value, *others):
    return lax.optimization_barrier((value, *others))[0]


def shards(
    tokens,
    cotangent,
    arrange,
    doc_lengths,
    routes,
    norm1_gain,
    qkv_weight,
    qkv_bias,
    out_weight,
    norm2_gain,
    router_weight,
    shared_gate_vec,
    shared_gate_up,
    shared_down,
    expert_gate_up,
    expert_down,
):
    highest = lax.Precision.HIGHEST
    tok_rows, width = tokens.shape
    n_seq = lax.axis_size("seq")
    n_head = lax.axis_size("head")
    seq = lax.axis_index("seq")
    head = lax.axis_index("head")
    group_tok = tok_rows * n_head
    heads_here = qkv_weight.shape[1]
    n_exp = router_weight.shape[1]
    hidden_all = expert_down.shape[1]
    parts = n_head // 2
    part = mesh_part()
    exp_units = hidden_all // parts
    share_all = shared_down.shape[0]
    share_units = share_all // n_seq
    share_rows = -(-share_units // 16) * 16
    base = exp_units + 2 * share_rows
    unit_rows = -(-(base + n_exp + 1) // LANES) * LANES
    seq_part = width // n_seq
    head_part = width // n_head

    wide = heads_here * HD
    out_blocks = out_weight.reshape(wide // seq_part, seq_part, seq_part)
    out_blocks = jnp.transpose(out_blocks, (1, 0, 2)).reshape(seq_part, wide)
    local = jnp.concatenate([qkv_weight.reshape(seq_part, 3 * wide), out_blocks], axis=1)
    gathered = lax.all_gather(local, "seq", axis=0, tiled=True)

    send = jnp.stack(
        [expert_gate_up[0, :, :hidden_all].T, expert_gate_up[0, :, hidden_all:].T, expert_down[0]]
    )
    experts = {}
    for t in range(parts):
        there = jnp.bitwise_xor(part, t)
        block = lax.dynamic_slice_in_dim(send, there * exp_units, exp_units, 1)
        experts[2 * t] = swap(block, "head", 2 * t) if t else block
    for t in range(parts):
        experts[2 * t + 1] = swap(experts[2 * t], "head", 1)
    send = jnp.stack([shared_gate_up[:, 0].T, shared_gate_up[:, 1].T, shared_down])
    send = jnp.transpose(send.reshape(3, n_seq, share_units, seq_part), (1, 0, 2, 3))
    if share_rows > share_units:
        send = jnp.pad(send, ((0, 0), (0, 0), (0, share_rows - share_units), (0, 0)))
    share_own = lax.all_to_all(send, "seq", split_axis=0, concat_axis=0)
    share_far = swap(share_own, "head", 1)
    gate_rows = jnp.concatenate([router_weight.T, shared_gate_vec[None, :]], axis=0)
    rest = jnp.zeros((3, unit_rows - base, width), bf16).at[0, : n_exp + 1].set(gate_rows)
    at = jnp.stack([head, seq]).astype(jnp.int32)
    full = pack(
        at, [experts[r] for r in range(n_head)], [share_own, share_far], rest, unit_rows
    )

    place, doc_index, position = layout_of(arrange[0], doc_lengths[0], group_tok)
    blocks = jnp.bitwise_xor(head, jnp.arange(n_head, dtype=jnp.int32))
    table = jnp.stack([place, doc_index, position]).reshape(3, n_head, tok_rows)
    place, doc_index, position = jnp.take(table, blocks, axis=1).reshape(3, group_tok)
    layout_row = jnp.stack([doc_index, place])
    layout_col = layout_row.T
    cosine, sine = rope_tables(position.astype(f32))
    cosine = jnp.concatenate([cosine, cosine], axis=1)
    sine = jnp.concatenate([-sine, sine], axis=1)

    stream = tokens.astype(f32)
    gain_first = norm1_gain.astype(f32)
    scale_first = rms_scale(stream)
    normed_first = stream * scale_first
    first_group = group_gather((normed_first * gain_first).astype(bf16))

    bias_here = lax.dynamic_slice_in_dim(qkv_bias, head * heads_here, heads_here, 0)
    qkv, merged, log_total, partial = attend(
        first_group, gathered, bias_here.astype(f32)[:, None, :], cosine, sine, layout_col, layout_row
    )
    attn_out = group_scatter(partial)
    middle = stream + attn_out.astype(f32)
    gain_second = norm2_gain.astype(f32)
    scale_second = rms_scale(middle)
    normed_second = middle * scale_second
    lowered_second = (normed_second * gain_second).astype(bf16)

    expert_ids = jnp.arange(n_exp, dtype=jnp.int32)
    chosen = jnp.any(routes[:, :, None] == expert_ids[None, None, :], axis=1)
    marks = jnp.concatenate(
        [chosen.astype(bf16), jnp.zeros((tok_rows, LANES - n_exp), bf16)], axis=1
    )
    grad_chunks = token_gather(after(jnp.concatenate([cotangent, marks], axis=1), gathered))
    second_chunks = token_gather(lowered_second)

    out_chunks = []
    back_chunks = []
    grad_units = 0.0
    for second, grad_ext in zip(second_chunks, grad_chunks):
        back, scaled, grad_gate_up = mix(at, second, grad_ext, full, exp_units, base, n_exp)
        back_chunks.append(back)
        out_chunks.append(dot(scaled, full[2], 1, 0).astype(bf16))
        grad_units = grad_units + jnp.concatenate(
            [
                dot(grad_gate_up[0], second, 0, 0)[None],
                dot(grad_gate_up[1], second, 0, 0)[None],
                dot(scaled, grad_ext[:, :width], 0, 0)[None],
            ],
            axis=0,
        )
    grad_units = grad_units.astype(bf16)

    back_own = token_scatter(back_chunks).astype(f32)
    out_own = token_scatter(out_chunks).astype(f32)
    mixed = (middle + out_own).astype(bf16)

    logits = dot(lowered_second, gate_rows, 1, 1)
    probs = jax.nn.softmax(logits[:, :n_exp], axis=-1)
    share_gate = jax.nn.sigmoid(logits[:, n_exp:])
    grad_probs = back_own[:, width : width + n_exp]
    grad_logits = probs * (grad_probs - jnp.sum(probs * grad_probs, axis=1, keepdims=True))
    grad_gate_logit = (
        back_own[:, width + n_exp : width + n_exp + 1] * share_gate * (1.0 - share_gate)
    )
    small = jnp.concatenate([grad_logits, grad_gate_logit], axis=1)
    grad_second = back_own[:, :width] + jnp.dot(
        small, gate_rows.astype(f32), precision=highest
    )
    grad_gate_cols = jnp.dot(small.T, lowered_second.astype(f32), precision=highest)
    grad_gain_second = jnp.sum(grad_second * normed_second, axis=0)
    grad_normed = grad_second * gain_second
    grad_middle = cotangent.astype(f32) + scale_second * (
        grad_normed - normed_second * jnp.mean(grad_normed * normed_second, axis=1, keepdims=True)
    )
    totals_second = total_over_all(
        jnp.concatenate([grad_gate_cols, grad_gain_second[None, :]], axis=0)
    )

    grad_attn = group_gather(grad_middle.astype(bf16))
    grad_first, grad_weight, grad_bias_here = attend_back(
        grad_attn, first_group, gathered, qkv, merged, log_total, cosine, sine, layout_col, layout_row
    )
    grad_first = group_scatter(grad_first).astype(f32)
    grad_weight = lax.psum_scatter(grad_weight, "seq", scatter_dimension=0, tiled=False)
    grad_bias = lax.dynamic_update_slice_in_dim(
        jnp.zeros(qkv_bias.shape, f32), grad_bias_here[:, 0], head * heads_here, 0
    )
    grad_gain_first = jnp.sum(grad_first * normed_first, axis=0)
    grad_normed_first = grad_first * gain_first
    input_grad = grad_middle + scale_first * (
        grad_normed_first
        - normed_first * jnp.mean(grad_normed_first * normed_first, axis=1, keepdims=True)
    )
    totals_first = total_over_all(
        jnp.concatenate([grad_gain_first, grad_bias.reshape(-1)]).reshape(-1, LANES)
    ).reshape(-1)

    grad_share = grad_units[:, exp_units + share_rows : exp_units + share_rows + share_units]
    grad_share = grad_units[:, exp_units : exp_units + share_units] + swap(grad_share, "head", 1)
    grad_share = jnp.transpose(grad_share.reshape(3, share_units, n_seq, seq_part), (2, 0, 1, 3))
    grad_share = lax.all_to_all(grad_share, "seq", split_axis=0, concat_axis=0)
    grad_share = jnp.transpose(grad_share, (1, 0, 2, 3)).reshape(3, share_all, seq_part).astype(f32)
    grad_expert = grad_units[:, :exp_units]
    own = {}
    for t in range(parts):
        near, far = (
            lax.dynamic_slice_in_dim(
                grad_expert, jnp.bitwise_xor(head, 2 * t + x) * head_part, head_part, 2
            )
            for x in range(2)
        )
        total = near + swap(far, "head", 1)
        own[t] = swap(total, "head", 2 * t) if t else total
    own = jnp.stack([own[t] for t in range(parts)])
    own = jnp.take(own, jnp.bitwise_xor(part, jnp.arange(parts, dtype=jnp.int32)), axis=0)
    own = jnp.transpose(own, (1, 0, 2, 3)).reshape(3, hidden_all, head_part).astype(f32)
    return (
        mixed,
        input_grad,
        totals_first[:width],
        grad_weight[: 3 * wide].astype(f32).T.reshape(qkv_weight.shape),
        totals_first[width:].reshape(qkv_bias.shape),
        grad_weight[3 * wide :].astype(f32),
        totals_second[n_exp + 1],
        totals_second[:n_exp].T,
        totals_second[n_exp],
        jnp.stack([grad_share[0].T, grad_share[1].T], axis=1),
        grad_share[2],
        jnp.concatenate([own[0].T, own[1].T], axis=1)[None],
        own[2][None],
    )


def solution(mesh):
    return jax.shard_map(
        shards,
        mesh=mesh,
        in_specs=(
            P(("seq", "head"), None),
            P(("seq", "head"), None),
            P("seq", None),
            P("seq", None),
            P(("seq", "head"), None),
            P(),
            P("seq", "head", None),
            P(),
            P("head", "seq"),
            P(),
            P(),
            P(),
            P("seq", None, "head"),
            P("head", "seq"),
            P("seq", "head", None),
            P("seq", None, "head"),
        ),
        out_specs=(
            P(("seq", "head"), None),
            P(("seq", "head"), None),
            P(),
            P("seq", "head", None),
            P(),
            P("head", "seq"),
            P(),
            P(),
            P(),
            P("seq", None, "head"),
            P("head", "seq"),
            P("seq", "head", None),
            P("seq", None, "head"),
        ),
        check_vma=False,
    )
```

```python
import functools

import jax
import jax.numpy as jnp
from jax import lax
from jax.experimental import pallas as pl
from jax.experimental.pallas import tpu as pltpu
from jax.sharding import PartitionSpec as P

HD = 128
EPS = 1e-06
THETA = 1000000.0
NEGATIVE = -1e30
LANES = 128
TILE = 512
VMEM_BYTES = 60 * 1024 * 1024
bf16 = jnp.bfloat16
f32 = jnp.float32


def rms_scale(values):
    return lax.rsqrt(jnp.mean(values * values, axis=-1, keepdims=True) + EPS)


def rope_tables(position):
    half = HD // 2
    exponent = jnp.arange(half, dtype=f32) * (2.0 / HD)
    frequency = THETA ** (-exponent)
    angle = position[:, None] * frequency[None, :]
    return (jnp.cos(angle), jnp.sin(angle))


def layout_of(arrange_row, length_row, group_tok):
    counter = jnp.arange(group_tok, dtype=jnp.int32)
    place = jnp.sum(
        jnp.where(arrange_row[None, :] == counter[:, None], counter[None, :], 0),
        axis=1,
        dtype=jnp.int32,
    )
    ends = jnp.cumsum(length_row, dtype=jnp.int32)
    starts = ends - length_row
    doc_index = jnp.sum(
        (place[:, None] >= ends[None, :]).astype(jnp.int32), axis=1, dtype=jnp.int32
    )
    picked = doc_index[:, None] == jnp.arange(length_row.shape[0], dtype=jnp.int32)[None, :]
    start_of = jnp.sum(jnp.where(picked, starts[None, :], 0), axis=1, dtype=jnp.int32)
    return (place, doc_index, place - start_of)


def dot(left, right, left_dim, right_dim):
    return lax.dot_general(
        left, right, (((left_dim,), (right_dim,)), ((), ())), preferred_element_type=f32
    )


def swap(block, axis, bit):
    size = lax.axis_size(axis)
    return lax.ppermute(block, axis, [(i, i ^ bit) for i in range(size)])


def bits_of(size):
    bits = []
    bit = 1
    while bit < size:
        bits.append(bit)
        bit *= 2
    return bits


def spread(block, order):
    found = {0: block}
    for bit in order:
        for near in sorted(found):
            found[near ^ bit] = swap(found[near], "head", bit)
    return found


def collect(parts, order):
    parts = dict(parts)
    for bit in reversed(order):
        for far in sorted((r for r in parts if r & bit), reverse=True):
            parts[far ^ bit] = parts[far ^ bit] + swap(parts.pop(far), "head", bit)
    return parts[0]


def group_gather(block):
    order = bits_of(lax.axis_size("head"))
    half = block.shape[0] // 2
    upper = spread(block[:half], order)
    lower = spread(block[half:], order[::-1])
    return jnp.concatenate([piece for r in sorted(upper) for piece in (upper[r], lower[r])], axis=0)


def group_scatter(block):
    n_head = lax.axis_size("head")
    order = bits_of(n_head)
    rows = block.shape[0] // n_head
    half = rows // 2
    upper = {r: block[r * rows : r * rows + half] for r in range(n_head)}
    lower = {r: block[r * rows + half : (r + 1) * rows] for r in range(n_head)}
    return jnp.concatenate([collect(upper, order), collect(lower, order[::-1])], axis=0)


def mesh_part():
    return lax.axis_index("head") // 2


def token_bits():
    return bits_of(lax.axis_size("head"))[1:]


def token_gather(block):
    order = token_bits()
    column = lax.all_gather(block, "seq", axis=0, tiled=True)
    share = column.shape[0] // 2
    half = share // 2
    core = lax.rem(lax.axis_index("seq"), 2)
    own = lax.dynamic_slice_in_dim(column, core * share, share, 0)
    upper = spread(own[:half], order)
    lower = spread(own[half:], order[::-1])
    chunks = [column]
    for r in sorted(upper)[1:]:
        for piece in (upper[r], lower[r]):
            chunks.append(jnp.concatenate([piece, swap(piece, "seq", 1)], axis=0))
    return chunks


def token_scatter(chunks):
    order = token_bits()
    column = chunks[0]
    share = column.shape[0] // 2
    half = share // 2
    core = lax.rem(lax.axis_index("seq"), 2)
    own = lax.dynamic_slice_in_dim(column, core * share, share, 0)
    sides = [{0: own[:half]}, {0: own[half:]}]
    for i, chunk in enumerate(chunks[1:]):
        sides[i % 2][2 * (i // 2 + 1)] = chunk[:half] + swap(chunk[half:], "seq", 1)
    total = jnp.concatenate([collect(sides[0], order), collect(sides[1], order[::-1])], axis=0)
    column = lax.dynamic_update_slice_in_dim(column, total, core * share, 0)
    return lax.psum_scatter(column, "seq", scatter_dimension=0, tiled=True)


def total_over_all(values):
    for axis in ("head", "seq"):
        for bit in bits_of(lax.axis_size(axis)):
            values = values + swap(values, axis, bit)
    return values


def turn(values, cosine, sine):
    return values * cosine + pltpu.roll(values, HD // 2, 1) * sine


def mask_of(layout_col, layout_row):
    doc_col, place_col = layout_col[:, 0:1], layout_col[:, 1:2]
    doc_row, place_row = layout_row[0:1, :], layout_row[1:2, :]
    return jnp.where((doc_col == doc_row) & (place_row <= place_col), 0.0, NEGATIVE)


def attend_kernel(
    first, weight, wout, bias, cosine, sine, layout_col, layout_row,
    qkv, merged, log_total, partial, mask,
):
    n = pl.program_id(0)
    heads = pl.num_programs(0)
    scale = HD ** (-0.5)

    @pl.when(n == 0)
    def _():
        mask[...] = mask_of(layout_col[...], layout_row[...])

    linear = dot(first[...], weight[...], 1, 0) + bias[0]
    cos, sin = cosine[...], sine[...]
    queries = turn(linear[:, :HD], cos, sin).astype(bf16)
    keys = turn(linear[:, HD : 2 * HD], cos, sin).astype(bf16)
    values = linear[:, 2 * HD :].astype(bf16)
    qkv[:, :HD] = queries
    qkv[:, HD : 2 * HD] = keys
    qkv[:, 2 * HD :] = values
    scores = dot(queries, keys, 1, 1) * scale + mask[...]
    largest = jnp.max(scores, axis=1, keepdims=True)
    weights = jnp.exp(scores - largest)
    total = jnp.sum(weights, axis=1, keepdims=True)
    probs = (weights / total).astype(bf16)
    output = dot(probs, values, 1, 0).astype(bf16)
    merged[:, pl.ds(pl.multiple_of(n * HD, HD), HD)] = output
    log_total[0] = jnp.broadcast_to(largest + jnp.log(total), log_total.shape[1:])

    @pl.when(n == heads - 1)
    def _():
        size = weight.shape[0] // lax.axis_size("seq")
        for s in range(partial.shape[1] // size):
            acc = jnp.zeros((partial.shape[0], size), f32)
            for k in range(wout.shape[1] // size):
                acc += dot(
                    merged[:, k * size : (k + 1) * size],
                    wout[s * size : (s + 1) * size, k * size : (k + 1) * size],
                    1,
                    0,
                )
            partial[:, s * size : (s + 1) * size] = acc.astype(bf16)


def attend(first, gathered, bias, cosine, sine, layout_col, layout_row):
    rows, width = first.shape
    heads = bias.shape[0]
    step = 3 * HD
    wide = heads * HD

    def whole(shape):
        return pl.BlockSpec(shape, lambda n: (0,) * len(shape))

    return pl.pallas_call(
        attend_kernel,
        grid=(heads,),
        in_specs=[
            whole((rows, width)),
            pl.BlockSpec((width, step), lambda n: (0, n)),
            pl.BlockSpec((width, wide), lambda n: (0, 3)),
            pl.BlockSpec((1, 1, step), lambda n: (n, 0, 0)),
            whole((rows, HD)),
            whole((rows, HD)),
            whole((rows, 2)),
            whole((2, rows)),
        ],
        out_specs=[
            pl.BlockSpec((rows, step), lambda n: (0, n)),
            whole((rows, wide)),
            pl.BlockSpec((1, rows, LANES), lambda n: (n, 0, 0)),
            whole((rows, width)),
        ],
        out_shape=[
            jax.ShapeDtypeStruct((rows, heads * step), bf16),
            jax.ShapeDtypeStruct((rows, wide), bf16),
            jax.ShapeDtypeStruct((heads, rows, LANES), f32),
            jax.ShapeDtypeStruct((rows, width), bf16),
        ],
        scratch_shapes=[pltpu.VMEM((rows, rows), f32)],
        compiler_params=pltpu.CompilerParams(vmem_limit_bytes=VMEM_BYTES),
        cost_estimate=pl.CostEstimate(
            flops=2 * rows * width * 4 * wide, bytes_accessed=8 * width * wide, transcendentals=0
        ),
        name="attend",
    )(first, gathered, gathered, bias, cosine, sine, layout_col, layout_row)


def attend_back_kernel(
    grad, first, weight, wout, qkv, merged, log_total, cosine, sine, layout_col, layout_row,
    grad_first, grad_weight, grad_bias, mask, grad_merged, acc,
):
    n = pl.program_id(0)
    heads = pl.num_programs(0)
    scale = HD ** (-0.5)
    blocks, _, size = grad_weight.shape
    wide = wout.shape[1]

    @pl.when(n == 0)
    def _():
        mask[...] = mask_of(layout_col[...], layout_row[...])
        acc[...] = jnp.zeros_like(acc)
        for k in range(wide // size):
            total = jnp.zeros((grad.shape[0], size), f32)
            for s in range(blocks):
                total += dot(
                    grad[:, s * size : (s + 1) * size],
                    wout[s * size : (s + 1) * size, k * size : (k + 1) * size],
                    1,
                    1,
                )
            grad_merged[:, k * size : (k + 1) * size] = total.astype(bf16)
        for s in range(blocks):
            grad_weight[s, 3 * wide :, :] = dot(
                merged[...], grad[:, s * size : (s + 1) * size], 0, 0
            ).astype(bf16)

    cos, sin = cosine[...], -sine[...]
    queries, keys, values = qkv[:, :HD], qkv[:, HD : 2 * HD], qkv[:, 2 * HD :]
    grad_out = grad_merged[:, pl.ds(pl.multiple_of(n * HD, HD), HD)]
    scores = dot(queries, keys, 1, 1) * scale + mask[...]
    probs = jnp.exp(scores - log_total[0][:, 0:1])
    grad_values = dot(probs.astype(bf16), grad_out, 0, 0).astype(bf16)
    grad_probs = dot(grad_out, values, 1, 1)
    centre = jnp.sum(probs * grad_probs, axis=1, keepdims=True)
    grad_scores = (probs * (grad_probs - centre)).astype(bf16)
    grad_queries = (dot(grad_scores, keys, 1, 0) * scale).astype(bf16).astype(f32)
    grad_keys = (dot(grad_scores, queries, 0, 0) * scale).astype(bf16).astype(f32)
    grad_linear = jnp.concatenate(
        [turn(grad_queries, cos, sin).astype(bf16), turn(grad_keys, cos, sin).astype(bf16), grad_values],
        axis=1,
    )
    grad_bias[0] = jnp.sum(grad_linear.astype(f32), axis=0, keepdims=True)
    acc[...] += dot(grad_linear, weight[...], 1, 1)
    step = 3 * HD
    for s in range(blocks):
        grad_weight[s, pl.ds(pl.multiple_of(n * step, HD), step), :] = dot(
            grad_linear, first[:, s * size : (s + 1) * size], 0, 0
        ).astype(bf16)

    @pl.when(n == heads - 1)
    def _():
        grad_first[...] = acc[...].astype(bf16)


def attend_back(grad, first, gathered, qkv, merged, log_total, cosine, sine, layout_col, layout_row):
    rows, width = first.shape
    heads = log_total.shape[0]
    step = 3 * HD
    wide = heads * HD
    n_seq = lax.axis_size("seq")
    size = width // n_seq

    def whole(shape):
        return pl.BlockSpec(shape, lambda n: (0,) * len(shape))

    return pl.pallas_call(
        attend_back_kernel,
        grid=(heads,),
        in_specs=[
            whole((rows, width)),
            whole((rows, width)),
            pl.BlockSpec((width, step), lambda n: (0, n)),
            pl.BlockSpec((width, wide), lambda n: (0, 3)),
            pl.BlockSpec((rows, step), lambda n: (0, n)),
            whole((rows, wide)),
            pl.BlockSpec((1, rows, LANES), lambda n: (n, 0, 0)),
            whole((rows, HD)),
            whole((rows, HD)),
            whole((rows, 2)),
            whole((2, rows)),
        ],
        out_specs=[
            whole((rows, width)),
            whole((n_seq, 4 * wide, size)),
            pl.BlockSpec((1, 1, step), lambda n: (n, 0, 0)),
        ],
        out_shape=[
            jax.ShapeDtypeStruct((rows, width), bf16),
            jax.ShapeDtypeStruct((n_seq, 4 * wide, size), bf16),
            jax.ShapeDtypeStruct((heads, 1, step), f32),
        ],
        scratch_shapes=[
            pltpu.VMEM((rows, rows), f32),
            pltpu.VMEM((rows, wide), bf16),
            pltpu.VMEM((rows, width), f32),
        ],
        compiler_params=pltpu.CompilerParams(vmem_limit_bytes=VMEM_BYTES),
        cost_estimate=pl.CostEstimate(
            flops=4 * rows * width * 4 * wide, bytes_accessed=16 * width * wide, transcendentals=0
        ),
        name="attend_back",
    )(grad, first, gathered, gathered, qkv, merged, log_total, cosine, sine, layout_col, layout_row)


def pack_kernel(exp_units, share_units, at, *refs):
    experts, shares = refs[:-5], refs[-5:-3]
    rest, full, sems = refs[-3:]
    head = at[0]
    copies = []
    for r, block in enumerate(experts):
        size = block.shape[2]
        start = pl.multiple_of(jnp.bitwise_xor(head, r) * size, size)
        copies.append(
            pltpu.make_async_copy(
                block, full.at[:, pl.ds(0, exp_units), pl.ds(start, size)], sems.at[len(copies)]
            )
        )
    for r, block in enumerate(shares):
        size = block.shape[3]
        for s in range(block.shape[0]):
            copies.append(
                pltpu.make_async_copy(
                    block.at[s],
                    full.at[:, pl.ds(exp_units + r * share_units, share_units), pl.ds(s * size, size)],
                    sems.at[len(copies)],
                )
            )
    base = exp_units + 2 * share_units
    copies.append(
        pltpu.make_async_copy(rest, full.at[:, pl.ds(base, rest.shape[1]), :], sems.at[len(copies)])
    )
    for copy in copies:
        copy.start()
    for copy in copies:
        copy.wait()


def pack(at, experts, shares, rest, unit_rows):
    exp_units, share_units = experts[0].shape[1], shares[0].shape[2]
    count = len(experts) + 2 * shares[0].shape[0] + 1
    anywhere = pl.BlockSpec(memory_space=pl.ANY)
    return pl.pallas_call(
        functools.partial(pack_kernel, exp_units, share_units),
        in_specs=[pl.BlockSpec(memory_space=pltpu.SMEM)] + [anywhere] * (len(experts) + 3),
        out_specs=anywhere,
        out_shape=jax.ShapeDtypeStruct((3, unit_rows, rest.shape[2]), bf16),
        scratch_shapes=[pltpu.SemaphoreType.DMA((count,))],
        compiler_params=pltpu.CompilerParams(vmem_limit_bytes=1 << 20),
        cost_estimate=pl.CostEstimate(
            flops=0, bytes_accessed=12 * unit_rows * rest.shape[2], transcendentals=0
        ),
        name="pack",
    )(at, *experts, *shares, rest)


def mix_kernel(
    exp_units, base, n_exp, at, second, grad_ext, w_hbm, back, unit_out, w, sems
):
    i = pl.program_id(0)
    copies = [pltpu.make_async_copy(w_hbm.at[m], w.at[m], sems.at[m]) for m in range(3)]
    seq = at[1]
    rows, width = second.shape
    unit_rows = w.shape[1]

    @pl.when(i == 0)
    def _():
        for copy in copies:
            copy.start()
        copies[0].wait()

    x = second[...]
    gate = dot(x, w[0], 1, 1)

    @pl.when(i == 0)
    def _():
        copies[1].wait()

    up = dot(x, w[1], 1, 1)

    @pl.when(i == 0)
    def _():
        copies[2].wait()

    raw = dot(grad_ext[:, :width], w[2], 1, 1)

    block = base // LANES * LANES
    logits = gate[:, block : block + LANES]
    lane = lax.broadcasted_iota(jnp.int32, (rows, LANES), 1)
    from_base = lane - (base - block)
    is_logit = (from_base >= 0) & (from_base < n_exp)
    largest = jnp.max(jnp.where(is_logit, logits, NEGATIVE), axis=1, keepdims=True)
    powers = jnp.where(is_logit, jnp.exp(jnp.where(is_logit, logits - largest, 0.0)), 0.0)
    chosen = jnp.sum(jnp.where(from_base == seq, powers, 0.0), axis=1, keepdims=True)
    marks = grad_ext[:, width:].astype(f32)
    mark = jnp.sum(jnp.where(lane == seq, marks, 0.0), axis=1, keepdims=True)
    gate_here = mark * chosen / jnp.sum(powers, axis=1, keepdims=True)
    share_gate = jax.nn.sigmoid(
        jnp.sum(jnp.where(from_base == n_exp, logits, 0.0), axis=1, keepdims=True)
    )
    unit = lax.broadcasted_iota(jnp.int32, (rows, unit_rows), 1)
    is_expert = unit < exp_units
    factor = jnp.where(is_expert, gate_here, share_gate)
    sigma = jax.nn.sigmoid(gate)
    silu = gate * sigma
    hidden = silu * up
    unit_out[2] = (hidden * factor).astype(bf16)
    both = hidden * raw
    all_sum = jnp.sum(both, axis=1, keepdims=True)
    exp_sum = jnp.sum(jnp.where(is_expert, both, 0.0), axis=1, keepdims=True)
    grad_hidden = raw * factor
    grad_gate = (grad_hidden * up * (sigma + silu * (1.0 - sigma))).astype(bf16)
    grad_up = (grad_hidden * silu).astype(bf16)
    unit_out[0] = grad_gate
    unit_out[1] = grad_up
    back[:, :width] = (dot(grad_gate, w[0], 1, 0) + dot(grad_up, w[1], 1, 0)).astype(bf16)
    back[:, width:] = jnp.where(
        lane == seq, exp_sum * mark, jnp.where(lane == n_exp, all_sum - exp_sum, 0.0)
    ).astype(bf16)


def mix(at, second, grad_ext, full, exp_units, base, n_exp):
    rows, width = second.shape
    unit_rows = full.shape[1]
    wide = grad_ext.shape[1]
    flops = 10 * rows * width * unit_rows
    return pl.pallas_call(
        functools.partial(mix_kernel, exp_units, base, n_exp),
        grid=(rows // TILE,),
        in_specs=[
            pl.BlockSpec(memory_space=pltpu.SMEM),
            pl.BlockSpec((TILE, width), lambda i: (i, 0)),
            pl.BlockSpec((TILE, wide), lambda i: (i, 0)),
            pl.BlockSpec(memory_space=pl.ANY),
        ],
        out_specs=[
            pl.BlockSpec((TILE, wide), lambda i: (i, 0)),
            pl.BlockSpec((3, TILE, unit_rows), lambda i: (0, i, 0)),
        ],
        out_shape=[
            jax.ShapeDtypeStruct((rows, wide), bf16),
            jax.ShapeDtypeStruct((3, rows, unit_rows), bf16),
        ],
        scratch_shapes=[
            pltpu.VMEM((3, unit_rows, width), bf16),
            pltpu.SemaphoreType.DMA((3,)),
        ],
        compiler_params=pltpu.CompilerParams(vmem_limit_bytes=VMEM_BYTES),
        cost_estimate=pl.CostEstimate(
            flops=flops, bytes_accessed=6 * unit_rows * width + 8 * rows * width, transcendentals=0
        ),
        name="mix",
    )(at, second, grad_ext, full)


def unit_grads_kernel(count, exp_units, share_rows, at, *refs):
    units, seconds, grads = refs[:count], refs[count : 2 * count], refs[2 * count : 3 * count]
    experts, share_own, share_far = refs[3 * count :]
    m = pl.program_id(0)

    def run(rights):
        acc = dot(units[0][0], rights[0][...], 0, 0)
        for left, right in zip(units[1:], rights[1:]):
            acc += dot(left[0], right[...], 0, 0)
        experts[0, 0] = acc[:exp_units].astype(bf16)
        size = share_own.shape[3]
        for s in range(share_own.shape[0]):
            piece = acc[exp_units : exp_units + 2 * share_rows, s * size : (s + 1) * size].astype(bf16)
            share_own[s, 0] = piece[:share_rows]
            share_far[s, 0] = piece[share_rows:]

    @pl.when(m < 2)
    def _():
        run(seconds)

    @pl.when(m == 2)
    def _():
        run(grads)


def unit_grads(at, units, seconds, grads, exp_units, share_rows):
    n_head, n_seq = lax.axis_size("head"), lax.axis_size("seq")
    width = seconds[0].shape[1]
    unit_rows = units[0].shape[2]
    head_part, seq_part = width // n_head, width // n_seq
    near = n_seq // n_head
    rows = sum(block.shape[0] for block in seconds)

    def far(r, at):
        return jnp.bitwise_xor(at[0], r)

    in_specs = [
        pl.BlockSpec((1, block.shape[1], unit_rows), lambda m, r, at: (m, 0, 0)) for block in units
    ]
    in_specs += [
        pl.BlockSpec(
            (block.shape[0], head_part), lambda m, r, at: (0, jnp.where(m < 2, far(r, at), far(n_head - 1, at)))
        )
        for block in seconds
    ]
    in_specs += [
        pl.BlockSpec(
            (block.shape[0], head_part), lambda m, r, at: (0, jnp.where(m < 2, far(0, at), far(r, at)))
        )
        for block in grads
    ]
    share_spec = pl.BlockSpec((near, 1, share_rows, seq_part), lambda m, r, at: (far(r, at), m, 0, 0))
    share_shape = jax.ShapeDtypeStruct((n_seq, 3, share_rows, seq_part), bf16)
    return pl.pallas_call(
        functools.partial(unit_grads_kernel, len(units), exp_units, share_rows),
        grid_spec=pltpu.PrefetchScalarGridSpec(
            num_scalar_prefetch=1,
            grid=(3, n_head),
            in_specs=in_specs,
            out_specs=[
                pl.BlockSpec((1, 1, exp_units, head_part), lambda m, r, at: (r, m, 0, 0)),
                share_spec,
                share_spec,
            ],
        ),
        out_shape=[
            jax.ShapeDtypeStruct((n_head, 3, exp_units, head_part), bf16),
            share_shape,
            share_shape,
        ],
        compiler_params=pltpu.CompilerParams(vmem_limit_bytes=VMEM_BYTES),
        cost_estimate=pl.CostEstimate(
            flops=6 * rows * width * unit_rows,
            bytes_accessed=6 * rows * unit_rows + 8 * rows * width + 6 * width * unit_rows,
            transcendentals=0,
        ),
        name="unit_grads",
    )(at, *units, *seconds, *grads)


def after(value, *others):
    return lax.optimization_barrier((value, *others))[0]


def shards(
    tokens,
    cotangent,
    arrange,
    doc_lengths,
    routes,
    norm1_gain,
    qkv_weight,
    qkv_bias,
    out_weight,
    norm2_gain,
    router_weight,
    shared_gate_vec,
    shared_gate_up,
    shared_down,
    expert_gate_up,
    expert_down,
):
    highest = lax.Precision.HIGHEST
    tok_rows, width = tokens.shape
    n_seq = lax.axis_size("seq")
    n_head = lax.axis_size("head")
    seq = lax.axis_index("seq")
    head = lax.axis_index("head")
    group_tok = tok_rows * n_head
    heads_here = qkv_weight.shape[1]
    n_exp = router_weight.shape[1]
    hidden_all = expert_down.shape[1]
    parts = n_head // 2
    part = mesh_part()
    exp_units = hidden_all // parts
    share_all = shared_down.shape[0]
    share_units = share_all // n_seq
    share_rows = -(-share_units // 16) * 16
    base = exp_units + 2 * share_rows
    unit_rows = -(-(base + n_exp + 1) // LANES) * LANES
    seq_part = width // n_seq
    head_part = width // n_head

    wide = heads_here * HD
    out_blocks = out_weight.reshape(wide // seq_part, seq_part, seq_part)
    out_blocks = jnp.transpose(out_blocks, (1, 0, 2)).reshape(seq_part, wide)
    local = jnp.concatenate([qkv_weight.reshape(seq_part, 3 * wide), out_blocks], axis=1)
    gathered = lax.all_gather(local, "seq", axis=0, tiled=True)

    send = jnp.stack(
        [expert_gate_up[0, :, :hidden_all].T, expert_gate_up[0, :, hidden_all:].T, expert_down[0]]
    )
    experts = {}
    for t in range(parts):
        there = jnp.bitwise_xor(part, t)
        block = lax.dynamic_slice_in_dim(send, there * exp_units, exp_units, 1)
        experts[2 * t] = swap(block, "head", 2 * t) if t else block
    for t in range(parts):
        experts[2 * t + 1] = swap(experts[2 * t], "head", 1)
    send = jnp.stack([shared_gate_up[:, 0].T, shared_gate_up[:, 1].T, shared_down])
    send = jnp.transpose(send.reshape(3, n_seq, share_units, seq_part), (1, 0, 2, 3))
    if share_rows > share_units:
        send = jnp.pad(send, ((0, 0), (0, 0), (0, share_rows - share_units), (0, 0)))
    share_own = lax.all_to_all(send, "seq", split_axis=0, concat_axis=0)
    share_far = swap(share_own, "head", 1)
    gate_rows = jnp.concatenate([router_weight.T, shared_gate_vec[None, :]], axis=0)
    rest = jnp.zeros((3, unit_rows - base, width), bf16).at[0, : n_exp + 1].set(gate_rows)
    at = jnp.stack([head, seq]).astype(jnp.int32)
    full = pack(
        at, [experts[r] for r in range(n_head)], [share_own, share_far], rest, unit_rows
    )

    place, doc_index, position = layout_of(arrange[0], doc_lengths[0], group_tok)
    blocks = jnp.bitwise_xor(head, jnp.arange(n_head, dtype=jnp.int32))
    table = jnp.stack([place, doc_index, position]).reshape(3, n_head, tok_rows)
    place, doc_index, position = jnp.take(table, blocks, axis=1).reshape(3, group_tok)
    layout_row = jnp.stack([doc_index, place])
    layout_col = layout_row.T
    cosine, sine = rope_tables(position.astype(f32))
    cosine = jnp.concatenate([cosine, cosine], axis=1)
    sine = jnp.concatenate([-sine, sine], axis=1)

    stream = tokens.astype(f32)
    gain_first = norm1_gain.astype(f32)
    scale_first = rms_scale(stream)
    normed_first = stream * scale_first
    first_group = group_gather((normed_first * gain_first).astype(bf16))
    gathered = after(gathered, first_group, experts[1], experts[2], share_own)

    bias_here = lax.dynamic_slice_in_dim(qkv_bias, head * heads_here, heads_here, 0)
    qkv, merged, log_total, partial = attend(
        first_group, gathered, bias_here.astype(f32)[:, None, :], cosine, sine, layout_col, layout_row
    )
    attn_out = group_scatter(partial)
    middle = stream + attn_out.astype(f32)
    gain_second = norm2_gain.astype(f32)
    scale_second = rms_scale(middle)
    normed_second = middle * scale_second
    lowered_second = (normed_second * gain_second).astype(bf16)

    expert_ids = jnp.arange(n_exp, dtype=jnp.int32)
    chosen = jnp.any(routes[:, :, None] == expert_ids[None, None, :], axis=1)
    marks = jnp.concatenate(
        [chosen.astype(bf16), jnp.zeros((tok_rows, LANES - n_exp), bf16)], axis=1
    )
    grad_chunks = token_gather(after(jnp.concatenate([cotangent, marks], axis=1), gathered))
    second_chunks = token_gather(after(lowered_second, experts[3]))

    second_chunks[0] = after(second_chunks[0], *grad_chunks)
    back_chunks = []
    unit_chunks = []
    for second, grad_ext in zip(second_chunks, grad_chunks):
        if back_chunks:
            second = after(second, back_chunks[-1])
        back, units = mix(at, second, grad_ext, full, exp_units, base, n_exp)
        back_chunks.append(back)
        unit_chunks.append(units)
    grad_experts, grad_share, grad_share_far = unit_grads(
        at, unit_chunks, second_chunks, grad_chunks, exp_units, share_rows
    )
    out_chunks = [dot(units[2], full[2], 1, 0).astype(bf16) for units in unit_chunks]

    back_own = after(token_scatter(back_chunks), grad_experts, *out_chunks).astype(f32)
    out_own = token_scatter(out_chunks).astype(f32)
    mixed = (middle + out_own).astype(bf16)

    logits = dot(lowered_second, gate_rows, 1, 1)
    probs = jax.nn.softmax(logits[:, :n_exp], axis=-1)
    share_gate = jax.nn.sigmoid(logits[:, n_exp:])
    grad_probs = back_own[:, width : width + n_exp]
    grad_logits = probs * (grad_probs - jnp.sum(probs * grad_probs, axis=1, keepdims=True))
    grad_gate_logit = (
        back_own[:, width + n_exp : width + n_exp + 1] * share_gate * (1.0 - share_gate)
    )
    small = jnp.concatenate([grad_logits, grad_gate_logit], axis=1)
    grad_second = back_own[:, :width] + jnp.dot(
        small, gate_rows.astype(f32), precision=highest
    )
    grad_gate_cols = jnp.dot(small.T, lowered_second.astype(f32), precision=highest)
    grad_gain_second = jnp.sum(grad_second * normed_second, axis=0)
    grad_normed = grad_second * gain_second
    grad_middle = cotangent.astype(f32) + scale_second * (
        grad_normed - normed_second * jnp.mean(grad_normed * normed_second, axis=1, keepdims=True)
    )
    totals_second = total_over_all(
        jnp.concatenate([grad_gate_cols, grad_gain_second[None, :]], axis=0)
    )

    grad_attn = group_gather(grad_middle.astype(bf16))
    grad_first, grad_weight, grad_bias_here = attend_back(
        grad_attn, first_group, gathered, qkv, merged, log_total, cosine, sine, layout_col, layout_row
    )
    grad_first = group_scatter(grad_first).astype(f32)
    grad_weight = lax.psum_scatter(grad_weight, "seq", scatter_dimension=0, tiled=False)
    grad_bias = lax.dynamic_update_slice_in_dim(
        jnp.zeros(qkv_bias.shape, f32), grad_bias_here[:, 0], head * heads_here, 0
    )
    grad_gain_first = jnp.sum(grad_first * normed_first, axis=0)
    grad_normed_first = grad_first * gain_first
    input_grad = grad_middle + scale_first * (
        grad_normed_first
        - normed_first * jnp.mean(grad_normed_first * normed_first, axis=1, keepdims=True)
    )
    totals_first = total_over_all(
        jnp.concatenate([grad_gain_first, grad_bias.reshape(-1)]).reshape(-1, LANES)
    ).reshape(-1)

    grad_share = grad_share + swap(grad_share_far, "head", 1)
    grad_share = lax.all_to_all(grad_share[:, :, :share_units], "seq", split_axis=0, concat_axis=0)
    grad_share = jnp.transpose(grad_share, (1, 0, 2, 3)).reshape(3, share_all, seq_part).astype(f32)
    own = {}
    for t in range(parts)[::-1]:
        total = grad_experts[2 * t] + swap(grad_experts[2 * t + 1], "head", 1)
        own[t] = swap(total, "head", 2 * t) if t else total
    own = jnp.stack([own[t] for t in range(parts)])
    own = jnp.take(own, jnp.bitwise_xor(part, jnp.arange(parts, dtype=jnp.int32)), axis=0)
    own = jnp.transpose(own, (1, 0, 2, 3)).reshape(3, hidden_all, head_part).astype(f32)
    return (
        mixed,
        input_grad,
        totals_first[:width],
        grad_weight[: 3 * wide].astype(f32).T.reshape(qkv_weight.shape),
        totals_first[width:].reshape(qkv_bias.shape),
        grad_weight[3 * wide :].astype(f32),
        totals_second[n_exp + 1],
        totals_second[:n_exp].T,
        totals_second[n_exp],
        jnp.stack([grad_share[0].T, grad_share[1].T], axis=1),
        grad_share[2],
        jnp.concatenate([own[0].T, own[1].T], axis=1)[None],
        own[2][None],
    )


def solution(mesh):
    return jax.shard_map(
        shards,
        mesh=mesh,
        in_specs=(
            P(("seq", "head"), None),
            P(("seq", "head"), None),
            P("seq", None),
            P("seq", None),
            P(("seq", "head"), None),
            P(),
            P("seq", "head", None),
            P(),
            P("head", "seq"),
            P(),
            P(),
            P(),
            P("seq", None, "head"),
            P("head", "seq"),
            P("seq", "head", None),
            P("seq", None, "head"),
        ),
        out_specs=(
            P(("seq", "head"), None),
            P(("seq", "head"), None),
            P(),
            P("seq", "head", None),
            P(),
            P("head", "seq"),
            P(),
            P(),
            P(),
            P("seq", None, "head"),
            P("head", "seq"),
            P("seq", "head", None),
            P("seq", None, "head"),
        ),
        check_vma=False,
    )
```

```python
import functools

import jax
import jax.numpy as jnp
from jax import lax
from jax.experimental import pallas as pl
from jax.experimental.pallas import tpu as pltpu
from jax.sharding import PartitionSpec as P

HD = 128
EPS = 1e-06
THETA = 1000000.0
NEGATIVE = -1e30
LANES = 128
TILE = 256
MESH = pl.DeviceIdType.MESH
VMEM_BYTES = 60 * 1024 * 1024
bf16 = jnp.bfloat16
f32 = jnp.float32


def rms_scale(values):
    return lax.rsqrt(jnp.mean(values * values, axis=-1, keepdims=True) + EPS)


def rope_tables(position):
    half = HD // 2
    exponent = jnp.arange(half, dtype=f32) * (2.0 / HD)
    frequency = THETA ** (-exponent)
    angle = position[:, None] * frequency[None, :]
    return (jnp.cos(angle), jnp.sin(angle))


def layout_of(arrange_row, length_row, group_tok):
    counter = jnp.arange(group_tok, dtype=jnp.int32)
    place = jnp.sum(
        jnp.where(arrange_row[None, :] == counter[:, None], counter[None, :], 0),
        axis=1,
        dtype=jnp.int32,
    )
    ends = jnp.cumsum(length_row, dtype=jnp.int32)
    starts = ends - length_row
    doc_index = jnp.sum(
        (place[:, None] >= ends[None, :]).astype(jnp.int32), axis=1, dtype=jnp.int32
    )
    picked = doc_index[:, None] == jnp.arange(length_row.shape[0], dtype=jnp.int32)[None, :]
    start_of = jnp.sum(jnp.where(picked, starts[None, :], 0), axis=1, dtype=jnp.int32)
    return (place, doc_index, place - start_of)


def dot(left, right, left_dim, right_dim):
    return lax.dot_general(
        left, right, (((left_dim,), (right_dim,)), ((), ())), preferred_element_type=f32
    )


def swap(block, axis, bit):
    size = lax.axis_size(axis)
    return lax.ppermute(block, axis, [(i, i ^ bit) for i in range(size)])


def bits_of(size):
    bits = []
    bit = 1
    while bit < size:
        bits.append(bit)
        bit *= 2
    return bits


def spread(block, order):
    found = {0: block}
    for bit in order:
        for near in sorted(found):
            found[near ^ bit] = swap(found[near], "head", bit)
    return found


def collect(parts, order):
    parts = dict(parts)
    for bit in reversed(order):
        for far in sorted((r for r in parts if r & bit), reverse=True):
            parts[far ^ bit] = parts[far ^ bit] + swap(parts.pop(far), "head", bit)
    return parts[0]


def shift(block, axis, step):
    size = lax.axis_size(axis)
    return lax.ppermute(block, axis, [((i + step) % size, i) for i in range(size)])


def group_gather(block):
    size = lax.axis_size("head")
    return jnp.concatenate([block] + [shift(block, "head", r) for r in range(1, size)], axis=0)


def group_scatter(block):
    size = lax.axis_size("head")
    rows = block.shape[0] // size
    total = block[:rows].astype(f32)
    for r in range(1, size):
        total += shift(block[r * rows : (r + 1) * rows], "head", size - r).astype(f32)
    return total


def remote(src, dst, send_sem, recv_sem, **place):
    return pltpu.make_async_remote_copy(
        src_ref=src,
        dst_ref=dst,
        send_sem=send_sem,
        recv_sem=recv_sem,
        device_id=place,
        device_id_type=MESH,
    )


def greet(places):
    barrier = pltpu.get_barrier_semaphore()
    for place in places:
        pl.semaphore_signal(barrier, inc=1, device_id=place, device_id_type=MESH)
    pl.semaphore_wait(barrier, len(places))


def plane_places():
    head, seq = lax.axis_index("head"), lax.axis_index("seq")
    x, y = head % 2, head // 2
    return y * 2 + (1 - x), (1 - y) * 2 + x, seq + 1 - 2 * (seq % 2)


def ring_places():
    size = lax.axis_size("head")
    head = lax.axis_index("head")
    return [(head + r) % size for r in range(size)]


def front_kernel(rows, blocks, group, experts, sems_a, sems_b, local):
    head = lax.axis_index("head")
    size = lax.axis_size("head")
    y = head // 2
    units = experts.shape[2]
    near_x, near_y, _ = plane_places()
    peers = ring_places()
    greet([{"head": peer} for peer in peers[1:]])
    copies = [
        remote(rows, group.at[r], sems_a.at[r], sems_b.at[r], head=peers[size - r])
        for r in range(1, size)
    ]
    mine = pl.ds(pl.multiple_of(y * units, 16), units)
    other = pl.ds(pl.multiple_of((1 - y) * units, 16), units)
    ups, sides, ons = [], [], []
    for m in range(3):
        ups.append(
            remote(blocks.at[m, other], experts.at[2, m], sems_a.at[4 + m], sems_b.at[4 + m], head=near_y)
        )
        sides.append(
            remote(blocks.at[m, mine], experts.at[1, m], sems_a.at[7 + m], sems_b.at[7 + m], head=near_x)
        )
        ons.append(
            remote(
                experts.at[2, m], experts.at[3, m], sems_a.at[10 + m], sems_b.at[10 + m], head=near_x
            )
        )
    for copy in copies + [c for pair in zip(ups, sides) for c in pair]:
        copy.start()
    keep = [
        pltpu.make_async_copy(rows, group.at[0], local.at[0]),
        pltpu.make_async_copy(blocks.at[:, mine], experts.at[0], local.at[1]),
    ]
    for copy in keep:
        copy.start()
    for m in range(3):
        ups[m].wait_recv()
        ons[m].start()
    for copy in keep:
        copy.wait()
    for copy in copies + sides + ons:
        copy.wait()
    for copy in ups:
        copy.wait_send()


def front(rows, blocks):
    n_head = lax.axis_size("head")
    anywhere = pl.BlockSpec(memory_space=pl.ANY)
    return pl.pallas_call(
        front_kernel,
        in_specs=[anywhere, anywhere],
        out_specs=[anywhere, anywhere],
        out_shape=[
            jax.ShapeDtypeStruct((n_head, *rows.shape), bf16),
            jax.ShapeDtypeStruct((4, 3, blocks.shape[1] // 2, blocks.shape[2]), bf16),
        ],
        scratch_shapes=[
            pltpu.SemaphoreType.DMA((13,)),
            pltpu.SemaphoreType.DMA((13,)),
            pltpu.SemaphoreType.DMA((2,)),
        ],
        compiler_params=pltpu.CompilerParams(
            collective_id=0, has_side_effects=True, vmem_limit_bytes=1 << 20
        ),
        cost_estimate=pl.CostEstimate(flops=0, bytes_accessed=1 << 28, transcendentals=0),
        name="front",
    )(rows, blocks)


def relay_kernel(pieces, column, share, both, share_far, sems_a, sems_b, local):
    near_x, near_y, near_core = plane_places()
    core = lax.axis_index("seq") % 2
    greet([{"head": near_x}, {"head": near_y}, {"seq": near_core}])
    half = column.shape[0] // 2
    rows = half // pieces
    ups, ons = [], []
    for j in range(pieces):
        at = pl.ds(pl.multiple_of(core * half + j * rows, 16), rows)
        ups.append(remote(column.at[at], both.at[1, at], sems_a.at[j], sems_b.at[j], head=near_y))
        k = pieces + j
        ons.append(remote(both.at[1, at], both.at[1, at], sems_a.at[k], sems_b.at[k], seq=near_core))
    k = 2 * pieces
    side = remote(share, share_far, sems_a.at[k], sems_b.at[k], head=near_x)
    keep = pltpu.make_async_copy(column, both.at[0], local)
    for copy in ups:
        copy.start()
    side.start()
    keep.start()
    for up, on in zip(ups, ons):
        up.wait_recv()
        on.start()
    keep.wait()
    side.wait()
    for copy in ons:
        copy.wait()
    for copy in ups:
        copy.wait_send()


def relay(column, share):
    pieces = 4
    anywhere = pl.BlockSpec(memory_space=pl.ANY)
    return pl.pallas_call(
        functools.partial(relay_kernel, pieces),
        in_specs=[anywhere, anywhere],
        out_specs=[anywhere, anywhere],
        out_shape=[
            jax.ShapeDtypeStruct((2, *column.shape), bf16),
            jax.ShapeDtypeStruct(share.shape, bf16),
        ],
        scratch_shapes=[
            pltpu.SemaphoreType.DMA((2 * pieces + 1,)),
            pltpu.SemaphoreType.DMA((2 * pieces + 1,)),
            pltpu.SemaphoreType.DMA,
        ],
        compiler_params=pltpu.CompilerParams(
            collective_id=1, has_side_effects=True, vmem_limit_bytes=1 << 20
        ),
        cost_estimate=pl.CostEstimate(flops=0, bytes_accessed=1 << 27, transcendentals=0),
        name="relay",
    )(column, share)


def mesh_part():
    return lax.axis_index("head") // 2


def token_bits():
    return bits_of(lax.axis_size("head"))[1:]


def token_gather(block):
    order = token_bits()
    column = lax.all_gather(block, "seq", axis=0, tiled=True)
    share = column.shape[0] // 2
    half = share // 2
    core = lax.rem(lax.axis_index("seq"), 2)
    own = lax.dynamic_slice_in_dim(column, core * share, share, 0)
    upper = spread(own[:half], order)
    lower = spread(own[half:], order[::-1])
    chunks = [column]
    for r in sorted(upper)[1:]:
        for piece in (upper[r], lower[r]):
            chunks.append(jnp.concatenate([piece, swap(piece, "seq", 1)], axis=0))
    return chunks


def token_scatter(chunks):
    order = token_bits()
    column = chunks[0]
    share = column.shape[0] // 2
    half = share // 2
    core = lax.rem(lax.axis_index("seq"), 2)
    own = lax.dynamic_slice_in_dim(column, core * share, share, 0)
    sides = [{0: own[:half]}, {0: own[half:]}]
    for i, chunk in enumerate(chunks[1:]):
        sides[i % 2][2 * (i // 2 + 1)] = chunk[:half] + swap(chunk[half:], "seq", 1)
    total = jnp.concatenate([collect(sides[0], order), collect(sides[1], order[::-1])], axis=0)
    column = lax.dynamic_update_slice_in_dim(column, total, core * share, 0)
    return lax.psum_scatter(column, "seq", scatter_dimension=0, tiled=True)


def total_over_all(values):
    for axis in ("head", "seq"):
        for bit in bits_of(lax.axis_size(axis)):
            values = values + swap(values, axis, bit)
    return values


def turn(values, cosine, sine):
    return values * cosine + pltpu.roll(values, HD // 2, 1) * sine


def mask_of(layout_col, layout_row):
    doc_col, place_col = layout_col[:, 0:1], layout_col[:, 1:2]
    doc_row, place_row = layout_row[0:1, :], layout_row[1:2, :]
    return jnp.where((doc_col == doc_row) & (place_row <= place_col), 0.0, NEGATIVE)


def attend_kernel(
    first, weight, wout, bias, cosine, sine, layout_col, layout_row, tokens, gain,
    qkv, merged, log_total, middle, lowered, mask, outgoing, incoming, sems_a, sems_b,
):
    n = pl.program_id(0)
    heads = pl.num_programs(0)
    scale = HD ** (-0.5)
    peers = ring_places()

    @pl.when(n == 0)
    def _():
        greet([{"head": peer} for peer in peers[1:]])
        mask[...] = mask_of(layout_col[...], layout_row[...])

    linear = dot(first[...], weight[...], 1, 0) + bias[0]
    cos, sin = cosine[...], sine[...]
    queries = turn(linear[:, :HD], cos, sin).astype(bf16)
    keys = turn(linear[:, HD : 2 * HD], cos, sin).astype(bf16)
    values = linear[:, 2 * HD :].astype(bf16)
    qkv[:, :HD] = queries
    qkv[:, HD : 2 * HD] = keys
    qkv[:, 2 * HD :] = values
    scores = dot(queries, keys, 1, 1) * scale + mask[...]
    largest = jnp.max(scores, axis=1, keepdims=True)
    weights = jnp.exp(scores - largest)
    total = jnp.sum(weights, axis=1, keepdims=True)
    probs = (weights / total).astype(bf16)
    output = dot(probs, values, 1, 0).astype(bf16)
    merged[:, pl.ds(pl.multiple_of(n * HD, HD), HD)] = output
    log_total[0] = jnp.broadcast_to(largest + jnp.log(total), log_total.shape[1:])

    @pl.when(n == heads - 1)
    def _():
        size = weight.shape[0] // lax.axis_size("seq")
        rows = tokens.shape[0]

        def product(r, s):
            acc = jnp.zeros((rows, size), f32)
            for k in range(wout.shape[1] // size):
                acc += dot(
                    merged[r * rows : (r + 1) * rows, k * size : (k + 1) * size],
                    wout[s * size : (s + 1) * size, k * size : (k + 1) * size],
                    1,
                    0,
                )
            return acc

        copies = []
        for r in range(len(peers) - 1, 0, -1):
            for s in range(tokens.shape[1] // size):
                outgoing[r - 1, :, s * size : (s + 1) * size] = product(r, s).astype(bf16)
            copies.append(
                remote(
                    outgoing.at[r - 1], incoming.at[r - 1], sems_a.at[r - 1], sems_b.at[r - 1],
                    head=peers[r],
                )
            )
            copies[-1].start()
        for s in range(tokens.shape[1] // size):
            cols = slice(s * size, (s + 1) * size)
            middle[:, cols] = tokens[:, cols].astype(f32) + product(0, s)
        for copy in copies:
            copy.wait()
        total = middle[...]
        for r in range(len(peers) - 1):
            total += incoming[r].astype(f32)
        middle[...] = total
        square = jnp.mean(total * total, axis=1, keepdims=True)
        lowered[...] = (total * lax.rsqrt(square + EPS) * gain[...]).astype(bf16)


def attend(first, gathered, bias, cosine, sine, layout_col, layout_row, tokens, gain):
    rows, width = first.shape
    heads = bias.shape[0]
    own = tokens.shape[0]
    others = lax.axis_size("head") - 1
    step = 3 * HD
    wide = heads * HD

    def whole(shape):
        return pl.BlockSpec(shape, lambda n: (0,) * len(shape))

    return pl.pallas_call(
        attend_kernel,
        grid=(heads,),
        in_specs=[
            whole((rows, width)),
            pl.BlockSpec((width, step), lambda n: (0, n)),
            pl.BlockSpec((width, wide), lambda n: (0, 3)),
            pl.BlockSpec((1, 1, step), lambda n: (n, 0, 0)),
            whole((rows, HD)),
            whole((rows, HD)),
            whole((rows, 2)),
            whole((2, rows)),
            whole((own, width)),
            whole((1, width)),
        ],
        out_specs=[
            pl.BlockSpec((rows, step), lambda n: (0, n)),
            whole((rows, wide)),
            pl.BlockSpec((1, rows, LANES), lambda n: (n, 0, 0)),
            whole((own, width)),
            whole((own, width)),
        ],
        out_shape=[
            jax.ShapeDtypeStruct((rows, heads * step), bf16),
            jax.ShapeDtypeStruct((rows, wide), bf16),
            jax.ShapeDtypeStruct((heads, rows, LANES), f32),
            jax.ShapeDtypeStruct((own, width), f32),
            jax.ShapeDtypeStruct((own, width), bf16),
        ],
        scratch_shapes=[
            pltpu.VMEM((rows, rows), f32),
            pltpu.VMEM((others, own, width), bf16),
            pltpu.VMEM((others, own, width), bf16),
            pltpu.SemaphoreType.DMA((others,)),
            pltpu.SemaphoreType.DMA((others,)),
        ],
        compiler_params=pltpu.CompilerParams(
            collective_id=2, has_side_effects=True, vmem_limit_bytes=VMEM_BYTES
        ),
        cost_estimate=pl.CostEstimate(
            flops=2 * rows * width * 4 * wide, bytes_accessed=8 * width * wide, transcendentals=0
        ),
        name="attend",
    )(first, gathered, gathered, bias, cosine, sine, layout_col, layout_row, tokens, gain)


def attend_back_kernel(
    grad_own, first, weight, wout, qkv, merged, log_total, cosine, sine, layout_col, layout_row,
    grad_first, grad_weight, grad_bias, mask, grad_merged, acc, grad, sems_a, sems_b,
):
    n = pl.program_id(0)
    peers = ring_places()
    own = grad_own.shape[0]
    heads = pl.num_programs(0)
    scale = HD ** (-0.5)
    blocks, _, size = grad_weight.shape
    wide = wout.shape[1]

    @pl.when(n == 0)
    def _():
        greet([{"head": peer} for peer in peers[1:]])
        copies = [
            remote(
                grad_own, grad.at[pl.ds(r * own, own)], sems_a.at[r - 1], sems_b.at[r - 1],
                head=peers[len(peers) - r],
            )
            for r in range(1, len(peers))
        ]
        for copy in copies:
            copy.start()
        grad[:own] = grad_own[...]
        mask[...] = mask_of(layout_col[...], layout_row[...])
        acc[...] = jnp.zeros_like(acc)
        for copy in copies:
            copy.wait()
        for k in range(wide // size):
            total = jnp.zeros((grad.shape[0], size), f32)
            for s in range(blocks):
                total += dot(
                    grad[:, s * size : (s + 1) * size],
                    wout[s * size : (s + 1) * size, k * size : (k + 1) * size],
                    1,
                    1,
                )
            grad_merged[:, k * size : (k + 1) * size] = total.astype(bf16)
        for s in range(blocks):
            grad_weight[s, 3 * wide :, :] = dot(
                merged[...], grad[:, s * size : (s + 1) * size], 0, 0
            ).astype(bf16)

    cos, sin = cosine[...], -sine[...]
    queries, keys, values = qkv[:, :HD], qkv[:, HD : 2 * HD], qkv[:, 2 * HD :]
    grad_out = grad_merged[:, pl.ds(pl.multiple_of(n * HD, HD), HD)]
    scores = dot(queries, keys, 1, 1) * scale + mask[...]
    probs = jnp.exp(scores - log_total[0][:, 0:1])
    grad_values = dot(probs.astype(bf16), grad_out, 0, 0).astype(bf16)
    grad_probs = dot(grad_out, values, 1, 1)
    centre = jnp.sum(probs * grad_probs, axis=1, keepdims=True)
    grad_scores = (probs * (grad_probs - centre)).astype(bf16)
    grad_queries = (dot(grad_scores, keys, 1, 0) * scale).astype(bf16).astype(f32)
    grad_keys = (dot(grad_scores, queries, 0, 0) * scale).astype(bf16).astype(f32)
    grad_linear = jnp.concatenate(
        [turn(grad_queries, cos, sin).astype(bf16), turn(grad_keys, cos, sin).astype(bf16), grad_values],
        axis=1,
    )
    grad_bias[0] = jnp.sum(grad_linear.astype(f32), axis=0, keepdims=True)
    acc[...] += dot(grad_linear, weight[...], 1, 1)
    step = 3 * HD
    for s in range(blocks):
        grad_weight[s, pl.ds(pl.multiple_of(n * step, HD), step), :] = dot(
            grad_linear, first[:, s * size : (s + 1) * size], 0, 0
        ).astype(bf16)

    @pl.when(n == heads - 1)
    def _():
        grad_first[...] = acc[...].astype(bf16)


def attend_back(grad, first, gathered, qkv, merged, log_total, cosine, sine, layout_col, layout_row):
    rows, width = first.shape
    heads = log_total.shape[0]
    step = 3 * HD
    wide = heads * HD
    n_seq = lax.axis_size("seq")
    size = width // n_seq
    own = grad.shape[0]
    others = lax.axis_size("head") - 1

    def whole(shape):
        return pl.BlockSpec(shape, lambda n: (0,) * len(shape))

    return pl.pallas_call(
        attend_back_kernel,
        grid=(heads,),
        in_specs=[
            whole((own, width)),
            whole((rows, width)),
            pl.BlockSpec((width, step), lambda n: (0, n)),
            pl.BlockSpec((width, wide), lambda n: (0, 3)),
            pl.BlockSpec((rows, step), lambda n: (0, n)),
            whole((rows, wide)),
            pl.BlockSpec((1, rows, LANES), lambda n: (n, 0, 0)),
            whole((rows, HD)),
            whole((rows, HD)),
            whole((rows, 2)),
            whole((2, rows)),
        ],
        out_specs=[
            whole((rows, width)),
            whole((n_seq, 4 * wide, size)),
            pl.BlockSpec((1, 1, step), lambda n: (n, 0, 0)),
        ],
        out_shape=[
            jax.ShapeDtypeStruct((rows, width), bf16),
            jax.ShapeDtypeStruct((n_seq, 4 * wide, size), bf16),
            jax.ShapeDtypeStruct((heads, 1, step), f32),
        ],
        scratch_shapes=[
            pltpu.VMEM((rows, rows), f32),
            pltpu.VMEM((rows, wide), bf16),
            pltpu.VMEM((rows, width), f32),
            pltpu.VMEM((rows, width), bf16),
            pltpu.SemaphoreType.DMA((others,)),
            pltpu.SemaphoreType.DMA((others,)),
        ],
        compiler_params=pltpu.CompilerParams(
            collective_id=3, has_side_effects=True, vmem_limit_bytes=VMEM_BYTES
        ),
        cost_estimate=pl.CostEstimate(
            flops=4 * rows * width * 4 * wide, bytes_accessed=16 * width * wide, transcendentals=0
        ),
        name="attend_back",
    )(grad, first, gathered, gathered, qkv, merged, log_total, cosine, sine, layout_col, layout_row)


def pack_kernel(exp_units, share_units, at, *refs):
    stacked, shares = refs[0], refs[-5:-3]
    experts = [stacked.at[r] for r in range(stacked.shape[0])]
    rest, full, sems = refs[-3:]
    head = at[0]
    copies = []
    for r, block in enumerate(experts):
        size = block.shape[2]
        start = pl.multiple_of(jnp.bitwise_xor(head, r) * size, size)
        copies.append(
            pltpu.make_async_copy(
                block, full.at[:, pl.ds(0, exp_units), pl.ds(start, size)], sems.at[len(copies)]
            )
        )
    for r, block in enumerate(shares):
        size = block.shape[3]
        for s in range(block.shape[0]):
            copies.append(
                pltpu.make_async_copy(
                    block.at[s],
                    full.at[:, pl.ds(exp_units + r * share_units, share_units), pl.ds(s * size, size)],
                    sems.at[len(copies)],
                )
            )
    base = exp_units + 2 * share_units
    copies.append(
        pltpu.make_async_copy(rest, full.at[:, pl.ds(base, rest.shape[1]), :], sems.at[len(copies)])
    )
    for copy in copies:
        copy.start()
    for copy in copies:
        copy.wait()


def pack(at, experts, shares, rest, unit_rows):
    exp_units, share_units = experts.shape[2], shares[0].shape[2]
    count = experts.shape[0] + 2 * shares[0].shape[0] + 1
    anywhere = pl.BlockSpec(memory_space=pl.ANY)
    return pl.pallas_call(
        functools.partial(pack_kernel, exp_units, share_units),
        in_specs=[pl.BlockSpec(memory_space=pltpu.SMEM)] + [anywhere] * 4,
        out_specs=anywhere,
        out_shape=jax.ShapeDtypeStruct((3, unit_rows, rest.shape[2]), bf16),
        scratch_shapes=[pltpu.SemaphoreType.DMA((count,))],
        compiler_params=pltpu.CompilerParams(vmem_limit_bytes=1 << 20),
        cost_estimate=pl.CostEstimate(
            flops=0, bytes_accessed=12 * unit_rows * rest.shape[2], transcendentals=0
        ),
        name="pack",
    )(at, experts, *shares, rest)


def mix_rows(exp_units, base, n_exp, x, grad_ext, w, wait=None):
    rows, width = x.shape
    unit_rows = w.shape[1]
    seq = lax.axis_index("seq")
    gate = dot(x, w[0], 1, 1)
    if wait is not None:
        wait(1)
    up = dot(x, w[1], 1, 1)
    if wait is not None:
        wait(2)
    raw = dot(grad_ext[:, :width], w[2], 1, 1)
    block = base // LANES * LANES
    logits = gate[:, block : block + LANES]
    lane = lax.broadcasted_iota(jnp.int32, (rows, LANES), 1)
    from_base = lane - (base - block)
    is_logit = (from_base >= 0) & (from_base < n_exp)
    largest = jnp.max(jnp.where(is_logit, logits, NEGATIVE), axis=1, keepdims=True)
    powers = jnp.where(is_logit, jnp.exp(jnp.where(is_logit, logits - largest, 0.0)), 0.0)
    chosen = jnp.sum(jnp.where(from_base == seq, powers, 0.0), axis=1, keepdims=True)
    marks = grad_ext[:, width:].astype(f32)
    mark = jnp.sum(jnp.where(lane == seq, marks, 0.0), axis=1, keepdims=True)
    gate_here = mark * chosen / jnp.sum(powers, axis=1, keepdims=True)
    share_gate = jax.nn.sigmoid(
        jnp.sum(jnp.where(from_base == n_exp, logits, 0.0), axis=1, keepdims=True)
    )
    unit = lax.broadcasted_iota(jnp.int32, (rows, unit_rows), 1)
    is_expert = unit < exp_units
    factor = jnp.where(is_expert, gate_here, share_gate)
    sigma = jax.nn.sigmoid(gate)
    silu = gate * sigma
    hidden = silu * up
    scaled = (hidden * factor).astype(bf16)
    both = hidden * raw
    all_sum = jnp.sum(both, axis=1, keepdims=True)
    exp_sum = jnp.sum(jnp.where(is_expert, both, 0.0), axis=1, keepdims=True)
    grad_hidden = raw * factor
    grad_gate = (grad_hidden * up * (sigma + silu * (1.0 - sigma))).astype(bf16)
    grad_up = (grad_hidden * silu).astype(bf16)
    back = dot(grad_gate, w[0], 1, 0) + dot(grad_up, w[1], 1, 0)
    extra = jnp.where(
        lane == seq, exp_sum * mark, jnp.where(lane == n_exp, all_sum - exp_sum, 0.0)
    )
    return (grad_gate, grad_up, scaled), back.astype(bf16), extra.astype(bf16)


def mix_local_kernel(exp_units, base, n_exp, second, grad_ext, w_hbm, back, unit_out, w, sems):
    copies = [pltpu.make_async_copy(w_hbm.at[m], w.at[m], sems.at[m]) for m in range(3)]
    width = second.shape[1]

    @pl.when(pl.program_id(0) == 0)
    def _():
        for copy in copies:
            copy.start()
        for copy in copies:
            copy.wait()

    units, rows_back, extra = mix_rows(exp_units, base, n_exp, second[...], grad_ext, w)
    for m in range(3):
        unit_out[m] = units[m]
    back[:, :width] = rows_back
    back[:, width:] = extra


def mix_local(second, grad_ext, full, exp_units, base, n_exp):
    rows, width = second.shape
    unit_rows = full.shape[1]
    wide = grad_ext.shape[1]
    return pl.pallas_call(
        functools.partial(mix_local_kernel, exp_units, base, n_exp),
        grid=(rows // TILE,),
        in_specs=[
            pl.BlockSpec((TILE, width), lambda i: (i, 0)),
            pl.BlockSpec((TILE, wide), lambda i: (i, 0)),
            pl.BlockSpec(memory_space=pl.ANY),
        ],
        out_specs=[
            pl.BlockSpec((TILE, wide), lambda i: (i, 0)),
            pl.BlockSpec((3, TILE, unit_rows), lambda i: (0, i, 0)),
        ],
        out_shape=[
            jax.ShapeDtypeStruct((rows, wide), bf16),
            jax.ShapeDtypeStruct((3, rows, unit_rows), bf16),
        ],
        scratch_shapes=[
            pltpu.VMEM((3, unit_rows, width), bf16),
            pltpu.SemaphoreType.DMA((3,)),
        ],
        compiler_params=pltpu.CompilerParams(vmem_limit_bytes=VMEM_BYTES),
        cost_estimate=pl.CostEstimate(
            flops=10 * rows * width * unit_rows,
            bytes_accessed=6 * unit_rows * width + 8 * rows * width,
            transcendentals=0,
        ),
        name="mix_local",
    )(second, grad_ext, full)


def mix_kernel(
    exp_units, base, n_exp, second, grad_ext, w_hbm, unit_out, far, back,
    w, x, held, core_in, sums, home, w_sem, x_sem, y_a, y_b, c_a, c_b, b_a, b_b, h_a, h_b, o_sem,
):
    i = pl.program_id(0)
    _, near_y, near_core = plane_places()
    core = lax.axis_index("seq") % 2
    rows = x.shape[1]
    width = x.shape[2]
    at = [pl.ds(j * rows, rows) for j in range(2)]
    loads = [pltpu.make_async_copy(w_hbm.at[m], w.at[m], w_sem.at[m]) for m in range(3)]
    tokens_y = [
        remote(second.at[core, at[j]], far.at[core, at[j]], y_a.at[j], y_b.at[j], head=near_y)
        for j in range(2)
    ]
    tokens_c = [
        remote(far.at[core, at[j]], far.at[core, at[j]], c_a.at[j], c_b.at[j], seq=near_core)
        for j in range(2)
    ]
    back_c = [
        remote(held.at[2 + j, 1 - core], core_in.at[j], b_a.at[j], b_b.at[j], seq=near_core)
        for j in range(2)
    ]
    back_y = [
        remote(sums.at[j], home.at[j], h_a.at[j], h_b.at[j], head=near_y) for j in range(2)
    ]

    def bring(source, j):
        copies = [
            pltpu.make_async_copy(source.at[c, at[j]], x.at[c], x_sem.at[c]) for c in range(2)
        ]
        for copy in copies:
            copy.start()
        for copy in copies:
            copy.wait()

    def pass_on(j):
        back_c[j].wait_recv()
        sums[j] = (held[2 + j, core].astype(f32) + core_in[j].astype(f32)).astype(bf16)
        back_y[j].start()

    def wait_weights(m):
        @pl.when(i == 0)
        def _():
            loads[m].wait()

    @pl.when(i == 0)
    def _():
        greet([{"head": near_y}, {"seq": near_core}])
        for copy in tokens_y:
            copy.start()
        for copy in loads:
            copy.start()
        bring(second, 0)

    @pl.when(i == 1)
    def _():
        bring(second, 1)

    for j in range(2):

        @pl.when(i == 2 + j)
        def _():
            tokens_c[j].wait_recv()
            bring(far, j)

    wait_weights(0)
    for c in range(2):
        units, rows_back, extra = mix_rows(
            exp_units, base, n_exp, x[c], grad_ext.at[0, c], w, wait_weights if c == 0 else None
        )
        for m in range(3):
            unit_out[m, 0, c] = units[m]
        held[i, c, :, :width] = rows_back
        held[i, c, :, width:] = extra
        if c == 0:

            for j in range(2):

                @pl.when(i == 1 + j)
                def _():
                    tokens_y[j].wait_recv()
                    tokens_c[j].start()

            @pl.when(i == 3)
            def _():
                pass_on(0)

    @pl.when(i == 2)
    def _():
        back_c[0].start()

    @pl.when(i == 3)
    def _():
        back_c[1].start()
        out = [
            [
                pltpu.make_async_copy(held.at[j, c], back.at[c, at[j]], o_sem.at[j, k])
                for k, c in enumerate((1 - core, core))
            ]
            for j in range(2)
        ]
        for j in range(2):
            out[j][0].start()
        pass_on(1)
        for j in range(2):
            back_y[j].wait_recv()
            held[j, core] = (held[j, core].astype(f32) + home[j].astype(f32)).astype(bf16)
            out[j][1].start()
        for j in range(2):
            out[j][0].wait()
            out[j][1].wait()
            tokens_y[j].wait_send()
            tokens_c[j].wait_send()
            back_c[j].wait_send()
            back_y[j].wait_send()


def mix(second, grads, full, exp_units, base, n_exp):
    rows, width = second.shape
    unit_rows = full.shape[1]
    wide = grads.shape[2]
    half = rows // 2
    piece = half // 2
    anywhere = pl.BlockSpec(memory_space=pl.ANY)
    pair = [pltpu.SemaphoreType.DMA((2,))] * 8
    units, far, back = pl.pallas_call(
        functools.partial(mix_kernel, exp_units, base, n_exp),
        grid=(4,),
        in_specs=[
            anywhere,
            pl.BlockSpec((1, 2, piece, wide), lambda i: (i // 2, 0, i % 2, 0)),
            anywhere,
        ],
        out_specs=[
            pl.BlockSpec((3, 1, 2, piece, unit_rows), lambda i: (0, i // 2, 0, i % 2, 0)),
            anywhere,
            anywhere,
        ],
        out_shape=[
            jax.ShapeDtypeStruct((3, 2, 2, half, unit_rows), bf16),
            jax.ShapeDtypeStruct((2, half, width), bf16),
            jax.ShapeDtypeStruct((2, half, wide), bf16),
        ],
        scratch_shapes=[
            pltpu.VMEM((3, unit_rows, width), bf16),
            pltpu.VMEM((2, piece, width), bf16),
            pltpu.VMEM((4, 2, piece, wide), bf16),
            pltpu.VMEM((2, piece, wide), bf16),
            pltpu.VMEM((2, piece, wide), bf16),
            pltpu.VMEM((2, piece, wide), bf16),
            pltpu.SemaphoreType.DMA((3,)),
            pltpu.SemaphoreType.DMA((2,)),
            *pair,
            pltpu.SemaphoreType.DMA((2, 2)),
        ],
        compiler_params=pltpu.CompilerParams(
            collective_id=4, has_side_effects=True, vmem_limit_bytes=VMEM_BYTES
        ),
        cost_estimate=pl.CostEstimate(
            flops=20 * rows * width * unit_rows,
            bytes_accessed=6 * unit_rows * width + 16 * rows * width,
            transcendentals=0,
        ),
        name="mix",
    )(second.reshape(2, half, width), grads.reshape(2, 2, half, wide), full)
    return units.reshape(3, 2, rows, unit_rows), far.reshape(rows, width), back.reshape(rows, wide)


def unit_grads_kernel(count, exp_units, share_rows, at, *refs):
    units, seconds, grads = refs[:count], refs[count : 2 * count], refs[2 * count : 3 * count]
    experts, share_own, share_far = refs[3 * count :]
    m = pl.program_id(0)

    def run(rights):
        acc = dot(units[0][...], rights[0][...], 0, 0)
        for left, right in zip(units[1:], rights[1:]):
            acc += dot(left[...], right[...], 0, 0)
        experts[0, 0] = acc[:exp_units].astype(bf16)
        size = share_own.shape[3]
        for s in range(share_own.shape[0]):
            piece = acc[exp_units : exp_units + 2 * share_rows, s * size : (s + 1) * size].astype(bf16)
            share_own[s, 0] = piece[:share_rows]
            share_far[s, 0] = piece[share_rows:]

    @pl.when(m < 2)
    def _():
        run(seconds)

    @pl.when(m == 2)
    def _():
        run(grads)


def unit_grads(at, units, seconds, grads, exp_units, share_rows):
    n_head, n_seq = lax.axis_size("head"), lax.axis_size("seq")
    width = seconds[0][0].shape[2]
    unit_rows = units[0][0].shape[3]
    head_part, seq_part = width // n_head, width // n_seq
    near = n_seq // n_head
    rows = sum(block.shape[1] for block, _ in seconds)

    def far(r, at):
        return jnp.bitwise_xor(at[0], r)

    def place(q, m, r, at):
        return (m, q, 0, 0)

    def second_place(q, m, r, at):
        return (q, 0, jnp.where(m < 2, far(r, at), far(n_head - 1, at)))

    def grad_place(q, m, r, at):
        return (q, 0, jnp.where(m < 2, far(0, at), far(r, at)))

    in_specs = [
        pl.BlockSpec((None, None, block.shape[2], unit_rows), functools.partial(place, q))
        for block, q in units
    ]
    in_specs += [
        pl.BlockSpec((None, block.shape[1], head_part), functools.partial(second_place, q))
        for block, q in seconds
    ]
    in_specs += [
        pl.BlockSpec((None, block.shape[1], head_part), functools.partial(grad_place, q))
        for block, q in grads
    ]
    share_spec = pl.BlockSpec((near, 1, share_rows, seq_part), lambda m, r, at: (far(r, at), m, 0, 0))
    share_shape = jax.ShapeDtypeStruct((n_seq, 3, share_rows, seq_part), bf16)
    return pl.pallas_call(
        functools.partial(unit_grads_kernel, len(units), exp_units, share_rows),
        grid_spec=pltpu.PrefetchScalarGridSpec(
            num_scalar_prefetch=1,
            grid=(3, n_head),
            in_specs=in_specs,
            out_specs=[
                pl.BlockSpec((1, 1, exp_units, head_part), lambda m, r, at: (r, m, 0, 0)),
                share_spec,
                share_spec,
            ],
        ),
        out_shape=[
            jax.ShapeDtypeStruct((n_head, 3, exp_units, head_part), bf16),
            share_shape,
            share_shape,
        ],
        compiler_params=pltpu.CompilerParams(vmem_limit_bytes=VMEM_BYTES),
        cost_estimate=pl.CostEstimate(
            flops=6 * rows * width * unit_rows,
            bytes_accessed=6 * rows * unit_rows + 8 * rows * width + 6 * width * unit_rows,
            transcendentals=0,
        ),
        name="unit_grads",
    )(at, *(block for block, _ in units + seconds + grads))


def after(value, *others):
    return lax.optimization_barrier((value, *others))[0]


def shards(
    tokens,
    cotangent,
    arrange,
    doc_lengths,
    routes,
    norm1_gain,
    qkv_weight,
    qkv_bias,
    out_weight,
    norm2_gain,
    router_weight,
    shared_gate_vec,
    shared_gate_up,
    shared_down,
    expert_gate_up,
    expert_down,
):
    highest = lax.Precision.HIGHEST
    tok_rows, width = tokens.shape
    n_seq = lax.axis_size("seq")
    n_head = lax.axis_size("head")
    seq = lax.axis_index("seq")
    head = lax.axis_index("head")
    group_tok = tok_rows * n_head
    heads_here = qkv_weight.shape[1]
    n_exp = router_weight.shape[1]
    hidden_all = expert_down.shape[1]
    parts = n_head // 2
    part = mesh_part()
    exp_units = hidden_all // parts
    share_all = shared_down.shape[0]
    share_units = share_all // n_seq
    share_rows = -(-share_units // 16) * 16
    base = exp_units + 2 * share_rows
    unit_rows = -(-(base + n_exp + 1) // LANES) * LANES
    seq_part = width // n_seq
    head_part = width // n_head

    wide = heads_here * HD
    out_blocks = out_weight.reshape(wide // seq_part, seq_part, seq_part)
    out_blocks = jnp.transpose(out_blocks, (1, 0, 2)).reshape(seq_part, wide)
    local = jnp.concatenate([qkv_weight.reshape(seq_part, 3 * wide), out_blocks], axis=1)
    gathered = lax.all_gather(local, "seq", axis=0, tiled=True)

    send = jnp.stack(
        [expert_gate_up[0, :, :hidden_all].T, expert_gate_up[0, :, hidden_all:].T, expert_down[0]]
    )
    stream = tokens.astype(f32)
    gain_first = norm1_gain.astype(f32)
    scale_first = rms_scale(stream)
    normed_first = stream * scale_first
    lowered_first = (normed_first * gain_first).astype(bf16)
    plane = parts == 2
    if plane:
        first_group, experts = front(lowered_first, send)
        first_group = first_group.reshape(group_tok, width)
    else:
        first_group = group_gather(lowered_first)
        near = []
        for t in range(parts):
            there = jnp.bitwise_xor(part, t)
            block = lax.dynamic_slice_in_dim(send, there * exp_units, exp_units, 1)
            near.append(swap(block, "head", 2 * t) if t else block)
        experts = jnp.stack([block for own in near for block in (own, swap(own, "head", 1))])
    send = jnp.stack([shared_gate_up[:, 0].T, shared_gate_up[:, 1].T, shared_down])
    send = jnp.transpose(send.reshape(3, n_seq, share_units, seq_part), (1, 0, 2, 3))
    if share_rows > share_units:
        send = jnp.pad(send, ((0, 0), (0, 0), (0, share_rows - share_units), (0, 0)))
    share_own = lax.all_to_all(after(send, gathered), "seq", split_axis=0, concat_axis=0)
    expert_ids = jnp.arange(n_exp, dtype=jnp.int32)
    chosen = jnp.any(routes[:, :, None] == expert_ids[None, None, :], axis=1)
    marks = jnp.concatenate(
        [chosen.astype(bf16), jnp.zeros((tok_rows, LANES - n_exp), bf16)], axis=1
    )
    grad_ext = after(jnp.concatenate([cotangent, marks], axis=1), gathered)
    if plane:
        grad_column = lax.all_gather(grad_ext, "seq", axis=0, tiled=True)
        grad_both, share_far = relay(grad_column, share_own)
    else:
        share_far = swap(share_own, "head", 1)
    gate_rows = jnp.concatenate([router_weight.T, shared_gate_vec[None, :]], axis=0)
    rest = jnp.zeros((3, unit_rows - base, width), bf16).at[0, : n_exp + 1].set(gate_rows)
    at = jnp.stack([head, seq]).astype(jnp.int32)
    full = pack(at, experts, [share_own, share_far], rest, unit_rows)

    place, doc_index, position = layout_of(arrange[0], doc_lengths[0], group_tok)
    blocks = (head + jnp.arange(n_head, dtype=jnp.int32)) % n_head
    table = jnp.stack([place, doc_index, position]).reshape(3, n_head, tok_rows)
    place, doc_index, position = jnp.take(table, blocks, axis=1).reshape(3, group_tok)
    layout_row = jnp.stack([doc_index, place])
    layout_col = layout_row.T
    cosine, sine = rope_tables(position.astype(f32))
    cosine = jnp.concatenate([cosine, cosine], axis=1)
    sine = jnp.concatenate([-sine, sine], axis=1)

    bias_here = lax.dynamic_slice_in_dim(qkv_bias, head * heads_here, heads_here, 0)
    gain_second = norm2_gain.astype(f32)
    qkv, merged, log_total, middle, lowered_second = attend(
        first_group,
        gathered,
        bias_here.astype(f32)[:, None, :],
        cosine,
        sine,
        layout_col,
        layout_row,
        tokens,
        gain_second[None, :],
    )
    scale_second = rms_scale(middle)
    normed_second = middle * scale_second

    if plane:
        second_column = lax.all_gather(lowered_second, "seq", axis=0, tiled=True)
        units, second_far, back_column = mix(second_column, grad_both, full, exp_units, base, n_exp)
        grad_experts, grad_share, grad_share_far = unit_grads(
            at,
            [(units, 0), (units, 1)],
            [(second_column[None], 0), (second_far[None], 0)],
            [(grad_both, 0), (grad_both, 1)],
            exp_units,
            share_rows,
        )
        back_own = lax.psum_scatter(back_column, "seq", scatter_dimension=0, tiled=True)
        half = second_column.shape[0] // 2
        out = dot(units[2].reshape(-1, unit_rows), full[2], 1, 0).astype(bf16)
        out = out.reshape(2, 2, half, width)
        core = lax.rem(seq, 2)
        pair = lax.dynamic_index_in_dim(out[1], core, 0, keepdims=False) + swap(
            lax.dynamic_index_in_dim(out[1], 1 - core, 0, keepdims=False), "seq", 1
        )
        pair = swap(pair, "head", 2)
        is_core = jnp.arange(2, dtype=jnp.int32)[:, None, None] == core
        out_column = out[0] + jnp.where(is_core, pair[None], 0.0).astype(bf16)
        out_own = lax.psum_scatter(
            out_column.reshape(2 * half, width), "seq", scatter_dimension=0, tiled=True
        )
    else:
        grad_chunks = token_gather(grad_ext)
        second_chunks = token_gather(lowered_second)
        back_chunks = []
        unit_chunks = []
        for second, grad in zip(second_chunks, grad_chunks):
            back, units = mix_local(second, grad, full, exp_units, base, n_exp)
            back_chunks.append(back)
            unit_chunks.append(units)
        grad_experts, grad_share, grad_share_far = unit_grads(
            at,
            [(units[:, None], 0) for units in unit_chunks],
            [(second[None], 0) for second in second_chunks],
            [(grad[None], 0) for grad in grad_chunks],
            exp_units,
            share_rows,
        )
        out_chunks = [dot(units[2], full[2], 1, 0).astype(bf16) for units in unit_chunks]
        back_own = token_scatter(back_chunks)
        out_own = token_scatter(out_chunks)

    back_own = after(back_own, grad_experts).astype(f32)
    out_own = out_own.astype(f32)
    mixed = (middle + out_own).astype(bf16)

    logits = dot(lowered_second, gate_rows, 1, 1)
    probs = jax.nn.softmax(logits[:, :n_exp], axis=-1)
    share_gate = jax.nn.sigmoid(logits[:, n_exp:])
    grad_probs = back_own[:, width : width + n_exp]
    grad_logits = probs * (grad_probs - jnp.sum(probs * grad_probs, axis=1, keepdims=True))
    grad_gate_logit = (
        back_own[:, width + n_exp : width + n_exp + 1] * share_gate * (1.0 - share_gate)
    )
    small = jnp.concatenate([grad_logits, grad_gate_logit], axis=1)
    grad_second = back_own[:, :width] + jnp.dot(
        small, gate_rows.astype(f32), precision=highest
    )
    grad_gate_cols = jnp.dot(small.T, lowered_second.astype(f32), precision=highest)
    grad_gain_second = jnp.sum(grad_second * normed_second, axis=0)
    grad_normed = grad_second * gain_second
    grad_middle = cotangent.astype(f32) + scale_second * (
        grad_normed - normed_second * jnp.mean(grad_normed * normed_second, axis=1, keepdims=True)
    )
    totals_second = total_over_all(
        jnp.concatenate([grad_gate_cols, grad_gain_second[None, :]], axis=0)
    )

    grad_first, grad_weight, grad_bias_here = attend_back(
        grad_middle.astype(bf16), first_group, gathered, qkv, merged, log_total, cosine, sine, layout_col, layout_row
    )
    grad_first = group_scatter(grad_first)
    grad_weight = lax.psum_scatter(grad_weight, "seq", scatter_dimension=0, tiled=False)
    grad_bias = lax.dynamic_update_slice_in_dim(
        jnp.zeros(qkv_bias.shape, f32), grad_bias_here[:, 0], head * heads_here, 0
    )
    grad_gain_first = jnp.sum(grad_first * normed_first, axis=0)
    grad_normed_first = grad_first * gain_first
    input_grad = grad_middle + scale_first * (
        grad_normed_first
        - normed_first * jnp.mean(grad_normed_first * normed_first, axis=1, keepdims=True)
    )
    totals_first = total_over_all(
        jnp.concatenate([grad_gain_first, grad_bias.reshape(-1)]).reshape(-1, LANES)
    ).reshape(-1)

    grad_share = grad_share + swap(grad_share_far, "head", 1)
    grad_share = lax.all_to_all(grad_share[:, :, :share_units], "seq", split_axis=0, concat_axis=0)
    grad_share = jnp.transpose(grad_share, (1, 0, 2, 3)).reshape(3, share_all, seq_part).astype(f32)
    own = {}
    for t in range(parts)[::-1]:
        total = grad_experts[2 * t] + swap(grad_experts[2 * t + 1], "head", 1)
        own[t] = swap(total, "head", 2 * t) if t else total
    own = jnp.stack([own[t] for t in range(parts)])
    own = jnp.take(own, jnp.bitwise_xor(part, jnp.arange(parts, dtype=jnp.int32)), axis=0)
    own = jnp.transpose(own, (1, 0, 2, 3)).reshape(3, hidden_all, head_part).astype(f32)
    return (
        mixed,
        input_grad,
        totals_first[:width],
        grad_weight[: 3 * wide].astype(f32).T.reshape(qkv_weight.shape),
        totals_first[width:].reshape(qkv_bias.shape),
        grad_weight[3 * wide :].astype(f32),
        totals_second[n_exp + 1],
        totals_second[:n_exp].T,
        totals_second[n_exp],
        jnp.stack([grad_share[0].T, grad_share[1].T], axis=1),
        grad_share[2],
        jnp.concatenate([own[0].T, own[1].T], axis=1)[None],
        own[2][None],
    )


def solution(mesh):
    return jax.shard_map(
        shards,
        mesh=mesh,
        in_specs=(
            P(("seq", "head"), None),
            P(("seq", "head"), None),
            P("seq", None),
            P("seq", None),
            P(("seq", "head"), None),
            P(),
            P("seq", "head", None),
            P(),
            P("head", "seq"),
            P(),
            P(),
            P(),
            P("seq", None, "head"),
            P("head", "seq"),
            P("seq", "head", None),
            P("seq", None, "head"),
        ),
        out_specs=(
            P(("seq", "head"), None),
            P(("seq", "head"), None),
            P(),
            P("seq", "head", None),
            P(),
            P("head", "seq"),
            P(),
            P(),
            P(),
            P("seq", None, "head"),
            P("head", "seq"),
            P("seq", "head", None),
            P("seq", None, "head"),
        ),
        check_vma=False,
    )
```

```python
import functools

import jax
import jax.numpy as jnp
from jax import lax
from jax.experimental import pallas as pl
from jax.experimental.pallas import tpu as pltpu
from jax.sharding import PartitionSpec as P

HD = 128
EPS = 1e-06
THETA = 1000000.0
NEGATIVE = -1e30
LANES = 128
TILE = 256
MESH = pl.DeviceIdType.MESH
VMEM_BYTES = 60 * 1024 * 1024
bf16 = jnp.bfloat16
f32 = jnp.float32


def rms_scale(values):
    return lax.rsqrt(jnp.mean(values * values, axis=-1, keepdims=True) + EPS)


def rope_tables(position):
    half = HD // 2
    exponent = jnp.arange(half, dtype=f32) * (2.0 / HD)
    frequency = THETA ** (-exponent)
    angle = position[:, None] * frequency[None, :]
    return (jnp.cos(angle), jnp.sin(angle))


def layout_of(arrange_row, length_row, group_tok):
    counter = jnp.arange(group_tok, dtype=jnp.int32)
    place = jnp.sum(
        jnp.where(arrange_row[None, :] == counter[:, None], counter[None, :], 0),
        axis=1,
        dtype=jnp.int32,
    )
    ends = jnp.cumsum(length_row, dtype=jnp.int32)
    starts = ends - length_row
    doc_index = jnp.sum(
        (place[:, None] >= ends[None, :]).astype(jnp.int32), axis=1, dtype=jnp.int32
    )
    picked = doc_index[:, None] == jnp.arange(length_row.shape[0], dtype=jnp.int32)[None, :]
    start_of = jnp.sum(jnp.where(picked, starts[None, :], 0), axis=1, dtype=jnp.int32)
    return (place, doc_index, place - start_of)


def dot(left, right, left_dim, right_dim):
    return lax.dot_general(
        left, right, (((left_dim,), (right_dim,)), ((), ())), preferred_element_type=f32
    )


def swap(block, axis, bit):
    size = lax.axis_size(axis)
    return lax.ppermute(block, axis, [(i, i ^ bit) for i in range(size)])


def bits_of(size):
    bits = []
    bit = 1
    while bit < size:
        bits.append(bit)
        bit *= 2
    return bits


def spread(block, order):
    found = {0: block}
    for bit in order:
        for near in sorted(found):
            found[near ^ bit] = swap(found[near], "head", bit)
    return found


def collect(parts, order):
    parts = dict(parts)
    for bit in reversed(order):
        for far in sorted((r for r in parts if r & bit), reverse=True):
            parts[far ^ bit] = parts[far ^ bit] + swap(parts.pop(far), "head", bit)
    return parts[0]


def shift(block, axis, step):
    size = lax.axis_size(axis)
    return lax.ppermute(block, axis, [((i + step) % size, i) for i in range(size)])


def group_gather(block):
    size = lax.axis_size("head")
    return jnp.concatenate([block] + [shift(block, "head", r) for r in range(1, size)], axis=0)


def group_scatter(block):
    size = lax.axis_size("head")
    rows = block.shape[0] // size
    total = block[:rows].astype(f32)
    for r in range(1, size):
        total += shift(block[r * rows : (r + 1) * rows], "head", size - r).astype(f32)
    return total


def remote(src, dst, send_sem, recv_sem, **place):
    return pltpu.make_async_remote_copy(
        src_ref=src,
        dst_ref=dst,
        send_sem=send_sem,
        recv_sem=recv_sem,
        device_id=place,
        device_id_type=MESH,
    )


def greet(places):
    barrier = pltpu.get_barrier_semaphore()
    for place in places:
        pl.semaphore_signal(barrier, inc=1, device_id=place, device_id_type=MESH)
    pl.semaphore_wait(barrier, len(places))


def plane_places():
    head, seq = lax.axis_index("head"), lax.axis_index("seq")
    x, y = head % 2, head // 2
    return y * 2 + (1 - x), (1 - y) * 2 + x, seq + 1 - 2 * (seq % 2)


def ring_places():
    size = lax.axis_size("head")
    head = lax.axis_index("head")
    return [(head + r) % size for r in range(size)]


class Line:
    def __init__(self, place, far, sems):
        self.seq = lax.axis_index("seq")
        self.count = lax.axis_size("seq") // 2
        self.depth = self.count - 1
        self.z = self.seq // 2
        _, self.near_y, self.near_core = plane_places()
        self.place, self.far = place, far
        self.sems = sems

    def index(self, j):
        if j == 0:
            return self.seq
        if j <= self.depth:
            return self.seq - 2 * j
        return self.seq + 2 * (j - self.depth)

    def valid(self, j):
        if j == 0:
            return self.z >= 0
        if j <= self.depth:
            return self.z - j >= 0
        return self.z + (j - self.depth) < self.count

    def line_copy(self, j, up):
        block = self.place(self.index(j))
        if up:
            to, k = self.seq + 2, j
        else:
            to, k = self.seq - 2, self.depth + (j - self.depth if j else 0)
        return remote(block, block, self.sems.at[0, k], self.sems.at[1, k], seq=to)

    def line_arrival(self, j):
        block = self.place(self.index(j))
        return remote(
            block, block, self.sems.at[0, j - 1], self.sems.at[1, j - 1], seq=self.near_core
        )

    def core_copy(self, j):
        block = self.place(self.index(j))
        return remote(block, block, self.sems.at[2, j], self.sems.at[3, j], seq=self.near_core)

    def core_arrival(self, j):
        block = self.place(self.index(j) + self.near_core - self.seq)
        return remote(block, block, self.sems.at[2, j], self.sems.at[3, j], seq=self.near_core)

    def far_copy(self, j):
        i = self.index(j)
        return remote(
            self.place(i), self.far(i), self.sems.at[4, j], self.sems.at[5, j], head=self.near_y
        )

    def far_core_copy(self, j):
        there = self.far(self.index(j))
        return remote(there, there, self.sems.at[6, j], self.sems.at[7, j], seq=self.near_core)

    def far_core_arrival(self, j):
        there = self.far(self.index(j) + self.near_core - self.seq)
        return remote(there, there, self.sems.at[6, j], self.sems.at[7, j], seq=self.near_core)

    def sides(self, j):
        self.core_copy(j).start()
        if self.far is not None:
            self.far_copy(j).start()

    def ups(self):
        return range(self.depth)

    def downs(self):
        return [0] + [self.depth + k for k in range(1, self.depth)]

    def has_above(self):
        return self.z + 1 < self.count

    def has_below(self):
        return self.z >= 1

    def begin(self):
        @pl.when(self.has_above())
        def _():
            self.line_copy(0, True).start()

        @pl.when(self.has_below())
        def _():
            self.line_copy(0, False).start()

        self.sides(0)

    def step(self, k):
        @pl.when(self.valid(1 + k))
        def _():
            self.line_arrival(1 + k).wait_recv()
            if 1 + k < self.depth:

                @pl.when(self.has_above())
                def _():
                    self.line_copy(1 + k, True).start()

            self.sides(1 + k)

        @pl.when(self.valid(self.depth + 1 + k))
        def _():
            self.line_arrival(self.depth + 1 + k).wait_recv()
            if 1 + k < self.depth:

                @pl.when(self.has_below())
                def _():
                    self.line_copy(self.depth + 1 + k, False).start()

            self.sides(self.depth + 1 + k)

    def side_step(self, j):
        @pl.when(self.valid(j))
        def _():
            self.far_copy(j).wait_recv()
            self.far_core_copy(j).start()

    def wait_blocks(self):
        for j in range(2 * self.depth + 1):

            @pl.when(self.valid(j))
            def _():
                self.core_arrival(j).wait_recv()
                if self.far is not None:
                    self.far_core_arrival(j).wait_recv()

    def wait_sends(self):
        for j in range(2 * self.depth + 1):

            @pl.when(self.valid(j))
            def _():
                self.core_copy(j).wait_send()
                if self.far is not None:
                    self.far_copy(j).wait_send()
                    self.far_core_copy(j).wait_send()

        for j in self.ups():

            @pl.when(self.valid(j) & self.has_above())
            def _():
                self.line_copy(j, True).wait_send()

        for j in self.downs():

            @pl.when(self.valid(j) & self.has_below())
            def _():
                self.line_copy(j, False).wait_send()


def forward_kernel(
    tokens, gain_first, gain_second, weight_own, wout_own, expert_up, expert_down, share_up, share_down,
    grad_ext, bias, cosine, sine, layout_col, layout_row,
    first_out, weight_out, wout_out, experts, share, share_far, grads, seconds, qkv, merged, log_total, middle,
    lowered,
    group, weight, wout, expert_raw, expert_pack, share_raw, share_pack, mask, outgoing, incoming,
    local, line_w, line_o, line_g, line_s, ring_a, ring_b, sc_a, sc_b, ex_a, ex_b, sh_a, sh_b,
):
    seq, head = lax.axis_index("seq"), lax.axis_index("head")
    n_seq = lax.axis_size("seq")
    near_x, near_y, near_core = plane_places()
    peers = ring_places()
    size = len(peers)
    rows, width = tokens.shape
    heads = bias.shape[0]
    units = experts.shape[2]
    y = head // 2
    share_rows = share.shape[2]
    hidden = expert_down.shape[0]
    part = weight_own.shape[0]

    fetch = [
        pltpu.make_async_copy(
            weight_own, weight.at[pl.ds(pl.multiple_of(seq * part, 16), part)], local.at[0]
        ),
        pltpu.make_async_copy(wout_own, wout.at[seq], local.at[1]),
        pltpu.make_async_copy(expert_up, expert_raw, local.at[2]),
        pltpu.make_async_copy(expert_down, expert_pack.at[2], local.at[3]),
        pltpu.make_async_copy(share_up, share_raw, local.at[4]),
        pltpu.make_async_copy(share_down, share_pack.at[2], local.at[5]),
        pltpu.make_async_copy(grad_ext, grads.at[0, seq], local.at[6]),
    ]
    for copy in fetch:
        copy.start()
    greet(
        [{"head": peer} for peer in peers[1:]]
        + [{"seq": (seq + k) % n_seq} for k in range(1, n_seq)]
    )

    gather_w = Line(lambda i: weight.at[pl.ds(pl.multiple_of(i * part, 16), part)], None, line_w)
    gather_o = Line(lambda i: wout.at[i], None, line_o)
    gather_g = Line(lambda i: grads.at[0, i], lambda i: grads.at[1, i], line_g)
    gather_s = Line(lambda i: seconds.at[0, i], lambda i: seconds.at[1, i], line_s)
    fetch[0].wait()
    gather_w.begin()
    fetch[1].wait()
    gather_o.begin()

    group[:rows] = norm_rows(tokens[...].astype(f32), gain_first[...])
    ring = [
        remote(
            group.at[pl.ds(0, rows)], group.at[pl.ds(r * rows, rows)],
            ring_a.at[r - 1], ring_b.at[r - 1], head=peers[size - r],
        )
        for r in range(1, size)
    ]
    for copy in ring:
        copy.start()

    fetch[2].wait()
    fetch[3].wait()
    mine = pl.ds(pl.multiple_of(y * units, 16), units)
    other = pl.ds(pl.multiple_of((1 - y) * units, 16), units)
    ups = [
        remote(expert_pack.at[m, other], experts.at[2, m], ex_a.at[m], ex_b.at[m], head=near_y)
        for m in range(3)
    ]
    sides = [
        remote(expert_pack.at[m, mine], experts.at[1, m], ex_a.at[3 + m], ex_b.at[3 + m], head=near_x)
        for m in range(3)
    ]
    ons = [
        remote(experts.at[2, m], experts.at[3, m], ex_a.at[6 + m], ex_b.at[6 + m], head=near_x)
        for m in range(3)
    ]
    order = (2, 0, 1)
    for m in order:
        if m < 2:
            expert_pack[m] = expert_raw[:, m * hidden : (m + 1) * hidden].T
        ups[m].start()
        sides[m].start()
    keep = [pltpu.make_async_copy(expert_pack.at[:, mine], experts.at[0], local.at[7])]
    keep[0].start()

    fetch[4].wait()
    fetch[5].wait()
    for m in range(2):
        share_pack[m] = share_raw[:, m * hidden : (m + 1) * hidden].T

    def share_block(i):
        return share_pack.at[:, pl.ds(pl.multiple_of(i * share_rows, 16), share_rows)]

    shares = [
        remote(
            share_block((seq + k) % n_seq), share.at[seq], sh_a.at[k], sh_b.at[k],
            seq=(seq + k) % n_seq,
        )
        for k in range(1, n_seq)
    ]
    share_own = pltpu.make_async_copy(share_block(seq), share.at[seq], local.at[8])
    share_own.start()
    arrivals = []
    for k in range(1, n_seq):
        block = share.at[(seq + n_seq - k) % n_seq]
        arrivals.append(remote(block, block, sh_a.at[k], sh_b.at[k], seq=(seq + k) % n_seq))
    crossings = []
    for k in range(n_seq):
        place = (seq + n_seq - k) % n_seq
        crossings.append(
            remote(
                share.at[place], share_far.at[place], sh_a.at[n_seq + k], sh_b.at[n_seq + k],
                head=near_x,
            )
        )

    mask[...] = mask_of(layout_col[...], layout_row[...])
    gather_w.step(0)
    gather_o.step(0)
    ups[2].wait_recv()
    ons[2].start()
    gather_w.step(1)
    gather_o.step(1)
    for m in (0, 1):
        ups[m].wait_recv()
        ons[m].start()
    fetch[6].wait()
    gather_w.step(2)
    gather_o.step(2)
    gather_g.begin()
    for copy in shares:
        copy.start()
    for copy in ring:
        copy.wait_recv()
    gather_w.wait_blocks()
    gather_o.wait_blocks()
    keep += [
        pltpu.make_async_copy(weight, weight_out, local.at[9]),
        pltpu.make_async_copy(wout, wout_out, local.at[10]),
        pltpu.make_async_copy(group, first_out, local.at[11]),
    ]
    for copy in keep[1:]:
        copy.start()

    step = 3 * HD
    for n in range(heads):
        linear = dot(group[...], weight[:, n * step : (n + 1) * step], 1, 0) + bias[n]
        parts, output, log_sum = head_forward(linear, cosine[...], sine[...], mask[...])
        for k in range(3):
            qkv[:, n * step + k * HD : n * step + (k + 1) * HD] = parts[k]
        merged[:, n * HD : (n + 1) * HD] = output
        log_total[n] = jnp.broadcast_to(log_sum, log_total.shape[1:])
        if n == 2:
            gather_g.step(0)
            gather_g.side_step(0)
    copies, own = scatter_start(merged, wout, outgoing, incoming, sc_a, sc_b, rows, peers)
    block = wout.shape[2]
    for b in range(len(own)):
        cols = slice(b * block, (b + 1) * block)
        middle[:, cols] = tokens[:, cols].astype(f32) + own[b]
    gather_g.step(1)
    for copy in copies:
        copy.wait_recv()
    total = middle[...]
    for r in range(size - 1):
        total += incoming[r].astype(f32)
    middle[...] = total
    lowered[...] = norm_rows(total, gain_second[...])
    last = pltpu.make_async_copy(lowered, seconds.at[0, seq], local.at[12])
    last.start()
    last.wait()
    gather_s.begin()

    share_own.wait()
    crossings[0].start()
    for j in (1, 1 + gather_g.depth):
        gather_g.side_step(j)
    for k in range(1, n_seq):
        arrivals[k - 1].wait_recv()
        crossings[k].start()
    gather_g.step(2)
    gather_s.step(0)
    for j in (2, 2 + gather_g.depth, 3, 3 + gather_g.depth):
        gather_g.side_step(j)
    gather_s.side_step(0)
    gather_s.step(1)
    for j in (1, 1 + gather_g.depth):
        gather_s.side_step(j)
    gather_s.step(2)
    for j in (2, 2 + gather_g.depth, 3, 3 + gather_g.depth):
        gather_s.side_step(j)

    gather_g.wait_blocks()
    gather_s.wait_blocks()
    for copy in sides + ons + crossings:
        copy.wait()
    for copy in ups + ring + copies + shares:
        copy.wait_send()
    for copy in keep:
        copy.wait()
    for line in (gather_w, gather_o, gather_g, gather_s):
        line.wait_sends()


def forward(
    tokens, gain_first, gain_second, weight_own, wout_own, expert_up, expert_down, share_up, share_down,
    grad_ext, bias, cosine, sine, layout_col, layout_row,
):
    n_seq, n_head = lax.axis_size("seq"), lax.axis_size("head")
    rows, width = tokens.shape
    group_tok = rows * n_head
    heads = bias.shape[0]
    wide = heads * HD
    part = weight_own.shape[0]
    hidden, head_part = expert_down.shape
    units = hidden // 2
    share_all, seq_part = share_down.shape
    share_rows = share_all // n_seq
    ext = grad_ext.shape[1]
    anywhere = pl.BlockSpec(memory_space=pl.ANY)
    vmem = pl.BlockSpec(memory_space=pltpu.VMEM)
    dma = pltpu.SemaphoreType.DMA
    lines = n_seq - 1

    def hbm(*shape):
        return (anywhere, jax.ShapeDtypeStruct(shape, bf16))

    outs = [
        hbm(group_tok, width),
        hbm(width, 3 * wide),
        hbm(n_seq, wide, part),
        hbm(4, 3, units, head_part),
        hbm(n_seq, 3, share_rows, seq_part),
        hbm(n_seq, 3, share_rows, seq_part),
        hbm(2, n_seq, rows, ext),
        hbm(2, n_seq, rows, width),
        (vmem, jax.ShapeDtypeStruct((group_tok, 3 * wide), bf16)),
        (vmem, jax.ShapeDtypeStruct((group_tok, wide), bf16)),
        (vmem, jax.ShapeDtypeStruct((heads, group_tok, LANES), f32)),
        (vmem, jax.ShapeDtypeStruct((rows, width), f32)),
        (vmem, jax.ShapeDtypeStruct((rows, width), bf16)),
    ]
    return pl.pallas_call(
        forward_kernel,
        in_specs=[vmem] * 3 + [anywhere] * 7 + [vmem] * 5,
        out_specs=[spec for spec, _ in outs],
        out_shape=[shape for _, shape in outs],
        scratch_shapes=[
            pltpu.VMEM((group_tok, width), bf16),
            pltpu.VMEM((width, 3 * wide), bf16),
            pltpu.VMEM((n_seq, wide, part), bf16),
            pltpu.VMEM(expert_up.shape, bf16),
            pltpu.VMEM((3, hidden, head_part), bf16),
            pltpu.VMEM(share_up.shape, bf16),
            pltpu.VMEM((3, share_all, seq_part), bf16),
            pltpu.VMEM((group_tok, group_tok), f32),
            pltpu.VMEM((n_head - 1, rows, width), bf16),
            pltpu.VMEM((n_head - 1, rows, width), bf16),
            dma((13,)),
            dma((4, lines)),
            dma((4, lines)),
            dma((8, lines)),
            dma((8, lines)),
            dma((n_head - 1,)),
            dma((n_head - 1,)),
            dma((n_head - 1,)),
            dma((n_head - 1,)),
            dma((9,)),
            dma((9,)),
            dma((2 * n_seq,)),
            dma((2 * n_seq,)),
        ],
        compiler_params=pltpu.CompilerParams(
            collective_id=0, has_side_effects=True, vmem_limit_bytes=VMEM_BYTES
        ),
        cost_estimate=pl.CostEstimate(
            flops=2 * group_tok * width * 4 * wide, bytes_accessed=1 << 29, transcendentals=0
        ),
        name="forward",
    )(
        tokens, gain_first, gain_second, weight_own, wout_own, expert_up, expert_down, share_up,
        share_down, grad_ext, bias, cosine, sine, layout_col, layout_row,
    )


def mesh_part():
    return lax.axis_index("head") // 2


def token_bits():
    return bits_of(lax.axis_size("head"))[1:]


def token_gather(block):
    order = token_bits()
    column = lax.all_gather(block, "seq", axis=0, tiled=True)
    share = column.shape[0] // 2
    half = share // 2
    core = lax.rem(lax.axis_index("seq"), 2)
    own = lax.dynamic_slice_in_dim(column, core * share, share, 0)
    upper = spread(own[:half], order)
    lower = spread(own[half:], order[::-1])
    chunks = [column]
    for r in sorted(upper)[1:]:
        for piece in (upper[r], lower[r]):
            chunks.append(jnp.concatenate([piece, swap(piece, "seq", 1)], axis=0))
    return chunks


def token_scatter(chunks):
    order = token_bits()
    column = chunks[0]
    share = column.shape[0] // 2
    half = share // 2
    core = lax.rem(lax.axis_index("seq"), 2)
    own = lax.dynamic_slice_in_dim(column, core * share, share, 0)
    sides = [{0: own[:half]}, {0: own[half:]}]
    for i, chunk in enumerate(chunks[1:]):
        sides[i % 2][2 * (i // 2 + 1)] = chunk[:half] + swap(chunk[half:], "seq", 1)
    total = jnp.concatenate([collect(sides[0], order), collect(sides[1], order[::-1])], axis=0)
    column = lax.dynamic_update_slice_in_dim(column, total, core * share, 0)
    return lax.psum_scatter(column, "seq", scatter_dimension=0, tiled=True)


def total_over_all(values):
    for axis in ("head", "seq"):
        for bit in bits_of(lax.axis_size(axis)):
            values = values + swap(values, axis, bit)
    return values


def turn(values, cosine, sine):
    return values * cosine + pltpu.roll(values, HD // 2, 1) * sine


def mask_of(layout_col, layout_row):
    doc_col, place_col = layout_col[:, 0:1], layout_col[:, 1:2]
    doc_row, place_row = layout_row[0:1, :], layout_row[1:2, :]
    return jnp.where((doc_col == doc_row) & (place_row <= place_col), 0.0, NEGATIVE)


def head_forward(linear, cos, sin, mask):
    queries = turn(linear[:, :HD], cos, sin).astype(bf16)
    keys = turn(linear[:, HD : 2 * HD], cos, sin).astype(bf16)
    values = linear[:, 2 * HD :].astype(bf16)
    scores = dot(queries, keys, 1, 1) * HD ** (-0.5) + mask
    largest = jnp.max(scores, axis=1, keepdims=True)
    weights = jnp.exp(scores - largest)
    total = jnp.sum(weights, axis=1, keepdims=True)
    probs = (weights / total).astype(bf16)
    output = dot(probs, values, 1, 0).astype(bf16)
    return (queries, keys, values), output, largest + jnp.log(total)


def norm_rows(rows, gain):
    square = jnp.mean(rows * rows, axis=1, keepdims=True)
    return (rows * lax.rsqrt(square + EPS) * gain).astype(bf16)


def scatter_start(merged, wout, outgoing, incoming, sems_a, sems_b, rows, peers):
    blocks, _, size = wout.shape
    copies = []
    for r in range(len(peers) - 1, 0, -1):
        for b in range(blocks):
            outgoing[r - 1, :, b * size : (b + 1) * size] = dot(
                merged[r * rows : (r + 1) * rows, :], wout[b], 1, 0
            ).astype(bf16)
        copies.append(
            remote(
                outgoing.at[r - 1], incoming.at[r - 1], sems_a.at[r - 1], sems_b.at[r - 1],
                head=peers[r],
            )
        )
        copies[-1].start()
    return copies, [dot(merged[:rows, :], wout[b], 1, 0) for b in range(blocks)]


def attend_kernel(
    first, weight, wout, bias, cosine, sine, layout_col, layout_row, tokens, gain,
    qkv, merged, log_total, middle, lowered, mask, outgoing, incoming, sems_a, sems_b,
):
    n = pl.program_id(0)
    heads = pl.num_programs(0)
    peers = ring_places()

    @pl.when(n == 0)
    def _():
        greet([{"head": peer} for peer in peers[1:]])
        mask[...] = mask_of(layout_col[...], layout_row[...])

    linear = dot(first[...], weight[...], 1, 0) + bias[0]
    parts, output, log_sum = head_forward(linear, cosine[...], sine[...], mask[...])
    for k in range(3):
        qkv[:, k * HD : (k + 1) * HD] = parts[k]
    merged[:, pl.ds(pl.multiple_of(n * HD, HD), HD)] = output
    log_total[0] = jnp.broadcast_to(log_sum, log_total.shape[1:])

    @pl.when(n == heads - 1)
    def _():
        copies, own = scatter_start(
            merged, wout, outgoing, incoming, sems_a, sems_b, tokens.shape[0], peers
        )
        size = wout.shape[2]
        for b, block in enumerate(own):
            cols = slice(b * size, (b + 1) * size)
            middle[:, cols] = tokens[:, cols].astype(f32) + block
        for copy in copies:
            copy.wait()
        total = middle[...]
        for r in range(len(peers) - 1):
            total += incoming[r].astype(f32)
        middle[...] = total
        lowered[...] = norm_rows(total, gain[...])


def attend(first, weight, wout, bias, cosine, sine, layout_col, layout_row, tokens, gain):
    rows, width = first.shape
    heads = bias.shape[0]
    own = tokens.shape[0]
    others = lax.axis_size("head") - 1
    step = 3 * HD
    wide = heads * HD

    def whole(shape):
        return pl.BlockSpec(shape, lambda n: (0,) * len(shape))

    return pl.pallas_call(
        attend_kernel,
        grid=(heads,),
        in_specs=[
            whole((rows, width)),
            pl.BlockSpec((width, step), lambda n: (0, n)),
            whole(wout.shape),
            pl.BlockSpec((1, 1, step), lambda n: (n, 0, 0)),
            whole((rows, HD)),
            whole((rows, HD)),
            whole((rows, 2)),
            whole((2, rows)),
            whole((own, width)),
            whole((1, width)),
        ],
        out_specs=[
            pl.BlockSpec((rows, step), lambda n: (0, n)),
            whole((rows, wide)),
            pl.BlockSpec((1, rows, LANES), lambda n: (n, 0, 0)),
            whole((own, width)),
            whole((own, width)),
        ],
        out_shape=[
            jax.ShapeDtypeStruct((rows, heads * step), bf16),
            jax.ShapeDtypeStruct((rows, wide), bf16),
            jax.ShapeDtypeStruct((heads, rows, LANES), f32),
            jax.ShapeDtypeStruct((own, width), f32),
            jax.ShapeDtypeStruct((own, width), bf16),
        ],
        scratch_shapes=[
            pltpu.VMEM((rows, rows), f32),
            pltpu.VMEM((others, own, width), bf16),
            pltpu.VMEM((others, own, width), bf16),
            pltpu.SemaphoreType.DMA((others,)),
            pltpu.SemaphoreType.DMA((others,)),
        ],
        compiler_params=pltpu.CompilerParams(
            collective_id=2, has_side_effects=True, vmem_limit_bytes=VMEM_BYTES
        ),
        cost_estimate=pl.CostEstimate(
            flops=2 * rows * width * 4 * wide, bytes_accessed=8 * width * wide, transcendentals=0
        ),
        name="attend",
    )(first, weight, wout, bias, cosine, sine, layout_col, layout_row, tokens, gain)


def attend_back_kernel(
    grad_own, first, weight, wout, qkv, merged, log_total, cosine, sine, layout_col, layout_row,
    grad_first, grad_weight, grad_bias, mask, grad_merged, acc, grad, sems_a, sems_b,
):
    n = pl.program_id(0)
    peers = ring_places()
    own = grad_own.shape[0]
    heads = pl.num_programs(0)
    scale = HD ** (-0.5)
    blocks, _, size = grad_weight.shape
    wide = wout.shape[1]

    @pl.when(n == 0)
    def _():
        greet([{"head": peer} for peer in peers[1:]])
        copies = [
            remote(
                grad_own, grad.at[pl.ds(r * own, own)], sems_a.at[r - 1], sems_b.at[r - 1],
                head=peers[len(peers) - r],
            )
            for r in range(1, len(peers))
        ]
        for copy in copies:
            copy.start()
        grad[:own] = grad_own[...]
        mask[...] = mask_of(layout_col[...], layout_row[...])
        acc[...] = jnp.zeros_like(acc)
        for copy in copies:
            copy.wait()
        total = jnp.zeros((grad.shape[0], wide), f32)
        for s in range(blocks):
            total += dot(grad[:, s * size : (s + 1) * size], wout[s], 1, 1)
        grad_merged[...] = total.astype(bf16)
        for s in range(blocks):
            grad_weight[s, 3 * wide :, :] = dot(
                merged[...], grad[:, s * size : (s + 1) * size], 0, 0
            ).astype(bf16)

    cos, sin = cosine[...], -sine[...]
    queries, keys, values = qkv[:, :HD], qkv[:, HD : 2 * HD], qkv[:, 2 * HD :]
    grad_out = grad_merged[:, pl.ds(pl.multiple_of(n * HD, HD), HD)]
    scores = dot(queries, keys, 1, 1) * scale + mask[...]
    probs = jnp.exp(scores - log_total[0][:, 0:1])
    grad_values = dot(probs.astype(bf16), grad_out, 0, 0).astype(bf16)
    grad_probs = dot(grad_out, values, 1, 1)
    centre = jnp.sum(probs * grad_probs, axis=1, keepdims=True)
    grad_scores = (probs * (grad_probs - centre)).astype(bf16)
    grad_queries = (dot(grad_scores, keys, 1, 0) * scale).astype(bf16).astype(f32)
    grad_keys = (dot(grad_scores, queries, 0, 0) * scale).astype(bf16).astype(f32)
    grad_linear = jnp.concatenate(
        [turn(grad_queries, cos, sin).astype(bf16), turn(grad_keys, cos, sin).astype(bf16), grad_values],
        axis=1,
    )
    grad_bias[0] = jnp.sum(grad_linear.astype(f32), axis=0, keepdims=True)
    acc[...] += dot(grad_linear, weight[...], 1, 1)
    step = 3 * HD
    for s in range(blocks):
        grad_weight[s, pl.ds(pl.multiple_of(n * step, HD), step), :] = dot(
            grad_linear, first[:, s * size : (s + 1) * size], 0, 0
        ).astype(bf16)

    @pl.when(n == heads - 1)
    def _():
        grad_first[...] = acc[...].astype(bf16)


def attend_back(grad, first, weight, wout, qkv, merged, log_total, cosine, sine, layout_col, layout_row):
    rows, width = first.shape
    heads = log_total.shape[0]
    step = 3 * HD
    wide = heads * HD
    n_seq = lax.axis_size("seq")
    size = width // n_seq
    own = grad.shape[0]
    others = lax.axis_size("head") - 1

    def whole(shape):
        return pl.BlockSpec(shape, lambda n: (0,) * len(shape))

    return pl.pallas_call(
        attend_back_kernel,
        grid=(heads,),
        in_specs=[
            whole((own, width)),
            whole((rows, width)),
            pl.BlockSpec((width, step), lambda n: (0, n)),
            whole(wout.shape),
            pl.BlockSpec((rows, step), lambda n: (0, n)),
            whole((rows, wide)),
            pl.BlockSpec((1, rows, LANES), lambda n: (n, 0, 0)),
            whole((rows, HD)),
            whole((rows, HD)),
            whole((rows, 2)),
            whole((2, rows)),
        ],
        out_specs=[
            whole((rows, width)),
            whole((n_seq, 4 * wide, size)),
            pl.BlockSpec((1, 1, step), lambda n: (n, 0, 0)),
        ],
        out_shape=[
            jax.ShapeDtypeStruct((rows, width), bf16),
            jax.ShapeDtypeStruct((n_seq, 4 * wide, size), bf16),
            jax.ShapeDtypeStruct((heads, 1, step), f32),
        ],
        scratch_shapes=[
            pltpu.VMEM((rows, rows), f32),
            pltpu.VMEM((rows, wide), bf16),
            pltpu.VMEM((rows, width), f32),
            pltpu.VMEM((rows, width), bf16),
            pltpu.SemaphoreType.DMA((others,)),
            pltpu.SemaphoreType.DMA((others,)),
        ],
        compiler_params=pltpu.CompilerParams(
            collective_id=3, has_side_effects=True, vmem_limit_bytes=VMEM_BYTES
        ),
        cost_estimate=pl.CostEstimate(
            flops=4 * rows * width * 4 * wide, bytes_accessed=16 * width * wide, transcendentals=0
        ),
        name="attend_back",
    )(grad, first, weight, wout, qkv, merged, log_total, cosine, sine, layout_col, layout_row)


def pack_kernel(exp_units, share_units, at, *refs):
    stacked, shares = refs[0], refs[-5:-3]
    experts = [stacked.at[r] for r in range(stacked.shape[0])]
    rest, full, sems = refs[-3:]
    head = at[0]
    copies = []
    for r, block in enumerate(experts):
        size = block.shape[2]
        start = pl.multiple_of(jnp.bitwise_xor(head, r) * size, size)
        copies.append(
            pltpu.make_async_copy(
                block, full.at[:, pl.ds(0, exp_units), pl.ds(start, size)], sems.at[len(copies)]
            )
        )
    for r, block in enumerate(shares):
        size = block.shape[3]
        for s in range(block.shape[0]):
            copies.append(
                pltpu.make_async_copy(
                    block.at[s],
                    full.at[:, pl.ds(exp_units + r * share_units, share_units), pl.ds(s * size, size)],
                    sems.at[len(copies)],
                )
            )
    base = exp_units + 2 * share_units
    copies.append(
        pltpu.make_async_copy(rest, full.at[:, pl.ds(base, rest.shape[1]), :], sems.at[len(copies)])
    )
    for copy in copies:
        copy.start()
    for copy in copies:
        copy.wait()


def pack(at, experts, shares, rest, unit_rows):
    exp_units, share_units = experts.shape[2], shares[0].shape[2]
    count = experts.shape[0] + 2 * shares[0].shape[0] + 1
    anywhere = pl.BlockSpec(memory_space=pl.ANY)
    return pl.pallas_call(
        functools.partial(pack_kernel, exp_units, share_units),
        in_specs=[pl.BlockSpec(memory_space=pltpu.SMEM)] + [anywhere] * 4,
        out_specs=anywhere,
        out_shape=jax.ShapeDtypeStruct((3, unit_rows, rest.shape[2]), bf16),
        scratch_shapes=[pltpu.SemaphoreType.DMA((count,))],
        compiler_params=pltpu.CompilerParams(vmem_limit_bytes=1 << 20),
        cost_estimate=pl.CostEstimate(
            flops=0, bytes_accessed=12 * unit_rows * rest.shape[2], transcendentals=0
        ),
        name="pack",
    )(at, experts, *shares, rest)


def mix_rows(exp_units, base, n_exp, x, grad_ext, w, wait=None):
    rows, width = x.shape
    unit_rows = w.shape[1]
    seq = lax.axis_index("seq")
    gate = dot(x, w[0], 1, 1)
    if wait is not None:
        wait(1)
    up = dot(x, w[1], 1, 1)
    if wait is not None:
        wait(2)
    raw = dot(grad_ext[:, :width], w[2], 1, 1)
    block = base // LANES * LANES
    logits = gate[:, block : block + LANES]
    lane = lax.broadcasted_iota(jnp.int32, (rows, LANES), 1)
    from_base = lane - (base - block)
    is_logit = (from_base >= 0) & (from_base < n_exp)
    largest = jnp.max(jnp.where(is_logit, logits, NEGATIVE), axis=1, keepdims=True)
    powers = jnp.where(is_logit, jnp.exp(jnp.where(is_logit, logits - largest, 0.0)), 0.0)
    chosen = jnp.sum(jnp.where(from_base == seq, powers, 0.0), axis=1, keepdims=True)
    marks = grad_ext[:, width:].astype(f32)
    mark = jnp.sum(jnp.where(lane == seq, marks, 0.0), axis=1, keepdims=True)
    gate_here = mark * chosen / jnp.sum(powers, axis=1, keepdims=True)
    share_gate = jax.nn.sigmoid(
        jnp.sum(jnp.where(from_base == n_exp, logits, 0.0), axis=1, keepdims=True)
    )
    unit = lax.broadcasted_iota(jnp.int32, (rows, unit_rows), 1)
    is_expert = unit < exp_units
    factor = jnp.where(is_expert, gate_here, share_gate)
    sigma = jax.nn.sigmoid(gate)
    silu = gate * sigma
    hidden = silu * up
    scaled = (hidden * factor).astype(bf16)
    both = hidden * raw
    all_sum = jnp.sum(both, axis=1, keepdims=True)
    exp_sum = jnp.sum(jnp.where(is_expert, both, 0.0), axis=1, keepdims=True)
    grad_hidden = raw * factor
    grad_gate = (grad_hidden * up * (sigma + silu * (1.0 - sigma))).astype(bf16)
    grad_up = (grad_hidden * silu).astype(bf16)
    back = dot(grad_gate, w[0], 1, 0) + dot(grad_up, w[1], 1, 0)
    extra = jnp.where(
        lane == seq, exp_sum * mark, jnp.where(lane == n_exp, all_sum - exp_sum, 0.0)
    )
    return (grad_gate, grad_up, scaled), back.astype(bf16), extra.astype(bf16)


def mix_local_kernel(exp_units, base, n_exp, second, grad_ext, w_hbm, back, unit_out, w, sems):
    copies = [pltpu.make_async_copy(w_hbm.at[m], w.at[m], sems.at[m]) for m in range(3)]
    width = second.shape[1]

    @pl.when(pl.program_id(0) == 0)
    def _():
        for copy in copies:
            copy.start()
        for copy in copies:
            copy.wait()

    units, rows_back, extra = mix_rows(exp_units, base, n_exp, second[...], grad_ext, w)
    for m in range(3):
        unit_out[m] = units[m]
    back[:, :width] = rows_back
    back[:, width:] = extra


def mix_local(second, grad_ext, full, exp_units, base, n_exp):
    rows, width = second.shape
    unit_rows = full.shape[1]
    wide = grad_ext.shape[1]
    return pl.pallas_call(
        functools.partial(mix_local_kernel, exp_units, base, n_exp),
        grid=(rows // TILE,),
        in_specs=[
            pl.BlockSpec((TILE, width), lambda i: (i, 0)),
            pl.BlockSpec((TILE, wide), lambda i: (i, 0)),
            pl.BlockSpec(memory_space=pl.ANY),
        ],
        out_specs=[
            pl.BlockSpec((TILE, wide), lambda i: (i, 0)),
            pl.BlockSpec((3, TILE, unit_rows), lambda i: (0, i, 0)),
        ],
        out_shape=[
            jax.ShapeDtypeStruct((rows, wide), bf16),
            jax.ShapeDtypeStruct((3, rows, unit_rows), bf16),
        ],
        scratch_shapes=[
            pltpu.VMEM((3, unit_rows, width), bf16),
            pltpu.SemaphoreType.DMA((3,)),
        ],
        compiler_params=pltpu.CompilerParams(vmem_limit_bytes=VMEM_BYTES),
        cost_estimate=pl.CostEstimate(
            flops=10 * rows * width * unit_rows,
            bytes_accessed=6 * unit_rows * width + 8 * rows * width,
            transcendentals=0,
        ),
        name="mix_local",
    )(second, grad_ext, full)


def mix_kernel(
    exp_units, base, n_exp, second, grad_ext, w_hbm, unit_out, back,
    w, held, core_in, home, w_sem, b_a, b_b, h_a, h_b, o_sem,
):
    i = pl.program_id(0)
    _, near_y, near_core = plane_places()
    core = lax.axis_index("seq") % 2
    rows, width = second.shape[2:]
    at = [pl.ds(j * rows, rows) for j in range(2)]
    loads = [pltpu.make_async_copy(w_hbm.at[m], w.at[m], w_sem.at[m]) for m in range(3)]
    back_c = [
        remote(held.at[j, 1 - core], core_in.at[j], b_a.at[j], b_b.at[j], seq=near_core)
        for j in range(2)
    ]
    back_y = [
        remote(held.at[j, core], home.at[j], h_a.at[j], h_b.at[j], head=near_y) for j in range(2)
    ]

    def wait_weights(m):
        @pl.when(i == 0)
        def _():
            loads[m].wait()

    @pl.when(i == 0)
    def _():
        greet([{"head": near_y}, {"seq": near_core}])
        for copy in loads:
            copy.start()

    wait_weights(0)
    for c in range(2):
        units, rows_back, extra = mix_rows(
            exp_units, base, n_exp, second[0, c], grad_ext.at[0, c], w, wait_weights if c == 0 else None
        )
        for m in range(3):
            unit_out[m, 0, c] = units[m]
        held[i, c, :, :width] = rows_back
        held[i, c, :, width:] = extra
        if c == 0:
            for j in range(2):

                @pl.when(i == 1 + j)
                def _():
                    back_c[j].wait_recv()
                    held[j, core] = (held[j, core].astype(f32) + core_in[j].astype(f32)).astype(bf16)
                    back_y[j].start()

    for j in range(2):

        @pl.when(i == j)
        def _():
            back_c[j].start()

    @pl.when(i == 3)
    def _():
        out = [
            [
                pltpu.make_async_copy(held.at[2 + j, c], back.at[c, at[j]], o_sem.at[j, k])
                for k, c in enumerate((1 - core, core))
            ]
            for j in range(2)
        ]
        for j in range(2):
            out[j][0].start()
        for j in range(2):
            back_y[j].wait_recv()
            held[2 + j, core] = (held[2 + j, core].astype(f32) + home[j].astype(f32)).astype(bf16)
            out[j][1].start()
        for j in range(2):
            out[j][0].wait()
            out[j][1].wait()
            back_c[j].wait_send()
            back_y[j].wait_send()


def mix(seconds, grads, full, exp_units, base, n_exp):
    rows, width = seconds.shape[1:]
    unit_rows = full.shape[1]
    wide = grads.shape[2]
    half = rows // 2
    piece = half // 2
    anywhere = pl.BlockSpec(memory_space=pl.ANY)
    units, back = pl.pallas_call(
        functools.partial(mix_kernel, exp_units, base, n_exp),
        grid=(4,),
        in_specs=[
            pl.BlockSpec((1, 2, piece, width), lambda i: (1 - i // 2, 0, i % 2, 0)),
            pl.BlockSpec((1, 2, piece, wide), lambda i: (1 - i // 2, 0, i % 2, 0)),
            anywhere,
        ],
        out_specs=[
            pl.BlockSpec((3, 1, 2, piece, unit_rows), lambda i: (0, 1 - i // 2, 0, i % 2, 0)),
            anywhere,
        ],
        out_shape=[
            jax.ShapeDtypeStruct((3, 2, 2, half, unit_rows), bf16),
            jax.ShapeDtypeStruct((2, half, wide), bf16),
        ],
        scratch_shapes=[
            pltpu.VMEM((3, unit_rows, width), bf16),
            pltpu.VMEM((4, 2, piece, wide), bf16),
            pltpu.VMEM((2, piece, wide), bf16),
            pltpu.VMEM((2, piece, wide), bf16),
            pltpu.SemaphoreType.DMA((3,)),
            *[pltpu.SemaphoreType.DMA((2,))] * 4,
            pltpu.SemaphoreType.DMA((2, 2)),
        ],
        compiler_params=pltpu.CompilerParams(
            collective_id=4, has_side_effects=True, vmem_limit_bytes=VMEM_BYTES
        ),
        cost_estimate=pl.CostEstimate(
            flops=20 * rows * width * unit_rows,
            bytes_accessed=6 * unit_rows * width + 16 * rows * width,
            transcendentals=0,
        ),
        name="mix",
    )(seconds.reshape(2, 2, half, width), grads.reshape(2, 2, half, wide), full)
    return units.reshape(3, 2, rows, unit_rows), back.reshape(rows, wide)


def unit_grads_kernel(count, exp_units, share_rows, at, *refs):
    units, seconds, grads = refs[:count], refs[count : 2 * count], refs[2 * count : 3 * count]
    experts, share_own, share_far = refs[3 * count :]
    m = pl.program_id(0)

    def run(rights):
        acc = dot(units[0][...], rights[0][...], 0, 0)
        for left, right in zip(units[1:], rights[1:]):
            acc += dot(left[...], right[...], 0, 0)
        experts[0, 0] = acc[:exp_units].astype(bf16)
        size = share_own.shape[3]
        for s in range(share_own.shape[0]):
            piece = acc[exp_units : exp_units + 2 * share_rows, s * size : (s + 1) * size].astype(bf16)
            share_own[s, 0] = piece[:share_rows]
            share_far[s, 0] = piece[share_rows:]

    @pl.when(m < 2)
    def _():
        run(seconds)

    @pl.when(m == 2)
    def _():
        run(grads)


def unit_grads(at, units, seconds, grads, exp_units, share_rows):
    n_head, n_seq = lax.axis_size("head"), lax.axis_size("seq")
    width = seconds[0][0].shape[2]
    unit_rows = units[0][0].shape[3]
    head_part, seq_part = width // n_head, width // n_seq
    near = n_seq // n_head
    rows = sum(block.shape[1] for block, _ in seconds)

    def far(r, at):
        return jnp.bitwise_xor(at[0], r)

    def place(q, m, r, at):
        return (m, q, 0, 0)

    def second_place(q, m, r, at):
        return (q, 0, jnp.where(m < 2, far(r, at), far(n_head - 1, at)))

    def grad_place(q, m, r, at):
        return (q, 0, jnp.where(m < 2, far(0, at), far(r, at)))

    in_specs = [
        pl.BlockSpec((None, None, block.shape[2], unit_rows), functools.partial(place, q))
        for block, q in units
    ]
    in_specs += [
        pl.BlockSpec((None, block.shape[1], head_part), functools.partial(second_place, q))
        for block, q in seconds
    ]
    in_specs += [
        pl.BlockSpec((None, block.shape[1], head_part), functools.partial(grad_place, q))
        for block, q in grads
    ]
    share_spec = pl.BlockSpec((near, 1, share_rows, seq_part), lambda m, r, at: (far(r, at), m, 0, 0))
    share_shape = jax.ShapeDtypeStruct((n_seq, 3, share_rows, seq_part), bf16)
    return pl.pallas_call(
        functools.partial(unit_grads_kernel, len(units), exp_units, share_rows),
        grid_spec=pltpu.PrefetchScalarGridSpec(
            num_scalar_prefetch=1,
            grid=(3, n_head),
            in_specs=in_specs,
            out_specs=[
                pl.BlockSpec((1, 1, exp_units, head_part), lambda m, r, at: (r, m, 0, 0)),
                share_spec,
                share_spec,
            ],
        ),
        out_shape=[
            jax.ShapeDtypeStruct((n_head, 3, exp_units, head_part), bf16),
            share_shape,
            share_shape,
        ],
        compiler_params=pltpu.CompilerParams(vmem_limit_bytes=VMEM_BYTES),
        cost_estimate=pl.CostEstimate(
            flops=6 * rows * width * unit_rows,
            bytes_accessed=6 * rows * unit_rows + 8 * rows * width + 6 * width * unit_rows,
            transcendentals=0,
        ),
        name="unit_grads",
    )(at, *(block for block, _ in units + seconds + grads))


def after(value, *others):
    return lax.optimization_barrier((value, *others))[0]


def shards(
    tokens,
    cotangent,
    arrange,
    doc_lengths,
    routes,
    norm1_gain,
    qkv_weight,
    qkv_bias,
    out_weight,
    norm2_gain,
    router_weight,
    shared_gate_vec,
    shared_gate_up,
    shared_down,
    expert_gate_up,
    expert_down,
):
    highest = lax.Precision.HIGHEST
    tok_rows, width = tokens.shape
    n_seq = lax.axis_size("seq")
    n_head = lax.axis_size("head")
    seq = lax.axis_index("seq")
    head = lax.axis_index("head")
    group_tok = tok_rows * n_head
    heads_here = qkv_weight.shape[1]
    n_exp = router_weight.shape[1]
    hidden_all = expert_down.shape[1]
    parts = n_head // 2
    part = mesh_part()
    exp_units = hidden_all // parts
    share_all = shared_down.shape[0]
    share_units = share_all // n_seq
    share_rows = -(-share_units // 16) * 16
    base = exp_units + 2 * share_rows
    unit_rows = -(-(base + n_exp + 1) // LANES) * LANES
    seq_part = width // n_seq
    head_part = width // n_head

    wide = heads_here * HD
    plane = parts == 2 and n_seq == 8
    expert_up = expert_gate_up[0]
    at = jnp.stack([head, seq]).astype(jnp.int32)
    gate_rows = jnp.concatenate([router_weight.T, shared_gate_vec[None, :]], axis=0)
    rest = jnp.zeros((3, unit_rows - base, width), bf16).at[0, : n_exp + 1].set(gate_rows)

    place, doc_index, position = layout_of(arrange[0], doc_lengths[0], group_tok)
    blocks = (head + jnp.arange(n_head, dtype=jnp.int32)) % n_head
    table = jnp.stack([place, doc_index, position]).reshape(3, n_head, tok_rows)
    place, doc_index, position = jnp.take(table, blocks, axis=1).reshape(3, group_tok)
    layout_row = jnp.stack([doc_index, place])
    layout_col = layout_row.T
    cosine, sine = rope_tables(position.astype(f32))
    cosine = jnp.concatenate([cosine, cosine], axis=1)
    sine = jnp.concatenate([-sine, sine], axis=1)
    bias_here = lax.dynamic_slice_in_dim(qkv_bias, head * heads_here, heads_here, 0)
    bias_here = bias_here.astype(f32)[:, None, :]

    expert_ids = jnp.arange(n_exp, dtype=jnp.int32)
    chosen = jnp.any(routes[:, :, None] == expert_ids[None, None, :], axis=1)
    marks = jnp.concatenate(
        [chosen.astype(bf16), jnp.zeros((tok_rows, LANES - n_exp), bf16)], axis=1
    )
    grad_ext = jnp.concatenate([cotangent, marks], axis=1)

    stream = tokens.astype(f32)
    gain_first = norm1_gain.astype(f32)
    scale_first = rms_scale(stream)
    normed_first = stream * scale_first
    gain_second = norm2_gain.astype(f32)
    weight_own = qkv_weight.reshape(seq_part, 3 * wide)
    if plane:
        (
            first_group, weight, wout, experts, share_own, share_far, grad_both, seconds,
            qkv, merged, log_total, middle, lowered_second,
        ) = forward(
            tokens, gain_first[None, :], gain_second[None, :], weight_own, out_weight, expert_up,
            expert_down[0], shared_gate_up.reshape(seq_part, 2 * share_all), shared_down, grad_ext,
            bias_here, cosine, sine, layout_col, layout_row,
        )
        full = pack(at, experts, [share_own, share_far], rest, unit_rows)
        grad_both = grad_both.reshape(2, n_seq * tok_rows, width + LANES)
        seconds = seconds.reshape(2, n_seq * tok_rows, width)
        units, back_column = mix(seconds, grad_both, full, exp_units, base, n_exp)
        grad_experts, grad_share, grad_share_far = unit_grads(
            at,
            [(units, 0), (units, 1)],
            [(seconds, 0), (seconds, 1)],
            [(grad_both, 0), (grad_both, 1)],
            exp_units,
            share_rows,
        )
        back_own = lax.psum_scatter(back_column, "seq", scatter_dimension=0, tiled=True)
        half = n_seq * tok_rows // 2
        out = dot(units[2].reshape(-1, unit_rows), full[2], 1, 0).astype(bf16)
        out = out.reshape(2, 2, half, width)
        core = lax.rem(seq, 2)
        pair = lax.dynamic_index_in_dim(out[1], core, 0, keepdims=False) + swap(
            lax.dynamic_index_in_dim(out[1], 1 - core, 0, keepdims=False), "seq", 1
        )
        pair = swap(pair, "head", 2)
        is_core = jnp.arange(2, dtype=jnp.int32)[:, None, None] == core
        out_column = out[0] + jnp.where(is_core, pair[None], 0.0).astype(bf16)
        out_own = lax.psum_scatter(
            out_column.reshape(2 * half, width), "seq", scatter_dimension=0, tiled=True
        )
    else:
        weight = lax.all_gather(weight_own, "seq", axis=0, tiled=True)
        wout = lax.all_gather(out_weight, "seq", axis=0)
        first_group = group_gather((normed_first * gain_first).astype(bf16))
        send = jnp.stack([expert_up[:, :hidden_all].T, expert_up[:, hidden_all:].T, expert_down[0]])
        near = []
        for t in range(parts):
            there = jnp.bitwise_xor(part, t)
            block = lax.dynamic_slice_in_dim(send, there * exp_units, exp_units, 1)
            near.append(swap(block, "head", 2 * t) if t else block)
        experts = jnp.stack([block for own in near for block in (own, swap(own, "head", 1))])
        send = jnp.stack([shared_gate_up[:, 0].T, shared_gate_up[:, 1].T, shared_down])
        send = jnp.transpose(send.reshape(3, n_seq, share_units, seq_part), (1, 0, 2, 3))
        if share_rows > share_units:
            send = jnp.pad(send, ((0, 0), (0, 0), (0, share_rows - share_units), (0, 0)))
        share_own = lax.all_to_all(send, "seq", split_axis=0, concat_axis=0)
        full = pack(at, experts, [share_own, swap(share_own, "head", 1)], rest, unit_rows)
        qkv, merged, log_total, middle, lowered_second = attend(
            first_group, weight, wout, bias_here, cosine, sine, layout_col, layout_row, tokens,
            gain_second[None, :],
        )
        grad_chunks = token_gather(grad_ext)
        second_chunks = token_gather(lowered_second)
        back_chunks = []
        unit_chunks = []
        for second, grad in zip(second_chunks, grad_chunks):
            back, units = mix_local(second, grad, full, exp_units, base, n_exp)
            back_chunks.append(back)
            unit_chunks.append(units)
        grad_experts, grad_share, grad_share_far = unit_grads(
            at,
            [(units[:, None], 0) for units in unit_chunks],
            [(second[None], 0) for second in second_chunks],
            [(grad[None], 0) for grad in grad_chunks],
            exp_units,
            share_rows,
        )
        out_chunks = [dot(units[2], full[2], 1, 0).astype(bf16) for units in unit_chunks]
        back_own = token_scatter(back_chunks)
        out_own = token_scatter(out_chunks)
    scale_second = rms_scale(middle)
    normed_second = middle * scale_second

    back_own = after(back_own, grad_experts).astype(f32)
    out_own = out_own.astype(f32)
    mixed = (middle + out_own).astype(bf16)

    logits = dot(lowered_second, gate_rows, 1, 1)
    probs = jax.nn.softmax(logits[:, :n_exp], axis=-1)
    share_gate = jax.nn.sigmoid(logits[:, n_exp:])
    grad_probs = back_own[:, width : width + n_exp]
    grad_logits = probs * (grad_probs - jnp.sum(probs * grad_probs, axis=1, keepdims=True))
    grad_gate_logit = (
        back_own[:, width + n_exp : width + n_exp + 1] * share_gate * (1.0 - share_gate)
    )
    small = jnp.concatenate([grad_logits, grad_gate_logit], axis=1)
    grad_second = back_own[:, :width] + jnp.dot(
        small, gate_rows.astype(f32), precision=highest
    )
    grad_gate_cols = jnp.dot(small.T, lowered_second.astype(f32), precision=highest)
    grad_gain_second = jnp.sum(grad_second * normed_second, axis=0)
    grad_normed = grad_second * gain_second
    grad_middle = cotangent.astype(f32) + scale_second * (
        grad_normed - normed_second * jnp.mean(grad_normed * normed_second, axis=1, keepdims=True)
    )
    totals_second = total_over_all(
        jnp.concatenate([grad_gate_cols, grad_gain_second[None, :]], axis=0)
    )

    grad_first, grad_weight, grad_bias_here = attend_back(
        grad_middle.astype(bf16), first_group, weight, wout, qkv, merged, log_total, cosine, sine, layout_col, layout_row
    )
    grad_first = group_scatter(grad_first)
    grad_weight = lax.psum_scatter(grad_weight, "seq", scatter_dimension=0, tiled=False)
    grad_bias = lax.dynamic_update_slice_in_dim(
        jnp.zeros(qkv_bias.shape, f32), grad_bias_here[:, 0], head * heads_here, 0
    )
    grad_gain_first = jnp.sum(grad_first * normed_first, axis=0)
    grad_normed_first = grad_first * gain_first
    input_grad = grad_middle + scale_first * (
        grad_normed_first
        - normed_first * jnp.mean(grad_normed_first * normed_first, axis=1, keepdims=True)
    )
    totals_first = total_over_all(
        jnp.concatenate([grad_gain_first, grad_bias.reshape(-1)]).reshape(-1, LANES)
    ).reshape(-1)

    grad_share = grad_share + swap(grad_share_far, "head", 1)
    grad_share = lax.all_to_all(grad_share[:, :, :share_units], "seq", split_axis=0, concat_axis=0)
    grad_share = jnp.transpose(grad_share, (1, 0, 2, 3)).reshape(3, share_all, seq_part).astype(f32)
    own = {}
    for t in range(parts)[::-1]:
        total = grad_experts[2 * t] + swap(grad_experts[2 * t + 1], "head", 1)
        own[t] = swap(total, "head", 2 * t) if t else total
    own = jnp.stack([own[t] for t in range(parts)])
    own = jnp.take(own, jnp.bitwise_xor(part, jnp.arange(parts, dtype=jnp.int32)), axis=0)
    own = jnp.transpose(own, (1, 0, 2, 3)).reshape(3, hidden_all, head_part).astype(f32)
    return (
        mixed,
        input_grad,
        totals_first[:width],
        grad_weight[: 3 * wide].astype(f32).T.reshape(qkv_weight.shape),
        totals_first[width:].reshape(qkv_bias.shape),
        grad_weight[3 * wide :].astype(f32),
        totals_second[n_exp + 1],
        totals_second[:n_exp].T,
        totals_second[n_exp],
        jnp.stack([grad_share[0].T, grad_share[1].T], axis=1),
        grad_share[2],
        jnp.concatenate([own[0].T, own[1].T], axis=1)[None],
        own[2][None],
    )


def solution(mesh):
    return jax.shard_map(
        shards,
        mesh=mesh,
        in_specs=(
            P(("seq", "head"), None),
            P(("seq", "head"), None),
            P("seq", None),
            P("seq", None),
            P(("seq", "head"), None),
            P(),
            P("seq", "head", None),
            P(),
            P("head", "seq"),
            P(),
            P(),
            P(),
            P("seq", None, "head"),
            P("head", "seq"),
            P("seq", "head", None),
            P("seq", None, "head"),
        ),
        out_specs=(
            P(("seq", "head"), None),
            P(("seq", "head"), None),
            P(),
            P("seq", "head", None),
            P(),
            P("head", "seq"),
            P(),
            P(),
            P(),
            P("seq", None, "head"),
            P("head", "seq"),
            P("seq", "head", None),
            P("seq", None, "head"),
        ),
        check_vma=False,
    )
```

```python
import functools

import jax
import jax.numpy as jnp
from jax import lax
from jax.experimental import pallas as pl
from jax.experimental.pallas import tpu as pltpu
from jax.sharding import PartitionSpec as P

HD = 128
EPS = 1e-06
THETA = 1000000.0
NEGATIVE = -1e30
LANES = 128
TILE = 256
MESH = pl.DeviceIdType.MESH
VMEM_BYTES = 60 * 1024 * 1024
bf16 = jnp.bfloat16
f32 = jnp.float32


def rms_scale(values):
    return lax.rsqrt(jnp.mean(values * values, axis=-1, keepdims=True) + EPS)


def rope_tables(position):
    half = HD // 2
    exponent = jnp.arange(half, dtype=f32) * (2.0 / HD)
    frequency = THETA ** (-exponent)
    angle = position[:, None] * frequency[None, :]
    return (jnp.cos(angle), jnp.sin(angle))


def layout_of(arrange_row, length_row, group_tok):
    counter = jnp.arange(group_tok, dtype=jnp.int32)
    place = jnp.sum(
        jnp.where(arrange_row[None, :] == counter[:, None], counter[None, :], 0),
        axis=1,
        dtype=jnp.int32,
    )
    ends = jnp.cumsum(length_row, dtype=jnp.int32)
    starts = ends - length_row
    doc_index = jnp.sum(
        (place[:, None] >= ends[None, :]).astype(jnp.int32), axis=1, dtype=jnp.int32
    )
    picked = doc_index[:, None] == jnp.arange(length_row.shape[0], dtype=jnp.int32)[None, :]
    start_of = jnp.sum(jnp.where(picked, starts[None, :], 0), axis=1, dtype=jnp.int32)
    return (place, doc_index, place - start_of)


def dot(left, right, left_dim, right_dim):
    return lax.dot_general(
        left, right, (((left_dim,), (right_dim,)), ((), ())), preferred_element_type=f32
    )


def swap(block, axis, bit):
    size = lax.axis_size(axis)
    return lax.ppermute(block, axis, [(i, i ^ bit) for i in range(size)])


def bits_of(size):
    bits = []
    bit = 1
    while bit < size:
        bits.append(bit)
        bit *= 2
    return bits


def spread(block, order):
    found = {0: block}
    for bit in order:
        for near in sorted(found):
            found[near ^ bit] = swap(found[near], "head", bit)
    return found


def collect(parts, order):
    parts = dict(parts)
    for bit in reversed(order):
        for far in sorted((r for r in parts if r & bit), reverse=True):
            parts[far ^ bit] = parts[far ^ bit] + swap(parts.pop(far), "head", bit)
    return parts[0]


def shift(block, axis, step):
    size = lax.axis_size(axis)
    return lax.ppermute(block, axis, [((i + step) % size, i) for i in range(size)])


def group_gather(block):
    size = lax.axis_size("head")
    return jnp.concatenate([block] + [shift(block, "head", r) for r in range(1, size)], axis=0)


def group_scatter(block):
    size = lax.axis_size("head")
    rows = block.shape[0] // size
    total = block[:rows].astype(f32)
    for r in range(1, size):
        total += shift(block[r * rows : (r + 1) * rows], "head", size - r).astype(f32)
    return total


def remote(src, dst, send_sem, recv_sem, **place):
    return pltpu.make_async_remote_copy(
        src_ref=src,
        dst_ref=dst,
        send_sem=send_sem,
        recv_sem=recv_sem,
        device_id=place,
        device_id_type=MESH,
    )


def greet(places):
    barrier = pltpu.get_barrier_semaphore()
    for place in places:
        pl.semaphore_signal(barrier, inc=1, device_id=place, device_id_type=MESH)
    pl.semaphore_wait(barrier, len(places))


def plane_places():
    head, seq = lax.axis_index("head"), lax.axis_index("seq")
    x, y = head % 2, head // 2
    return y * 2 + (1 - x), (1 - y) * 2 + x, seq + 1 - 2 * (seq % 2)


def plane_owners():
    head = lax.axis_index("head")
    near_x, near_y, _ = plane_places()
    return head, near_x, near_y, near_y + 1 - 2 * (head % 2)


def ring_places():
    size = lax.axis_size("head")
    head = lax.axis_index("head")
    return [(head + r) % size for r in range(size)]


class Line:
    def __init__(self, place, far, sems):
        self.seq = lax.axis_index("seq")
        self.count = lax.axis_size("seq") // 2
        self.depth = self.count - 1
        self.z = self.seq // 2
        _, self.near_y, self.near_core = plane_places()
        self.place, self.far = place, far
        self.sems = sems

    def index(self, j):
        if j == 0:
            return self.seq
        if j <= self.depth:
            return self.seq - 2 * j
        return self.seq + 2 * (j - self.depth)

    def valid(self, j):
        if j == 0:
            return self.z >= 0
        if j <= self.depth:
            return self.z - j >= 0
        return self.z + (j - self.depth) < self.count

    def line_copy(self, j, up):
        block = self.place(self.index(j))
        if up:
            to, k = self.seq + 2, j
        else:
            to, k = self.seq - 2, self.depth + (j - self.depth if j else 0)
        return remote(block, block, self.sems.at[0, k], self.sems.at[1, k], seq=to)

    def line_arrival(self, j):
        block = self.place(self.index(j))
        return remote(
            block, block, self.sems.at[0, j - 1], self.sems.at[1, j - 1], seq=self.near_core
        )

    def core_copy(self, j):
        block = self.place(self.index(j))
        return remote(block, block, self.sems.at[2, j], self.sems.at[3, j], seq=self.near_core)

    def core_arrival(self, j):
        block = self.place(self.index(j) + self.near_core - self.seq)
        return remote(block, block, self.sems.at[2, j], self.sems.at[3, j], seq=self.near_core)

    def far_copy(self, j):
        i = self.index(j)
        return remote(
            self.place(i), self.far(i), self.sems.at[4, j], self.sems.at[5, j], head=self.near_y
        )

    def far_core_copy(self, j):
        there = self.far(self.index(j))
        return remote(there, there, self.sems.at[6, j], self.sems.at[7, j], seq=self.near_core)

    def far_core_arrival(self, j):
        there = self.far(self.index(j) + self.near_core - self.seq)
        return remote(there, there, self.sems.at[6, j], self.sems.at[7, j], seq=self.near_core)

    def sides(self, j):
        self.core_copy(j).start()
        if self.far is not None:
            self.far_copy(j).start()

    def ups(self):
        return range(self.depth)

    def downs(self):
        return [0] + [self.depth + k for k in range(1, self.depth)]

    def has_above(self):
        return self.z + 1 < self.count

    def has_below(self):
        return self.z >= 1

    def begin(self):
        @pl.when(self.has_above())
        def _():
            self.line_copy(0, True).start()

        @pl.when(self.has_below())
        def _():
            self.line_copy(0, False).start()

        self.sides(0)

    def step(self, k):
        @pl.when(self.valid(1 + k))
        def _():
            self.line_arrival(1 + k).wait_recv()
            if 1 + k < self.depth:

                @pl.when(self.has_above())
                def _():
                    self.line_copy(1 + k, True).start()

            self.sides(1 + k)

        @pl.when(self.valid(self.depth + 1 + k))
        def _():
            self.line_arrival(self.depth + 1 + k).wait_recv()
            if 1 + k < self.depth:

                @pl.when(self.has_below())
                def _():
                    self.line_copy(self.depth + 1 + k, False).start()

            self.sides(self.depth + 1 + k)

    def side_step(self, j):
        @pl.when(self.valid(j))
        def _():
            self.far_copy(j).wait_recv()
            self.far_core_copy(j).start()

    def wait_blocks(self):
        for j in range(2 * self.depth + 1):

            @pl.when(self.valid(j))
            def _():
                self.core_arrival(j).wait_recv()
                if self.far is not None:
                    self.far_core_arrival(j).wait_recv()

    def wait_sends(self):
        for j in range(2 * self.depth + 1):

            @pl.when(self.valid(j))
            def _():
                self.core_copy(j).wait_send()
                if self.far is not None:
                    self.far_copy(j).wait_send()
                    self.far_core_copy(j).wait_send()

        for j in self.ups():

            @pl.when(self.valid(j) & self.has_above())
            def _():
                self.line_copy(j, True).wait_send()

        for j in self.downs():

            @pl.when(self.valid(j) & self.has_below())
            def _():
                self.line_copy(j, False).wait_send()


def forward_kernel(
    tokens, gain_first, gain_second, weight_own, wout_own, expert_up, expert_down, share_up, share_down,
    grad_ext, bias, cosine, sine, layout_col, layout_row,
    first_out, weight_out, wout_out, experts, share, share_far, grads, seconds, qkv, merged, log_total, middle,
    lowered,
    group, weight, wout, expert_raw, expert_pack, share_raw, share_pack, mask, outgoing, incoming,
    local, line_w, line_o, line_g, line_s, ring_a, ring_b, sc_a, sc_b, ex_a, ex_b, sh_a, sh_b,
):
    seq, head = lax.axis_index("seq"), lax.axis_index("head")
    n_seq = lax.axis_size("seq")
    near_x, near_y, near_core = plane_places()
    peers = ring_places()
    size = len(peers)
    rows, width = tokens.shape
    heads = bias.shape[0]
    units = experts.shape[2]
    y = head // 2
    share_rows = share.shape[2]
    hidden = expert_down.shape[0]
    part = weight_own.shape[0]

    fetch = [
        pltpu.make_async_copy(
            weight_own, weight.at[pl.ds(pl.multiple_of(seq * part, 16), part)], local.at[0]
        ),
        pltpu.make_async_copy(wout_own, wout.at[seq], local.at[1]),
        pltpu.make_async_copy(expert_up, expert_raw, local.at[2]),
        pltpu.make_async_copy(expert_down, expert_pack.at[2], local.at[3]),
        pltpu.make_async_copy(share_up, share_raw, local.at[4]),
        pltpu.make_async_copy(share_down, share_pack.at[2], local.at[5]),
        pltpu.make_async_copy(grad_ext, grads.at[0, seq], local.at[6]),
    ]
    for copy in fetch:
        copy.start()
    greet(
        [{"head": peer} for peer in peers[1:]]
        + [{"seq": (seq + k) % n_seq} for k in range(1, n_seq)]
    )

    gather_w = Line(lambda i: weight.at[pl.ds(pl.multiple_of(i * part, 16), part)], None, line_w)
    gather_o = Line(lambda i: wout.at[i], None, line_o)
    gather_g = Line(lambda i: grads.at[0, i], lambda i: grads.at[1, i], line_g)
    gather_s = Line(lambda i: seconds.at[0, i], lambda i: seconds.at[1, i], line_s)
    fetch[0].wait()
    gather_w.begin()
    fetch[1].wait()
    gather_o.begin()

    group[:rows] = norm_rows(tokens[...].astype(f32), gain_first[...])
    ring = [
        remote(
            group.at[pl.ds(0, rows)], group.at[pl.ds(r * rows, rows)],
            ring_a.at[r - 1], ring_b.at[r - 1], head=peers[size - r],
        )
        for r in range(1, size)
    ]
    for copy in ring:
        copy.start()

    fetch[2].wait()
    fetch[3].wait()
    mine = pl.ds(pl.multiple_of(y * units, 16), units)
    other = pl.ds(pl.multiple_of((1 - y) * units, 16), units)
    ups = [
        remote(expert_pack.at[m, other], experts.at[2, m], ex_a.at[m], ex_b.at[m], head=near_y)
        for m in range(3)
    ]
    sides = [
        remote(expert_pack.at[m, mine], experts.at[1, m], ex_a.at[3 + m], ex_b.at[3 + m], head=near_x)
        for m in range(3)
    ]
    ons = [
        remote(experts.at[2, m], experts.at[3, m], ex_a.at[6 + m], ex_b.at[6 + m], head=near_x)
        for m in range(3)
    ]
    order = (2, 0, 1)
    for m in order:
        if m < 2:
            expert_pack[m] = expert_raw[:, m * hidden : (m + 1) * hidden].T
        ups[m].start()
        sides[m].start()
    keep = [pltpu.make_async_copy(expert_pack.at[:, mine], experts.at[0], local.at[7])]
    keep[0].start()

    fetch[4].wait()
    fetch[5].wait()
    for m in range(2):
        share_pack[m] = share_raw[:, m * hidden : (m + 1) * hidden].T

    def share_block(i):
        return share_pack.at[:, pl.ds(pl.multiple_of(i * share_rows, 16), share_rows)]

    shares = [
        remote(
            share_block((seq + k) % n_seq), share.at[seq], sh_a.at[k], sh_b.at[k],
            seq=(seq + k) % n_seq,
        )
        for k in range(1, n_seq)
    ]
    share_own = pltpu.make_async_copy(share_block(seq), share.at[seq], local.at[8])
    share_own.start()
    arrivals = []
    for k in range(1, n_seq):
        block = share.at[(seq + n_seq - k) % n_seq]
        arrivals.append(remote(block, block, sh_a.at[k], sh_b.at[k], seq=(seq + k) % n_seq))
    crossings = []
    for k in range(n_seq):
        place = (seq + n_seq - k) % n_seq
        crossings.append(
            remote(
                share.at[place], share_far.at[place], sh_a.at[n_seq + k], sh_b.at[n_seq + k],
                head=near_x,
            )
        )

    mask[...] = mask_of(layout_col[...], layout_row[...])
    gather_w.step(0)
    gather_o.step(0)
    ups[2].wait_recv()
    ons[2].start()
    gather_w.step(1)
    gather_o.step(1)
    for m in (0, 1):
        ups[m].wait_recv()
        ons[m].start()
    fetch[6].wait()
    gather_w.step(2)
    gather_o.step(2)
    gather_g.begin()
    for copy in shares:
        copy.start()
    for copy in ring:
        copy.wait_recv()
    gather_w.wait_blocks()
    gather_o.wait_blocks()
    keep += [
        pltpu.make_async_copy(weight, weight_out, local.at[9]),
        pltpu.make_async_copy(wout, wout_out, local.at[10]),
        pltpu.make_async_copy(group, first_out, local.at[11]),
    ]
    for copy in keep[1:]:
        copy.start()

    step = 3 * HD
    for n in range(heads):
        linear = dot(group[...], weight[:, n * step : (n + 1) * step], 1, 0) + bias[n]
        parts, output, log_sum = head_forward(linear, cosine[...], sine[...], mask[...])
        for k in range(3):
            qkv[:, n * step + k * HD : n * step + (k + 1) * HD] = parts[k]
        merged[:, n * HD : (n + 1) * HD] = output
        log_total[n] = jnp.broadcast_to(log_sum, log_total.shape[1:])
        if n == 2:
            gather_g.step(0)
            gather_g.side_step(0)
    copies, own = scatter_start(merged, wout, outgoing, incoming, sc_a, sc_b, rows, peers)
    block = wout.shape[2]
    for b in range(len(own)):
        cols = slice(b * block, (b + 1) * block)
        middle[:, cols] = tokens[:, cols].astype(f32) + own[b]
    gather_g.step(1)
    for copy in copies:
        copy.wait_recv()
    total = middle[...]
    for r in range(size - 1):
        total += incoming[r].astype(f32)
    middle[...] = total
    lowered[...] = norm_rows(total, gain_second[...])
    last = pltpu.make_async_copy(lowered, seconds.at[0, seq], local.at[12])
    last.start()
    last.wait()
    gather_s.begin()

    share_own.wait()
    crossings[0].start()
    for j in (1, 1 + gather_g.depth):
        gather_g.side_step(j)
    for k in range(1, n_seq):
        arrivals[k - 1].wait_recv()
        crossings[k].start()
    gather_g.step(2)
    gather_s.step(0)
    for j in (2, 2 + gather_g.depth, 3, 3 + gather_g.depth):
        gather_g.side_step(j)
    gather_s.side_step(0)
    gather_s.step(1)
    for j in (1, 1 + gather_g.depth):
        gather_s.side_step(j)
    gather_s.step(2)
    for j in (2, 2 + gather_g.depth, 3, 3 + gather_g.depth):
        gather_s.side_step(j)

    gather_g.wait_blocks()
    gather_s.wait_blocks()
    for copy in sides + ons + crossings:
        copy.wait()
    for copy in ups + ring + copies + shares:
        copy.wait_send()
    for copy in keep:
        copy.wait()
    for line in (gather_w, gather_o, gather_g, gather_s):
        line.wait_sends()


def forward(
    tokens, gain_first, gain_second, weight_own, wout_own, expert_up, expert_down, share_up, share_down,
    grad_ext, bias, cosine, sine, layout_col, layout_row,
):
    n_seq, n_head = lax.axis_size("seq"), lax.axis_size("head")
    rows, width = tokens.shape
    group_tok = rows * n_head
    heads = bias.shape[0]
    wide = heads * HD
    part = weight_own.shape[0]
    hidden, head_part = expert_down.shape
    units = hidden // 2
    share_all, seq_part = share_down.shape
    share_rows = share_all // n_seq
    ext = grad_ext.shape[1]
    anywhere = pl.BlockSpec(memory_space=pl.ANY)
    vmem = pl.BlockSpec(memory_space=pltpu.VMEM)
    dma = pltpu.SemaphoreType.DMA
    lines = n_seq - 1

    def hbm(*shape):
        return (anywhere, jax.ShapeDtypeStruct(shape, bf16))

    outs = [
        hbm(group_tok, width),
        hbm(width, 3 * wide),
        hbm(n_seq, wide, part),
        hbm(4, 3, units, head_part),
        hbm(n_seq, 3, share_rows, seq_part),
        hbm(n_seq, 3, share_rows, seq_part),
        hbm(2, n_seq, rows, ext),
        hbm(2, n_seq, rows, width),
        (vmem, jax.ShapeDtypeStruct((group_tok, 3 * wide), bf16)),
        (vmem, jax.ShapeDtypeStruct((group_tok, wide), bf16)),
        (vmem, jax.ShapeDtypeStruct((heads, group_tok, LANES), f32)),
        (vmem, jax.ShapeDtypeStruct((rows, width), f32)),
        (vmem, jax.ShapeDtypeStruct((rows, width), bf16)),
    ]
    return pl.pallas_call(
        forward_kernel,
        in_specs=[vmem] * 3 + [anywhere] * 7 + [vmem] * 5,
        out_specs=[spec for spec, _ in outs],
        out_shape=[shape for _, shape in outs],
        scratch_shapes=[
            pltpu.VMEM((group_tok, width), bf16),
            pltpu.VMEM((width, 3 * wide), bf16),
            pltpu.VMEM((n_seq, wide, part), bf16),
            pltpu.VMEM(expert_up.shape, bf16),
            pltpu.VMEM((3, hidden, head_part), bf16),
            pltpu.VMEM(share_up.shape, bf16),
            pltpu.VMEM((3, share_all, seq_part), bf16),
            pltpu.VMEM((group_tok, group_tok), f32),
            pltpu.VMEM((n_head - 1, rows, width), bf16),
            pltpu.VMEM((n_head - 1, rows, width), bf16),
            dma((13,)),
            dma((4, lines)),
            dma((4, lines)),
            dma((8, lines)),
            dma((8, lines)),
            dma((n_head - 1,)),
            dma((n_head - 1,)),
            dma((n_head - 1,)),
            dma((n_head - 1,)),
            dma((9,)),
            dma((9,)),
            dma((2 * n_seq,)),
            dma((2 * n_seq,)),
        ],
        compiler_params=pltpu.CompilerParams(
            collective_id=0, has_side_effects=True, vmem_limit_bytes=VMEM_BYTES
        ),
        cost_estimate=pl.CostEstimate(
            flops=2 * group_tok * width * 4 * wide, bytes_accessed=1 << 29, transcendentals=0
        ),
        name="forward",
    )(
        tokens, gain_first, gain_second, weight_own, wout_own, expert_up, expert_down, share_up,
        share_down, grad_ext, bias, cosine, sine, layout_col, layout_row,
    )


def mesh_part():
    return lax.axis_index("head") // 2


def token_bits():
    return bits_of(lax.axis_size("head"))[1:]


def token_gather(block):
    order = token_bits()
    column = lax.all_gather(block, "seq", axis=0, tiled=True)
    share = column.shape[0] // 2
    half = share // 2
    core = lax.rem(lax.axis_index("seq"), 2)
    own = lax.dynamic_slice_in_dim(column, core * share, share, 0)
    upper = spread(own[:half], order)
    lower = spread(own[half:], order[::-1])
    chunks = [column]
    for r in sorted(upper)[1:]:
        for piece in (upper[r], lower[r]):
            chunks.append(jnp.concatenate([piece, swap(piece, "seq", 1)], axis=0))
    return chunks


def token_scatter(chunks):
    order = token_bits()
    column = chunks[0]
    share = column.shape[0] // 2
    half = share // 2
    core = lax.rem(lax.axis_index("seq"), 2)
    own = lax.dynamic_slice_in_dim(column, core * share, share, 0)
    sides = [{0: own[:half]}, {0: own[half:]}]
    for i, chunk in enumerate(chunks[1:]):
        sides[i % 2][2 * (i // 2 + 1)] = chunk[:half] + swap(chunk[half:], "seq", 1)
    total = jnp.concatenate([collect(sides[0], order), collect(sides[1], order[::-1])], axis=0)
    column = lax.dynamic_update_slice_in_dim(column, total, core * share, 0)
    return lax.psum_scatter(column, "seq", scatter_dimension=0, tiled=True)


def total_over_all(values):
    for axis in ("head", "seq"):
        for bit in bits_of(lax.axis_size(axis)):
            values = values + swap(values, axis, bit)
    return values


def turn(values, cosine, sine):
    return values * cosine + pltpu.roll(values, HD // 2, 1) * sine


def mask_of(layout_col, layout_row):
    doc_col, place_col = layout_col[:, 0:1], layout_col[:, 1:2]
    doc_row, place_row = layout_row[0:1, :], layout_row[1:2, :]
    return jnp.where((doc_col == doc_row) & (place_row <= place_col), 0.0, NEGATIVE)


def head_forward(linear, cos, sin, mask):
    queries = turn(linear[:, :HD], cos, sin).astype(bf16)
    keys = turn(linear[:, HD : 2 * HD], cos, sin).astype(bf16)
    values = linear[:, 2 * HD :].astype(bf16)
    scores = dot(queries, keys, 1, 1) * HD ** (-0.5) + mask
    largest = jnp.max(scores, axis=1, keepdims=True)
    weights = jnp.exp(scores - largest)
    total = jnp.sum(weights, axis=1, keepdims=True)
    probs = (weights / total).astype(bf16)
    output = dot(probs, values, 1, 0).astype(bf16)
    return (queries, keys, values), output, largest + jnp.log(total)


def norm_rows(rows, gain):
    square = jnp.mean(rows * rows, axis=1, keepdims=True)
    return (rows * lax.rsqrt(square + EPS) * gain).astype(bf16)


def scatter_start(merged, wout, outgoing, incoming, sems_a, sems_b, rows, peers):
    blocks, _, size = wout.shape
    copies = []
    for r in range(len(peers) - 1, 0, -1):
        for b in range(blocks):
            outgoing[r - 1, :, b * size : (b + 1) * size] = dot(
                merged[r * rows : (r + 1) * rows, :], wout[b], 1, 0
            ).astype(bf16)
        copies.append(
            remote(
                outgoing.at[r - 1], incoming.at[r - 1], sems_a.at[r - 1], sems_b.at[r - 1],
                head=peers[r],
            )
        )
        copies[-1].start()
    return copies, [dot(merged[:rows, :], wout[b], 1, 0) for b in range(blocks)]


def attend_kernel(
    first, weight, wout, bias, cosine, sine, layout_col, layout_row, tokens, gain,
    qkv, merged, log_total, middle, lowered, mask, outgoing, incoming, sems_a, sems_b,
):
    n = pl.program_id(0)
    heads = pl.num_programs(0)
    peers = ring_places()

    @pl.when(n == 0)
    def _():
        greet([{"head": peer} for peer in peers[1:]])
        mask[...] = mask_of(layout_col[...], layout_row[...])

    linear = dot(first[...], weight[...], 1, 0) + bias[0]
    parts, output, log_sum = head_forward(linear, cosine[...], sine[...], mask[...])
    for k in range(3):
        qkv[:, k * HD : (k + 1) * HD] = parts[k]
    merged[:, pl.ds(pl.multiple_of(n * HD, HD), HD)] = output
    log_total[0] = jnp.broadcast_to(log_sum, log_total.shape[1:])

    @pl.when(n == heads - 1)
    def _():
        copies, own = scatter_start(
            merged, wout, outgoing, incoming, sems_a, sems_b, tokens.shape[0], peers
        )
        size = wout.shape[2]
        for b, block in enumerate(own):
            cols = slice(b * size, (b + 1) * size)
            middle[:, cols] = tokens[:, cols].astype(f32) + block
        for copy in copies:
            copy.wait()
        total = middle[...]
        for r in range(len(peers) - 1):
            total += incoming[r].astype(f32)
        middle[...] = total
        lowered[...] = norm_rows(total, gain[...])


def attend(first, weight, wout, bias, cosine, sine, layout_col, layout_row, tokens, gain):
    rows, width = first.shape
    heads = bias.shape[0]
    own = tokens.shape[0]
    others = lax.axis_size("head") - 1
    step = 3 * HD
    wide = heads * HD

    def whole(shape):
        return pl.BlockSpec(shape, lambda n: (0,) * len(shape))

    return pl.pallas_call(
        attend_kernel,
        grid=(heads,),
        in_specs=[
            whole((rows, width)),
            pl.BlockSpec((width, step), lambda n: (0, n)),
            whole(wout.shape),
            pl.BlockSpec((1, 1, step), lambda n: (n, 0, 0)),
            whole((rows, HD)),
            whole((rows, HD)),
            whole((rows, 2)),
            whole((2, rows)),
            whole((own, width)),
            whole((1, width)),
        ],
        out_specs=[
            pl.BlockSpec((rows, step), lambda n: (0, n)),
            whole((rows, wide)),
            pl.BlockSpec((1, rows, LANES), lambda n: (n, 0, 0)),
            whole((own, width)),
            whole((own, width)),
        ],
        out_shape=[
            jax.ShapeDtypeStruct((rows, heads * step), bf16),
            jax.ShapeDtypeStruct((rows, wide), bf16),
            jax.ShapeDtypeStruct((heads, rows, LANES), f32),
            jax.ShapeDtypeStruct((own, width), f32),
            jax.ShapeDtypeStruct((own, width), bf16),
        ],
        scratch_shapes=[
            pltpu.VMEM((rows, rows), f32),
            pltpu.VMEM((others, own, width), bf16),
            pltpu.VMEM((others, own, width), bf16),
            pltpu.SemaphoreType.DMA((others,)),
            pltpu.SemaphoreType.DMA((others,)),
        ],
        compiler_params=pltpu.CompilerParams(
            collective_id=2, has_side_effects=True, vmem_limit_bytes=VMEM_BYTES
        ),
        cost_estimate=pl.CostEstimate(
            flops=2 * rows * width * 4 * wide, bytes_accessed=8 * width * wide, transcendentals=0
        ),
        name="attend",
    )(first, weight, wout, bias, cosine, sine, layout_col, layout_row, tokens, gain)


def attend_back_kernel(
    plane, grad_own, first, weight, wout, qkv, merged, log_total, cosine, sine, layout_col, layout_row,
    *refs,
):
    if plane:
        experts, share_own, share_in, grad_first, grad_weight, grad_bias, expert_in, share_all = refs[:8]
        share_sum, share_add, l_sem, x_a, x_b, z_a, z_b = refs[-7:]
        refs = refs[8:-7]
    else:
        grad_first, grad_weight, grad_bias = refs[:3]
        refs = refs[3:]
    mask, grad_merged, acc, grad, sems_a, sems_b = refs
    n = pl.program_id(0)
    peers = ring_places()
    own = grad_own.shape[0]
    heads = pl.num_programs(0)
    seq, n_seq = lax.axis_index("seq"), lax.axis_size("seq")
    if plane:
        near_x = plane_places()[0]
        cross = [
            remote(experts.at[3, m], expert_in.at[m], x_a.at[m], x_b.at[m], head=near_x)
            for m in range(2)
        ]
        spread_out, spread_in = [], []
        for k in range(1, n_seq):
            to, source = (seq + k) % n_seq, (seq + n_seq - k) % n_seq
            spread_out.append(
                remote(share_sum.at[to], share_all.at[seq], z_a.at[k], z_b.at[k], seq=to)
            )
            block = share_all.at[source]
            spread_in.append(remote(block, block, z_a.at[k], z_b.at[k], seq=to))
        spread_own = pltpu.make_async_copy(share_sum.at[seq], share_all.at[seq], z_a.at[0])
    scale = HD ** (-0.5)
    blocks, _, size = grad_weight.shape
    wide = wout.shape[1]

    @pl.when(n == 0)
    def _():
        if plane:
            loads = [
                pltpu.make_async_copy(share_own, share_sum, l_sem.at[0]),
                pltpu.make_async_copy(share_in, share_add, l_sem.at[1]),
            ]
            for copy in loads:
                copy.start()
        greet(
            [{"head": peer} for peer in peers[1:]]
            + [{"seq": (seq + k) % n_seq} for k in range(1, n_seq) if plane]
        )
        copies = [
            remote(
                grad_own, grad.at[pl.ds(r * own, own)], sems_a.at[r - 1], sems_b.at[r - 1],
                head=peers[len(peers) - r],
            )
            for r in range(1, len(peers))
        ]
        for copy in copies:
            copy.start()
        grad[:own] = grad_own[...]
        mask[...] = mask_of(layout_col[...], layout_row[...])
        acc[...] = jnp.zeros_like(acc)
        if plane:
            for copy in loads:
                copy.wait()
            share_sum[...] = (share_sum[...].astype(f32) + share_add[...].astype(f32)).astype(bf16)
            for copy in spread_out:
                copy.start()
            spread_own.start()
        for copy in copies:
            copy.wait()
        if plane:
            for copy in cross:
                copy.start()
        total = jnp.zeros((grad.shape[0], wide), f32)
        for s in range(blocks):
            total += dot(grad[:, s * size : (s + 1) * size], wout[s], 1, 1)
        grad_merged[...] = total.astype(bf16)
        for s in range(blocks):
            grad_weight[s, 3 * wide :, :] = dot(
                merged[...], grad[:, s * size : (s + 1) * size], 0, 0
            ).astype(bf16)

    cos, sin = cosine[...], -sine[...]
    queries, keys, values = qkv[:, :HD], qkv[:, HD : 2 * HD], qkv[:, 2 * HD :]
    grad_out = grad_merged[:, pl.ds(pl.multiple_of(n * HD, HD), HD)]
    scores = dot(queries, keys, 1, 1) * scale + mask[...]
    probs = jnp.exp(scores - log_total[0][:, 0:1])
    grad_values = dot(probs.astype(bf16), grad_out, 0, 0).astype(bf16)
    grad_probs = dot(grad_out, values, 1, 1)
    centre = jnp.sum(probs * grad_probs, axis=1, keepdims=True)
    grad_scores = (probs * (grad_probs - centre)).astype(bf16)
    grad_queries = (dot(grad_scores, keys, 1, 0) * scale).astype(bf16).astype(f32)
    grad_keys = (dot(grad_scores, queries, 0, 0) * scale).astype(bf16).astype(f32)
    grad_linear = jnp.concatenate(
        [turn(grad_queries, cos, sin).astype(bf16), turn(grad_keys, cos, sin).astype(bf16), grad_values],
        axis=1,
    )
    grad_bias[0] = jnp.sum(grad_linear.astype(f32), axis=0, keepdims=True)
    acc[...] += dot(grad_linear, weight[...], 1, 1)
    step = 3 * HD
    for s in range(blocks):
        grad_weight[s, pl.ds(pl.multiple_of(n * step, HD), step), :] = dot(
            grad_linear, first[:, s * size : (s + 1) * size], 0, 0
        ).astype(bf16)

    @pl.when(n == heads - 1)
    def _():
        grad_first[...] = acc[...].astype(bf16)
        if plane:
            spread_own.wait()
            for copy in spread_in:
                copy.wait_recv()
            for copy in spread_out:
                copy.wait_send()
            for copy in cross:
                copy.wait()


def attend_back(
    grad, first, weight, wout, qkv, merged, log_total, cosine, sine, layout_col, layout_row, extra=()
):
    rows, width = first.shape
    heads = log_total.shape[0]
    step = 3 * HD
    wide = heads * HD
    n_seq = lax.axis_size("seq")
    size = width // n_seq
    own = grad.shape[0]
    others = lax.axis_size("head") - 1

    anywhere = pl.BlockSpec(memory_space=pl.ANY)
    more_outs, more_scratch = [], []
    if extra:
        experts, share, _ = extra
        more_outs = [
            jax.ShapeDtypeStruct((2, *experts.shape[2:]), bf16),
            jax.ShapeDtypeStruct(share.shape, bf16),
        ]
        more_scratch = [
            pltpu.VMEM(share.shape, bf16),
            pltpu.VMEM(share.shape, bf16),
            pltpu.SemaphoreType.DMA((2,)),
            *[pltpu.SemaphoreType.DMA((2,))] * 2,
            *[pltpu.SemaphoreType.DMA((n_seq,))] * 2,
        ]

    def whole(shape):
        return pl.BlockSpec(shape, lambda n: (0,) * len(shape))

    return pl.pallas_call(
        functools.partial(attend_back_kernel, bool(extra)),
        grid=(heads,),
        in_specs=[
            whole((own, width)),
            whole((rows, width)),
            pl.BlockSpec((width, step), lambda n: (0, n)),
            whole(wout.shape),
            pl.BlockSpec((rows, step), lambda n: (0, n)),
            whole((rows, wide)),
            pl.BlockSpec((1, rows, LANES), lambda n: (n, 0, 0)),
            whole((rows, HD)),
            whole((rows, HD)),
            whole((rows, 2)),
            whole((2, rows)),
        ]
        + [anywhere] * len(extra),
        out_specs=[
            whole((rows, width)),
            whole((n_seq, 4 * wide, size)),
            pl.BlockSpec((1, 1, step), lambda n: (n, 0, 0)),
        ]
        + [anywhere] * len(more_outs),
        out_shape=[
            jax.ShapeDtypeStruct((rows, width), bf16),
            jax.ShapeDtypeStruct((n_seq, 4 * wide, size), bf16),
            jax.ShapeDtypeStruct((heads, 1, step), f32),
        ]
        + more_outs,
        scratch_shapes=[
            pltpu.VMEM((rows, rows), f32),
            pltpu.VMEM((rows, wide), bf16),
            pltpu.VMEM((rows, width), f32),
            pltpu.VMEM((rows, width), bf16),
            pltpu.SemaphoreType.DMA((others,)),
            pltpu.SemaphoreType.DMA((others,)),
        ]
        + more_scratch,
        compiler_params=pltpu.CompilerParams(
            collective_id=3, has_side_effects=True, vmem_limit_bytes=VMEM_BYTES
        ),
        cost_estimate=pl.CostEstimate(
            flops=4 * rows * width * 4 * wide, bytes_accessed=16 * width * wide, transcendentals=0
        ),
        name="attend_back",
    )(grad, first, weight, wout, qkv, merged, log_total, cosine, sine, layout_col, layout_row, *extra)


def pack_kernel(exp_units, share_units, at, *refs):
    stacked, shares = refs[0], refs[-5:-3]
    experts = [stacked.at[r] for r in range(stacked.shape[0])]
    rest, full, sems = refs[-3:]
    head = at[0]
    copies = []
    for r, block in enumerate(experts):
        size = block.shape[2]
        start = pl.multiple_of(jnp.bitwise_xor(head, r) * size, size)
        copies.append(
            pltpu.make_async_copy(
                block, full.at[:, pl.ds(0, exp_units), pl.ds(start, size)], sems.at[len(copies)]
            )
        )
    for r, block in enumerate(shares):
        size = block.shape[3]
        for s in range(block.shape[0]):
            copies.append(
                pltpu.make_async_copy(
                    block.at[s],
                    full.at[:, pl.ds(exp_units + r * share_units, share_units), pl.ds(s * size, size)],
                    sems.at[len(copies)],
                )
            )
    base = exp_units + 2 * share_units
    copies.append(
        pltpu.make_async_copy(rest, full.at[:, pl.ds(base, rest.shape[1]), :], sems.at[len(copies)])
    )
    for copy in copies:
        copy.start()
    for copy in copies:
        copy.wait()


def pack(at, experts, shares, rest, unit_rows):
    exp_units, share_units = experts.shape[2], shares[0].shape[2]
    count = experts.shape[0] + 2 * shares[0].shape[0] + 1
    anywhere = pl.BlockSpec(memory_space=pl.ANY)
    return pl.pallas_call(
        functools.partial(pack_kernel, exp_units, share_units),
        in_specs=[pl.BlockSpec(memory_space=pltpu.SMEM)] + [anywhere] * 4,
        out_specs=anywhere,
        out_shape=jax.ShapeDtypeStruct((3, unit_rows, rest.shape[2]), bf16),
        scratch_shapes=[pltpu.SemaphoreType.DMA((count,))],
        compiler_params=pltpu.CompilerParams(vmem_limit_bytes=1 << 20),
        cost_estimate=pl.CostEstimate(
            flops=0, bytes_accessed=12 * unit_rows * rest.shape[2], transcendentals=0
        ),
        name="pack",
    )(at, experts, *shares, rest)


def mix_rows(exp_units, base, n_exp, x, grad_ext, w, wait=None):
    rows, width = x.shape
    unit_rows = w.shape[1]
    seq = lax.axis_index("seq")
    gate = dot(x, w[0], 1, 1)
    if wait is not None:
        wait(1)
    up = dot(x, w[1], 1, 1)
    if wait is not None:
        wait(2)
    raw = dot(grad_ext[:, :width], w[2], 1, 1)
    block = base // LANES * LANES
    logits = gate[:, block : block + LANES]
    lane = lax.broadcasted_iota(jnp.int32, (rows, LANES), 1)
    from_base = lane - (base - block)
    is_logit = (from_base >= 0) & (from_base < n_exp)
    largest = jnp.max(jnp.where(is_logit, logits, NEGATIVE), axis=1, keepdims=True)
    powers = jnp.where(is_logit, jnp.exp(jnp.where(is_logit, logits - largest, 0.0)), 0.0)
    chosen = jnp.sum(jnp.where(from_base == seq, powers, 0.0), axis=1, keepdims=True)
    marks = grad_ext[:, width:].astype(f32)
    mark = jnp.sum(jnp.where(lane == seq, marks, 0.0), axis=1, keepdims=True)
    gate_here = mark * chosen / jnp.sum(powers, axis=1, keepdims=True)
    share_gate = jax.nn.sigmoid(
        jnp.sum(jnp.where(from_base == n_exp, logits, 0.0), axis=1, keepdims=True)
    )
    unit = lax.broadcasted_iota(jnp.int32, (rows, unit_rows), 1)
    is_expert = unit < exp_units
    factor = jnp.where(is_expert, gate_here, share_gate)
    sigma = jax.nn.sigmoid(gate)
    silu = gate * sigma
    hidden = silu * up
    scaled = (hidden * factor).astype(bf16)
    both = hidden * raw
    all_sum = jnp.sum(both, axis=1, keepdims=True)
    exp_sum = jnp.sum(jnp.where(is_expert, both, 0.0), axis=1, keepdims=True)
    grad_hidden = raw * factor
    grad_gate = (grad_hidden * up * (sigma + silu * (1.0 - sigma))).astype(bf16)
    grad_up = (grad_hidden * silu).astype(bf16)
    back = dot(grad_gate, w[0], 1, 0) + dot(grad_up, w[1], 1, 0)
    extra = jnp.where(
        lane == seq, exp_sum * mark, jnp.where(lane == n_exp, all_sum - exp_sum, 0.0)
    )
    return (grad_gate, grad_up, scaled), back.astype(bf16), extra.astype(bf16)


def mix_local_kernel(exp_units, base, n_exp, second, grad_ext, w_hbm, back, unit_out, w, sems):
    copies = [pltpu.make_async_copy(w_hbm.at[m], w.at[m], sems.at[m]) for m in range(3)]
    width = second.shape[1]

    @pl.when(pl.program_id(0) == 0)
    def _():
        for copy in copies:
            copy.start()
        for copy in copies:
            copy.wait()

    units, rows_back, extra = mix_rows(exp_units, base, n_exp, second[...], grad_ext, w)
    for m in range(3):
        unit_out[m] = units[m]
    back[:, :width] = rows_back
    back[:, width:] = extra


def mix_local(second, grad_ext, full, exp_units, base, n_exp):
    rows, width = second.shape
    unit_rows = full.shape[1]
    wide = grad_ext.shape[1]
    return pl.pallas_call(
        functools.partial(mix_local_kernel, exp_units, base, n_exp),
        grid=(rows // TILE,),
        in_specs=[
            pl.BlockSpec((TILE, width), lambda i: (i, 0)),
            pl.BlockSpec((TILE, wide), lambda i: (i, 0)),
            pl.BlockSpec(memory_space=pl.ANY),
        ],
        out_specs=[
            pl.BlockSpec((TILE, wide), lambda i: (i, 0)),
            pl.BlockSpec((3, TILE, unit_rows), lambda i: (0, i, 0)),
        ],
        out_shape=[
            jax.ShapeDtypeStruct((rows, wide), bf16),
            jax.ShapeDtypeStruct((3, rows, unit_rows), bf16),
        ],
        scratch_shapes=[
            pltpu.VMEM((3, unit_rows, width), bf16),
            pltpu.SemaphoreType.DMA((3,)),
        ],
        compiler_params=pltpu.CompilerParams(vmem_limit_bytes=VMEM_BYTES),
        cost_estimate=pl.CostEstimate(
            flops=10 * rows * width * unit_rows,
            bytes_accessed=6 * unit_rows * width + 8 * rows * width,
            transcendentals=0,
        ),
        name="mix_local",
    )(second, grad_ext, full)


def mix_kernel(
    exp_units, base, n_exp, second, grad_ext, experts, share_own, share_far, rest, unit_out, back, down_out,
    w, held, core_in, home, e_sem, s_sem, r_sem, b_a, b_b, h_a, h_b, o_sem, d_sem,
):
    i = pl.program_id(0)
    _, near_y, near_core = plane_places()
    core = lax.axis_index("seq") % 2
    rows, width = second.shape[2:]
    at = [pl.ds(j * rows, rows) for j in range(2)]
    loads = [[], [], []]
    for m in range(3):
        for r, owner in enumerate(plane_owners()):
            size = experts.shape[3]
            start = pl.multiple_of(owner * size, size)
            loads[m].append(
                pltpu.make_async_copy(
                    experts.at[r, m], w.at[m, pl.ds(0, exp_units), pl.ds(start, size)], e_sem.at[m, r]
                )
            )
    share_rows, size = share_own.shape[2:]
    for r, share in enumerate((share_own, share_far)):
        for place in range(share.shape[0]):
            loads[0].append(
                pltpu.make_async_copy(
                    share.at[place],
                    w.at[
                        :,
                        pl.ds(exp_units + r * share_rows, share_rows),
                        pl.ds(place * size, size),
                    ],
                    s_sem.at[r, place],
                )
            )
    loads[0].append(
        pltpu.make_async_copy(rest, w.at[:, pl.ds(base, rest.shape[1])], r_sem)
    )
    keep = pltpu.make_async_copy(w.at[2], down_out, d_sem)
    back_c = [
        remote(held.at[j, 1 - core], core_in.at[j], b_a.at[j], b_b.at[j], seq=near_core)
        for j in range(2)
    ]
    back_y = [
        remote(held.at[j, core], home.at[j], h_a.at[j], h_b.at[j], head=near_y) for j in range(2)
    ]

    def wait_weights(m):
        @pl.when(i == 0)
        def _():
            for copy in loads[m]:
                copy.wait()

    @pl.when(i == 0)
    def _():
        for group in loads:
            for copy in group:
                copy.start()
        greet([{"head": near_y}, {"seq": near_core}])

    wait_weights(0)
    for c in range(2):
        units, rows_back, extra = mix_rows(
            exp_units, base, n_exp, second[0, c], grad_ext.at[0, c], w, wait_weights if c == 0 else None
        )
        for m in range(3):
            unit_out[m, 0, c] = units[m]
        held[i, c, :, :width] = rows_back
        held[i, c, :, width:] = extra
        if c == 0:
            for j in range(2):

                @pl.when(i == 1 + j)
                def _():
                    back_c[j].wait_recv()
                    held[j, core] = (held[j, core].astype(f32) + core_in[j].astype(f32)).astype(bf16)
                    back_y[j].start()

    for j in range(2):

        @pl.when(i == j)
        def _():
            back_c[j].start()
            if j == 0:
                keep.start()

    @pl.when(i == 3)
    def _():
        out = [
            [
                pltpu.make_async_copy(held.at[2 + j, c], back.at[c, at[j]], o_sem.at[j, k])
                for k, c in enumerate((1 - core, core))
            ]
            for j in range(2)
        ]
        for j in range(2):
            out[j][0].start()
        for j in range(2):
            back_y[j].wait_recv()
            held[2 + j, core] = (held[2 + j, core].astype(f32) + home[j].astype(f32)).astype(bf16)
            out[j][1].start()
        for j in range(2):
            out[j][0].wait()
            out[j][1].wait()
            back_c[j].wait_send()
            back_y[j].wait_send()
        keep.wait()


def mix(seconds, grads, experts, share_own, share_far, rest, exp_units, base, n_exp):
    rows, width = seconds.shape[1:]
    unit_rows = base + rest.shape[1]
    wide = grads.shape[2]
    half = rows // 2
    piece = half // 2
    anywhere = pl.BlockSpec(memory_space=pl.ANY)
    units, back, down_rows = pl.pallas_call(
        functools.partial(mix_kernel, exp_units, base, n_exp),
        grid=(4,),
        in_specs=[
            pl.BlockSpec((1, 2, piece, width), lambda i: (1 - i // 2, 0, i % 2, 0)),
            pl.BlockSpec((1, 2, piece, wide), lambda i: (1 - i // 2, 0, i % 2, 0)),
            anywhere,
            anywhere,
            anywhere,
            anywhere,
        ],
        out_specs=[
            pl.BlockSpec((3, 1, 2, piece, unit_rows), lambda i: (0, 1 - i // 2, 0, i % 2, 0)),
            anywhere,
            anywhere,
        ],
        out_shape=[
            jax.ShapeDtypeStruct((3, 2, 2, half, unit_rows), bf16),
            jax.ShapeDtypeStruct((2, half, wide), bf16),
            jax.ShapeDtypeStruct((unit_rows, width), bf16),
        ],
        scratch_shapes=[
            pltpu.VMEM((3, unit_rows, width), bf16),
            pltpu.VMEM((4, 2, piece, wide), bf16),
            pltpu.VMEM((2, piece, wide), bf16),
            pltpu.VMEM((2, piece, wide), bf16),
            pltpu.SemaphoreType.DMA((3, 4)),
            pltpu.SemaphoreType.DMA((2, share_own.shape[0])),
            pltpu.SemaphoreType.DMA,
            *[pltpu.SemaphoreType.DMA((2,))] * 4,
            pltpu.SemaphoreType.DMA((2, 2)),
            pltpu.SemaphoreType.DMA,
        ],
        compiler_params=pltpu.CompilerParams(
            collective_id=4, has_side_effects=True, vmem_limit_bytes=VMEM_BYTES
        ),
        cost_estimate=pl.CostEstimate(
            flops=20 * rows * width * unit_rows,
            bytes_accessed=6 * unit_rows * width + 16 * rows * width,
            transcendentals=0,
        ),
        name="mix",
    )(
        seconds.reshape(2, 2, half, width), grads.reshape(2, 2, half, wide), experts, share_own, share_far, rest
    )
    return units.reshape(3, 2, rows, unit_rows), back.reshape(rows, wide), down_rows


def unit_grads_kernel(count, exp_units, share_rows, at, *refs):
    units, seconds, grads = refs[:count], refs[count : 2 * count], refs[2 * count : 3 * count]
    experts, share_own, share_far = refs[3 * count :]
    m = pl.program_id(0)

    def run(rights):
        acc = dot(units[0][...], rights[0][...], 0, 0)
        for left, right in zip(units[1:], rights[1:]):
            acc += dot(left[...], right[...], 0, 0)
        experts[0, 0] = acc[:exp_units].astype(bf16)
        size = share_own.shape[3]
        for s in range(share_own.shape[0]):
            piece = acc[exp_units : exp_units + 2 * share_rows, s * size : (s + 1) * size].astype(bf16)
            share_own[s, 0] = piece[:share_rows]
            share_far[s, 0] = piece[share_rows:]

    @pl.when(m < 2)
    def _():
        run(seconds)

    @pl.when(m == 2)
    def _():
        run(grads)


def unit_grads(at, units, seconds, grads, exp_units, share_rows):
    n_head, n_seq = lax.axis_size("head"), lax.axis_size("seq")
    width = seconds[0][0].shape[2]
    unit_rows = units[0][0].shape[3]
    head_part, seq_part = width // n_head, width // n_seq
    near = n_seq // n_head
    rows = sum(block.shape[1] for block, _ in seconds)

    def far(r, at):
        return jnp.bitwise_xor(at[0], r)

    def place(q, m, r, at):
        return (m, q, 0, 0)

    def second_place(q, m, r, at):
        return (q, 0, jnp.where(m < 2, far(r, at), far(n_head - 1, at)))

    def grad_place(q, m, r, at):
        return (q, 0, jnp.where(m < 2, far(0, at), far(r, at)))

    in_specs = [
        pl.BlockSpec((None, None, block.shape[2], unit_rows), functools.partial(place, q))
        for block, q in units
    ]
    in_specs += [
        pl.BlockSpec((None, block.shape[1], head_part), functools.partial(second_place, q))
        for block, q in seconds
    ]
    in_specs += [
        pl.BlockSpec((None, block.shape[1], head_part), functools.partial(grad_place, q))
        for block, q in grads
    ]
    share_spec = pl.BlockSpec((near, 1, share_rows, seq_part), lambda m, r, at: (far(r, at), m, 0, 0))
    share_shape = jax.ShapeDtypeStruct((n_seq, 3, share_rows, seq_part), bf16)
    return pl.pallas_call(
        functools.partial(unit_grads_kernel, len(units), exp_units, share_rows),
        grid_spec=pltpu.PrefetchScalarGridSpec(
            num_scalar_prefetch=1,
            grid=(3, n_head),
            in_specs=in_specs,
            out_specs=[
                pl.BlockSpec((1, 1, exp_units, head_part), lambda m, r, at: (r, m, 0, 0)),
                share_spec,
                share_spec,
            ],
        ),
        out_shape=[
            jax.ShapeDtypeStruct((n_head, 3, exp_units, head_part), bf16),
            share_shape,
            share_shape,
        ],
        compiler_params=pltpu.CompilerParams(vmem_limit_bytes=VMEM_BYTES),
        cost_estimate=pl.CostEstimate(
            flops=6 * rows * width * unit_rows,
            bytes_accessed=6 * rows * unit_rows + 8 * rows * width + 6 * width * unit_rows,
            transcendentals=0,
        ),
        name="unit_grads",
    )(at, *(block for block, _ in units + seconds + grads))


def products_kernel(
    units, seconds, grads, down_rows, out, experts, share_own, share_in,
    u, right, down, far_half, column, core_in, home, share, stage,
    u_sem, r_sem, d_sem, c_a, c_b, y_a, y_b, x_a, x_b, e_sem, o_sem, k_sem,
):
    near_x, near_y, near_core = plane_places()
    core = lax.axis_index("seq") % 2
    width = down.shape[1]
    rows = column.shape[1]
    piece = rows // 2
    exp_units = experts.shape[2]
    share_rows = share_own.shape[2]
    head_part = experts.shape[3]
    seq_part = share_own.shape[3]
    n_head = width // head_part
    edge = exp_units // LANES * LANES
    tail = exp_units - edge
    order = (2, 0, 1)

    load_u = [
        [
            pltpu.make_async_copy(
                units.at[m, q], u.at[m, pl.ds(q * 2 * rows, 2 * rows)], u_sem.at[m, q]
            )
            for q in range(2)
        ]
        for m in range(3)
    ]

    def load_right(k):
        source = grads if k else seconds
        return [
            pltpu.make_async_copy(
                source.at[q, :, pl.ds(f * head_part, head_part)],
                right.at[k, pl.ds(q * 2 * rows, 2 * rows), pl.ds(f * head_part, head_part)],
                r_sem.at[k, q, f],
            )
            for q in range(2)
            for f in range(n_head)
        ]

    load_down = pltpu.make_async_copy(down_rows, down, d_sem)
    rights = [load_right(0), load_right(1)]
    load_u[2][1].start()
    load_down.start()
    for copy in rights[1]:
        copy.start()
    load_u[2][0].start()
    for copy in load_u[0]:
        copy.start()
    for copy in rights[0]:
        copy.start()
    for copy in load_u[1]:
        copy.start()
    greet([{"head": near_x}, {"head": near_y}, {"seq": near_core}])

    pieces = [pl.ds(j * piece, piece) for j in range(2)]
    to_core = [
        remote(far_half.at[0, at], core_in.at[at], c_a.at[j], c_b.at[j], seq=near_core)
        for j, at in enumerate(pieces)
    ]
    to_y = [
        remote(far_half.at[1, at], home.at[at], y_a.at[j], y_b.at[j], head=near_y)
        for j, at in enumerate(pieces)
    ]
    to_x = [
        remote(share.at[1, :, m], share_in.at[:, m], x_a.at[m], x_b.at[m], head=near_x)
        for m in range(3)
    ]

    def out_rows(start):
        return dot(u[2, pl.ds(pl.multiple_of(start, 16), piece), :], down[...], 1, 0)

    load_u[2][1].wait()
    load_down.wait()
    for k, half in ((0, 1 - core), (1, core)):
        for j in range(2):
            far_half[k, pieces[j]] = out_rows(2 * rows + half * rows + j * piece).astype(bf16)
            if k == 0:
                to_core[j].start()

    def pass_on(j):
        to_core[j].wait_recv()
        total = far_half[1, pieces[j]].astype(f32) + core_in[pieces[j]].astype(f32)
        far_half[1, pieces[j]] = total.astype(bf16)
        to_y[j].start()

    load_u[2][0].wait()
    for i, m in enumerate(order):
        if m != 2:
            for copy in load_u[m]:
                copy.wait()
        for f in range(n_head):
            if i < 2:
                for copy in rights[1 if m == 2 else 0][f::n_head]:
                    copy.wait()
            block = right[1 if m == 2 else 0, :, f * head_part : (f + 1) * head_part]
            acc = dot(u[m, :, edge:], block, 0, 0)
            for b in range(head_part // seq_part):
                part = acc[tail : tail + 2 * share_rows, b * seq_part : (b + 1) * seq_part]
                place = f * (head_part // seq_part) + b
                share[0, place, m] = part[:share_rows].astype(bf16)
                share[1, place, m] = part[share_rows:].astype(bf16)
            if i == 0 and f < 2:
                pass_on(f)
        to_x[m].start()
    keep = pltpu.make_async_copy(share.at[0], share_own, k_sem)
    keep.start()

    wide = -(-exp_units // LANES) * LANES
    writes = []
    owners = plane_owners()
    for i, r in enumerate((3, 1, 2, 0)):
        owner = owners[r]
        for m in range(3):
            n = 3 * i + m
            if n >= 2:
                writes[n - 2].wait()
            start = pl.multiple_of(owner * head_part, head_part)
            acc = dot(u[m, :, :wide], right[1 if m == 2 else 0, :, pl.ds(start, head_part)], 0, 0)
            stage[n % 2] = acc[:exp_units].astype(bf16)
            writes.append(pltpu.make_async_copy(stage.at[n % 2], experts.at[r, m], e_sem.at[n % 2]))
            writes[-1].start()

    for c in range(2):
        for j in range(2):
            column[c, pieces[j]] = out_rows(c * rows + j * piece).astype(bf16)
    write = [
        pltpu.make_async_copy(column.at[c], out.at[c], o_sem.at[k]) for k, c in enumerate((1 - core, core))
    ]
    write[0].start()
    for j in range(2):
        to_y[j].wait_recv()
        total = column[core, pieces[j]].astype(f32) + home[pieces[j]].astype(f32)
        column[core, pieces[j]] = total.astype(bf16)
    write[1].start()
    for copy in to_x:
        copy.wait()
    for copy in to_core + to_y:
        copy.wait_send()
    for copy in writes[-2:] + write + [keep]:
        copy.wait()


def products(units, seconds, grads, down_rows, exp_units, share_rows):
    n_head, n_seq = lax.axis_size("head"), lax.axis_size("seq")
    _, rows, width = seconds.shape
    unit_rows = units.shape[3]
    half = rows // 2
    head_part, seq_part = width // n_head, width // n_seq
    anywhere = pl.BlockSpec(memory_space=pl.ANY)
    dma = pltpu.SemaphoreType.DMA
    share_shape = (n_seq, 3, share_rows, seq_part)
    return pl.pallas_call(
        products_kernel,
        in_specs=[anywhere] * 4,
        out_specs=[anywhere] * 4,
        out_shape=[
            jax.ShapeDtypeStruct((2, half, width), bf16),
            jax.ShapeDtypeStruct((n_head, 3, exp_units, head_part), bf16),
            jax.ShapeDtypeStruct(share_shape, bf16),
            jax.ShapeDtypeStruct(share_shape, bf16),
        ],
        scratch_shapes=[
            pltpu.VMEM((3, 2 * rows, unit_rows), bf16),
            pltpu.VMEM((2, 2 * rows, width), bf16),
            pltpu.VMEM((unit_rows, width), bf16),
            pltpu.VMEM((2, half, width), bf16),
            pltpu.VMEM((2, half, width), bf16),
            pltpu.VMEM((half, width), bf16),
            pltpu.VMEM((half, width), bf16),
            pltpu.VMEM((2, *share_shape), bf16),
            pltpu.VMEM((2, exp_units, head_part), bf16),
            dma((3, 2)),
            dma((2, 2, n_head)),
            dma,
            *[dma((2,))] * 4,
            *[dma((3,))] * 2,
            *[dma((2,))] * 2,
            dma,
        ],
        compiler_params=pltpu.CompilerParams(
            collective_id=5, has_side_effects=True, vmem_limit_bytes=VMEM_BYTES
        ),
        cost_estimate=pl.CostEstimate(
            flops=16 * rows * width * unit_rows,
            bytes_accessed=40 * rows * width,
            transcendentals=0,
        ),
        name="products",
    )(units, seconds, grads, down_rows)


def finish_kernel(
    experts, expert_in, share_all, partial, grad_middle, tokens, gain, small,
    grad_up, grad_down, grad_share_up, grad_share_down, input_grad, totals,
    near, far, far_in, near_in, last_in, pack, share_pack, incoming, slots,
    l_sem, x_a, x_b, y_a, y_b, s_a, s_b, t_a, t_b, p_sem,
):
    seq, head = lax.axis_index("seq"), lax.axis_index("head")
    near_x, near_y, near_core = plane_places()
    peers = ring_places()
    y = head // 2
    rows, width = grad_middle.shape
    units = near.shape[1]
    share_rows = share_all.shape[2]
    hidden = pack.shape[1]
    steps = [{"head": near_x}, {"head": near_y}, {"seq": near_core}]
    for bit in (2, 4):
        steps.append({"seq": seq + bit - 2 * bit * ((seq // bit) % 2)})

    loads = [
        [pltpu.make_async_copy(experts.at[2, m], far.at[m], l_sem.at[m]) for m in range(3)],
        [pltpu.make_async_copy(expert_in.at[m], far_in.at[m], l_sem.at[3 + m]) for m in range(2)],
        [pltpu.make_async_copy(experts.at[0, m], near.at[m], l_sem.at[5 + m]) for m in range(3)],
    ]
    for group in loads:
        for copy in group:
            copy.start()
    share_loads = [
        pltpu.make_async_copy(
            share_all.at[i], share_pack.at[:, pl.ds(i * share_rows, share_rows)], p_sem.at[i]
        )
        for i in range(share_all.shape[0])
    ]
    for copy in share_loads:
        copy.start()
    greet(steps + [{"head": peers[2] + 1 - 2 * (head % 2)}])
    scatter = [
        remote(
            partial.at[pl.ds(r * rows, rows)], incoming.at[r - 1], s_a.at[r - 1], s_b.at[r - 1],
            head=peers[r],
        )
        for r in range(1, len(peers))
    ]
    for copy in scatter:
        copy.start()
    last = remote(experts.at[3, 2], last_in, x_a.at[3], x_b.at[3], head=near_x)
    sides = [
        remote(experts.at[1, m], near_in.at[m], x_a.at[m], x_b.at[m], head=near_x) for m in range(3)
    ]
    here = pl.ds(pl.multiple_of(y * units, 16), units)
    there = pl.ds(pl.multiple_of((1 - y) * units, 16), units)
    across = [
        remote(far.at[m], pack.at[m, here], y_a.at[m], y_b.at[m], head=near_y) for m in range(3)
    ]
    across_in = [
        remote(far.at[m], pack.at[m, there], y_a.at[m], y_b.at[m], head=near_y) for m in range(3)
    ]
    for m in range(2):
        loads[0][m].wait()
        loads[1][m].wait()
        far[m] = (far[m].astype(f32) + far_in[m].astype(f32)).astype(bf16)
        across[m].start()
    loads[0][2].wait()
    for copy in loads[2]:
        copy.wait()

    for copy in scatter:
        copy.wait_recv()
    last.start()
    for copy in sides:
        copy.start()
    total = partial[:rows].astype(f32)
    for r in range(len(peers) - 1):
        total += incoming[r].astype(f32)
    x = tokens[...].astype(f32)
    inverse = lax.rsqrt(jnp.mean(x * x, axis=1, keepdims=True) + EPS)
    normed = x * inverse
    slots[0] = small[...]
    slots[0, 10:11] = jnp.sum(total * normed, axis=0, keepdims=True)
    grad_normed = total * gain[...]
    mean = jnp.mean(grad_normed * normed, axis=1, keepdims=True)
    input_grad[...] = grad_middle[...] + inverse * (grad_normed - normed * mean)

    exchanges = [
        remote(slots.at[2 * k], slots.at[2 * k + 1], t_a.at[k], t_b.at[k], **place)
        for k, place in enumerate(steps)
    ]

    def exchange(k):
        exchanges[k].wait_recv()
        slots[2 * k + 2] = slots[2 * k] + slots[2 * k + 1]
        if k + 1 < len(steps):
            exchanges[k + 1].start()

    exchanges[0].start()

    for copy in share_loads:
        copy.wait()
    exchange(0)
    for m in range(2):
        grad_share_up[:, m * hidden : (m + 1) * hidden] = share_pack[m].T
        exchange(1 + m)
    grad_share_down[...] = share_pack[2]
    exchange(3)
    exchange(4)
    totals[...] = slots[2 * len(steps)]

    last.wait_recv()
    far[2] = (far[2].astype(f32) + last_in[...].astype(f32)).astype(bf16)
    across[2].start()
    for m in range(3):
        sides[m].wait_recv()
        pack[m, here] = (near[m].astype(f32) + near_in[m].astype(f32)).astype(bf16)
        across_in[m].wait_recv()
        if m < 2:
            grad_up[:, m * hidden : (m + 1) * hidden] = pack[m].T
        else:
            grad_down[...] = pack[m]
    for copy in scatter + exchanges + sides + across + [last]:
        copy.wait_send()


def finish(experts, expert_in, share_all, partial, grad_middle, tokens, gain, small):
    n_head, n_seq = lax.axis_size("head"), lax.axis_size("seq")
    rows, width = tokens.shape
    _, _, units, head_part = experts.shape
    share_rows, seq_part = share_all.shape[2:]
    hidden, share_units = 2 * units, n_seq * share_rows
    anywhere = pl.BlockSpec(memory_space=pl.ANY)
    vmem = pl.BlockSpec(memory_space=pltpu.VMEM)
    dma = pltpu.SemaphoreType.DMA
    return pl.pallas_call(
        finish_kernel,
        in_specs=[anywhere] * 3 + [vmem] * 5,
        out_specs=[vmem] * 6,
        out_shape=[
            jax.ShapeDtypeStruct((head_part, 2 * hidden), bf16),
            jax.ShapeDtypeStruct((hidden, head_part), bf16),
            jax.ShapeDtypeStruct((seq_part, 2 * share_units), bf16),
            jax.ShapeDtypeStruct((share_units, seq_part), bf16),
            jax.ShapeDtypeStruct((rows, width), f32),
            jax.ShapeDtypeStruct(small.shape, f32),
        ],
        scratch_shapes=[
            pltpu.VMEM((3, units, head_part), bf16),
            pltpu.VMEM((3, units, head_part), bf16),
            pltpu.VMEM((2, units, head_part), bf16),
            pltpu.VMEM((3, units, head_part), bf16),
            pltpu.VMEM((units, head_part), bf16),
            pltpu.VMEM((3, hidden, head_part), bf16),
            pltpu.VMEM((3, share_units, seq_part), bf16),
            pltpu.VMEM((n_head - 1, rows, width), bf16),
            pltpu.VMEM((11, *small.shape), f32),
            dma((8,)),
            *[dma((4,))] * 2,
            *[dma((3,))] * 2,
            *[dma((n_head - 1,))] * 2,
            *[dma((5,))] * 2,
            dma((n_seq,)),
        ],
        compiler_params=pltpu.CompilerParams(
            collective_id=6, has_side_effects=True, vmem_limit_bytes=VMEM_BYTES
        ),
        cost_estimate=pl.CostEstimate(flops=0, bytes_accessed=1 << 27, transcendentals=0),
        name="finish",
    )(experts, expert_in, share_all, partial, grad_middle, tokens, gain, small)


def after(value, *others):
    return lax.optimization_barrier((value, *others))[0]


def shards(
    tokens,
    cotangent,
    arrange,
    doc_lengths,
    routes,
    norm1_gain,
    qkv_weight,
    qkv_bias,
    out_weight,
    norm2_gain,
    router_weight,
    shared_gate_vec,
    shared_gate_up,
    shared_down,
    expert_gate_up,
    expert_down,
):
    highest = lax.Precision.HIGHEST
    tok_rows, width = tokens.shape
    n_seq = lax.axis_size("seq")
    n_head = lax.axis_size("head")
    seq = lax.axis_index("seq")
    head = lax.axis_index("head")
    group_tok = tok_rows * n_head
    heads_here = qkv_weight.shape[1]
    n_exp = router_weight.shape[1]
    hidden_all = expert_down.shape[1]
    parts = n_head // 2
    part = mesh_part()
    exp_units = hidden_all // parts
    share_all = shared_down.shape[0]
    share_units = share_all // n_seq
    share_rows = -(-share_units // 16) * 16
    base = exp_units + 2 * share_rows
    unit_rows = -(-(base + n_exp + 1) // LANES) * LANES
    seq_part = width // n_seq
    head_part = width // n_head

    wide = heads_here * HD
    plane = parts == 2 and n_seq == 8
    expert_up = expert_gate_up[0]
    at = jnp.stack([head, seq]).astype(jnp.int32)
    gate_rows = jnp.concatenate([router_weight.T, shared_gate_vec[None, :]], axis=0)
    rest = jnp.zeros((3, unit_rows - base, width), bf16).at[0, : n_exp + 1].set(gate_rows)

    place, doc_index, position = layout_of(arrange[0], doc_lengths[0], group_tok)
    blocks = (head + jnp.arange(n_head, dtype=jnp.int32)) % n_head
    table = jnp.stack([place, doc_index, position]).reshape(3, n_head, tok_rows)
    place, doc_index, position = jnp.take(table, blocks, axis=1).reshape(3, group_tok)
    layout_row = jnp.stack([doc_index, place])
    layout_col = layout_row.T
    cosine, sine = rope_tables(position.astype(f32))
    cosine = jnp.concatenate([cosine, cosine], axis=1)
    sine = jnp.concatenate([-sine, sine], axis=1)
    bias_here = lax.dynamic_slice_in_dim(qkv_bias, head * heads_here, heads_here, 0)
    bias_here = bias_here.astype(f32)[:, None, :]

    expert_ids = jnp.arange(n_exp, dtype=jnp.int32)
    chosen = jnp.any(routes[:, :, None] == expert_ids[None, None, :], axis=1)
    marks = jnp.concatenate(
        [chosen.astype(bf16), jnp.zeros((tok_rows, LANES - n_exp), bf16)], axis=1
    )
    grad_ext = jnp.concatenate([cotangent, marks], axis=1)

    stream = tokens.astype(f32)
    gain_first = norm1_gain.astype(f32)
    scale_first = rms_scale(stream)
    normed_first = stream * scale_first
    gain_second = norm2_gain.astype(f32)
    weight_own = qkv_weight.reshape(seq_part, 3 * wide)
    if plane:
        (
            first_group, weight, wout, experts, share_own, share_far, grad_both, seconds,
            qkv, merged, log_total, middle, lowered_second,
        ) = forward(
            tokens, gain_first[None, :], gain_second[None, :], weight_own, out_weight, expert_up,
            expert_down[0], shared_gate_up.reshape(seq_part, 2 * share_all), shared_down, grad_ext,
            bias_here, cosine, sine, layout_col, layout_row,
        )
        grad_both = grad_both.reshape(2, n_seq * tok_rows, width + LANES)
        seconds = seconds.reshape(2, n_seq * tok_rows, width)
        units, back_column, down_rows = mix(
            seconds, grad_both, experts, share_own, share_far, rest, exp_units, base, n_exp
        )
        out_column, grad_experts, grad_share, grad_share_in = products(
            units, seconds, grad_both, down_rows, exp_units, share_rows
        )
        back_own = lax.psum_scatter(back_column, "seq", scatter_dimension=0, tiled=True)
    else:
        weight = lax.all_gather(weight_own, "seq", axis=0, tiled=True)
        wout = lax.all_gather(out_weight, "seq", axis=0)
        first_group = group_gather((normed_first * gain_first).astype(bf16))
        send = jnp.stack([expert_up[:, :hidden_all].T, expert_up[:, hidden_all:].T, expert_down[0]])
        near = []
        for t in range(parts):
            there = jnp.bitwise_xor(part, t)
            block = lax.dynamic_slice_in_dim(send, there * exp_units, exp_units, 1)
            near.append(swap(block, "head", 2 * t) if t else block)
        experts = jnp.stack([block for own in near for block in (own, swap(own, "head", 1))])
        send = jnp.stack([shared_gate_up[:, 0].T, shared_gate_up[:, 1].T, shared_down])
        send = jnp.transpose(send.reshape(3, n_seq, share_units, seq_part), (1, 0, 2, 3))
        if share_rows > share_units:
            send = jnp.pad(send, ((0, 0), (0, 0), (0, share_rows - share_units), (0, 0)))
        share_own = lax.all_to_all(send, "seq", split_axis=0, concat_axis=0)
        full = pack(at, experts, [share_own, swap(share_own, "head", 1)], rest, unit_rows)
        qkv, merged, log_total, middle, lowered_second = attend(
            first_group, weight, wout, bias_here, cosine, sine, layout_col, layout_row, tokens,
            gain_second[None, :],
        )
        grad_chunks = token_gather(grad_ext)
        second_chunks = token_gather(lowered_second)
        back_chunks = []
        unit_chunks = []
        for second, grad in zip(second_chunks, grad_chunks):
            back, units = mix_local(second, grad, full, exp_units, base, n_exp)
            back_chunks.append(back)
            unit_chunks.append(units)
        grad_experts, grad_share, grad_share_far = unit_grads(
            at,
            [(units[:, None], 0) for units in unit_chunks],
            [(second[None], 0) for second in second_chunks],
            [(grad[None], 0) for grad in grad_chunks],
            exp_units,
            share_rows,
        )
        out_chunks = [dot(units[2], full[2], 1, 0).astype(bf16) for units in unit_chunks]
        back_own = token_scatter(back_chunks)
        out_own = token_scatter(out_chunks)
    scale_second = rms_scale(middle)
    normed_second = middle * scale_second

    back_own = after(back_own, grad_experts).astype(f32)

    logits = dot(lowered_second, gate_rows, 1, 1)
    probs = jax.nn.softmax(logits[:, :n_exp], axis=-1)
    share_gate = jax.nn.sigmoid(logits[:, n_exp:])
    grad_probs = back_own[:, width : width + n_exp]
    grad_logits = probs * (grad_probs - jnp.sum(probs * grad_probs, axis=1, keepdims=True))
    grad_gate_logit = (
        back_own[:, width + n_exp : width + n_exp + 1] * share_gate * (1.0 - share_gate)
    )
    grad_gates = jnp.concatenate([grad_logits, grad_gate_logit], axis=1)
    grad_second = back_own[:, :width] + jnp.dot(
        grad_gates, gate_rows.astype(f32), precision=highest
    )
    grad_gate_cols = jnp.dot(grad_gates.T, lowered_second.astype(f32), precision=highest)
    grad_gain_second = jnp.sum(grad_second * normed_second, axis=0)
    grad_normed = grad_second * gain_second
    grad_middle = cotangent.astype(f32) + scale_second * (
        grad_normed - normed_second * jnp.mean(grad_normed * normed_second, axis=1, keepdims=True)
    )
    grad_attn = grad_middle.astype(bf16)
    if plane:
        out_own = lax.psum_scatter(
            after(out_column, grad_attn).reshape(n_seq * tok_rows, width),
            "seq",
            scatter_dimension=0,
            tiled=True,
        )
    mixed = (middle + out_own.astype(f32)).astype(bf16)
    back_args = (
        grad_attn, first_group, weight, wout, qkv, merged, log_total, cosine, sine, layout_col, layout_row
    )
    if plane:
        grad_first, grad_weight, grad_bias_here, expert_in, share_parts = attend_back(
            *back_args, extra=(grad_experts, grad_share, grad_share_in)
        )
    else:
        grad_first, grad_weight, grad_bias_here = attend_back(*back_args)
    grad_weight = lax.psum_scatter(grad_weight, "seq", scatter_dimension=0, tiled=False)
    grad_bias = lax.dynamic_update_slice_in_dim(
        jnp.zeros(qkv_bias.shape, f32), grad_bias_here[:, 0], head * heads_here, 0
    )
    small = jnp.concatenate(
        [grad_gate_cols, grad_gain_second[None, :], jnp.zeros((1, width), f32), grad_bias.reshape(-1, width)],
        axis=0,
    )
    if plane:
        small = jnp.pad(small, ((0, 16 - small.shape[0]), (0, 0)))
        own_up, own_down, grad_share_up, grad_share_down, input_grad, totals = finish(
            grad_experts, expert_in, share_parts, grad_first, grad_middle, tokens, gain_first[None, :],
            small,
        )
    else:
        grad_first = group_scatter(grad_first)
        small = small.at[n_exp + 2].set(jnp.sum(grad_first * normed_first, axis=0))
        grad_normed_first = grad_first * gain_first
        input_grad = grad_middle + scale_first * (
            grad_normed_first
            - normed_first * jnp.mean(grad_normed_first * normed_first, axis=1, keepdims=True)
        )
        totals = total_over_all(small)
        grad_share = grad_share + swap(grad_share_far, "head", 1)
        grad_share = lax.all_to_all(grad_share[:, :, :share_units], "seq", split_axis=0, concat_axis=0)
        grad_share = jnp.transpose(grad_share, (1, 0, 2, 3)).reshape(3, share_all, seq_part)
        own = {}
        for t in range(parts)[::-1]:
            total = grad_experts[2 * t] + swap(grad_experts[2 * t + 1], "head", 1)
            own[t] = swap(total, "head", 2 * t) if t else total
        own = jnp.stack([own[t] for t in range(parts)])
        own = jnp.take(own, jnp.bitwise_xor(part, jnp.arange(parts, dtype=jnp.int32)), axis=0)
        own = jnp.transpose(own, (1, 0, 2, 3)).reshape(3, hidden_all, head_part)
        own_up, own_down = jnp.concatenate([own[0].T, own[1].T], axis=1), own[2]
        grad_share_up = jnp.concatenate([grad_share[0].T, grad_share[1].T], axis=1)
        grad_share_down = grad_share[2]
    return (
        mixed,
        input_grad,
        totals[n_exp + 2],
        grad_weight[: 3 * wide].astype(f32).T.reshape(qkv_weight.shape),
        totals[n_exp + 3 : n_exp + 3 + 3].reshape(qkv_bias.shape),
        grad_weight[3 * wide :].astype(f32),
        totals[n_exp + 1],
        totals[:n_exp].T,
        totals[n_exp],
        grad_share_up.reshape(shared_gate_up.shape).astype(f32),
        grad_share_down.astype(f32),
        own_up.astype(f32)[None],
        own_down.astype(f32)[None],
    )


def solution(mesh):
    return jax.shard_map(
        shards,
        mesh=mesh,
        in_specs=(
            P(("seq", "head"), None),
            P(("seq", "head"), None),
            P("seq", None),
            P("seq", None),
            P(("seq", "head"), None),
            P(),
            P("seq", "head", None),
            P(),
            P("head", "seq"),
            P(),
            P(),
            P(),
            P("seq", None, "head"),
            P("head", "seq"),
            P("seq", "head", None),
            P("seq", None, "head"),
        ),
        out_specs=(
            P(("seq", "head"), None),
            P(("seq", "head"), None),
            P(),
            P("seq", "head", None),
            P(),
            P("head", "seq"),
            P(),
            P(),
            P(),
            P("seq", None, "head"),
            P("head", "seq"),
            P("seq", "head", None),
            P("seq", None, "head"),
        ),
        check_vma=False,
    )
```

```python
import functools

import jax
import jax.numpy as jnp
from jax import lax
from jax.experimental import pallas as pl
from jax.experimental.pallas import tpu as pltpu
from jax.sharding import PartitionSpec as P

HD = 128
EPS = 1e-06
THETA = 1000000.0
NEGATIVE = -1e30
LANES = 128
TILE = 256
MESH = pl.DeviceIdType.MESH
VMEM_BYTES = 61 * 1024 * 1024
bf16 = jnp.bfloat16
f32 = jnp.float32


def rms_scale(values):
    return lax.rsqrt(jnp.mean(values * values, axis=-1, keepdims=True) + EPS)


def rope_tables(position):
    half = HD // 2
    exponent = jnp.arange(half, dtype=f32) * (2.0 / HD)
    frequency = THETA ** (-exponent)
    angle = position[:, None] * frequency[None, :]
    return (jnp.cos(angle), jnp.sin(angle))


def layout_of(arrange_row, length_row, group_tok):
    counter = jnp.arange(group_tok, dtype=jnp.int32)
    place = jnp.sum(
        jnp.where(arrange_row[None, :] == counter[:, None], counter[None, :], 0),
        axis=1,
        dtype=jnp.int32,
    )
    ends = jnp.cumsum(length_row, dtype=jnp.int32)
    starts = ends - length_row
    doc_index = jnp.sum(
        (place[:, None] >= ends[None, :]).astype(jnp.int32), axis=1, dtype=jnp.int32
    )
    picked = doc_index[:, None] == jnp.arange(length_row.shape[0], dtype=jnp.int32)[None, :]
    start_of = jnp.sum(jnp.where(picked, starts[None, :], 0), axis=1, dtype=jnp.int32)
    return (place, doc_index, place - start_of)


def dot(left, right, left_dim, right_dim):
    return lax.dot_general(
        left, right, (((left_dim,), (right_dim,)), ((), ())), preferred_element_type=f32
    )


def swap(block, axis, bit):
    size = lax.axis_size(axis)
    return lax.ppermute(block, axis, [(i, i ^ bit) for i in range(size)])


def bits_of(size):
    bits = []
    bit = 1
    while bit < size:
        bits.append(bit)
        bit *= 2
    return bits


def spread(block, order):
    found = {0: block}
    for bit in order:
        for near in sorted(found):
            found[near ^ bit] = swap(found[near], "head", bit)
    return found


def collect(parts, order):
    parts = dict(parts)
    for bit in reversed(order):
        for far in sorted((r for r in parts if r & bit), reverse=True):
            parts[far ^ bit] = parts[far ^ bit] + swap(parts.pop(far), "head", bit)
    return parts[0]


def shift(block, axis, step):
    size = lax.axis_size(axis)
    return lax.ppermute(block, axis, [((i + step) % size, i) for i in range(size)])


def group_gather(block):
    size = lax.axis_size("head")
    return jnp.concatenate([block] + [shift(block, "head", r) for r in range(1, size)], axis=0)


def group_scatter(block):
    size = lax.axis_size("head")
    rows = block.shape[0] // size
    total = block[:rows].astype(f32)
    for r in range(1, size):
        total += shift(block[r * rows : (r + 1) * rows], "head", size - r).astype(f32)
    return total


def remote(src, dst, send_sem, recv_sem, **place):
    return pltpu.make_async_remote_copy(
        src_ref=src,
        dst_ref=dst,
        send_sem=send_sem,
        recv_sem=recv_sem,
        device_id=place,
        device_id_type=MESH,
    )


def greet(places):
    barrier = pltpu.get_barrier_semaphore()
    for place in places:
        pl.semaphore_signal(barrier, inc=1, device_id=place, device_id_type=MESH)
    pl.semaphore_wait(barrier, len(places))


def plane_places():
    head, seq = lax.axis_index("head"), lax.axis_index("seq")
    x, y = head % 2, head // 2
    return y * 2 + (1 - x), (1 - y) * 2 + x, seq + 1 - 2 * (seq % 2)


def plane_owners():
    head = lax.axis_index("head")
    near_x, near_y, _ = plane_places()
    return head, near_x, near_y, near_y + 1 - 2 * (head % 2)


def ring_places():
    size = lax.axis_size("head")
    head = lax.axis_index("head")
    return [(head + r) % size for r in range(size)]


class Line:
    def __init__(self, place, far, sems):
        self.seq = lax.axis_index("seq")
        self.count = lax.axis_size("seq") // 2
        self.depth = self.count - 1
        self.z = self.seq // 2
        _, self.near_y, self.near_core = plane_places()
        self.place, self.far = place, far
        self.sems = sems

    def index(self, j):
        if j == 0:
            return self.seq
        if j <= self.depth:
            return self.seq - 2 * j
        return self.seq + 2 * (j - self.depth)

    def valid(self, j):
        if j == 0:
            return self.z >= 0
        if j <= self.depth:
            return self.z - j >= 0
        return self.z + (j - self.depth) < self.count

    def line_copy(self, j, up):
        block = self.place(self.index(j))
        if up:
            to, k = self.seq + 2, j
        else:
            to, k = self.seq - 2, self.depth + (j - self.depth if j else 0)
        return remote(block, block, self.sems.at[0, k], self.sems.at[1, k], seq=to)

    def line_arrival(self, j):
        block = self.place(self.index(j))
        return remote(
            block, block, self.sems.at[0, j - 1], self.sems.at[1, j - 1], seq=self.near_core
        )

    def core_copy(self, j):
        block = self.place(self.index(j))
        return remote(block, block, self.sems.at[2, j], self.sems.at[3, j], seq=self.near_core)

    def core_arrival(self, j):
        block = self.place(self.index(j) + self.near_core - self.seq)
        return remote(block, block, self.sems.at[2, j], self.sems.at[3, j], seq=self.near_core)

    def far_copy(self, j):
        i = self.index(j)
        return remote(
            self.place(i), self.far(i), self.sems.at[4, j], self.sems.at[5, j], head=self.near_y
        )

    def far_core_copy(self, j):
        there = self.far(self.index(j))
        return remote(there, there, self.sems.at[6, j], self.sems.at[7, j], seq=self.near_core)

    def far_core_arrival(self, j):
        there = self.far(self.index(j) + self.near_core - self.seq)
        return remote(there, there, self.sems.at[6, j], self.sems.at[7, j], seq=self.near_core)

    def sides(self, j):
        self.core_copy(j).start()
        if self.far is not None:
            self.far_copy(j).start()

    def ups(self):
        return range(self.depth)

    def downs(self):
        return [0] + [self.depth + k for k in range(1, self.depth)]

    def has_above(self):
        return self.z + 1 < self.count

    def has_below(self):
        return self.z >= 1

    def begin(self):
        @pl.when(self.has_above())
        def _():
            self.line_copy(0, True).start()

        @pl.when(self.has_below())
        def _():
            self.line_copy(0, False).start()

        self.sides(0)

    def step(self, k):
        @pl.when(self.valid(1 + k))
        def _():
            self.line_arrival(1 + k).wait_recv()
            if 1 + k < self.depth:

                @pl.when(self.has_above())
                def _():
                    self.line_copy(1 + k, True).start()

            self.sides(1 + k)

        @pl.when(self.valid(self.depth + 1 + k))
        def _():
            self.line_arrival(self.depth + 1 + k).wait_recv()
            if 1 + k < self.depth:

                @pl.when(self.has_below())
                def _():
                    self.line_copy(self.depth + 1 + k, False).start()

            self.sides(self.depth + 1 + k)

    def side_step(self, j):
        @pl.when(self.valid(j))
        def _():
            self.far_copy(j).wait_recv()
            self.far_core_copy(j).start()

    def wait_blocks(self):
        for j in range(2 * self.depth + 1):

            @pl.when(self.valid(j))
            def _():
                self.core_arrival(j).wait_recv()
                if self.far is not None:
                    self.far_core_arrival(j).wait_recv()

    def wait_sends(self):
        for j in range(2 * self.depth + 1):

            @pl.when(self.valid(j))
            def _():
                self.core_copy(j).wait_send()
                if self.far is not None:
                    self.far_copy(j).wait_send()
                    self.far_core_copy(j).wait_send()

        for j in self.ups():

            @pl.when(self.valid(j) & self.has_above())
            def _():
                self.line_copy(j, True).wait_send()

        for j in self.downs():

            @pl.when(self.valid(j) & self.has_below())
            def _():
                self.line_copy(j, False).wait_send()


def forward_kernel(
    tokens, gain_first, gain_second, weight_own, wout_own, expert_up, expert_down, share_up, share_down,
    grad_ext, bias, cosine, sine, layout_col, layout_row,
    first_out, weight_out, wout_out, experts, share, share_far, grads, seconds, qkv, merged, log_total, middle,
    lowered,
    group, weight, wout, expert_raw, expert_pack, share_raw, share_pack, mask, outgoing, incoming,
    local, line_w, line_o, line_g, line_s, ring_a, ring_b, sc_a, sc_b, ex_a, ex_b, sh_a, sh_b,
):
    seq, head = lax.axis_index("seq"), lax.axis_index("head")
    n_seq = lax.axis_size("seq")
    near_x, near_y, near_core = plane_places()
    peers = ring_places()
    size = len(peers)
    rows, width = tokens.shape
    heads = bias.shape[0]
    units = experts.shape[2]
    y = head // 2
    share_rows = share.shape[2]
    hidden = expert_down.shape[0]
    part = weight_own.shape[0]

    fetch = [
        pltpu.make_async_copy(
            weight_own, weight.at[pl.ds(pl.multiple_of(seq * part, 16), part)], local.at[0]
        ),
        pltpu.make_async_copy(wout_own, wout.at[seq], local.at[1]),
        pltpu.make_async_copy(expert_up, expert_raw, local.at[2]),
        pltpu.make_async_copy(expert_down, expert_pack.at[2], local.at[3]),
        pltpu.make_async_copy(share_up, share_raw, local.at[4]),
        pltpu.make_async_copy(share_down, share_pack.at[2], local.at[5]),
        pltpu.make_async_copy(grad_ext, grads.at[0, seq], local.at[6]),
    ]
    for copy in fetch:
        copy.start()
    greet(
        [{"head": peer} for peer in peers[1:]]
        + [{"seq": (seq + k) % n_seq} for k in range(1, n_seq)]
    )

    gather_w = Line(lambda i: weight.at[pl.ds(pl.multiple_of(i * part, 16), part)], None, line_w)
    gather_o = Line(lambda i: wout.at[i], None, line_o)
    gather_g = Line(lambda i: grads.at[0, i], lambda i: grads.at[1, i], line_g)
    gather_s = Line(lambda i: seconds.at[0, i], lambda i: seconds.at[1, i], line_s)
    fetch[0].wait()
    gather_w.begin()
    fetch[1].wait()
    gather_o.begin()

    group[:rows] = norm_rows(tokens[...].astype(f32), gain_first[...])
    ring = [
        remote(
            group.at[pl.ds(0, rows)], group.at[pl.ds(r * rows, rows)],
            ring_a.at[r - 1], ring_b.at[r - 1], head=peers[size - r],
        )
        for r in range(1, size)
    ]
    for copy in ring:
        copy.start()

    fetch[2].wait()
    fetch[3].wait()
    mine = pl.ds(pl.multiple_of(y * units, 16), units)
    other = pl.ds(pl.multiple_of((1 - y) * units, 16), units)
    ups = [
        remote(expert_pack.at[m, other], experts.at[2, m], ex_a.at[m], ex_b.at[m], head=near_y)
        for m in range(3)
    ]
    sides = [
        remote(expert_pack.at[m, mine], experts.at[1, m], ex_a.at[3 + m], ex_b.at[3 + m], head=near_x)
        for m in range(3)
    ]
    ons = [
        remote(experts.at[2, m], experts.at[3, m], ex_a.at[6 + m], ex_b.at[6 + m], head=near_x)
        for m in range(3)
    ]
    order = (2, 0, 1)
    for m in order:
        if m < 2:
            expert_pack[m] = expert_raw[:, m * hidden : (m + 1) * hidden].T
        ups[m].start()
        sides[m].start()
    keep = [pltpu.make_async_copy(expert_pack.at[:, mine], experts.at[0], local.at[7])]
    keep[0].start()

    fetch[4].wait()
    fetch[5].wait()
    for m in range(2):
        share_pack[m] = share_raw[:, m * hidden : (m + 1) * hidden].T

    def share_block(i):
        return share_pack.at[:, pl.ds(pl.multiple_of(i * share_rows, 16), share_rows)]

    shares = [
        remote(
            share_block((seq + k) % n_seq), share.at[seq], sh_a.at[k], sh_b.at[k],
            seq=(seq + k) % n_seq,
        )
        for k in range(1, n_seq)
    ]
    share_own = pltpu.make_async_copy(share_block(seq), share.at[seq], local.at[8])
    share_own.start()
    arrivals = []
    for k in range(1, n_seq):
        block = share.at[(seq + n_seq - k) % n_seq]
        arrivals.append(remote(block, block, sh_a.at[k], sh_b.at[k], seq=(seq + k) % n_seq))
    crossings = []
    for k in range(n_seq):
        place = (seq + n_seq - k) % n_seq
        crossings.append(
            remote(
                share.at[place], share_far.at[place], sh_a.at[n_seq + k], sh_b.at[n_seq + k],
                head=near_x,
            )
        )

    mask[...] = mask_of(layout_col[...], layout_row[...])
    gather_w.step(0)
    gather_o.step(0)
    gather_w.step(1)
    gather_o.step(1)
    ups[2].wait_recv()
    ons[2].start()
    fetch[6].wait()
    gather_w.step(2)
    gather_o.step(2)
    gather_g.begin()
    for copy in shares:
        copy.start()
    for copy in ring:
        copy.wait_recv()
    gather_w.wait_blocks()
    gather_o.wait_blocks()
    keep += [
        pltpu.make_async_copy(weight, weight_out, local.at[9]),
        pltpu.make_async_copy(wout, wout_out, local.at[10]),
        pltpu.make_async_copy(group, first_out, local.at[11]),
    ]
    for copy in keep[1:]:
        copy.start()

    step = 3 * HD
    for n in range(heads):
        linear = dot(group[...], weight[:, n * step : (n + 1) * step], 1, 0) + bias[n]
        parts, output, log_sum = head_forward(linear, cosine[...], sine[...], mask[...])
        for k in range(3):
            qkv[:, n * step + k * HD : n * step + (k + 1) * HD] = parts[k]
        merged[:, n * HD : (n + 1) * HD] = output
        log_total[n] = jnp.broadcast_to(log_sum, log_total.shape[1:])
        if n == 2:
            gather_g.step(0)
            gather_g.side_step(0)
    copies, own = scatter_start(merged, wout, outgoing, incoming, sc_a, sc_b, rows, peers)
    ups[0].wait_recv()
    ons[0].start()
    block = wout.shape[2]
    for b in range(len(own)):
        cols = slice(b * block, (b + 1) * block)
        middle[:, cols] = tokens[:, cols].astype(f32) + own[b]
    gather_g.step(1)
    for copy in copies:
        copy.wait_recv()
    total = middle[...]
    for r in range(size - 1):
        total += incoming[r].astype(f32)
    middle[...] = total
    lowered[...] = norm_rows(total, gain_second[...])
    last = pltpu.make_async_copy(lowered, seconds.at[0, seq], local.at[12])
    last.start()
    last.wait()
    gather_s.begin()
    ups[1].wait_recv()
    ons[1].start()

    share_own.wait()
    crossings[0].start()
    gather_g.step(2)
    for j in (1, 1 + gather_g.depth, 2, 2 + gather_g.depth):
        gather_g.side_step(j)
    gather_s.step(0)
    for k in range(1, 4):
        arrivals[k - 1].wait_recv()
        crossings[k].start()
    for j in (3, 3 + gather_g.depth):
        gather_g.side_step(j)
    gather_s.side_step(0)
    gather_s.step(1)
    for k in range(4, n_seq):
        arrivals[k - 1].wait_recv()
        crossings[k].start()
    for j in (1, 1 + gather_g.depth):
        gather_s.side_step(j)
    gather_s.step(2)
    for j in (2, 2 + gather_g.depth, 3, 3 + gather_g.depth):
        gather_s.side_step(j)

    gather_g.wait_blocks()
    gather_s.wait_blocks()
    for copy in sides + ons + crossings:
        copy.wait()
    for copy in ups + ring + copies + shares:
        copy.wait_send()
    for copy in keep:
        copy.wait()
    for line in (gather_w, gather_o, gather_g, gather_s):
        line.wait_sends()


def forward(
    tokens, gain_first, gain_second, weight_own, wout_own, expert_up, expert_down, share_up, share_down,
    grad_ext, bias, cosine, sine, layout_col, layout_row,
):
    n_seq, n_head = lax.axis_size("seq"), lax.axis_size("head")
    rows, width = tokens.shape
    group_tok = rows * n_head
    heads = bias.shape[0]
    wide = heads * HD
    part = weight_own.shape[0]
    hidden, head_part = expert_down.shape
    units = hidden // 2
    share_all, seq_part = share_down.shape
    share_rows = share_all // n_seq
    ext = grad_ext.shape[1]
    anywhere = pl.BlockSpec(memory_space=pl.ANY)
    vmem = pl.BlockSpec(memory_space=pltpu.VMEM)
    dma = pltpu.SemaphoreType.DMA
    lines = n_seq - 1

    def hbm(*shape):
        return (anywhere, jax.ShapeDtypeStruct(shape, bf16))

    outs = [
        hbm(group_tok, width),
        hbm(width, 3 * wide),
        hbm(n_seq, wide, part),
        hbm(4, 3, units, head_part),
        hbm(n_seq, 3, share_rows, seq_part),
        hbm(n_seq, 3, share_rows, seq_part),
        hbm(2, n_seq, rows, ext),
        hbm(2, n_seq, rows, width),
        (vmem, jax.ShapeDtypeStruct((group_tok, 3 * wide), bf16)),
        (vmem, jax.ShapeDtypeStruct((group_tok, wide), bf16)),
        (vmem, jax.ShapeDtypeStruct((heads, group_tok, LANES), f32)),
        (vmem, jax.ShapeDtypeStruct((rows, width), f32)),
        (vmem, jax.ShapeDtypeStruct((rows, width), bf16)),
    ]
    return pl.pallas_call(
        forward_kernel,
        in_specs=[vmem] * 3 + [anywhere] * 7 + [vmem] * 5,
        out_specs=[spec for spec, _ in outs],
        out_shape=[shape for _, shape in outs],
        scratch_shapes=[
            pltpu.VMEM((group_tok, width), bf16),
            pltpu.VMEM((width, 3 * wide), bf16),
            pltpu.VMEM((n_seq, wide, part), bf16),
            pltpu.VMEM(expert_up.shape, bf16),
            pltpu.VMEM((3, hidden, head_part), bf16),
            pltpu.VMEM(share_up.shape, bf16),
            pltpu.VMEM((3, share_all, seq_part), bf16),
            pltpu.VMEM((group_tok, group_tok), f32),
            pltpu.VMEM((n_head - 1, rows, width), bf16),
            pltpu.VMEM((n_head - 1, rows, width), bf16),
            dma((13,)),
            dma((4, lines)),
            dma((4, lines)),
            dma((8, lines)),
            dma((8, lines)),
            dma((n_head - 1,)),
            dma((n_head - 1,)),
            dma((n_head - 1,)),
            dma((n_head - 1,)),
            dma((9,)),
            dma((9,)),
            dma((2 * n_seq,)),
            dma((2 * n_seq,)),
        ],
        compiler_params=pltpu.CompilerParams(
            collective_id=0, has_side_effects=True, vmem_limit_bytes=VMEM_BYTES
        ),
        cost_estimate=pl.CostEstimate(
            flops=2 * group_tok * width * 4 * wide, bytes_accessed=1 << 29, transcendentals=0
        ),
        name="forward",
    )(
        tokens, gain_first, gain_second, weight_own, wout_own, expert_up, expert_down, share_up,
        share_down, grad_ext, bias, cosine, sine, layout_col, layout_row,
    )


def mesh_part():
    return lax.axis_index("head") // 2


def token_bits():
    return bits_of(lax.axis_size("head"))[1:]


def token_gather(block):
    order = token_bits()
    column = lax.all_gather(block, "seq", axis=0, tiled=True)
    share = column.shape[0] // 2
    half = share // 2
    core = lax.rem(lax.axis_index("seq"), 2)
    own = lax.dynamic_slice_in_dim(column, core * share, share, 0)
    upper = spread(own[:half], order)
    lower = spread(own[half:], order[::-1])
    chunks = [column]
    for r in sorted(upper)[1:]:
        for piece in (upper[r], lower[r]):
            chunks.append(jnp.concatenate([piece, swap(piece, "seq", 1)], axis=0))
    return chunks


def token_scatter(chunks):
    order = token_bits()
    column = chunks[0]
    share = column.shape[0] // 2
    half = share // 2
    core = lax.rem(lax.axis_index("seq"), 2)
    own = lax.dynamic_slice_in_dim(column, core * share, share, 0)
    sides = [{0: own[:half]}, {0: own[half:]}]
    for i, chunk in enumerate(chunks[1:]):
        sides[i % 2][2 * (i // 2 + 1)] = chunk[:half] + swap(chunk[half:], "seq", 1)
    total = jnp.concatenate([collect(sides[0], order), collect(sides[1], order[::-1])], axis=0)
    column = lax.dynamic_update_slice_in_dim(column, total, core * share, 0)
    return lax.psum_scatter(column, "seq", scatter_dimension=0, tiled=True)


def total_over_all(values):
    for axis in ("head", "seq"):
        for bit in bits_of(lax.axis_size(axis)):
            values = values + swap(values, axis, bit)
    return values


def turn(values, cosine, sine):
    return values * cosine + pltpu.roll(values, HD // 2, 1) * sine


def mask_of(layout_col, layout_row):
    doc_col, place_col = layout_col[:, 0:1], layout_col[:, 1:2]
    doc_row, place_row = layout_row[0:1, :], layout_row[1:2, :]
    return jnp.where((doc_col == doc_row) & (place_row <= place_col), 0.0, NEGATIVE)


def head_forward(linear, cos, sin, mask):
    queries = turn(linear[:, :HD], cos, sin).astype(bf16)
    keys = turn(linear[:, HD : 2 * HD], cos, sin).astype(bf16)
    values = linear[:, 2 * HD :].astype(bf16)
    scores = dot(queries, keys, 1, 1) * HD ** (-0.5) + mask
    largest = jnp.max(scores, axis=1, keepdims=True)
    weights = jnp.exp(scores - largest)
    total = jnp.sum(weights, axis=1, keepdims=True)
    probs = (weights / total).astype(bf16)
    output = dot(probs, values, 1, 0).astype(bf16)
    return (queries, keys, values), output, largest + jnp.log(total)


def norm_rows(rows, gain):
    square = jnp.mean(rows * rows, axis=1, keepdims=True)
    return (rows * lax.rsqrt(square + EPS) * gain).astype(bf16)


def scatter_start(merged, wout, outgoing, incoming, sems_a, sems_b, rows, peers):
    blocks, _, size = wout.shape
    copies = []
    for r in range(len(peers) - 1, 0, -1):
        for b in range(blocks):
            outgoing[r - 1, :, b * size : (b + 1) * size] = dot(
                merged[r * rows : (r + 1) * rows, :], wout[b], 1, 0
            ).astype(bf16)
        copies.append(
            remote(
                outgoing.at[r - 1], incoming.at[r - 1], sems_a.at[r - 1], sems_b.at[r - 1],
                head=peers[r],
            )
        )
        copies[-1].start()
    return copies, [dot(merged[:rows, :], wout[b], 1, 0) for b in range(blocks)]


def attend_kernel(
    first, weight, wout, bias, cosine, sine, layout_col, layout_row, tokens, gain,
    qkv, merged, log_total, middle, lowered, mask, outgoing, incoming, sems_a, sems_b,
):
    n = pl.program_id(0)
    heads = pl.num_programs(0)
    peers = ring_places()

    @pl.when(n == 0)
    def _():
        greet([{"head": peer} for peer in peers[1:]])
        mask[...] = mask_of(layout_col[...], layout_row[...])

    linear = dot(first[...], weight[...], 1, 0) + bias[0]
    parts, output, log_sum = head_forward(linear, cosine[...], sine[...], mask[...])
    for k in range(3):
        qkv[:, k * HD : (k + 1) * HD] = parts[k]
    merged[:, pl.ds(pl.multiple_of(n * HD, HD), HD)] = output
    log_total[0] = jnp.broadcast_to(log_sum, log_total.shape[1:])

    @pl.when(n == heads - 1)
    def _():
        copies, own = scatter_start(
            merged, wout, outgoing, incoming, sems_a, sems_b, tokens.shape[0], peers
        )
        size = wout.shape[2]
        for b, block in enumerate(own):
            cols = slice(b * size, (b + 1) * size)
            middle[:, cols] = tokens[:, cols].astype(f32) + block
        for copy in copies:
            copy.wait()
        total = middle[...]
        for r in range(len(peers) - 1):
            total += incoming[r].astype(f32)
        middle[...] = total
        lowered[...] = norm_rows(total, gain[...])


def attend(first, weight, wout, bias, cosine, sine, layout_col, layout_row, tokens, gain):
    rows, width = first.shape
    heads = bias.shape[0]
    own = tokens.shape[0]
    others = lax.axis_size("head") - 1
    step = 3 * HD
    wide = heads * HD

    def whole(shape):
        return pl.BlockSpec(shape, lambda n: (0,) * len(shape))

    return pl.pallas_call(
        attend_kernel,
        grid=(heads,),
        in_specs=[
            whole((rows, width)),
            pl.BlockSpec((width, step), lambda n: (0, n)),
            whole(wout.shape),
            pl.BlockSpec((1, 1, step), lambda n: (n, 0, 0)),
            whole((rows, HD)),
            whole((rows, HD)),
            whole((rows, 2)),
            whole((2, rows)),
            whole((own, width)),
            whole((1, width)),
        ],
        out_specs=[
            pl.BlockSpec((rows, step), lambda n: (0, n)),
            whole((rows, wide)),
            pl.BlockSpec((1, rows, LANES), lambda n: (n, 0, 0)),
            whole((own, width)),
            whole((own, width)),
        ],
        out_shape=[
            jax.ShapeDtypeStruct((rows, heads * step), bf16),
            jax.ShapeDtypeStruct((rows, wide), bf16),
            jax.ShapeDtypeStruct((heads, rows, LANES), f32),
            jax.ShapeDtypeStruct((own, width), f32),
            jax.ShapeDtypeStruct((own, width), bf16),
        ],
        scratch_shapes=[
            pltpu.VMEM((rows, rows), f32),
            pltpu.VMEM((others, own, width), bf16),
            pltpu.VMEM((others, own, width), bf16),
            pltpu.SemaphoreType.DMA((others,)),
            pltpu.SemaphoreType.DMA((others,)),
        ],
        compiler_params=pltpu.CompilerParams(
            collective_id=2, has_side_effects=True, vmem_limit_bytes=VMEM_BYTES
        ),
        cost_estimate=pl.CostEstimate(
            flops=2 * rows * width * 4 * wide, bytes_accessed=8 * width * wide, transcendentals=0
        ),
        name="attend",
    )(first, weight, wout, bias, cosine, sine, layout_col, layout_row, tokens, gain)


def attend_back_kernel(
    plane, grad_own, first, weight, wout, qkv, merged, log_total, cosine, sine, layout_col, layout_row,
    *refs,
):
    if plane:
        experts, grad_first, grad_weight, grad_bias, expert_in, x_a, x_b = refs[:5] + refs[-2:]
        refs = refs[5:-2]
    else:
        grad_first, grad_weight, grad_bias = refs[:3]
        refs = refs[3:]
    mask, grad_merged, acc, grad, sems_a, sems_b = refs
    n = pl.program_id(0)
    peers = ring_places()
    own = grad_own.shape[0]
    heads = pl.num_programs(0)
    if plane:
        near_x = plane_places()[0]
        cross = [remote(experts.at[3, 0], expert_in, x_a, x_b, head=near_x)]
    scale = HD ** (-0.5)
    blocks, _, size = grad_weight.shape
    wide = wout.shape[1]

    @pl.when(n == 0)
    def _():
        greet([{"head": peer} for peer in peers[1:]])
        copies = [
            remote(
                grad_own, grad.at[pl.ds(r * own, own)], sems_a.at[r - 1], sems_b.at[r - 1],
                head=peers[len(peers) - r],
            )
            for r in range(1, len(peers))
        ]
        for copy in copies:
            copy.start()
        grad[:own] = grad_own[...]
        mask[...] = mask_of(layout_col[...], layout_row[...])
        acc[...] = jnp.zeros_like(acc)
        for copy in copies:
            copy.wait()
        if plane:
            for copy in cross:
                copy.start()
        total = jnp.zeros((grad.shape[0], wide), f32)
        for s in range(blocks):
            total += dot(grad[:, s * size : (s + 1) * size], wout[s], 1, 1)
        grad_merged[...] = total.astype(bf16)
        for s in range(blocks):
            grad_weight[s, 3 * wide :, :] = dot(
                merged[...], grad[:, s * size : (s + 1) * size], 0, 0
            ).astype(bf16)

    cos, sin = cosine[...], -sine[...]
    queries, keys, values = qkv[:, :HD], qkv[:, HD : 2 * HD], qkv[:, 2 * HD :]
    grad_out = grad_merged[:, pl.ds(pl.multiple_of(n * HD, HD), HD)]
    scores = dot(queries, keys, 1, 1) * scale + mask[...]
    probs = jnp.exp(scores - log_total[0][:, 0:1])
    grad_values = dot(probs.astype(bf16), grad_out, 0, 0).astype(bf16)
    grad_probs = dot(grad_out, values, 1, 1)
    centre = jnp.sum(probs * grad_probs, axis=1, keepdims=True)
    grad_scores = (probs * (grad_probs - centre)).astype(bf16)
    grad_queries = (dot(grad_scores, keys, 1, 0) * scale).astype(bf16).astype(f32)
    grad_keys = (dot(grad_scores, queries, 0, 0) * scale).astype(bf16).astype(f32)
    grad_linear = jnp.concatenate(
        [turn(grad_queries, cos, sin).astype(bf16), turn(grad_keys, cos, sin).astype(bf16), grad_values],
        axis=1,
    )
    grad_bias[0] = jnp.sum(grad_linear.astype(f32), axis=0, keepdims=True)
    acc[...] += dot(grad_linear, weight[...], 1, 1)
    step = 3 * HD
    for s in range(blocks):
        grad_weight[s, pl.ds(pl.multiple_of(n * step, HD), step), :] = dot(
            grad_linear, first[:, s * size : (s + 1) * size], 0, 0
        ).astype(bf16)

    @pl.when(n == heads - 1)
    def _():
        grad_first[...] = acc[...].astype(bf16)
        if plane:
            for copy in cross:
                copy.wait()


def attend_back(
    grad, first, weight, wout, qkv, merged, log_total, cosine, sine, layout_col, layout_row, extra=()
):
    rows, width = first.shape
    heads = log_total.shape[0]
    step = 3 * HD
    wide = heads * HD
    n_seq = lax.axis_size("seq")
    size = width // n_seq
    own = grad.shape[0]
    others = lax.axis_size("head") - 1

    anywhere = pl.BlockSpec(memory_space=pl.ANY)
    more_outs, more_scratch = [], []
    if extra:
        more_outs = [jax.ShapeDtypeStruct(extra[0].shape[2:], bf16)]
        more_scratch = [pltpu.SemaphoreType.DMA] * 2

    def whole(shape):
        return pl.BlockSpec(shape, lambda n: (0,) * len(shape))

    return pl.pallas_call(
        functools.partial(attend_back_kernel, bool(extra)),
        grid=(heads,),
        in_specs=[
            whole((own, width)),
            whole((rows, width)),
            pl.BlockSpec((width, step), lambda n: (0, n)),
            whole(wout.shape),
            pl.BlockSpec((rows, step), lambda n: (0, n)),
            whole((rows, wide)),
            pl.BlockSpec((1, rows, LANES), lambda n: (n, 0, 0)),
            whole((rows, HD)),
            whole((rows, HD)),
            whole((rows, 2)),
            whole((2, rows)),
        ]
        + [anywhere] * len(extra),
        out_specs=[
            whole((rows, width)),
            whole((n_seq, 4 * wide, size)),
            pl.BlockSpec((1, 1, step), lambda n: (n, 0, 0)),
        ]
        + [anywhere] * len(more_outs),
        out_shape=[
            jax.ShapeDtypeStruct((rows, width), bf16),
            jax.ShapeDtypeStruct((n_seq, 4 * wide, size), bf16),
            jax.ShapeDtypeStruct((heads, 1, step), f32),
        ]
        + more_outs,
        scratch_shapes=[
            pltpu.VMEM((rows, rows), f32),
            pltpu.VMEM((rows, wide), bf16),
            pltpu.VMEM((rows, width), f32),
            pltpu.VMEM((rows, width), bf16),
            pltpu.SemaphoreType.DMA((others,)),
            pltpu.SemaphoreType.DMA((others,)),
        ]
        + more_scratch,
        compiler_params=pltpu.CompilerParams(
            collective_id=3, has_side_effects=True, vmem_limit_bytes=VMEM_BYTES
        ),
        cost_estimate=pl.CostEstimate(
            flops=4 * rows * width * 4 * wide, bytes_accessed=16 * width * wide, transcendentals=0
        ),
        name="attend_back",
    )(grad, first, weight, wout, qkv, merged, log_total, cosine, sine, layout_col, layout_row, *extra)


def pack_kernel(exp_units, share_units, at, *refs):
    stacked, shares = refs[0], refs[-5:-3]
    experts = [stacked.at[r] for r in range(stacked.shape[0])]
    rest, full, sems = refs[-3:]
    head = at[0]
    copies = []
    for r, block in enumerate(experts):
        size = block.shape[2]
        start = pl.multiple_of(jnp.bitwise_xor(head, r) * size, size)
        copies.append(
            pltpu.make_async_copy(
                block, full.at[:, pl.ds(0, exp_units), pl.ds(start, size)], sems.at[len(copies)]
            )
        )
    for r, block in enumerate(shares):
        size = block.shape[3]
        for s in range(block.shape[0]):
            copies.append(
                pltpu.make_async_copy(
                    block.at[s],
                    full.at[:, pl.ds(exp_units + r * share_units, share_units), pl.ds(s * size, size)],
                    sems.at[len(copies)],
                )
            )
    base = exp_units + 2 * share_units
    copies.append(
        pltpu.make_async_copy(rest, full.at[:, pl.ds(base, rest.shape[1]), :], sems.at[len(copies)])
    )
    for copy in copies:
        copy.start()
    for copy in copies:
        copy.wait()


def pack(at, experts, shares, rest, unit_rows):
    exp_units, share_units = experts.shape[2], shares[0].shape[2]
    count = experts.shape[0] + 2 * shares[0].shape[0] + 1
    anywhere = pl.BlockSpec(memory_space=pl.ANY)
    return pl.pallas_call(
        functools.partial(pack_kernel, exp_units, share_units),
        in_specs=[pl.BlockSpec(memory_space=pltpu.SMEM)] + [anywhere] * 4,
        out_specs=anywhere,
        out_shape=jax.ShapeDtypeStruct((3, unit_rows, rest.shape[2]), bf16),
        scratch_shapes=[pltpu.SemaphoreType.DMA((count,))],
        compiler_params=pltpu.CompilerParams(vmem_limit_bytes=1 << 20),
        cost_estimate=pl.CostEstimate(
            flops=0, bytes_accessed=12 * unit_rows * rest.shape[2], transcendentals=0
        ),
        name="pack",
    )(at, experts, *shares, rest)


def mix_rows(exp_units, base, n_exp, x, grad_ext, w, units, wait=None):
    rows, width = x.shape
    unit_rows = w.shape[1]
    seq = lax.axis_index("seq")
    block = base // LANES * LANES
    chunks = [(block, unit_rows)] + [(a, min(a + 512, block)) for a in range(0, block, 512)]
    lane = lax.broadcasted_iota(jnp.int32, (rows, LANES), 1)
    marks = grad_ext[:, width:].astype(f32)
    mark = jnp.sum(jnp.where(lane == seq, marks, 0.0), axis=1, keepdims=True)
    exp_sum = share_sum = gate_here = share_gate = 0.0
    for i, (a, b) in enumerate(chunks):
        if wait is not None and i < 2:
            wait(i)
        gate = dot(x, w[0, a:b], 1, 1)
        up = dot(x, w[1, a:b], 1, 1)
        raw = dot(grad_ext[:, :width], w[2, a:b], 1, 1)
        if i == 0:
            logits = gate[:, :LANES]
            from_base = lane - (base - block)
            is_logit = (from_base >= 0) & (from_base < n_exp)
            largest = jnp.max(jnp.where(is_logit, logits, NEGATIVE), axis=1, keepdims=True)
            powers = jnp.where(is_logit, jnp.exp(jnp.where(is_logit, logits - largest, 0.0)), 0.0)
            chosen = jnp.sum(jnp.where(from_base == seq, powers, 0.0), axis=1, keepdims=True)
            gate_here = mark * chosen / jnp.sum(powers, axis=1, keepdims=True)
            share_gate = jax.nn.sigmoid(
                jnp.sum(jnp.where(from_base == n_exp, logits, 0.0), axis=1, keepdims=True)
            )
        sigma = 0.5 * jnp.tanh(0.5 * gate) + 0.5
        silu = gate * sigma
        hidden = silu * up
        both = hidden * raw
        if b <= exp_units:
            factor = gate_here
            exp_sum += jnp.sum(both, axis=1, keepdims=True)
        elif a >= exp_units:
            factor = share_gate
            share_sum += jnp.sum(both, axis=1, keepdims=True)
        else:
            is_expert = lax.broadcasted_iota(jnp.int32, both.shape, 1) < exp_units - a
            factor = jnp.where(is_expert, gate_here, share_gate)
            part = jnp.sum(jnp.where(is_expert, both, 0.0), axis=1, keepdims=True)
            exp_sum += part
            share_sum += jnp.sum(both, axis=1, keepdims=True) - part
        grad_hidden = raw * factor
        units[0][:, a:b] = (grad_hidden * (sigma * up + hidden * (1.0 - sigma))).astype(bf16)
        units[1][:, a:b] = (grad_hidden * silu).astype(bf16)
        units[2][:, a:b] = (hidden * factor).astype(bf16)
    back = dot(units[0][...], w[0], 1, 0) + dot(units[1][...], w[1], 1, 0)
    extra = jnp.where(lane == seq, exp_sum * mark, jnp.where(lane == n_exp, share_sum, 0.0))
    return back.astype(bf16), extra.astype(bf16)


def mix_local_kernel(exp_units, base, n_exp, second, grad_ext, w_hbm, back, unit_out, w, sems):
    copies = [pltpu.make_async_copy(w_hbm.at[m], w.at[m], sems.at[m]) for m in range(3)]
    width = second.shape[1]

    @pl.when(pl.program_id(0) == 0)
    def _():
        for copy in copies:
            copy.start()
        for copy in copies:
            copy.wait()

    units = [unit_out.at[m] for m in range(3)]
    rows_back, extra = mix_rows(exp_units, base, n_exp, second[...], grad_ext, w, units)
    back[:, :width] = rows_back
    back[:, width:] = extra


def mix_local(second, grad_ext, full, exp_units, base, n_exp):
    rows, width = second.shape
    unit_rows = full.shape[1]
    wide = grad_ext.shape[1]
    return pl.pallas_call(
        functools.partial(mix_local_kernel, exp_units, base, n_exp),
        grid=(rows // TILE,),
        in_specs=[
            pl.BlockSpec((TILE, width), lambda i: (i, 0)),
            pl.BlockSpec((TILE, wide), lambda i: (i, 0)),
            pl.BlockSpec(memory_space=pl.ANY),
        ],
        out_specs=[
            pl.BlockSpec((TILE, wide), lambda i: (i, 0)),
            pl.BlockSpec((3, TILE, unit_rows), lambda i: (0, i, 0)),
        ],
        out_shape=[
            jax.ShapeDtypeStruct((rows, wide), bf16),
            jax.ShapeDtypeStruct((3, rows, unit_rows), bf16),
        ],
        scratch_shapes=[
            pltpu.VMEM((3, unit_rows, width), bf16),
            pltpu.SemaphoreType.DMA((3,)),
        ],
        compiler_params=pltpu.CompilerParams(vmem_limit_bytes=VMEM_BYTES),
        cost_estimate=pl.CostEstimate(
            flops=10 * rows * width * unit_rows,
            bytes_accessed=6 * unit_rows * width + 8 * rows * width,
            transcendentals=0,
        ),
        name="mix_local",
    )(second, grad_ext, full)


def mix_kernel(
    exp_units, base, n_exp, second, grad_ext, experts, share_own, share_far, rest, unit_out, back, down_out,
    w, held, core_in, home, e_sem, s_sem, r_sem, b_a, b_b, h_a, h_b, o_sem, d_sem,
):
    i = pl.program_id(0)
    _, near_y, near_core = plane_places()
    core = lax.axis_index("seq") % 2
    rows, width = second.shape[2:]
    at = [pl.ds(j * rows, rows) for j in range(2)]
    loads = [[], []]
    for m in range(3):
        for r, owner in enumerate(plane_owners()):
            size = experts.shape[3]
            start = pl.multiple_of(owner * size, size)
            loads[1].append(
                pltpu.make_async_copy(
                    experts.at[r, m], w.at[m, pl.ds(0, exp_units), pl.ds(start, size)], e_sem.at[m, r]
                )
            )
    share_rows, size = share_own.shape[2:]
    for r, share in enumerate((share_own, share_far)):
        for place in range(share.shape[0]):
            loads[0].append(
                pltpu.make_async_copy(
                    share.at[place],
                    w.at[
                        :,
                        pl.ds(exp_units + r * share_rows, share_rows),
                        pl.ds(place * size, size),
                    ],
                    s_sem.at[r, place],
                )
            )
    loads[0].append(
        pltpu.make_async_copy(rest, w.at[:, pl.ds(base, rest.shape[1])], r_sem)
    )
    keep = pltpu.make_async_copy(w.at[2], down_out, d_sem)
    back_c = [
        remote(held.at[j, 1 - core], core_in.at[j], b_a.at[j], b_b.at[j], seq=near_core)
        for j in range(2)
    ]
    back_y = [
        remote(held.at[j, core], home.at[j], h_a.at[j], h_b.at[j], head=near_y) for j in range(2)
    ]

    def wait_weights(m):
        @pl.when(i == 0)
        def _():
            for copy in loads[m]:
                copy.wait()

    @pl.when(i == 0)
    def _():
        for group in loads:
            for copy in group:
                copy.start()
        greet([{"head": near_y}, {"seq": near_core}])

    for c in range(2):
        units = [unit_out.at[m, 0, c] for m in range(3)]
        rows_back, extra = mix_rows(
            exp_units, base, n_exp, second[0, c], grad_ext.at[0, c], w, units,
            wait_weights if c == 0 else None,
        )
        held[i, c, :, :width] = rows_back
        held[i, c, :, width:] = extra
        if c == 0:
            for j in range(2):

                @pl.when(i == 1 + j)
                def _():
                    back_c[j].wait_recv()
                    held[j, core] = (held[j, core].astype(f32) + core_in[j].astype(f32)).astype(bf16)
                    back_y[j].start()

    for j in range(2):

        @pl.when(i == j)
        def _():
            back_c[j].start()
            if j == 0:
                keep.start()

    @pl.when(i == 3)
    def _():
        out = [
            [
                pltpu.make_async_copy(held.at[2 + j, c], back.at[c, at[j]], o_sem.at[j, k])
                for k, c in enumerate((1 - core, core))
            ]
            for j in range(2)
        ]
        for j in range(2):
            out[j][0].start()
        for j in range(2):
            back_y[j].wait_recv()
            held[2 + j, core] = (held[2 + j, core].astype(f32) + home[j].astype(f32)).astype(bf16)
            out[j][1].start()
        for j in range(2):
            out[j][0].wait()
            out[j][1].wait()
            back_c[j].wait_send()
            back_y[j].wait_send()
        keep.wait()


def mix(seconds, grads, experts, share_own, share_far, rest, exp_units, base, n_exp):
    rows, width = seconds.shape[1:]
    unit_rows = base + rest.shape[1]
    wide = grads.shape[2]
    half = rows // 2
    piece = half // 2
    anywhere = pl.BlockSpec(memory_space=pl.ANY)
    units, back, down_rows = pl.pallas_call(
        functools.partial(mix_kernel, exp_units, base, n_exp),
        grid=(4,),
        in_specs=[
            pl.BlockSpec((1, 2, piece, width), lambda i: (1 - i // 2, 0, i % 2, 0)),
            pl.BlockSpec((1, 2, piece, wide), lambda i: (1 - i // 2, 0, i % 2, 0)),
            anywhere,
            anywhere,
            anywhere,
            anywhere,
        ],
        out_specs=[
            pl.BlockSpec((3, 1, 2, piece, unit_rows), lambda i: (0, 1 - i // 2, 0, i % 2, 0)),
            anywhere,
            anywhere,
        ],
        out_shape=[
            jax.ShapeDtypeStruct((3, 2, 2, half, unit_rows), bf16),
            jax.ShapeDtypeStruct((2, half, wide), bf16),
            jax.ShapeDtypeStruct((unit_rows, width), bf16),
        ],
        scratch_shapes=[
            pltpu.VMEM((3, unit_rows, width), bf16),
            pltpu.VMEM((4, 2, piece, wide), bf16),
            pltpu.VMEM((2, piece, wide), bf16),
            pltpu.VMEM((2, piece, wide), bf16),
            pltpu.SemaphoreType.DMA((3, 4)),
            pltpu.SemaphoreType.DMA((2, share_own.shape[0])),
            pltpu.SemaphoreType.DMA,
            *[pltpu.SemaphoreType.DMA((2,))] * 4,
            pltpu.SemaphoreType.DMA((2, 2)),
            pltpu.SemaphoreType.DMA,
        ],
        compiler_params=pltpu.CompilerParams(
            collective_id=4, has_side_effects=True, vmem_limit_bytes=VMEM_BYTES
        ),
        cost_estimate=pl.CostEstimate(
            flops=20 * rows * width * unit_rows,
            bytes_accessed=6 * unit_rows * width + 16 * rows * width,
            transcendentals=0,
        ),
        name="mix",
    )(
        seconds.reshape(2, 2, half, width), grads.reshape(2, 2, half, wide), experts, share_own, share_far, rest
    )
    return units.reshape(3, 2, rows, unit_rows), back.reshape(rows, wide), down_rows


def unit_grads_kernel(count, exp_units, share_rows, at, *refs):
    units, seconds, grads = refs[:count], refs[count : 2 * count], refs[2 * count : 3 * count]
    experts, share_own, share_far = refs[3 * count :]
    m = pl.program_id(0)

    def run(rights):
        acc = dot(units[0][...], rights[0][...], 0, 0)
        for left, right in zip(units[1:], rights[1:]):
            acc += dot(left[...], right[...], 0, 0)
        experts[0, 0] = acc[:exp_units].astype(bf16)
        size = share_own.shape[3]
        for s in range(share_own.shape[0]):
            piece = acc[exp_units : exp_units + 2 * share_rows, s * size : (s + 1) * size].astype(bf16)
            share_own[s, 0] = piece[:share_rows]
            share_far[s, 0] = piece[share_rows:]

    @pl.when(m < 2)
    def _():
        run(seconds)

    @pl.when(m == 2)
    def _():
        run(grads)


def unit_grads(at, units, seconds, grads, exp_units, share_rows):
    n_head, n_seq = lax.axis_size("head"), lax.axis_size("seq")
    width = seconds[0][0].shape[2]
    unit_rows = units[0][0].shape[3]
    head_part, seq_part = width // n_head, width // n_seq
    near = n_seq // n_head
    rows = sum(block.shape[1] for block, _ in seconds)

    def far(r, at):
        return jnp.bitwise_xor(at[0], r)

    def place(q, m, r, at):
        return (m, q, 0, 0)

    def second_place(q, m, r, at):
        return (q, 0, jnp.where(m < 2, far(r, at), far(n_head - 1, at)))

    def grad_place(q, m, r, at):
        return (q, 0, jnp.where(m < 2, far(0, at), far(r, at)))

    in_specs = [
        pl.BlockSpec((None, None, block.shape[2], unit_rows), functools.partial(place, q))
        for block, q in units
    ]
    in_specs += [
        pl.BlockSpec((None, block.shape[1], head_part), functools.partial(second_place, q))
        for block, q in seconds
    ]
    in_specs += [
        pl.BlockSpec((None, block.shape[1], head_part), functools.partial(grad_place, q))
        for block, q in grads
    ]
    share_spec = pl.BlockSpec((near, 1, share_rows, seq_part), lambda m, r, at: (far(r, at), m, 0, 0))
    share_shape = jax.ShapeDtypeStruct((n_seq, 3, share_rows, seq_part), bf16)
    return pl.pallas_call(
        functools.partial(unit_grads_kernel, len(units), exp_units, share_rows),
        grid_spec=pltpu.PrefetchScalarGridSpec(
            num_scalar_prefetch=1,
            grid=(3, n_head),
            in_specs=in_specs,
            out_specs=[
                pl.BlockSpec((1, 1, exp_units, head_part), lambda m, r, at: (r, m, 0, 0)),
                share_spec,
                share_spec,
            ],
        ),
        out_shape=[
            jax.ShapeDtypeStruct((n_head, 3, exp_units, head_part), bf16),
            share_shape,
            share_shape,
        ],
        compiler_params=pltpu.CompilerParams(vmem_limit_bytes=VMEM_BYTES),
        cost_estimate=pl.CostEstimate(
            flops=6 * rows * width * unit_rows,
            bytes_accessed=6 * rows * unit_rows + 8 * rows * width + 6 * width * unit_rows,
            transcendentals=0,
        ),
        name="unit_grads",
    )(at, *(block for block, _ in units + seconds + grads))


def products_kernel(
    units, seconds, grads, down_rows, out, experts, expert_in_down, share_all,
    u, sides, right, far_half, column, core_in, home, share, share_in, stage,
    u_sem, r_sem, d_sem, c_a, c_b, y_a, y_b, x_a, x_b, z_a, z_b, e_sem, o_sem,
):
    seq, n_seq = lax.axis_index("seq"), lax.axis_size("seq")
    near_x, near_y, near_core = plane_places()
    core = seq % 2
    width = right.shape[2]
    rows = column.shape[0]
    piece = rows // 2
    exp_units = experts.shape[2]
    share_rows, seq_part = share_all.shape[2:]
    head_part = experts.shape[3]
    n_head = width // head_part
    edge = exp_units // LANES * LANES
    tail = exp_units - edge
    slot = {2: 1, 0: 2, 1: 0}

    def load_units(m):
        return [
            pltpu.make_async_copy(
                units.at[m, q], u.at[pl.ds(q * 2 * rows, 2 * rows)], u_sem.at[m, q]
            )
            for q in range(2)
        ]

    def load_right(k):
        source = grads if k else seconds
        return [
            pltpu.make_async_copy(
                source.at[q, :, pl.ds(f * head_part, head_part)],
                right.at[k, pl.ds(q * 2 * rows, 2 * rows), pl.ds(f * head_part, head_part)],
                r_sem.at[k, q, f],
            )
            for q in range(2)
            for f in range(n_head)
        ]

    down = sides.at[0]
    load_down = pltpu.make_async_copy(down_rows, down, d_sem)
    rights = [load_right(0), load_right(1)]
    first = load_units(2)
    first[1].start()
    load_down.start()
    first[0].start()
    for copy in rights[1] + rights[0]:
        copy.start()
    greet(
        [{"head": near_x}, {"head": near_y}] + [{"seq": (seq + k) % n_seq} for k in range(1, n_seq)]
    )

    pieces = [pl.ds(j * piece, piece) for j in range(2)]
    to_core = [
        remote(far_half.at[0, at], core_in.at[at], c_a.at[j], c_b.at[j], seq=near_core)
        for j, at in enumerate(pieces)
    ]
    to_y = [
        remote(far_half.at[1, at], home.at[at], y_a.at[j], y_b.at[j], head=near_y)
        for j, at in enumerate(pieces)
    ]
    to_x = [
        remote(share.at[1, :, m], share_in.at[:, m], x_a.at[m], x_b.at[m], head=near_x)
        for m in range(3)
    ]
    cross = remote(experts.at[3, 2], expert_in_down, x_a.at[3], x_b.at[3], head=near_x)
    spread_out = [[] for _ in range(3)]
    spread_in = []
    spread_own = []
    for m in range(3):
        for k in range(1, n_seq):
            to, source = (seq + k) % n_seq, (seq + n_seq - k) % n_seq
            spread_out[m].append(
                remote(
                    share.at[0, to, m], share_all.at[seq, m], z_a.at[m, k], z_b.at[m, k], seq=to
                )
            )
            block = share_all.at[source, m]
            spread_in.append(remote(block, block, z_a.at[m, k], z_b.at[m, k], seq=to))
        spread_own.append(
            pltpu.make_async_copy(share.at[0, seq, m], share_all.at[seq, m], z_a.at[m, 0])
        )

    def spread_share(m):
        to_x[m].wait_recv()
        for place in range(n_seq):
            total = share[0, place, m].astype(f32) + share_in[place, m].astype(f32)
            share[0, place, m] = total.astype(bf16)
        for copy in spread_out[m]:
            copy.start()
        spread_own[m].start()

    def out_rows(start):
        return dot(u[pl.ds(pl.multiple_of(start, 16), piece), :], down[...], 1, 0)

    def turn_units(m):
        block = 2 * piece
        for k in range(u.shape[0] // block):
            at = slice(k * block, (k + 1) * block)
            sides[slot[m], :, at] = u[at, :].T

    def share_part(m):
        for f in range(n_head):
            for copy in rights[1 if m == 2 else 0][f::n_head] if m < 3 else []:
                if m != 1:
                    copy.wait()
            block = right[1 if m == 2 else 0, :, f * head_part : (f + 1) * head_part]
            acc = dot(sides[slot[m], edge:], block, 1, 0)
            for b in range(head_part // seq_part):
                part = acc[tail : tail + 2 * share_rows, b * seq_part : (b + 1) * seq_part]
                place = f * (head_part // seq_part) + b
                share[0, place, m] = part[:share_rows].astype(bf16)
                share[1, place, m] = part[share_rows:].astype(bf16)
        to_x[m].start()

    owners = plane_owners()
    writes = []

    def expert_part(r, m):
        n = len(writes)
        if n >= 2:
            writes[n - 2].wait()
        start = pl.multiple_of(owners[r] * head_part, head_part)
        acc = dot(
            sides[slot[m], :exp_units],
            right[1 if m == 2 else 0, :, pl.ds(start, head_part)],
            1,
            0,
        )
        stage[n % 2] = acc.astype(bf16)
        writes.append(pltpu.make_async_copy(stage.at[n % 2], experts.at[r, m], e_sem.at[n % 2]))
        writes[-1].start()

    def pass_on(j):
        to_core[j].wait_recv()
        total = far_half[1, pieces[j]].astype(f32) + core_in[pieces[j]].astype(f32)
        far_half[1, pieces[j]] = total.astype(bf16)
        to_y[j].start()

    first[1].wait()
    load_down.wait()
    for k, half in ((0, 1 - core), (1, core)):
        for j in range(2):
            far_half[k, pieces[j]] = out_rows(2 * rows + half * rows + j * piece).astype(bf16)
            if k == 0:
                to_core[j].start()
            else:
                pass_on(j)
    first[0].wait()
    turn_units(2)
    share_part(2)
    for copy in to_core:
        copy.wait_send()
    for j in range(2):
        far_half[0, pieces[j]] = out_rows((1 - core) * rows + j * piece).astype(bf16)
    write = [
        pltpu.make_async_copy(far_half.at[0], out.at[1 - core], o_sem.at[0]),
        pltpu.make_async_copy(column, out.at[core], o_sem.at[1]),
    ]
    write[0].start()
    for j in range(2):
        column[pieces[j]] = out_rows(core * rows + j * piece).astype(bf16)
    for i, m in enumerate((0, 1)):
        load = load_units(m)
        for copy in load:
            copy.start()
        expert_part(3, 0 if i else 2)
        for copy in load:
            copy.wait()
        turn_units(m)
        share_part(m)
        spread_share(0 if i else 2)
    expert_part(3, 1)
    cross.start()
    for m in (2, 0, 1):
        expert_part(1, m)
    for m in (2, 0, 1):
        expert_part(2, m)
    spread_share(1)
    for m in (2, 0, 1):
        expert_part(0, m)

    for j in range(2):
        to_y[j].wait_recv()
        column[pieces[j]] = (column[pieces[j]].astype(f32) + home[pieces[j]].astype(f32)).astype(bf16)
    write[1].start()
    for copy in to_x + to_y:
        copy.wait_send()
    cross.wait()
    for group in spread_out:
        for copy in group:
            copy.wait_send()
    for copy in spread_in:
        copy.wait_recv()
    for copy in writes[-2:] + write + spread_own:
        copy.wait()


def products(units, seconds, grads, down_rows, exp_units, share_rows):
    n_head, n_seq = lax.axis_size("head"), lax.axis_size("seq")
    _, rows, width = seconds.shape
    unit_rows = units.shape[3]
    half = rows // 2
    head_part, seq_part = width // n_head, width // n_seq
    anywhere = pl.BlockSpec(memory_space=pl.ANY)
    dma = pltpu.SemaphoreType.DMA
    share_shape = (n_seq, 3, share_rows, seq_part)
    return pl.pallas_call(
        products_kernel,
        in_specs=[anywhere] * 4,
        out_specs=[anywhere] * 4,
        out_shape=[
            jax.ShapeDtypeStruct((2, half, width), bf16),
            jax.ShapeDtypeStruct((n_head, 3, exp_units, head_part), bf16),
            jax.ShapeDtypeStruct((exp_units, head_part), bf16),
            jax.ShapeDtypeStruct(share_shape, bf16),
        ],
        scratch_shapes=[
            pltpu.VMEM((2 * rows, unit_rows), bf16),
            pltpu.VMEM((3, unit_rows, 2 * rows), bf16),
            pltpu.VMEM((2, 2 * rows, width), bf16),
            pltpu.VMEM((2, half, width), bf16),
            pltpu.VMEM((half, width), bf16),
            pltpu.VMEM((half, width), bf16),
            pltpu.VMEM((half, width), bf16),
            pltpu.VMEM((2, *share_shape), bf16),
            pltpu.VMEM(share_shape, bf16),
            pltpu.VMEM((2, exp_units, head_part), bf16),
            dma((3, 2)),
            dma((2, 2, n_head)),
            dma,
            *[dma((2,))] * 4,
            *[dma((4,))] * 2,
            *[dma((3, n_seq))] * 2,
            *[dma((2,))] * 2,
        ],
        compiler_params=pltpu.CompilerParams(
            collective_id=5, has_side_effects=True, vmem_limit_bytes=VMEM_BYTES
        ),
        cost_estimate=pl.CostEstimate(
            flops=16 * rows * width * unit_rows,
            bytes_accessed=40 * rows * width,
            transcendentals=0,
        ),
        name="products",
    )(units, seconds, grads, down_rows)


def finish_kernel(
    experts, expert_in, expert_in_down, share_all, partial, grad_middle, tokens, gain, small,
    grad_up, grad_down, grad_share_up, grad_share_down, input_grad, totals,
    near, far, far_in, near_in, last_in, pack, share_pack, incoming, slots,
    l_sem, x_a, x_b, y_a, y_b, s_a, s_b, t_a, t_b, p_sem,
):
    seq, head = lax.axis_index("seq"), lax.axis_index("head")
    near_x, near_y, near_core = plane_places()
    peers = ring_places()
    y = head // 2
    rows, width = grad_middle.shape
    units = near.shape[1]
    share_rows = share_all.shape[2]
    hidden = pack.shape[1]
    steps = [{"seq": near_core}]
    for bit in (2, 4):
        steps.append({"seq": seq + bit - 2 * bit * ((seq // bit) % 2)})
    steps += [{"head": near_x}, {"head": near_y}]

    loads = [
        [pltpu.make_async_copy(experts.at[2, m], far.at[m], l_sem.at[m]) for m in range(3)],
        [
            pltpu.make_async_copy(block, far_in.at[k], l_sem.at[3 + k])
            for k, block in enumerate((expert_in, expert_in_down))
        ],
        [pltpu.make_async_copy(experts.at[0, m], near.at[m], l_sem.at[5 + m]) for m in range(3)],
    ]
    for group in loads:
        for copy in group:
            copy.start()
    share_loads = [
        pltpu.make_async_copy(
            share_all.at[i], share_pack.at[:, pl.ds(i * share_rows, share_rows)], p_sem.at[i]
        )
        for i in range(share_all.shape[0])
    ]
    for copy in share_loads:
        copy.start()
    greet(steps + [{"head": peers[2] + 1 - 2 * (head % 2)}])
    scatter = [
        remote(
            partial.at[pl.ds(r * rows, rows)], incoming.at[r - 1], s_a.at[r - 1], s_b.at[r - 1],
            head=peers[r],
        )
        for r in range(1, len(peers))
    ]
    last = remote(experts.at[3, 1], last_in, x_a.at[3], x_b.at[3], head=near_x)
    sides = [
        remote(experts.at[1, m], near_in.at[m], x_a.at[m], x_b.at[m], head=near_x) for m in range(3)
    ]
    for copy in scatter + [last, sides[0]]:
        copy.start()
    here = pl.ds(pl.multiple_of(y * units, 16), units)
    there = pl.ds(pl.multiple_of((1 - y) * units, 16), units)
    across = [
        remote(far.at[m], pack.at[m, here], y_a.at[m], y_b.at[m], head=near_y) for m in range(3)
    ]
    across_in = [
        remote(far.at[m], pack.at[m, there], y_a.at[m], y_b.at[m], head=near_y) for m in range(3)
    ]
    for k, m in enumerate((0, 2)):
        loads[0][m].wait()
        loads[1][k].wait()
        far[m] = (far[m].astype(f32) + far_in[k].astype(f32)).astype(bf16)
        across[m].start()
    loads[0][1].wait()
    for copy in loads[2]:
        copy.wait()

    for copy in scatter:
        copy.wait_recv()
    total = partial[:rows].astype(f32)
    for r in range(len(peers) - 1):
        total += incoming[r].astype(f32)
    x = tokens[...].astype(f32)
    inverse = lax.rsqrt(jnp.mean(x * x, axis=1, keepdims=True) + EPS)
    normed = x * inverse
    slots[0] = small[...]
    slots[0, 10:11] = jnp.sum(total * normed, axis=0, keepdims=True)
    grad_normed = total * gain[...]
    mean = jnp.mean(grad_normed * normed, axis=1, keepdims=True)
    input_grad[...] = grad_middle[...] + inverse * (grad_normed - normed * mean)

    exchanges = [
        remote(slots.at[2 * k], slots.at[2 * k + 1], t_a.at[k], t_b.at[k], **place)
        for k, place in enumerate(steps)
    ]

    def exchange(k):
        exchanges[k].wait_recv()
        slots[2 * k + 2] = slots[2 * k] + slots[2 * k + 1]
        if k + 1 < len(steps):
            exchanges[k + 1].start()

    exchanges[0].start()

    for copy in share_loads:
        copy.wait()
    grad_share_down[...] = share_pack[2]
    exchange(0)
    grad_share_up[:, :hidden] = share_pack[0].T
    exchange(1)
    grad_share_up[:, hidden:] = share_pack[1].T
    last.wait_recv()
    far[1] = (far[1].astype(f32) + last_in[...].astype(f32)).astype(bf16)
    across[1].start()
    exchange(2)
    for copy in sides[1:]:
        copy.start()

    def place_block(m):
        sides[m].wait_recv()
        pack[m, here] = (near[m].astype(f32) + near_in[m].astype(f32)).astype(bf16)
        across_in[m].wait_recv()
        if m < 2:
            grad_up[:, m * hidden : (m + 1) * hidden] = pack[m].T
        else:
            grad_down[...] = pack[m]

    place_block(0)
    exchange(3)
    place_block(1)
    exchange(4)
    totals[...] = slots[2 * len(steps)]
    place_block(2)
    for copy in scatter + exchanges + sides + across + [last]:
        copy.wait_send()


def finish(experts, expert_in, expert_in_down, share_all, partial, grad_middle, tokens, gain, small):
    n_head, n_seq = lax.axis_size("head"), lax.axis_size("seq")
    rows, width = tokens.shape
    _, _, units, head_part = experts.shape
    share_rows, seq_part = share_all.shape[2:]
    hidden, share_units = 2 * units, n_seq * share_rows
    anywhere = pl.BlockSpec(memory_space=pl.ANY)
    vmem = pl.BlockSpec(memory_space=pltpu.VMEM)
    dma = pltpu.SemaphoreType.DMA
    return pl.pallas_call(
        finish_kernel,
        in_specs=[anywhere] * 4 + [vmem] * 5,
        out_specs=[vmem] * 6,
        out_shape=[
            jax.ShapeDtypeStruct((head_part, 2 * hidden), bf16),
            jax.ShapeDtypeStruct((hidden, head_part), bf16),
            jax.ShapeDtypeStruct((seq_part, 2 * share_units), bf16),
            jax.ShapeDtypeStruct((share_units, seq_part), bf16),
            jax.ShapeDtypeStruct((rows, width), f32),
            jax.ShapeDtypeStruct(small.shape, f32),
        ],
        scratch_shapes=[
            pltpu.VMEM((3, units, head_part), bf16),
            pltpu.VMEM((3, units, head_part), bf16),
            pltpu.VMEM((2, units, head_part), bf16),
            pltpu.VMEM((3, units, head_part), bf16),
            pltpu.VMEM((units, head_part), bf16),
            pltpu.VMEM((3, hidden, head_part), bf16),
            pltpu.VMEM((3, share_units, seq_part), bf16),
            pltpu.VMEM((n_head - 1, rows, width), bf16),
            pltpu.VMEM((11, *small.shape), f32),
            dma((8,)),
            *[dma((4,))] * 2,
            *[dma((3,))] * 2,
            *[dma((n_head - 1,))] * 2,
            *[dma((5,))] * 2,
            dma((n_seq,)),
        ],
        compiler_params=pltpu.CompilerParams(
            collective_id=6, has_side_effects=True, vmem_limit_bytes=VMEM_BYTES
        ),
        cost_estimate=pl.CostEstimate(flops=0, bytes_accessed=1 << 27, transcendentals=0),
        name="finish",
    )(experts, expert_in, expert_in_down, share_all, partial, grad_middle, tokens, gain, small)


def after(value, *others):
    return lax.optimization_barrier((value, *others))[0]


def shards(
    tokens,
    cotangent,
    arrange,
    doc_lengths,
    routes,
    norm1_gain,
    qkv_weight,
    qkv_bias,
    out_weight,
    norm2_gain,
    router_weight,
    shared_gate_vec,
    shared_gate_up,
    shared_down,
    expert_gate_up,
    expert_down,
):
    highest = lax.Precision.HIGHEST
    tok_rows, width = tokens.shape
    n_seq = lax.axis_size("seq")
    n_head = lax.axis_size("head")
    seq = lax.axis_index("seq")
    head = lax.axis_index("head")
    group_tok = tok_rows * n_head
    heads_here = qkv_weight.shape[1]
    n_exp = router_weight.shape[1]
    hidden_all = expert_down.shape[1]
    parts = n_head // 2
    part = mesh_part()
    exp_units = hidden_all // parts
    share_all = shared_down.shape[0]
    share_units = share_all // n_seq
    share_rows = -(-share_units // 16) * 16
    base = exp_units + 2 * share_rows
    unit_rows = -(-(base + n_exp + 1) // LANES) * LANES
    seq_part = width // n_seq
    head_part = width // n_head

    wide = heads_here * HD
    plane = parts == 2 and n_seq == 8 and 2 * n_seq * tok_rows == width
    expert_up = expert_gate_up[0]
    at = jnp.stack([head, seq]).astype(jnp.int32)
    gate_rows = jnp.concatenate([router_weight.T, shared_gate_vec[None, :]], axis=0)
    rest = jnp.zeros((3, unit_rows - base, width), bf16).at[0, : n_exp + 1].set(gate_rows)

    place, doc_index, position = layout_of(arrange[0], doc_lengths[0], group_tok)
    blocks = (head + jnp.arange(n_head, dtype=jnp.int32)) % n_head
    table = jnp.stack([place, doc_index, position]).reshape(3, n_head, tok_rows)
    place, doc_index, position = jnp.take(table, blocks, axis=1).reshape(3, group_tok)
    layout_row = jnp.stack([doc_index, place])
    layout_col = layout_row.T
    cosine, sine = rope_tables(position.astype(f32))
    cosine = jnp.concatenate([cosine, cosine], axis=1)
    sine = jnp.concatenate([-sine, sine], axis=1)
    bias_here = lax.dynamic_slice_in_dim(qkv_bias, head * heads_here, heads_here, 0)
    bias_here = bias_here.astype(f32)[:, None, :]

    expert_ids = jnp.arange(n_exp, dtype=jnp.int32)
    chosen = jnp.any(routes[:, :, None] == expert_ids[None, None, :], axis=1)
    marks = jnp.concatenate(
        [chosen.astype(bf16), jnp.zeros((tok_rows, LANES - n_exp), bf16)], axis=1
    )
    grad_ext = jnp.concatenate([cotangent, marks], axis=1)

    stream = tokens.astype(f32)
    gain_first = norm1_gain.astype(f32)
    scale_first = rms_scale(stream)
    normed_first = stream * scale_first
    gain_second = norm2_gain.astype(f32)
    weight_own = qkv_weight.reshape(seq_part, 3 * wide)
    if plane:
        (
            first_group, weight, wout, experts, share_own, share_far, grad_both, seconds,
            qkv, merged, log_total, middle, lowered_second,
        ) = forward(
            tokens, gain_first[None, :], gain_second[None, :], weight_own, out_weight, expert_up,
            expert_down[0], shared_gate_up.reshape(seq_part, 2 * share_all), shared_down, grad_ext,
            bias_here, cosine, sine, layout_col, layout_row,
        )
        grad_both = grad_both.reshape(2, n_seq * tok_rows, width + LANES)
        seconds = seconds.reshape(2, n_seq * tok_rows, width)
        units, back_column, down_rows = mix(
            seconds, grad_both, experts, share_own, share_far, rest, exp_units, base, n_exp
        )
        out_column, grad_experts, expert_in_down, share_parts = products(
            units, seconds, grad_both, down_rows, exp_units, share_rows
        )
        back_own = lax.psum_scatter(back_column, "seq", scatter_dimension=0, tiled=True)
    else:
        weight = lax.all_gather(weight_own, "seq", axis=0, tiled=True)
        wout = lax.all_gather(out_weight, "seq", axis=0)
        first_group = group_gather((normed_first * gain_first).astype(bf16))
        send = jnp.stack([expert_up[:, :hidden_all].T, expert_up[:, hidden_all:].T, expert_down[0]])
        near = []
        for t in range(parts):
            there = jnp.bitwise_xor(part, t)
            block = lax.dynamic_slice_in_dim(send, there * exp_units, exp_units, 1)
            near.append(swap(block, "head", 2 * t) if t else block)
        experts = jnp.stack([block for own in near for block in (own, swap(own, "head", 1))])
        send = jnp.stack([shared_gate_up[:, 0].T, shared_gate_up[:, 1].T, shared_down])
        send = jnp.transpose(send.reshape(3, n_seq, share_units, seq_part), (1, 0, 2, 3))
        if share_rows > share_units:
            send = jnp.pad(send, ((0, 0), (0, 0), (0, share_rows - share_units), (0, 0)))
        share_own = lax.all_to_all(send, "seq", split_axis=0, concat_axis=0)
        full = pack(at, experts, [share_own, swap(share_own, "head", 1)], rest, unit_rows)
        qkv, merged, log_total, middle, lowered_second = attend(
            first_group, weight, wout, bias_here, cosine, sine, layout_col, layout_row, tokens,
            gain_second[None, :],
        )
        grad_chunks = token_gather(grad_ext)
        second_chunks = token_gather(lowered_second)
        back_chunks = []
        unit_chunks = []
        for second, grad in zip(second_chunks, grad_chunks):
            back, units = mix_local(second, grad, full, exp_units, base, n_exp)
            back_chunks.append(back)
            unit_chunks.append(units)
        grad_experts, grad_share, grad_share_far = unit_grads(
            at,
            [(units[:, None], 0) for units in unit_chunks],
            [(second[None], 0) for second in second_chunks],
            [(grad[None], 0) for grad in grad_chunks],
            exp_units,
            share_rows,
        )
        out_chunks = [dot(units[2], full[2], 1, 0).astype(bf16) for units in unit_chunks]
        back_own = token_scatter(back_chunks)
        out_own = token_scatter(out_chunks)
    scale_second = rms_scale(middle)
    normed_second = middle * scale_second

    back_own = after(back_own, grad_experts).astype(f32)

    logits = dot(lowered_second, gate_rows, 1, 1)
    probs = jax.nn.softmax(logits[:, :n_exp], axis=-1)
    share_gate = jax.nn.sigmoid(logits[:, n_exp:])
    grad_probs = back_own[:, width : width + n_exp]
    grad_logits = probs * (grad_probs - jnp.sum(probs * grad_probs, axis=1, keepdims=True))
    grad_gate_logit = (
        back_own[:, width + n_exp : width + n_exp + 1] * share_gate * (1.0 - share_gate)
    )
    grad_gates = jnp.concatenate([grad_logits, grad_gate_logit], axis=1)
    grad_second = back_own[:, :width] + jnp.dot(
        grad_gates, gate_rows.astype(f32), precision=highest
    )
    grad_gate_cols = jnp.dot(grad_gates.T, lowered_second.astype(f32), precision=highest)
    grad_gain_second = jnp.sum(grad_second * normed_second, axis=0)
    grad_normed = grad_second * gain_second
    grad_middle = cotangent.astype(f32) + scale_second * (
        grad_normed - normed_second * jnp.mean(grad_normed * normed_second, axis=1, keepdims=True)
    )
    grad_attn = grad_middle.astype(bf16)
    if plane:
        out_own = lax.psum_scatter(
            after(out_column, grad_attn).reshape(n_seq * tok_rows, width),
            "seq",
            scatter_dimension=0,
            tiled=True,
        )
    mixed = (middle + out_own.astype(f32)).astype(bf16)
    back_args = (
        grad_attn, first_group, weight, wout, qkv, merged, log_total, cosine, sine, layout_col, layout_row
    )
    if plane:
        grad_first, grad_weight, grad_bias_here, expert_in = attend_back(
            *back_args, extra=(grad_experts,)
        )
    else:
        grad_first, grad_weight, grad_bias_here = attend_back(*back_args)
    grad_weight = lax.psum_scatter(grad_weight, "seq", scatter_dimension=0, tiled=False)
    grad_bias = lax.dynamic_update_slice_in_dim(
        jnp.zeros(qkv_bias.shape, f32), grad_bias_here[:, 0], head * heads_here, 0
    )
    small = jnp.concatenate(
        [grad_gate_cols, grad_gain_second[None, :], jnp.zeros((1, width), f32), grad_bias.reshape(-1, width)],
        axis=0,
    )
    if plane:
        small = jnp.pad(small, ((0, 16 - small.shape[0]), (0, 0)))
        own_up, own_down, grad_share_up, grad_share_down, input_grad, totals = finish(
            grad_experts, expert_in, expert_in_down, share_parts, grad_first, grad_middle, tokens, gain_first[None, :],
            small,
        )
    else:
        grad_first = group_scatter(grad_first)
        small = small.at[n_exp + 2].set(jnp.sum(grad_first * normed_first, axis=0))
        grad_normed_first = grad_first * gain_first
        input_grad = grad_middle + scale_first * (
            grad_normed_first
            - normed_first * jnp.mean(grad_normed_first * normed_first, axis=1, keepdims=True)
        )
        totals = total_over_all(small)
        grad_share = grad_share + swap(grad_share_far, "head", 1)
        grad_share = lax.all_to_all(grad_share[:, :, :share_units], "seq", split_axis=0, concat_axis=0)
        grad_share = jnp.transpose(grad_share, (1, 0, 2, 3)).reshape(3, share_all, seq_part)
        own = {}
        for t in range(parts)[::-1]:
            total = grad_experts[2 * t] + swap(grad_experts[2 * t + 1], "head", 1)
            own[t] = swap(total, "head", 2 * t) if t else total
        own = jnp.stack([own[t] for t in range(parts)])
        own = jnp.take(own, jnp.bitwise_xor(part, jnp.arange(parts, dtype=jnp.int32)), axis=0)
        own = jnp.transpose(own, (1, 0, 2, 3)).reshape(3, hidden_all, head_part)
        own_up, own_down = jnp.concatenate([own[0].T, own[1].T], axis=1), own[2]
        grad_share_up = jnp.concatenate([grad_share[0].T, grad_share[1].T], axis=1)
        grad_share_down = grad_share[2]
    return (
        mixed,
        input_grad,
        totals[n_exp + 2],
        grad_weight[: 3 * wide].astype(f32).T.reshape(qkv_weight.shape),
        totals[n_exp + 3 : n_exp + 3 + 3].reshape(qkv_bias.shape),
        grad_weight[3 * wide :].astype(f32),
        totals[n_exp + 1],
        totals[:n_exp].T,
        totals[n_exp],
        grad_share_up.reshape(shared_gate_up.shape).astype(f32),
        grad_share_down.astype(f32),
        own_up.astype(f32)[None],
        own_down.astype(f32)[None],
    )


def solution(mesh):
    return jax.shard_map(
        shards,
        mesh=mesh,
        in_specs=(
            P(("seq", "head"), None),
            P(("seq", "head"), None),
            P("seq", None),
            P("seq", None),
            P(("seq", "head"), None),
            P(),
            P("seq", "head", None),
            P(),
            P("head", "seq"),
            P(),
            P(),
            P(),
            P("seq", None, "head"),
            P("head", "seq"),
            P("seq", "head", None),
            P("seq", None, "head"),
        ),
        out_specs=(
            P(("seq", "head"), None),
            P(("seq", "head"), None),
            P(),
            P("seq", "head", None),
            P(),
            P("head", "seq"),
            P(),
            P(),
            P(),
            P("seq", None, "head"),
            P("head", "seq"),
            P("seq", "head", None),
            P("seq", None, "head"),
        ),
        check_vma=False,
    )
```

```python
import functools

import jax
import jax.numpy as jnp
from jax import lax
from jax.experimental import pallas as pl
from jax.experimental.pallas import tpu as pltpu
from jax.sharding import PartitionSpec as P

HD = 128
EPS = 1e-06
THETA = 1000000.0
NEGATIVE = -1e30
LANES = 128
TILE = 256
MESH = pl.DeviceIdType.MESH
VMEM_BYTES = 61 * 1024 * 1024
bf16 = jnp.bfloat16
f32 = jnp.float32


def rms_scale(values):
    return lax.rsqrt(jnp.mean(values * values, axis=-1, keepdims=True) + EPS)


def rope_tables(position):
    half = HD // 2
    exponent = jnp.arange(half, dtype=f32) * (2.0 / HD)
    frequency = THETA ** (-exponent)
    angle = position[:, None] * frequency[None, :]
    return (jnp.cos(angle), jnp.sin(angle))


def layout_of(arrange_row, length_row, group_tok):
    counter = jnp.arange(group_tok, dtype=jnp.int32)
    place = jnp.sum(
        jnp.where(arrange_row[None, :] == counter[:, None], counter[None, :], 0),
        axis=1,
        dtype=jnp.int32,
    )
    doc_index = jnp.zeros_like(place)
    start = jnp.zeros_like(place)
    end = jnp.int32(0)
    for k in range(length_row.shape[0]):
        end = end + length_row[k]
        doc_index += (place >= end).astype(jnp.int32)
        start += jnp.where(place >= end, length_row[k], 0)
    return (place, doc_index, place - start)


def dot(left, right, left_dim, right_dim):
    return lax.dot_general(
        left, right, (((left_dim,), (right_dim,)), ((), ())), preferred_element_type=f32
    )


def swap(block, axis, bit):
    size = lax.axis_size(axis)
    return lax.ppermute(block, axis, [(i, i ^ bit) for i in range(size)])


def bits_of(size):
    bits = []
    bit = 1
    while bit < size:
        bits.append(bit)
        bit *= 2
    return bits


def spread(block, order):
    found = {0: block}
    for bit in order:
        for near in sorted(found):
            found[near ^ bit] = swap(found[near], "head", bit)
    return found


def collect(parts, order):
    parts = dict(parts)
    for bit in reversed(order):
        for far in sorted((r for r in parts if r & bit), reverse=True):
            parts[far ^ bit] = parts[far ^ bit] + swap(parts.pop(far), "head", bit)
    return parts[0]


def shift(block, axis, step):
    size = lax.axis_size(axis)
    return lax.ppermute(block, axis, [((i + step) % size, i) for i in range(size)])


def group_gather(block):
    size = lax.axis_size("head")
    return jnp.concatenate([block] + [shift(block, "head", r) for r in range(1, size)], axis=0)


def group_scatter(block):
    size = lax.axis_size("head")
    rows = block.shape[0] // size
    total = block[:rows].astype(f32)
    for r in range(1, size):
        total += shift(block[r * rows : (r + 1) * rows], "head", size - r).astype(f32)
    return total


def remote(src, dst, send_sem, recv_sem, **place):
    return pltpu.make_async_remote_copy(
        src_ref=src,
        dst_ref=dst,
        send_sem=send_sem,
        recv_sem=recv_sem,
        device_id=place,
        device_id_type=MESH,
    )


def greet(places):
    barrier = pltpu.get_barrier_semaphore()
    for place in places:
        pl.semaphore_signal(barrier, inc=1, device_id=place, device_id_type=MESH)
    pl.semaphore_wait(barrier, len(places))


def plane_places():
    head, seq = lax.axis_index("head"), lax.axis_index("seq")
    x, y = head % 2, head // 2
    return y * 2 + (1 - x), (1 - y) * 2 + x, seq + 1 - 2 * (seq % 2)


def plane_owners():
    head = lax.axis_index("head")
    near_x, near_y, _ = plane_places()
    return head, near_x, near_y, near_y + 1 - 2 * (head % 2)


def ring_places():
    size = lax.axis_size("head")
    head = lax.axis_index("head")
    return [(head + r) % size for r in range(size)]


class Line:
    def __init__(self, place, far, sems):
        self.seq = lax.axis_index("seq")
        self.count = lax.axis_size("seq") // 2
        self.depth = self.count - 1
        self.z = self.seq // 2
        _, self.near_y, self.near_core = plane_places()
        self.place, self.far = place, far
        self.sems = sems

    def index(self, j):
        if j == 0:
            return self.seq
        if j <= self.depth:
            return self.seq - 2 * j
        return self.seq + 2 * (j - self.depth)

    def valid(self, j):
        if j == 0:
            return self.z >= 0
        if j <= self.depth:
            return self.z - j >= 0
        return self.z + (j - self.depth) < self.count

    def line_copy(self, j, up):
        block = self.place(self.index(j))
        if up:
            to, k = self.seq + 2, j
        else:
            to, k = self.seq - 2, self.depth + (j - self.depth if j else 0)
        return remote(block, block, self.sems.at[0, k], self.sems.at[1, k], seq=to)

    def line_arrival(self, j):
        block = self.place(self.index(j))
        return remote(
            block, block, self.sems.at[0, j - 1], self.sems.at[1, j - 1], seq=self.near_core
        )

    def core_copy(self, j):
        block = self.place(self.index(j))
        return remote(block, block, self.sems.at[2, j], self.sems.at[3, j], seq=self.near_core)

    def core_arrival(self, j):
        block = self.place(self.index(j) + self.near_core - self.seq)
        return remote(block, block, self.sems.at[2, j], self.sems.at[3, j], seq=self.near_core)

    def far_copy(self, j):
        i = self.index(j)
        return remote(
            self.place(i), self.far(i), self.sems.at[4, j], self.sems.at[5, j], head=self.near_y
        )

    def far_core_copy(self, j):
        there = self.far(self.index(j))
        return remote(there, there, self.sems.at[6, j], self.sems.at[7, j], seq=self.near_core)

    def far_core_arrival(self, j):
        there = self.far(self.index(j) + self.near_core - self.seq)
        return remote(there, there, self.sems.at[6, j], self.sems.at[7, j], seq=self.near_core)

    def sides(self, j):
        self.core_copy(j).start()
        if self.far is not None:
            self.far_copy(j).start()

    def ups(self):
        return range(self.depth)

    def downs(self):
        return [0] + [self.depth + k for k in range(1, self.depth)]

    def has_above(self):
        return self.z + 1 < self.count

    def has_below(self):
        return self.z >= 1

    def begin(self):
        @pl.when(self.has_above())
        def _():
            self.line_copy(0, True).start()

        @pl.when(self.has_below())
        def _():
            self.line_copy(0, False).start()

        self.sides(0)

    def step(self, k):
        @pl.when(self.valid(1 + k))
        def _():
            self.line_arrival(1 + k).wait_recv()
            if 1 + k < self.depth:

                @pl.when(self.has_above())
                def _():
                    self.line_copy(1 + k, True).start()

            self.sides(1 + k)

        @pl.when(self.valid(self.depth + 1 + k))
        def _():
            self.line_arrival(self.depth + 1 + k).wait_recv()
            if 1 + k < self.depth:

                @pl.when(self.has_below())
                def _():
                    self.line_copy(self.depth + 1 + k, False).start()

            self.sides(self.depth + 1 + k)

    def side_step(self, j):
        @pl.when(self.valid(j))
        def _():
            self.far_copy(j).wait_recv()
            self.far_core_copy(j).start()

    def wait_blocks(self):
        for j in range(2 * self.depth + 1):

            @pl.when(self.valid(j))
            def _():
                self.core_arrival(j).wait_recv()
                if self.far is not None:
                    self.far_core_arrival(j).wait_recv()

    def wait_sends(self):
        for j in range(2 * self.depth + 1):

            @pl.when(self.valid(j))
            def _():
                self.core_copy(j).wait_send()
                if self.far is not None:
                    self.far_copy(j).wait_send()
                    self.far_core_copy(j).wait_send()

        for j in self.ups():

            @pl.when(self.valid(j) & self.has_above())
            def _():
                self.line_copy(j, True).wait_send()

        for j in self.downs():

            @pl.when(self.valid(j) & self.has_below())
            def _():
                self.line_copy(j, False).wait_send()


def forward_kernel(
    tokens, gain_first, gain_second, weight_own, wout_own, expert_up, expert_down, share_up, share_down,
    cotangent, marks, bias, cosine, sine, layout,
    first_out, weight_out, wout_out, experts, share, share_far, grads, seconds, qkv, merged, log_total, middle,
    lowered,
    group, weight, wout, expert_raw, expert_pack, share_raw, share_pack, mask, outgoing, incoming,
    local, line_w, line_o, line_g, line_s, ring_a, ring_b, sc_a, sc_b, ex_a, ex_b, sh_a, sh_b,
):
    seq, head = lax.axis_index("seq"), lax.axis_index("head")
    n_seq = lax.axis_size("seq")
    near_x, near_y, near_core = plane_places()
    peers = ring_places()
    size = len(peers)
    rows, width = tokens.shape
    heads = qkv.shape[1] // (3 * HD)
    units = experts.shape[2]
    y = head // 2
    share_rows = share.shape[2]
    hidden = expert_down.shape[0]
    part = weight_own.shape[0]

    fetch = [
        pltpu.make_async_copy(
            weight_own, weight.at[pl.ds(pl.multiple_of(seq * part, 16), part)], local.at[0]
        ),
        pltpu.make_async_copy(wout_own, wout.at[seq], local.at[1]),
        pltpu.make_async_copy(expert_up, expert_raw, local.at[2]),
        pltpu.make_async_copy(expert_down, expert_pack.at[2], local.at[3]),
        pltpu.make_async_copy(share_up, share_raw, local.at[4]),
        pltpu.make_async_copy(share_down, share_pack.at[2], local.at[5]),
        pltpu.make_async_copy(cotangent, grads.at[0, seq, :, pl.ds(0, width)], local.at[6]),
        pltpu.make_async_copy(marks, grads.at[0, seq, :, pl.ds(width, marks.shape[1])], local.at[13]),
    ]
    for copy in fetch:
        copy.start()
    greet(
        [{"head": peer} for peer in peers[1:]]
        + [{"seq": (seq + k) % n_seq} for k in range(1, n_seq)]
    )

    gather_w = Line(lambda i: weight.at[pl.ds(pl.multiple_of(i * part, 16), part)], None, line_w)
    gather_o = Line(lambda i: wout.at[i], None, line_o)
    gather_g = Line(lambda i: grads.at[0, i], lambda i: grads.at[1, i], line_g)
    gather_s = Line(lambda i: seconds.at[0, i], lambda i: seconds.at[1, i], line_s)
    fetch[0].wait()
    gather_w.begin()
    fetch[1].wait()
    gather_o.begin()

    group[:rows] = norm_rows(tokens[...].astype(f32), gain_first[...].astype(f32))
    ring = [
        remote(
            group.at[pl.ds(0, rows)], group.at[pl.ds(r * rows, rows)],
            ring_a.at[r - 1], ring_b.at[r - 1], head=peers[size - r],
        )
        for r in range(1, size)
    ]
    for copy in ring:
        copy.start()

    fetch[2].wait()
    fetch[3].wait()
    mine = pl.ds(pl.multiple_of(y * units, 16), units)
    other = pl.ds(pl.multiple_of((1 - y) * units, 16), units)
    ups = [
        remote(expert_pack.at[m, other], experts.at[2, m], ex_a.at[m], ex_b.at[m], head=near_y)
        for m in range(3)
    ]
    sides = [
        remote(expert_pack.at[m, mine], experts.at[1, m], ex_a.at[3 + m], ex_b.at[3 + m], head=near_x)
        for m in range(3)
    ]
    ons = [
        remote(experts.at[2, m], experts.at[3, m], ex_a.at[6 + m], ex_b.at[6 + m], head=near_x)
        for m in range(3)
    ]
    order = (2, 0, 1)
    for m in order:
        if m < 2:
            expert_pack[m] = expert_raw[:, m * hidden : (m + 1) * hidden].T
        ups[m].start()
        sides[m].start()
    keep = [pltpu.make_async_copy(expert_pack.at[:, mine], experts.at[0], local.at[7])]
    keep[0].start()

    fetch[4].wait()
    fetch[5].wait()
    for m in range(2):
        share_pack[m] = share_raw[:, m * hidden : (m + 1) * hidden].T

    def share_block(i):
        return share_pack.at[:, pl.ds(pl.multiple_of(i * share_rows, 16), share_rows)]

    share_own = pltpu.make_async_copy(share_block(seq), share.at[seq], local.at[8])
    share_own.start()
    z, depth = seq // 2, n_seq // 2

    def share_send(distance, up, flip):
        to = (seq + 2 * distance if up else seq - 2 * distance) + flip * (near_core - seq)
        j = (2 * distance + up) * 2 + flip
        return remote(share_block(to), share.at[seq], sh_a.at[j], sh_b.at[j], seq=to)

    def share_source(distance, up, flip):
        return (seq - 2 * distance if up else seq + 2 * distance) + flip * (near_core - seq)

    def share_arrival(distance, up, flip):
        j = (2 * distance + up) * 2 + flip
        block = share.at[share_source(distance, up, flip)]
        return remote(block, block, sh_a.at[j], sh_b.at[j], seq=near_core)

    def share_cross(distance, up, flip):
        source = share_source(distance, up, flip)
        j = 4 * depth + (2 * distance + up) * 2 + flip
        return remote(
            share.at[source], share_far.at[source], sh_a.at[j], sh_b.at[j], head=near_x
        )

    def each_share(distance, arriving, act):
        if distance == 0:
            act(0, 1, 1)
            return
        for up in (0, 1):
            below = z >= distance
            above = z + distance < depth
            there = (below if up else above) if arriving else (above if up else below)

            @pl.when(there)
            def _():
                for flip in (0, 1):
                    act(distance, up, flip)

    def share_on(distance):
        def act(*at):
            share_arrival(*at).wait_recv()
            share_cross(*at).start()

        each_share(distance, True, act)

    mask[...] = mask_of(layout[...])
    gather_w.step(0)
    gather_o.step(0)
    gather_w.step(1)
    gather_o.step(1)
    ups[2].wait_recv()
    ons[2].start()
    fetch[6].wait()
    fetch[7].wait()
    gather_w.step(2)
    gather_o.step(2)
    gather_g.begin()
    for distance in range(depth):
        each_share(distance, False, lambda *at: share_send(*at).start())
    for copy in ring:
        copy.wait_recv()
    gather_w.wait_blocks()
    gather_o.wait_blocks()
    keep += [
        pltpu.make_async_copy(weight, weight_out, local.at[9]),
        pltpu.make_async_copy(wout, wout_out, local.at[10]),
        pltpu.make_async_copy(group, first_out, local.at[11]),
    ]
    for copy in keep[1:]:
        copy.start()

    step = 3 * HD
    cos, sin = wide_tables(cosine[...], sine[...])
    every_bias = bias[...].astype(f32)
    bias_row = lax.broadcasted_iota(jnp.int32, every_bias.shape, 0)
    for n in range(heads):
        shift_row = jnp.where(bias_row == head * heads + n, every_bias, 0.0)
        linear = dot(group[...], weight[:, n * step : (n + 1) * step], 1, 0)
        linear = linear + jnp.sum(shift_row, axis=0, keepdims=True)
        parts, output, log_sum = head_forward(linear, cos, sin, mask[...])
        for k in range(3):
            qkv[:, n * step + k * HD : n * step + (k + 1) * HD] = parts[k]
        merged[:, n * HD : (n + 1) * HD] = output
        log_total[n] = jnp.broadcast_to(log_sum, log_total.shape[1:])
        if n == 2:
            gather_g.step(0)
            gather_g.side_step(0)
    copies, own = scatter_start(merged, wout, outgoing, incoming, sc_a, sc_b, rows, peers)
    ups[0].wait_recv()
    ons[0].start()
    block = wout.shape[2]
    for b in range(len(own)):
        cols = slice(b * block, (b + 1) * block)
        middle[:, cols] = tokens[:, cols].astype(f32) + own[b]
    gather_g.step(1)
    for copy in copies:
        copy.wait_recv()
    total = middle[...]
    for r in range(size - 1):
        total += incoming[r].astype(f32)
    middle[...] = total
    lowered[...] = norm_rows(total, gain_second[...].astype(f32))
    last = pltpu.make_async_copy(lowered, seconds.at[0, seq], local.at[12])
    last.start()
    last.wait()
    gather_s.begin()
    ups[1].wait_recv()
    ons[1].start()

    share_own.wait()
    cross_own = remote(share.at[seq], share_far.at[seq], sh_a.at[0], sh_b.at[0], head=near_x)
    cross_own.start()
    gather_g.step(2)
    share_on(0)
    share_on(1)
    for j in (1, 1 + gather_g.depth, 2, 2 + gather_g.depth):
        gather_g.side_step(j)
    gather_s.step(0)
    share_on(2)
    for j in (3, 3 + gather_g.depth):
        gather_g.side_step(j)
    gather_s.side_step(0)
    gather_s.step(1)
    for j in (1, 1 + gather_g.depth):
        gather_s.side_step(j)
    gather_s.step(2)
    share_on(3)
    for j in (2, 2 + gather_g.depth, 3, 3 + gather_g.depth):
        gather_s.side_step(j)

    gather_g.wait_blocks()
    gather_s.wait_blocks()
    for copy in sides + ons + [cross_own]:
        copy.wait()
    for distance in range(depth):
        each_share(distance, True, lambda *at: share_cross(*at).wait())
        each_share(distance, False, lambda *at: share_send(*at).wait_send())
    for copy in ups + ring + copies:
        copy.wait_send()
    for copy in keep:
        copy.wait()
    for line in (gather_w, gather_o, gather_g, gather_s):
        line.wait_sends()


def forward(
    tokens, gain_first, gain_second, weight_own, wout_own, expert_up, expert_down, share_up, share_down,
    cotangent, marks, bias, cosine, sine, layout,
):
    n_seq, n_head = lax.axis_size("seq"), lax.axis_size("head")
    rows, width = tokens.shape
    group_tok = rows * n_head
    wide = wout_own.shape[0]
    heads = wide // HD
    part = weight_own.shape[0]
    hidden, head_part = expert_down.shape
    units = hidden // 2
    share_all, seq_part = share_down.shape
    share_rows = share_all // n_seq
    ext = width + marks.shape[1]
    anywhere = pl.BlockSpec(memory_space=pl.ANY)
    vmem = pl.BlockSpec(memory_space=pltpu.VMEM)
    dma = pltpu.SemaphoreType.DMA
    lines = n_seq - 1

    def hbm(*shape):
        return (anywhere, jax.ShapeDtypeStruct(shape, bf16))

    outs = [
        hbm(group_tok, width),
        hbm(width, 3 * wide),
        hbm(n_seq, wide, part),
        hbm(4, 3, units, head_part),
        hbm(n_seq, 3, share_rows, seq_part),
        hbm(n_seq, 3, share_rows, seq_part),
        hbm(2, n_seq, rows, ext),
        hbm(2, n_seq, rows, width),
        (vmem, jax.ShapeDtypeStruct((group_tok, 3 * wide), bf16)),
        (vmem, jax.ShapeDtypeStruct((group_tok, wide), bf16)),
        (vmem, jax.ShapeDtypeStruct((heads, group_tok, LANES), f32)),
        (vmem, jax.ShapeDtypeStruct((rows, width), f32)),
        (vmem, jax.ShapeDtypeStruct((rows, width), bf16)),
    ]
    return pl.pallas_call(
        forward_kernel,
        in_specs=[vmem] * 3 + [anywhere] * 8 + [vmem] * 4,
        out_specs=[spec for spec, _ in outs],
        out_shape=[shape for _, shape in outs],
        scratch_shapes=[
            pltpu.VMEM((group_tok, width), bf16),
            pltpu.VMEM((width, 3 * wide), bf16),
            pltpu.VMEM((n_seq, wide, part), bf16),
            pltpu.VMEM(expert_up.shape, bf16),
            pltpu.VMEM((3, hidden, head_part), bf16),
            pltpu.VMEM(share_up.shape, bf16),
            pltpu.VMEM((3, share_all, seq_part), bf16),
            pltpu.VMEM((group_tok, group_tok), f32),
            pltpu.VMEM((n_head - 1, rows, width), bf16),
            pltpu.VMEM((n_head - 1, rows, width), bf16),
            dma((14,)),
            dma((4, lines)),
            dma((4, lines)),
            dma((8, lines)),
            dma((8, lines)),
            dma((n_head - 1,)),
            dma((n_head - 1,)),
            dma((n_head - 1,)),
            dma((n_head - 1,)),
            dma((9,)),
            dma((9,)),
            dma((4 * n_seq,)),
            dma((4 * n_seq,)),
        ],
        compiler_params=pltpu.CompilerParams(
            collective_id=0, has_side_effects=True, vmem_limit_bytes=VMEM_BYTES
        ),
        cost_estimate=pl.CostEstimate(
            flops=2 * group_tok * width * 4 * wide, bytes_accessed=1 << 29, transcendentals=0
        ),
        name="forward",
    )(
        tokens, gain_first, gain_second, weight_own, wout_own, expert_up, expert_down, share_up,
        share_down, cotangent, marks, bias, cosine, sine, layout,
    )


def mesh_part():
    return lax.axis_index("head") // 2


def token_bits():
    return bits_of(lax.axis_size("head"))[1:]


def token_gather(block):
    order = token_bits()
    column = lax.all_gather(block, "seq", axis=0, tiled=True)
    share = column.shape[0] // 2
    half = share // 2
    core = lax.rem(lax.axis_index("seq"), 2)
    own = lax.dynamic_slice_in_dim(column, core * share, share, 0)
    upper = spread(own[:half], order)
    lower = spread(own[half:], order[::-1])
    chunks = [column]
    for r in sorted(upper)[1:]:
        for piece in (upper[r], lower[r]):
            chunks.append(jnp.concatenate([piece, swap(piece, "seq", 1)], axis=0))
    return chunks


def token_scatter(chunks):
    order = token_bits()
    column = chunks[0]
    share = column.shape[0] // 2
    half = share // 2
    core = lax.rem(lax.axis_index("seq"), 2)
    own = lax.dynamic_slice_in_dim(column, core * share, share, 0)
    sides = [{0: own[:half]}, {0: own[half:]}]
    for i, chunk in enumerate(chunks[1:]):
        sides[i % 2][2 * (i // 2 + 1)] = chunk[:half] + swap(chunk[half:], "seq", 1)
    total = jnp.concatenate([collect(sides[0], order), collect(sides[1], order[::-1])], axis=0)
    column = lax.dynamic_update_slice_in_dim(column, total, core * share, 0)
    return lax.psum_scatter(column, "seq", scatter_dimension=0, tiled=True)


def total_over_all(values):
    for axis in ("head", "seq"):
        for bit in bits_of(lax.axis_size(axis)):
            values = values + swap(values, axis, bit)
    return values


def turn(values, cosine, sine):
    return values * cosine + pltpu.roll(values, HD // 2, 1) * sine


def mask_of(layout):
    rows = layout.shape[1]
    cols = jnp.concatenate([layout, jnp.zeros((6, rows), f32)], axis=0).T
    same = cols[:, 0:1] == layout[0:1, :]
    return jnp.where(same & (layout[1:2, :] <= cols[:, 1:2]), 0.0, NEGATIVE)


def wide_tables(cosine, sine):
    return (
        jnp.concatenate([cosine, cosine], axis=1),
        jnp.concatenate([-sine, sine], axis=1),
    )


def head_forward(linear, cos, sin, mask):
    queries = turn(linear[:, :HD], cos, sin).astype(bf16)
    keys = turn(linear[:, HD : 2 * HD], cos, sin).astype(bf16)
    values = linear[:, 2 * HD :].astype(bf16)
    scores = dot(queries, keys, 1, 1) * HD ** (-0.5) + mask
    largest = jnp.max(scores, axis=1, keepdims=True)
    weights = jnp.exp(scores - largest)
    total = jnp.sum(weights, axis=1, keepdims=True)
    probs = (weights / total).astype(bf16)
    output = dot(probs, values, 1, 0).astype(bf16)
    return (queries, keys, values), output, largest + jnp.log(total)


def norm_rows(rows, gain):
    square = jnp.mean(rows * rows, axis=1, keepdims=True)
    return (rows * lax.rsqrt(square + EPS) * gain).astype(bf16)


def scatter_start(merged, wout, outgoing, incoming, sems_a, sems_b, rows, peers):
    blocks, _, size = wout.shape
    copies = []
    for r in range(len(peers) - 1, 0, -1):
        for b in range(blocks):
            outgoing[r - 1, :, b * size : (b + 1) * size] = dot(
                merged[r * rows : (r + 1) * rows, :], wout[b], 1, 0
            ).astype(bf16)
        copies.append(
            remote(
                outgoing.at[r - 1], incoming.at[r - 1], sems_a.at[r - 1], sems_b.at[r - 1],
                head=peers[r],
            )
        )
        copies[-1].start()
    return copies, [dot(merged[:rows, :], wout[b], 1, 0) for b in range(blocks)]


def attend_kernel(
    first, weight, wout, bias, cosine, sine, layout, tokens, gain,
    qkv, merged, log_total, middle, lowered, mask, outgoing, incoming, sems_a, sems_b,
):
    n = pl.program_id(0)
    heads = pl.num_programs(0)
    peers = ring_places()

    @pl.when(n == 0)
    def _():
        greet([{"head": peer} for peer in peers[1:]])
        mask[...] = mask_of(layout[...])

    linear = dot(first[...], weight[...], 1, 0) + bias[0]
    cos, sin = wide_tables(cosine[...], sine[...])
    parts, output, log_sum = head_forward(linear, cos, sin, mask[...])
    for k in range(3):
        qkv[:, k * HD : (k + 1) * HD] = parts[k]
    merged[:, pl.ds(pl.multiple_of(n * HD, HD), HD)] = output
    log_total[0] = jnp.broadcast_to(log_sum, log_total.shape[1:])

    @pl.when(n == heads - 1)
    def _():
        copies, own = scatter_start(
            merged, wout, outgoing, incoming, sems_a, sems_b, tokens.shape[0], peers
        )
        size = wout.shape[2]
        for b, block in enumerate(own):
            cols = slice(b * size, (b + 1) * size)
            middle[:, cols] = tokens[:, cols].astype(f32) + block
        for copy in copies:
            copy.wait()
        total = middle[...]
        for r in range(len(peers) - 1):
            total += incoming[r].astype(f32)
        middle[...] = total
        lowered[...] = norm_rows(total, gain[...])


def attend(first, weight, wout, bias, cosine, sine, layout, tokens, gain):
    rows, width = first.shape
    heads = bias.shape[0]
    own = tokens.shape[0]
    others = lax.axis_size("head") - 1
    step = 3 * HD
    wide = heads * HD

    def whole(shape):
        return pl.BlockSpec(shape, lambda n: (0,) * len(shape))

    return pl.pallas_call(
        attend_kernel,
        grid=(heads,),
        in_specs=[
            whole((rows, width)),
            pl.BlockSpec((width, step), lambda n: (0, n)),
            whole(wout.shape),
            pl.BlockSpec((1, 1, step), lambda n: (n, 0, 0)),
            whole((rows, HD // 2)),
            whole((rows, HD // 2)),
            whole((2, rows)),
            whole((own, width)),
            whole((1, width)),
        ],
        out_specs=[
            pl.BlockSpec((rows, step), lambda n: (0, n)),
            whole((rows, wide)),
            pl.BlockSpec((1, rows, LANES), lambda n: (n, 0, 0)),
            whole((own, width)),
            whole((own, width)),
        ],
        out_shape=[
            jax.ShapeDtypeStruct((rows, heads * step), bf16),
            jax.ShapeDtypeStruct((rows, wide), bf16),
            jax.ShapeDtypeStruct((heads, rows, LANES), f32),
            jax.ShapeDtypeStruct((own, width), f32),
            jax.ShapeDtypeStruct((own, width), bf16),
        ],
        scratch_shapes=[
            pltpu.VMEM((rows, rows), f32),
            pltpu.VMEM((others, own, width), bf16),
            pltpu.VMEM((others, own, width), bf16),
            pltpu.SemaphoreType.DMA((others,)),
            pltpu.SemaphoreType.DMA((others,)),
        ],
        compiler_params=pltpu.CompilerParams(
            collective_id=2, has_side_effects=True, vmem_limit_bytes=VMEM_BYTES
        ),
        cost_estimate=pl.CostEstimate(
            flops=2 * rows * width * 4 * wide, bytes_accessed=8 * width * wide, transcendentals=0
        ),
        name="attend",
    )(first, weight, wout, bias, cosine, sine, layout, tokens, gain)


def attend_back_kernel(
    plane, grad_own, first, weight, wout, qkv, merged, log_total, cosine, sine, layout,
    *refs,
):
    if plane:
        experts, grad_first, grad_weight, grad_bias, expert_in, x_a, x_b = refs[:5] + refs[-2:]
        refs = refs[5:-2]
    else:
        grad_first, grad_weight, grad_bias = refs[:3]
        refs = refs[3:]
    mask, grad_merged, acc, grad, sems_a, sems_b = refs
    n = pl.program_id(0)
    peers = ring_places()
    own = grad_own.shape[0]
    heads = pl.num_programs(0)
    if plane:
        near_x = plane_places()[0]
        cross = [remote(experts.at[3, 0], expert_in, x_a, x_b, head=near_x)]
    scale = HD ** (-0.5)
    blocks, _, size = grad_weight.shape
    wide = wout.shape[1]

    @pl.when(n == 0)
    def _():
        greet([{"head": peer} for peer in peers[1:]])
        copies = [
            remote(
                grad_own, grad.at[pl.ds(r * own, own)], sems_a.at[r - 1], sems_b.at[r - 1],
                head=peers[len(peers) - r],
            )
            for r in range(1, len(peers))
        ]
        for copy in copies:
            copy.start()
        grad[:own] = grad_own[...]
        mask[...] = mask_of(layout[...])
        acc[...] = jnp.zeros_like(acc)
        for copy in copies:
            copy.wait()
        if plane:
            for copy in cross:
                copy.start()
        total = jnp.zeros((grad.shape[0], wide), f32)
        for s in range(blocks):
            total += dot(grad[:, s * size : (s + 1) * size], wout[s], 1, 1)
        grad_merged[...] = total.astype(bf16)
        for s in range(blocks):
            grad_weight[s, 3 * wide :, :] = dot(
                merged[...], grad[:, s * size : (s + 1) * size], 0, 0
            ).astype(bf16)

    cos, sin = wide_tables(cosine[...], -sine[...])
    queries, keys, values = qkv[:, :HD], qkv[:, HD : 2 * HD], qkv[:, 2 * HD :]
    grad_out = grad_merged[:, pl.ds(pl.multiple_of(n * HD, HD), HD)]
    scores = dot(queries, keys, 1, 1) * scale + mask[...]
    probs = jnp.exp(scores - log_total[0][:, 0:1])
    grad_values = dot(probs.astype(bf16), grad_out, 0, 0).astype(bf16)
    grad_probs = dot(grad_out, values, 1, 1)
    centre = jnp.sum(probs * grad_probs, axis=1, keepdims=True)
    grad_scores = (probs * (grad_probs - centre)).astype(bf16)
    grad_queries = (dot(grad_scores, keys, 1, 0) * scale).astype(bf16).astype(f32)
    grad_keys = (dot(grad_scores, queries, 0, 0) * scale).astype(bf16).astype(f32)
    grad_linear = jnp.concatenate(
        [turn(grad_queries, cos, sin).astype(bf16), turn(grad_keys, cos, sin).astype(bf16), grad_values],
        axis=1,
    )
    grad_bias[0] = jnp.sum(grad_linear.astype(f32), axis=0, keepdims=True)
    acc[...] += dot(grad_linear, weight[...], 1, 1)
    step = 3 * HD
    for s in range(blocks):
        grad_weight[s, pl.ds(pl.multiple_of(n * step, HD), step), :] = dot(
            grad_linear, first[:, s * size : (s + 1) * size], 0, 0
        ).astype(bf16)

    @pl.when(n == heads - 1)
    def _():
        grad_first[...] = acc[...].astype(bf16)
        if plane:
            for copy in cross:
                copy.wait()


def attend_back(
    grad, first, weight, wout, qkv, merged, log_total, cosine, sine, layout, extra=()
):
    rows, width = first.shape
    heads = log_total.shape[0]
    step = 3 * HD
    wide = heads * HD
    n_seq = lax.axis_size("seq")
    size = width // n_seq
    own = grad.shape[0]
    others = lax.axis_size("head") - 1

    anywhere = pl.BlockSpec(memory_space=pl.ANY)
    more_outs, more_scratch = [], []
    if extra:
        more_outs = [jax.ShapeDtypeStruct(extra[0].shape[2:], bf16)]
        more_scratch = [pltpu.SemaphoreType.DMA] * 2

    def whole(shape):
        return pl.BlockSpec(shape, lambda n: (0,) * len(shape))

    return pl.pallas_call(
        functools.partial(attend_back_kernel, bool(extra)),
        grid=(heads,),
        in_specs=[
            whole((own, width)),
            whole((rows, width)),
            pl.BlockSpec((width, step), lambda n: (0, n)),
            whole(wout.shape),
            pl.BlockSpec((rows, step), lambda n: (0, n)),
            whole((rows, wide)),
            pl.BlockSpec((1, rows, LANES), lambda n: (n, 0, 0)),
            whole((rows, HD // 2)),
            whole((rows, HD // 2)),
            whole((2, rows)),
        ]
        + [anywhere] * len(extra),
        out_specs=[
            whole((rows, width)),
            whole((n_seq, 4 * wide, size)),
            pl.BlockSpec((1, 1, step), lambda n: (n, 0, 0)),
        ]
        + [anywhere] * len(more_outs),
        out_shape=[
            jax.ShapeDtypeStruct((rows, width), bf16),
            jax.ShapeDtypeStruct((n_seq, 4 * wide, size), bf16),
            jax.ShapeDtypeStruct((heads, 1, step), f32),
        ]
        + more_outs,
        scratch_shapes=[
            pltpu.VMEM((rows, rows), f32),
            pltpu.VMEM((rows, wide), bf16),
            pltpu.VMEM((rows, width), f32),
            pltpu.VMEM((rows, width), bf16),
            pltpu.SemaphoreType.DMA((others,)),
            pltpu.SemaphoreType.DMA((others,)),
        ]
        + more_scratch,
        compiler_params=pltpu.CompilerParams(
            collective_id=3, has_side_effects=True, vmem_limit_bytes=VMEM_BYTES
        ),
        cost_estimate=pl.CostEstimate(
            flops=4 * rows * width * 4 * wide, bytes_accessed=16 * width * wide, transcendentals=0
        ),
        name="attend_back",
    )(grad, first, weight, wout, qkv, merged, log_total, cosine, sine, layout, *extra)


def pack_kernel(exp_units, share_units, at, *refs):
    stacked, shares = refs[0], refs[-5:-3]
    experts = [stacked.at[r] for r in range(stacked.shape[0])]
    rest, full, sems = refs[-3:]
    head = at[0]
    copies = []
    for r, block in enumerate(experts):
        size = block.shape[2]
        start = pl.multiple_of(jnp.bitwise_xor(head, r) * size, size)
        copies.append(
            pltpu.make_async_copy(
                block, full.at[:, pl.ds(0, exp_units), pl.ds(start, size)], sems.at[len(copies)]
            )
        )
    for r, block in enumerate(shares):
        size = block.shape[3]
        for s in range(block.shape[0]):
            copies.append(
                pltpu.make_async_copy(
                    block.at[s],
                    full.at[:, pl.ds(exp_units + r * share_units, share_units), pl.ds(s * size, size)],
                    sems.at[len(copies)],
                )
            )
    base = exp_units + 2 * share_units
    copies.append(
        pltpu.make_async_copy(rest, full.at[:, pl.ds(base, rest.shape[1]), :], sems.at[len(copies)])
    )
    for copy in copies:
        copy.start()
    for copy in copies:
        copy.wait()


def pack(at, experts, shares, rest, unit_rows):
    exp_units, share_units = experts.shape[2], shares[0].shape[2]
    count = experts.shape[0] + 2 * shares[0].shape[0] + 1
    anywhere = pl.BlockSpec(memory_space=pl.ANY)
    return pl.pallas_call(
        functools.partial(pack_kernel, exp_units, share_units),
        in_specs=[pl.BlockSpec(memory_space=pltpu.SMEM)] + [anywhere] * 4,
        out_specs=anywhere,
        out_shape=jax.ShapeDtypeStruct((3, unit_rows, rest.shape[2]), bf16),
        scratch_shapes=[pltpu.SemaphoreType.DMA((count,))],
        compiler_params=pltpu.CompilerParams(vmem_limit_bytes=1 << 20),
        cost_estimate=pl.CostEstimate(
            flops=0, bytes_accessed=12 * unit_rows * rest.shape[2], transcendentals=0
        ),
        name="pack",
    )(at, experts, *shares, rest)


def mix_rows(exp_units, base, n_exp, x, grad_ext, w, units, wait=None):
    rows, width = x.shape
    unit_rows = w.shape[1]
    seq = lax.axis_index("seq")
    block = base // LANES * LANES
    chunks = [(block, unit_rows)] + [(a, min(a + 512, block)) for a in range(0, block, 512)]
    lane = lax.broadcasted_iota(jnp.int32, (rows, LANES), 1)
    marks = grad_ext[:, width:].astype(f32)
    mark = jnp.sum(jnp.where(lane == seq, marks, 0.0), axis=1, keepdims=True)
    exp_sum = share_sum = gate_here = share_gate = 0.0
    for i, (a, b) in enumerate(chunks):
        if wait is not None and i < 2:
            wait(i)
        gate = dot(x, w[0, a:b], 1, 1)
        up = dot(x, w[1, a:b], 1, 1)
        raw = dot(grad_ext[:, :width], w[2, a:b], 1, 1)
        if i == 0:
            logits = gate[:, :LANES]
            from_base = lane - (base - block)
            is_logit = (from_base >= 0) & (from_base < n_exp)
            largest = jnp.max(jnp.where(is_logit, logits, NEGATIVE), axis=1, keepdims=True)
            powers = jnp.where(is_logit, jnp.exp(jnp.where(is_logit, logits - largest, 0.0)), 0.0)
            chosen = jnp.sum(jnp.where(from_base == seq, powers, 0.0), axis=1, keepdims=True)
            gate_here = mark * chosen / jnp.sum(powers, axis=1, keepdims=True)
            share_gate = jax.nn.sigmoid(
                jnp.sum(jnp.where(from_base == n_exp, logits, 0.0), axis=1, keepdims=True)
            )
        sigma = 0.5 * jnp.tanh(0.5 * gate) + 0.5
        silu = gate * sigma
        hidden = silu * up
        both = hidden * raw
        if b <= exp_units:
            factor = gate_here
            exp_sum += jnp.sum(both, axis=1, keepdims=True)
        elif a >= exp_units:
            factor = share_gate
            share_sum += jnp.sum(both, axis=1, keepdims=True)
        else:
            is_expert = lax.broadcasted_iota(jnp.int32, both.shape, 1) < exp_units - a
            factor = jnp.where(is_expert, gate_here, share_gate)
            part = jnp.sum(jnp.where(is_expert, both, 0.0), axis=1, keepdims=True)
            exp_sum += part
            share_sum += jnp.sum(both, axis=1, keepdims=True) - part
        grad_hidden = raw * factor
        units[0][:, a:b] = (grad_hidden * (sigma * up + hidden * (1.0 - sigma))).astype(bf16)
        units[1][:, a:b] = (grad_hidden * silu).astype(bf16)
        units[2][:, a:b] = (hidden * factor).astype(bf16)
    back = dot(units[0][...], w[0], 1, 0) + dot(units[1][...], w[1], 1, 0)
    extra = jnp.where(lane == seq, exp_sum * mark, jnp.where(lane == n_exp, share_sum, 0.0))
    return back.astype(bf16), extra.astype(bf16)


def mix_local_kernel(exp_units, base, n_exp, second, grad_ext, w_hbm, back, unit_out, w, sems):
    copies = [pltpu.make_async_copy(w_hbm.at[m], w.at[m], sems.at[m]) for m in range(3)]
    width = second.shape[1]

    @pl.when(pl.program_id(0) == 0)
    def _():
        for copy in copies:
            copy.start()
        for copy in copies:
            copy.wait()

    units = [unit_out.at[m] for m in range(3)]
    rows_back, extra = mix_rows(exp_units, base, n_exp, second[...], grad_ext, w, units)
    back[:, :width] = rows_back
    back[:, width:] = extra


def mix_local(second, grad_ext, full, exp_units, base, n_exp):
    rows, width = second.shape
    unit_rows = full.shape[1]
    wide = grad_ext.shape[1]
    return pl.pallas_call(
        functools.partial(mix_local_kernel, exp_units, base, n_exp),
        grid=(rows // TILE,),
        in_specs=[
            pl.BlockSpec((TILE, width), lambda i: (i, 0)),
            pl.BlockSpec((TILE, wide), lambda i: (i, 0)),
            pl.BlockSpec(memory_space=pl.ANY),
        ],
        out_specs=[
            pl.BlockSpec((TILE, wide), lambda i: (i, 0)),
            pl.BlockSpec((3, TILE, unit_rows), lambda i: (0, i, 0)),
        ],
        out_shape=[
            jax.ShapeDtypeStruct((rows, wide), bf16),
            jax.ShapeDtypeStruct((3, rows, unit_rows), bf16),
        ],
        scratch_shapes=[
            pltpu.VMEM((3, unit_rows, width), bf16),
            pltpu.SemaphoreType.DMA((3,)),
        ],
        compiler_params=pltpu.CompilerParams(vmem_limit_bytes=VMEM_BYTES),
        cost_estimate=pl.CostEstimate(
            flops=10 * rows * width * unit_rows,
            bytes_accessed=6 * unit_rows * width + 8 * rows * width,
            transcendentals=0,
        ),
        name="mix_local",
    )(second, grad_ext, full)


def mix_kernel(
    exp_units, base, n_exp, second, grad_ext, experts, share_own, share_far, rest, unit_out, back, down_out,
    w, held, core_in, home, e_sem, s_sem, r_sem, b_a, b_b, h_a, h_b, o_sem, d_sem,
):
    i = pl.program_id(0)
    _, near_y, near_core = plane_places()
    core = lax.axis_index("seq") % 2
    rows, width = second.shape[2:]
    at = [pl.ds(j * rows, rows) for j in range(2)]
    loads = [[], []]
    for m in range(3):
        for r, owner in enumerate(plane_owners()):
            size = experts.shape[3]
            start = pl.multiple_of(owner * size, size)
            loads[1].append(
                pltpu.make_async_copy(
                    experts.at[r, m], w.at[m, pl.ds(0, exp_units), pl.ds(start, size)], e_sem.at[m, r]
                )
            )
    share_rows, size = share_own.shape[2:]
    for r, share in enumerate((share_own, share_far)):
        for place in range(share.shape[0]):
            loads[0].append(
                pltpu.make_async_copy(
                    share.at[place],
                    w.at[
                        :,
                        pl.ds(exp_units + r * share_rows, share_rows),
                        pl.ds(place * size, size),
                    ],
                    s_sem.at[r, place],
                )
            )
    loads[0].append(pltpu.make_async_copy(rest, w.at[0, pl.ds(base, rest.shape[0])], r_sem))
    keep = pltpu.make_async_copy(w.at[2], down_out, d_sem)
    back_c = [
        remote(held.at[j, 1 - core], core_in.at[j], b_a.at[j], b_b.at[j], seq=near_core)
        for j in range(2)
    ]
    back_y = [
        remote(held.at[j, core], home.at[j], h_a.at[j], h_b.at[j], head=near_y) for j in range(2)
    ]

    def wait_weights(m):
        @pl.when(i == 0)
        def _():
            for copy in loads[m]:
                copy.wait()

    @pl.when(i == 0)
    def _():
        for group in loads:
            for copy in group:
                copy.start()
        w[0, base + rest.shape[0] :] = jnp.zeros((w.shape[1] - base - rest.shape[0], width), bf16)
        for m in (1, 2):
            w[m, base:] = jnp.zeros((w.shape[1] - base, width), bf16)
        greet([{"head": near_y}, {"seq": near_core}])

    for c in range(2):
        units = [unit_out.at[m, 0, c] for m in range(3)]
        rows_back, extra = mix_rows(
            exp_units, base, n_exp, second[0, c], grad_ext.at[0, c], w, units,
            wait_weights if c == 0 else None,
        )
        held[i, c, :, :width] = rows_back
        held[i, c, :, width:] = extra
        if c == 0:
            for j in range(2):

                @pl.when(i == 1 + j)
                def _():
                    back_c[j].wait_recv()
                    held[j, core] = (held[j, core].astype(f32) + core_in[j].astype(f32)).astype(bf16)
                    back_y[j].start()

    for j in range(2):

        @pl.when(i == j)
        def _():
            back_c[j].start()
            if j == 0:
                keep.start()

    @pl.when(i == 3)
    def _():
        out = [
            [
                pltpu.make_async_copy(held.at[2 + j, c], back.at[c, at[j]], o_sem.at[j, k])
                for k, c in enumerate((1 - core, core))
            ]
            for j in range(2)
        ]
        for j in range(2):
            out[j][0].start()
        for j in range(2):
            back_y[j].wait_recv()
            held[2 + j, core] = (held[2 + j, core].astype(f32) + home[j].astype(f32)).astype(bf16)
            out[j][1].start()
        for j in range(2):
            out[j][0].wait()
            out[j][1].wait()
            back_c[j].wait_send()
            back_y[j].wait_send()
        keep.wait()


def mix(seconds, grads, experts, share_own, share_far, rest, exp_units, base, n_exp, unit_rows):
    rows, width = seconds.shape[1:]
    wide = grads.shape[2]
    half = rows // 2
    piece = half // 2
    anywhere = pl.BlockSpec(memory_space=pl.ANY)
    units, back, down_rows = pl.pallas_call(
        functools.partial(mix_kernel, exp_units, base, n_exp),
        grid=(4,),
        in_specs=[
            pl.BlockSpec((1, 2, piece, width), lambda i: (1 - i // 2, 0, i % 2, 0)),
            pl.BlockSpec((1, 2, piece, wide), lambda i: (1 - i // 2, 0, i % 2, 0)),
            anywhere,
            anywhere,
            anywhere,
            anywhere,
        ],
        out_specs=[
            pl.BlockSpec((3, 1, 2, piece, unit_rows), lambda i: (0, 1 - i // 2, 0, i % 2, 0)),
            anywhere,
            anywhere,
        ],
        out_shape=[
            jax.ShapeDtypeStruct((3, 2, 2, half, unit_rows), bf16),
            jax.ShapeDtypeStruct((2, half, wide), bf16),
            jax.ShapeDtypeStruct((unit_rows, width), bf16),
        ],
        scratch_shapes=[
            pltpu.VMEM((3, unit_rows, width), bf16),
            pltpu.VMEM((4, 2, piece, wide), bf16),
            pltpu.VMEM((2, piece, wide), bf16),
            pltpu.VMEM((2, piece, wide), bf16),
            pltpu.SemaphoreType.DMA((3, 4)),
            pltpu.SemaphoreType.DMA((2, share_own.shape[0])),
            pltpu.SemaphoreType.DMA,
            *[pltpu.SemaphoreType.DMA((2,))] * 4,
            pltpu.SemaphoreType.DMA((2, 2)),
            pltpu.SemaphoreType.DMA,
        ],
        compiler_params=pltpu.CompilerParams(
            collective_id=4, has_side_effects=True, vmem_limit_bytes=VMEM_BYTES
        ),
        cost_estimate=pl.CostEstimate(
            flops=20 * rows * width * unit_rows,
            bytes_accessed=6 * unit_rows * width + 16 * rows * width,
            transcendentals=0,
        ),
        name="mix",
    )(
        seconds.reshape(2, 2, half, width), grads.reshape(2, 2, half, wide), experts, share_own, share_far, rest
    )
    return units.reshape(3, 2, rows, unit_rows), back.reshape(rows, wide), down_rows


def unit_grads_kernel(count, exp_units, share_rows, at, *refs):
    units, seconds, grads = refs[:count], refs[count : 2 * count], refs[2 * count : 3 * count]
    experts, share_own, share_far = refs[3 * count :]
    m = pl.program_id(0)

    def run(rights):
        acc = dot(units[0][...], rights[0][...], 0, 0)
        for left, right in zip(units[1:], rights[1:]):
            acc += dot(left[...], right[...], 0, 0)
        experts[0, 0] = acc[:exp_units].astype(bf16)
        size = share_own.shape[3]
        for s in range(share_own.shape[0]):
            piece = acc[exp_units : exp_units + 2 * share_rows, s * size : (s + 1) * size].astype(bf16)
            share_own[s, 0] = piece[:share_rows]
            share_far[s, 0] = piece[share_rows:]

    @pl.when(m < 2)
    def _():
        run(seconds)

    @pl.when(m == 2)
    def _():
        run(grads)


def unit_grads(at, units, seconds, grads, exp_units, share_rows):
    n_head, n_seq = lax.axis_size("head"), lax.axis_size("seq")
    width = seconds[0][0].shape[2]
    unit_rows = units[0][0].shape[3]
    head_part, seq_part = width // n_head, width // n_seq
    near = n_seq // n_head
    rows = sum(block.shape[1] for block, _ in seconds)

    def far(r, at):
        return jnp.bitwise_xor(at[0], r)

    def place(q, m, r, at):
        return (m, q, 0, 0)

    def second_place(q, m, r, at):
        return (q, 0, jnp.where(m < 2, far(r, at), far(n_head - 1, at)))

    def grad_place(q, m, r, at):
        return (q, 0, jnp.where(m < 2, far(0, at), far(r, at)))

    in_specs = [
        pl.BlockSpec((None, None, block.shape[2], unit_rows), functools.partial(place, q))
        for block, q in units
    ]
    in_specs += [
        pl.BlockSpec((None, block.shape[1], head_part), functools.partial(second_place, q))
        for block, q in seconds
    ]
    in_specs += [
        pl.BlockSpec((None, block.shape[1], head_part), functools.partial(grad_place, q))
        for block, q in grads
    ]
    share_spec = pl.BlockSpec((near, 1, share_rows, seq_part), lambda m, r, at: (far(r, at), m, 0, 0))
    share_shape = jax.ShapeDtypeStruct((n_seq, 3, share_rows, seq_part), bf16)
    return pl.pallas_call(
        functools.partial(unit_grads_kernel, len(units), exp_units, share_rows),
        grid_spec=pltpu.PrefetchScalarGridSpec(
            num_scalar_prefetch=1,
            grid=(3, n_head),
            in_specs=in_specs,
            out_specs=[
                pl.BlockSpec((1, 1, exp_units, head_part), lambda m, r, at: (r, m, 0, 0)),
                share_spec,
                share_spec,
            ],
        ),
        out_shape=[
            jax.ShapeDtypeStruct((n_head, 3, exp_units, head_part), bf16),
            share_shape,
            share_shape,
        ],
        compiler_params=pltpu.CompilerParams(vmem_limit_bytes=VMEM_BYTES),
        cost_estimate=pl.CostEstimate(
            flops=6 * rows * width * unit_rows,
            bytes_accessed=6 * rows * unit_rows + 8 * rows * width + 6 * width * unit_rows,
            transcendentals=0,
        ),
        name="unit_grads",
    )(at, *(block for block, _ in units + seconds + grads))


def products_kernel(
    units, seconds, grads, down_rows, out, experts, expert_in_down, share_all,
    u, sides, right, far_half, column, core_in, home, share, share_in, stage,
    u_sem, r_sem, d_sem, c_a, c_b, y_a, y_b, x_a, x_b, z_a, z_b, e_sem, o_sem,
):
    seq, n_seq = lax.axis_index("seq"), lax.axis_size("seq")
    near_x, near_y, near_core = plane_places()
    core = seq % 2
    width = right.shape[2]
    rows = column.shape[0]
    piece = rows // 2
    exp_units = experts.shape[2]
    share_rows, seq_part = share_all.shape[2:]
    head_part = experts.shape[3]
    n_head = width // head_part
    edge = exp_units // LANES * LANES
    tail = exp_units - edge
    slot = {2: 1, 0: 2, 1: 0}

    def load_units(m):
        return [
            pltpu.make_async_copy(
                units.at[m, q], u.at[pl.ds(q * 2 * rows, 2 * rows)], u_sem.at[m, q]
            )
            for q in range(2)
        ]

    def load_right(k):
        source = grads if k else seconds
        return [
            pltpu.make_async_copy(
                source.at[q, :, pl.ds(f * head_part, head_part)],
                right.at[k, pl.ds(q * 2 * rows, 2 * rows), pl.ds(f * head_part, head_part)],
                r_sem.at[k, q, f],
            )
            for q in range(2)
            for f in range(n_head)
        ]

    down = sides.at[0]
    load_down = pltpu.make_async_copy(down_rows, down, d_sem)
    rights = [load_right(0), load_right(1)]
    first = load_units(2)
    first[1].start()
    load_down.start()
    first[0].start()
    for copy in rights[1] + rights[0]:
        copy.start()
    greet(
        [{"head": near_x}, {"head": near_y}] + [{"seq": (seq + k) % n_seq} for k in range(1, n_seq)]
    )

    pieces = [pl.ds(j * piece, piece) for j in range(2)]
    to_core = [
        remote(far_half.at[0, at], core_in.at[at], c_a.at[j], c_b.at[j], seq=near_core)
        for j, at in enumerate(pieces)
    ]
    to_y = [
        remote(far_half.at[1, at], home.at[at], y_a.at[j], y_b.at[j], head=near_y)
        for j, at in enumerate(pieces)
    ]
    to_x = [
        remote(share.at[1, :, m], share_in.at[:, m], x_a.at[m], x_b.at[m], head=near_x)
        for m in range(3)
    ]
    cross = remote(experts.at[3, 2], expert_in_down, x_a.at[3], x_b.at[3], head=near_x)
    spread_out = [[] for _ in range(3)]
    spread_in = []
    spread_own = []
    for m in range(3):
        for k in range(1, n_seq):
            to, source = (seq + k) % n_seq, (seq + n_seq - k) % n_seq
            spread_out[m].append(
                remote(
                    share.at[0, to, m], share_all.at[seq, m], z_a.at[m, k], z_b.at[m, k], seq=to
                )
            )
            block = share_all.at[source, m]
            spread_in.append(remote(block, block, z_a.at[m, k], z_b.at[m, k], seq=to))
        spread_own.append(
            pltpu.make_async_copy(share.at[0, seq, m], share_all.at[seq, m], z_a.at[m, 0])
        )

    def spread_share(m):
        to_x[m].wait_recv()
        for place in range(n_seq):
            total = share[0, place, m].astype(f32) + share_in[place, m].astype(f32)
            share[0, place, m] = total.astype(bf16)
        for copy in spread_out[m]:
            copy.start()
        spread_own[m].start()

    def out_rows(start):
        return dot(u[pl.ds(pl.multiple_of(start, 16), piece), :], down[...], 1, 0)

    def turn_units(m):
        block = 2 * piece
        for k in range(u.shape[0] // block):
            at = slice(k * block, (k + 1) * block)
            sides[slot[m], :, at] = u[at, :].T

    def share_part(m):
        for f in range(n_head):
            for copy in rights[1 if m == 2 else 0][f::n_head] if m < 3 else []:
                if m != 1:
                    copy.wait()
            block = right[1 if m == 2 else 0, :, f * head_part : (f + 1) * head_part]
            acc = dot(sides[slot[m], edge:], block, 1, 0)
            for b in range(head_part // seq_part):
                part = acc[tail : tail + 2 * share_rows, b * seq_part : (b + 1) * seq_part]
                place = f * (head_part // seq_part) + b
                share[0, place, m] = part[:share_rows].astype(bf16)
                share[1, place, m] = part[share_rows:].astype(bf16)
        to_x[m].start()

    owners = plane_owners()
    writes = []

    def expert_part(r, m):
        n = len(writes)
        if n >= 2:
            writes[n - 2].wait()
        start = pl.multiple_of(owners[r] * head_part, head_part)
        acc = dot(
            sides[slot[m], :exp_units],
            right[1 if m == 2 else 0, :, pl.ds(start, head_part)],
            1,
            0,
        )
        stage[n % 2] = acc.astype(bf16)
        writes.append(pltpu.make_async_copy(stage.at[n % 2], experts.at[r, m], e_sem.at[n % 2]))
        writes[-1].start()

    def pass_on(j):
        to_core[j].wait_recv()
        total = far_half[1, pieces[j]].astype(f32) + core_in[pieces[j]].astype(f32)
        far_half[1, pieces[j]] = total.astype(bf16)
        to_y[j].start()

    first[1].wait()
    load_down.wait()
    for k, half in ((0, 1 - core), (1, core)):
        for j in range(2):
            far_half[k, pieces[j]] = out_rows(2 * rows + half * rows + j * piece).astype(bf16)
            if k == 0:
                to_core[j].start()
            else:
                pass_on(j)
    first[0].wait()
    turn_units(2)
    share_part(2)
    for copy in to_core:
        copy.wait_send()
    for j in range(2):
        far_half[0, pieces[j]] = out_rows((1 - core) * rows + j * piece).astype(bf16)
    write = [
        pltpu.make_async_copy(far_half.at[0], out.at[1 - core], o_sem.at[0]),
        pltpu.make_async_copy(column, out.at[core], o_sem.at[1]),
    ]
    write[0].start()
    for j in range(2):
        column[pieces[j]] = out_rows(core * rows + j * piece).astype(bf16)
    for i, m in enumerate((0, 1)):
        load = load_units(m)
        for copy in load:
            copy.start()
        expert_part(3, 0 if i else 2)
        for copy in load:
            copy.wait()
        turn_units(m)
        share_part(m)
        spread_share(0 if i else 2)
    expert_part(3, 1)
    cross.start()
    for m in (2, 0, 1):
        expert_part(1, m)
    for m in (2, 0, 1):
        expert_part(2, m)
    spread_share(1)
    for m in (2, 0, 1):
        expert_part(0, m)

    for j in range(2):
        to_y[j].wait_recv()
        column[pieces[j]] = (column[pieces[j]].astype(f32) + home[pieces[j]].astype(f32)).astype(bf16)
    write[1].start()
    for copy in to_x + to_y:
        copy.wait_send()
    cross.wait()
    for group in spread_out:
        for copy in group:
            copy.wait_send()
    for copy in spread_in:
        copy.wait_recv()
    for copy in writes[-2:] + write + spread_own:
        copy.wait()


def products(units, seconds, grads, down_rows, exp_units, share_rows):
    n_head, n_seq = lax.axis_size("head"), lax.axis_size("seq")
    _, rows, width = seconds.shape
    unit_rows = units.shape[3]
    half = rows // 2
    head_part, seq_part = width // n_head, width // n_seq
    anywhere = pl.BlockSpec(memory_space=pl.ANY)
    dma = pltpu.SemaphoreType.DMA
    share_shape = (n_seq, 3, share_rows, seq_part)
    return pl.pallas_call(
        products_kernel,
        in_specs=[anywhere] * 4,
        out_specs=[anywhere] * 4,
        out_shape=[
            jax.ShapeDtypeStruct((2, half, width), bf16),
            jax.ShapeDtypeStruct((n_head, 3, exp_units, head_part), bf16),
            jax.ShapeDtypeStruct((exp_units, head_part), bf16),
            jax.ShapeDtypeStruct(share_shape, bf16),
        ],
        scratch_shapes=[
            pltpu.VMEM((2 * rows, unit_rows), bf16),
            pltpu.VMEM((3, unit_rows, 2 * rows), bf16),
            pltpu.VMEM((2, 2 * rows, width), bf16),
            pltpu.VMEM((2, half, width), bf16),
            pltpu.VMEM((half, width), bf16),
            pltpu.VMEM((half, width), bf16),
            pltpu.VMEM((half, width), bf16),
            pltpu.VMEM((2, *share_shape), bf16),
            pltpu.VMEM(share_shape, bf16),
            pltpu.VMEM((2, exp_units, head_part), bf16),
            dma((3, 2)),
            dma((2, 2, n_head)),
            dma,
            *[dma((2,))] * 4,
            *[dma((4,))] * 2,
            *[dma((3, n_seq))] * 2,
            *[dma((2,))] * 2,
        ],
        compiler_params=pltpu.CompilerParams(
            collective_id=5, has_side_effects=True, vmem_limit_bytes=VMEM_BYTES
        ),
        cost_estimate=pl.CostEstimate(
            flops=16 * rows * width * unit_rows,
            bytes_accessed=40 * rows * width,
            transcendentals=0,
        ),
        name="products",
    )(units, seconds, grads, down_rows)


def finish_kernel(
    experts, expert_in, expert_in_down, share_all, partial, grad_middle, tokens, gain, small,
    grad_up, grad_down, grad_share_up, grad_share_down, input_grad, totals,
    near, far, far_in, near_in, last_in, pack, share_pack, incoming, slots,
    l_sem, x_a, x_b, y_a, y_b, s_a, s_b, t_a, t_b, p_sem,
):
    seq, head = lax.axis_index("seq"), lax.axis_index("head")
    near_x, near_y, near_core = plane_places()
    peers = ring_places()
    y = head // 2
    rows, width = grad_middle.shape
    units = near.shape[1]
    share_rows = share_all.shape[2]
    hidden = pack.shape[1]
    steps = [{"seq": near_core}]
    for bit in (2, 4):
        steps.append({"seq": seq + bit - 2 * bit * ((seq // bit) % 2)})
    steps += [{"head": near_x}, {"head": near_y}]

    loads = [
        [pltpu.make_async_copy(experts.at[2, m], far.at[m], l_sem.at[m]) for m in range(3)],
        [
            pltpu.make_async_copy(block, far_in.at[k], l_sem.at[3 + k])
            for k, block in enumerate((expert_in, expert_in_down))
        ],
        [pltpu.make_async_copy(experts.at[0, m], near.at[m], l_sem.at[5 + m]) for m in range(3)],
    ]
    for group in loads:
        for copy in group:
            copy.start()
    share_loads = [
        pltpu.make_async_copy(
            share_all.at[i], share_pack.at[:, pl.ds(i * share_rows, share_rows)], p_sem.at[i]
        )
        for i in range(share_all.shape[0])
    ]
    for copy in share_loads:
        copy.start()
    greet(steps + [{"head": peers[2] + 1 - 2 * (head % 2)}])
    scatter = [
        remote(
            partial.at[pl.ds(r * rows, rows)], incoming.at[r - 1], s_a.at[r - 1], s_b.at[r - 1],
            head=peers[r],
        )
        for r in range(1, len(peers))
    ]
    last = remote(experts.at[3, 1], last_in, x_a.at[3], x_b.at[3], head=near_x)
    sides = [
        remote(experts.at[1, m], near_in.at[m], x_a.at[m], x_b.at[m], head=near_x) for m in range(3)
    ]
    for copy in scatter + [last] + sides[:2]:
        copy.start()
    here = pl.ds(pl.multiple_of(y * units, 16), units)
    there = pl.ds(pl.multiple_of((1 - y) * units, 16), units)
    across = [
        remote(far.at[m], pack.at[m, here], y_a.at[m], y_b.at[m], head=near_y) for m in range(3)
    ]
    across_in = [
        remote(far.at[m], pack.at[m, there], y_a.at[m], y_b.at[m], head=near_y) for m in range(3)
    ]
    for k, m in enumerate((0, 2)):
        loads[0][m].wait()
        loads[1][k].wait()
        far[m] = (far[m].astype(f32) + far_in[k].astype(f32)).astype(bf16)
        across[m].start()
    loads[0][1].wait()
    for copy in loads[2]:
        copy.wait()

    for copy in scatter:
        copy.wait_recv()
    total = partial[:rows].astype(f32)
    for r in range(len(peers) - 1):
        total += incoming[r].astype(f32)
    x = tokens[...].astype(f32)
    inverse = lax.rsqrt(jnp.mean(x * x, axis=1, keepdims=True) + EPS)
    normed = x * inverse
    slots[0] = small[...]
    slots[0, 10:11] = jnp.sum(total * normed, axis=0, keepdims=True)
    grad_normed = total * gain[...].astype(f32)
    mean = jnp.mean(grad_normed * normed, axis=1, keepdims=True)
    input_grad[...] = grad_middle[...] + inverse * (grad_normed - normed * mean)

    exchanges = [
        remote(slots.at[2 * k], slots.at[2 * k + 1], t_a.at[k], t_b.at[k], **place)
        for k, place in enumerate(steps)
    ]

    def exchange(k):
        exchanges[k].wait_recv()
        slots[2 * k + 2] = slots[2 * k] + slots[2 * k + 1]
        if k + 1 < len(steps):
            exchanges[k + 1].start()

    exchanges[0].start()

    for copy in share_loads:
        copy.wait()
    grad_share_down[...] = share_pack[2]
    exchange(0)
    grad_share_up[:, :hidden] = share_pack[0].T
    exchange(1)
    grad_share_up[:, hidden:] = share_pack[1].T
    last.wait_recv()
    far[1] = (far[1].astype(f32) + last_in[...].astype(f32)).astype(bf16)
    across[1].start()
    exchange(2)
    sides[2].start()

    def place_block(m):
        sides[m].wait_recv()
        pack[m, here] = (near[m].astype(f32) + near_in[m].astype(f32)).astype(bf16)
        across_in[m].wait_recv()
        if m < 2:
            grad_up[:, m * hidden : (m + 1) * hidden] = pack[m].T
        else:
            grad_down[...] = pack[m]

    place_block(0)
    exchange(3)
    place_block(1)
    exchange(4)
    totals[...] = slots[2 * len(steps)]
    place_block(2)
    for copy in scatter + exchanges + sides + across + [last]:
        copy.wait_send()


def finish(experts, expert_in, expert_in_down, share_all, partial, grad_middle, tokens, gain, small):
    n_head, n_seq = lax.axis_size("head"), lax.axis_size("seq")
    rows, width = tokens.shape
    _, _, units, head_part = experts.shape
    share_rows, seq_part = share_all.shape[2:]
    hidden, share_units = 2 * units, n_seq * share_rows
    anywhere = pl.BlockSpec(memory_space=pl.ANY)
    vmem = pl.BlockSpec(memory_space=pltpu.VMEM)
    dma = pltpu.SemaphoreType.DMA
    return pl.pallas_call(
        finish_kernel,
        in_specs=[anywhere] * 4 + [vmem] * 5,
        out_specs=[vmem] * 6,
        out_shape=[
            jax.ShapeDtypeStruct((head_part, 2 * hidden), bf16),
            jax.ShapeDtypeStruct((hidden, head_part), bf16),
            jax.ShapeDtypeStruct((seq_part, 2 * share_units), bf16),
            jax.ShapeDtypeStruct((share_units, seq_part), bf16),
            jax.ShapeDtypeStruct((rows, width), f32),
            jax.ShapeDtypeStruct(small.shape, f32),
        ],
        scratch_shapes=[
            pltpu.VMEM((3, units, head_part), bf16),
            pltpu.VMEM((3, units, head_part), bf16),
            pltpu.VMEM((2, units, head_part), bf16),
            pltpu.VMEM((3, units, head_part), bf16),
            pltpu.VMEM((units, head_part), bf16),
            pltpu.VMEM((3, hidden, head_part), bf16),
            pltpu.VMEM((3, share_units, seq_part), bf16),
            pltpu.VMEM((n_head - 1, rows, width), bf16),
            pltpu.VMEM((11, *small.shape), f32),
            dma((8,)),
            *[dma((4,))] * 2,
            *[dma((3,))] * 2,
            *[dma((n_head - 1,))] * 2,
            *[dma((5,))] * 2,
            dma((n_seq,)),
        ],
        compiler_params=pltpu.CompilerParams(
            collective_id=6, has_side_effects=True, vmem_limit_bytes=VMEM_BYTES
        ),
        cost_estimate=pl.CostEstimate(flops=0, bytes_accessed=1 << 27, transcendentals=0),
        name="finish",
    )(experts, expert_in, expert_in_down, share_all, partial, grad_middle, tokens, gain, small)


def after(value, *others):
    return lax.optimization_barrier((value, *others))[0]


def shards(
    tokens,
    cotangent,
    arrange,
    doc_lengths,
    routes,
    norm1_gain,
    qkv_weight,
    qkv_bias,
    out_weight,
    norm2_gain,
    router_weight,
    shared_gate_vec,
    shared_gate_up,
    shared_down,
    expert_gate_up,
    expert_down,
):
    highest = lax.Precision.HIGHEST
    tok_rows, width = tokens.shape
    n_seq = lax.axis_size("seq")
    n_head = lax.axis_size("head")
    seq = lax.axis_index("seq")
    head = lax.axis_index("head")
    group_tok = tok_rows * n_head
    heads_here = qkv_weight.shape[1]
    n_exp = router_weight.shape[1]
    hidden_all = expert_down.shape[1]
    parts = n_head // 2
    part = mesh_part()
    exp_units = hidden_all // parts
    share_all = shared_down.shape[0]
    share_units = share_all // n_seq
    share_rows = -(-share_units // 16) * 16
    base = exp_units + 2 * share_rows
    unit_rows = -(-(base + n_exp + 1) // LANES) * LANES
    seq_part = width // n_seq
    head_part = width // n_head

    wide = heads_here * HD
    plane = parts == 2 and n_seq == 8 and 2 * n_seq * tok_rows == width
    expert_up = expert_gate_up[0]
    at = jnp.stack([head, seq]).astype(jnp.int32)
    gate_rows = jnp.concatenate([router_weight.T, shared_gate_vec[None, :]], axis=0)

    place, doc_index, position = layout_of(arrange[0], doc_lengths[0], group_tok)
    blocks = (head + jnp.arange(n_head, dtype=jnp.int32)) % n_head
    table = jnp.stack([place, doc_index, position]).reshape(3, n_head, tok_rows)
    place, doc_index, position = jnp.take(table, blocks, axis=1).reshape(3, group_tok)
    layout = jnp.stack([doc_index, place]).astype(f32)
    cosine, sine = rope_tables(position.astype(f32))

    expert_ids = jnp.arange(n_exp, dtype=jnp.int32)
    chosen = jnp.any(routes[:, :, None] == expert_ids[None, None, :], axis=1)
    marks = jnp.concatenate(
        [chosen.astype(bf16), jnp.zeros((tok_rows, LANES - n_exp), bf16)], axis=1
    )

    stream = tokens.astype(f32)
    gain_first = norm1_gain.astype(f32)
    scale_first = rms_scale(stream)
    normed_first = stream * scale_first
    gain_second = norm2_gain.astype(f32)
    weight_own = qkv_weight.reshape(seq_part, 3 * wide)
    if plane:
        (
            first_group, weight, wout, experts, share_own, share_far, grad_both, seconds,
            qkv, merged, log_total, middle, lowered_second,
        ) = forward(
            tokens, norm1_gain[None, :], norm2_gain[None, :], weight_own, out_weight, expert_up,
            expert_down[0], shared_gate_up.reshape(seq_part, 2 * share_all), shared_down, cotangent,
            marks, qkv_bias, cosine, sine, layout,
        )
        grad_both = grad_both.reshape(2, n_seq * tok_rows, width + LANES)
        seconds = seconds.reshape(2, n_seq * tok_rows, width)
        units, back_column, down_rows = mix(
            seconds,
            grad_both,
            experts,
            share_own,
            share_far,
            jnp.pad(gate_rows, ((0, -(n_exp + 1) % 16), (0, 0))),
            exp_units,
            base,
            n_exp,
            unit_rows,
        )
        out_column, grad_experts, expert_in_down, share_parts = products(
            units, seconds, grad_both, down_rows, exp_units, share_rows
        )
        back_own = lax.psum_scatter(back_column, "seq", scatter_dimension=0, tiled=True)
    else:
        grad_ext = jnp.concatenate([cotangent, marks], axis=1)
        rest = jnp.zeros((3, unit_rows - base, width), bf16).at[0, : n_exp + 1].set(gate_rows)
        bias_here = lax.dynamic_slice_in_dim(qkv_bias, head * heads_here, heads_here, 0)
        bias_here = bias_here.astype(f32)[:, None, :]
        weight = lax.all_gather(weight_own, "seq", axis=0, tiled=True)
        wout = lax.all_gather(out_weight, "seq", axis=0)
        first_group = group_gather((normed_first * gain_first).astype(bf16))
        send = jnp.stack([expert_up[:, :hidden_all].T, expert_up[:, hidden_all:].T, expert_down[0]])
        near = []
        for t in range(parts):
            there = jnp.bitwise_xor(part, t)
            block = lax.dynamic_slice_in_dim(send, there * exp_units, exp_units, 1)
            near.append(swap(block, "head", 2 * t) if t else block)
        experts = jnp.stack([block for own in near for block in (own, swap(own, "head", 1))])
        send = jnp.stack([shared_gate_up[:, 0].T, shared_gate_up[:, 1].T, shared_down])
        send = jnp.transpose(send.reshape(3, n_seq, share_units, seq_part), (1, 0, 2, 3))
        if share_rows > share_units:
            send = jnp.pad(send, ((0, 0), (0, 0), (0, share_rows - share_units), (0, 0)))
        share_own = lax.all_to_all(send, "seq", split_axis=0, concat_axis=0)
        full = pack(at, experts, [share_own, swap(share_own, "head", 1)], rest, unit_rows)
        qkv, merged, log_total, middle, lowered_second = attend(
            first_group, weight, wout, bias_here, cosine, sine, layout, tokens,
            gain_second[None, :],
        )
        grad_chunks = token_gather(grad_ext)
        second_chunks = token_gather(lowered_second)
        back_chunks = []
        unit_chunks = []
        for second, grad in zip(second_chunks, grad_chunks):
            back, units = mix_local(second, grad, full, exp_units, base, n_exp)
            back_chunks.append(back)
            unit_chunks.append(units)
        grad_experts, grad_share, grad_share_far = unit_grads(
            at,
            [(units[:, None], 0) for units in unit_chunks],
            [(second[None], 0) for second in second_chunks],
            [(grad[None], 0) for grad in grad_chunks],
            exp_units,
            share_rows,
        )
        out_chunks = [dot(units[2], full[2], 1, 0).astype(bf16) for units in unit_chunks]
        back_own = token_scatter(back_chunks)
        out_own = token_scatter(out_chunks)
    scale_second = rms_scale(middle)
    normed_second = middle * scale_second

    back_own = after(back_own, grad_experts).astype(f32)

    logits = dot(lowered_second, gate_rows, 1, 1)
    probs = jax.nn.softmax(logits[:, :n_exp], axis=-1)
    share_gate = jax.nn.sigmoid(logits[:, n_exp:])
    grad_probs = back_own[:, width : width + n_exp]
    grad_logits = probs * (grad_probs - jnp.sum(probs * grad_probs, axis=1, keepdims=True))
    grad_gate_logit = (
        back_own[:, width + n_exp : width + n_exp + 1] * share_gate * (1.0 - share_gate)
    )
    grad_gates = jnp.concatenate([grad_logits, grad_gate_logit], axis=1)
    grad_second = back_own[:, :width] + jnp.dot(
        grad_gates, gate_rows.astype(f32), precision=highest
    )
    grad_gate_cols = jnp.dot(grad_gates.T, lowered_second.astype(f32), precision=highest)
    grad_gain_second = jnp.sum(grad_second * normed_second, axis=0)
    grad_normed = grad_second * gain_second
    grad_middle = cotangent.astype(f32) + scale_second * (
        grad_normed - normed_second * jnp.mean(grad_normed * normed_second, axis=1, keepdims=True)
    )
    grad_attn = grad_middle.astype(bf16)
    if plane:
        out_own = lax.psum_scatter(
            after(out_column, grad_attn).reshape(n_seq * tok_rows, width),
            "seq",
            scatter_dimension=0,
            tiled=True,
        )
    mixed = (middle + out_own.astype(f32)).astype(bf16)
    back_args = (
        grad_attn, first_group, weight, wout, qkv, merged, log_total, cosine, sine, layout
    )
    if plane:
        grad_first, grad_weight, grad_bias_here, expert_in = attend_back(
            *back_args, extra=(grad_experts,)
        )
    else:
        grad_first, grad_weight, grad_bias_here = attend_back(*back_args)
    grad_weight = lax.psum_scatter(grad_weight, "seq", scatter_dimension=0, tiled=False)
    grad_bias = lax.dynamic_update_slice_in_dim(
        jnp.zeros(qkv_bias.shape, f32), grad_bias_here[:, 0], head * heads_here, 0
    )
    small = jnp.concatenate(
        [grad_gate_cols, grad_gain_second[None, :], jnp.zeros((1, width), f32), grad_bias.reshape(-1, width)],
        axis=0,
    )
    if plane:
        small = jnp.pad(small, ((0, 16 - small.shape[0]), (0, 0)))
        own_up, own_down, grad_share_up, grad_share_down, input_grad, totals = finish(
            grad_experts, expert_in, expert_in_down, share_parts, grad_first, grad_middle, tokens, norm1_gain[None, :],
            small,
        )
    else:
        grad_first = group_scatter(grad_first)
        small = small.at[n_exp + 2].set(jnp.sum(grad_first * normed_first, axis=0))
        grad_normed_first = grad_first * gain_first
        input_grad = grad_middle + scale_first * (
            grad_normed_first
            - normed_first * jnp.mean(grad_normed_first * normed_first, axis=1, keepdims=True)
        )
        totals = total_over_all(small)
        grad_share = grad_share + swap(grad_share_far, "head", 1)
        grad_share = lax.all_to_all(grad_share[:, :, :share_units], "seq", split_axis=0, concat_axis=0)
        grad_share = jnp.transpose(grad_share, (1, 0, 2, 3)).reshape(3, share_all, seq_part)
        own = {}
        for t in range(parts)[::-1]:
            total = grad_experts[2 * t] + swap(grad_experts[2 * t + 1], "head", 1)
            own[t] = swap(total, "head", 2 * t) if t else total
        own = jnp.stack([own[t] for t in range(parts)])
        own = jnp.take(own, jnp.bitwise_xor(part, jnp.arange(parts, dtype=jnp.int32)), axis=0)
        own = jnp.transpose(own, (1, 0, 2, 3)).reshape(3, hidden_all, head_part)
        own_up, own_down = jnp.concatenate([own[0].T, own[1].T], axis=1), own[2]
        grad_share_up = jnp.concatenate([grad_share[0].T, grad_share[1].T], axis=1)
        grad_share_down = grad_share[2]
    return (
        mixed,
        input_grad,
        totals[n_exp + 2],
        grad_weight[: 3 * wide].astype(f32).T.reshape(qkv_weight.shape),
        totals[n_exp + 3 : n_exp + 3 + 3].reshape(qkv_bias.shape),
        grad_weight[3 * wide :].astype(f32),
        totals[n_exp + 1],
        totals[:n_exp].T,
        totals[n_exp],
        grad_share_up.reshape(shared_gate_up.shape).astype(f32),
        grad_share_down.astype(f32),
        own_up.astype(f32)[None],
        own_down.astype(f32)[None],
    )


def solution(mesh):
    return jax.shard_map(
        shards,
        mesh=mesh,
        in_specs=(
            P(("seq", "head"), None),
            P(("seq", "head"), None),
            P("seq", None),
            P("seq", None),
            P(("seq", "head"), None),
            P(),
            P("seq", "head", None),
            P(),
            P("head", "seq"),
            P(),
            P(),
            P(),
            P("seq", None, "head"),
            P("head", "seq"),
            P("seq", "head", None),
            P("seq", None, "head"),
        ),
        out_specs=(
            P(("seq", "head"), None),
            P(("seq", "head"), None),
            P(),
            P("seq", "head", None),
            P(),
            P("head", "seq"),
            P(),
            P(),
            P(),
            P("seq", None, "head"),
            P("head", "seq"),
            P("seq", "head", None),
            P("seq", None, "head"),
        ),
        check_vma=False,
    )
```

```python
import functools
import math

import jax
import jax.numpy as jnp
from jax import lax
from jax.experimental import pallas as pl
from jax.experimental.pallas import tpu as pltpu
from jax.sharding import PartitionSpec as P

HD = 128
EPS = 1e-06
THETA = 1000000.0
NEGATIVE = -1e30
LANES = 128
TILE = 256
MESH = pl.DeviceIdType.MESH
VMEM_BYTES = 61 * 1024 * 1024
bf16 = jnp.bfloat16
f32 = jnp.float32


def rms_scale(values):
    return lax.rsqrt(jnp.mean(values * values, axis=-1, keepdims=True) + EPS)


def rope_tables(position):
    half = HD // 2
    exponent = jnp.arange(half, dtype=f32) * (2.0 / HD)
    frequency = THETA ** (-exponent)
    angle = position[:, None] * frequency[None, :]
    return (jnp.cos(angle), jnp.sin(angle))


def layout_of(arrange_row, length_row, group_tok):
    counter = jnp.arange(group_tok, dtype=jnp.int32)
    place = jnp.sum(
        jnp.where(arrange_row[None, :] == counter[:, None], counter[None, :], 0),
        axis=1,
        dtype=jnp.int32,
    )
    doc_index = jnp.zeros_like(place)
    start = jnp.zeros_like(place)
    end = jnp.int32(0)
    for k in range(length_row.shape[0]):
        end = end + length_row[k]
        doc_index += (place >= end).astype(jnp.int32)
        start += jnp.where(place >= end, length_row[k], 0)
    return (place, doc_index, place - start)


def dot(left, right, left_dim, right_dim):
    return lax.dot_general(
        left, right, (((left_dim,), (right_dim,)), ((), ())), preferred_element_type=f32
    )


def swap(block, axis, bit):
    size = lax.axis_size(axis)
    return lax.ppermute(block, axis, [(i, i ^ bit) for i in range(size)])


def bits_of(size):
    bits = []
    bit = 1
    while bit < size:
        bits.append(bit)
        bit *= 2
    return bits


def spread(block, order):
    found = {0: block}
    for bit in order:
        for near in sorted(found):
            found[near ^ bit] = swap(found[near], "head", bit)
    return found


def collect(parts, order):
    parts = dict(parts)
    for bit in reversed(order):
        for far in sorted((r for r in parts if r & bit), reverse=True):
            parts[far ^ bit] = parts[far ^ bit] + swap(parts.pop(far), "head", bit)
    return parts[0]


def shift(block, axis, step):
    size = lax.axis_size(axis)
    return lax.ppermute(block, axis, [((i + step) % size, i) for i in range(size)])


def group_gather(block):
    size = lax.axis_size("head")
    return jnp.concatenate([block] + [shift(block, "head", r) for r in range(1, size)], axis=0)


def group_scatter(block):
    size = lax.axis_size("head")
    rows = block.shape[0] // size
    total = block[:rows].astype(f32)
    for r in range(1, size):
        total += shift(block[r * rows : (r + 1) * rows], "head", size - r).astype(f32)
    return total


def remote(src, dst, send_sem, recv_sem, **place):
    return pltpu.make_async_remote_copy(
        src_ref=src,
        dst_ref=dst,
        send_sem=send_sem,
        recv_sem=recv_sem,
        device_id=place,
        device_id_type=MESH,
    )


def greet(places):
    barrier = pltpu.get_barrier_semaphore()
    for place in places:
        pl.semaphore_signal(barrier, inc=1, device_id=place, device_id_type=MESH)
    pl.semaphore_wait(barrier, len(places))


def plane_places():
    head, seq = lax.axis_index("head"), lax.axis_index("seq")
    x, y = head % 2, head // 2
    return y * 2 + (1 - x), (1 - y) * 2 + x, seq + 1 - 2 * (seq % 2)


def plane_owners():
    head = lax.axis_index("head")
    near_x, near_y, _ = plane_places()
    return head, near_x, near_y, near_y + 1 - 2 * (head % 2)


def ring_places():
    size = lax.axis_size("head")
    head = lax.axis_index("head")
    return [(head + r) % size for r in range(size)]


class Line:
    def __init__(self, place, far, sems):
        self.seq = lax.axis_index("seq")
        self.count = lax.axis_size("seq") // 2
        self.depth = self.count - 1
        self.z = self.seq // 2
        _, self.near_y, self.near_core = plane_places()
        self.place, self.far = place, far
        self.sems = sems

    def index(self, j):
        if j == 0:
            return self.seq
        if j <= self.depth:
            return self.seq - 2 * j
        return self.seq + 2 * (j - self.depth)

    def valid(self, j):
        if j == 0:
            return self.z >= 0
        if j <= self.depth:
            return self.z - j >= 0
        return self.z + (j - self.depth) < self.count

    def line_copy(self, j, up):
        block = self.place(self.index(j))
        if up:
            to, k = self.seq + 2, j
        else:
            to, k = self.seq - 2, self.depth + (j - self.depth if j else 0)
        return remote(block, block, self.sems.at[0, k], self.sems.at[1, k], seq=to)

    def line_arrival(self, j):
        block = self.place(self.index(j))
        return remote(
            block, block, self.sems.at[0, j - 1], self.sems.at[1, j - 1], seq=self.near_core
        )

    def core_copy(self, j):
        block = self.place(self.index(j))
        return remote(block, block, self.sems.at[2, j], self.sems.at[3, j], seq=self.near_core)

    def core_arrival(self, j):
        block = self.place(self.index(j) + self.near_core - self.seq)
        return remote(block, block, self.sems.at[2, j], self.sems.at[3, j], seq=self.near_core)

    def far_copy(self, j):
        i = self.index(j)
        return remote(
            self.place(i), self.far(i), self.sems.at[4, j], self.sems.at[5, j], head=self.near_y
        )

    def far_core_copy(self, j):
        there = self.far(self.index(j))
        return remote(there, there, self.sems.at[6, j], self.sems.at[7, j], seq=self.near_core)

    def far_core_arrival(self, j):
        there = self.far(self.index(j) + self.near_core - self.seq)
        return remote(there, there, self.sems.at[6, j], self.sems.at[7, j], seq=self.near_core)

    def sides(self, j):
        self.core_copy(j).start()
        if self.far is not None:
            self.far_copy(j).start()

    def ups(self):
        return range(self.depth)

    def downs(self):
        return [0] + [self.depth + k for k in range(1, self.depth)]

    def has_above(self):
        return self.z + 1 < self.count

    def has_below(self):
        return self.z >= 1

    def begin(self):
        @pl.when(self.has_above())
        def _():
            self.line_copy(0, True).start()

        @pl.when(self.has_below())
        def _():
            self.line_copy(0, False).start()

        self.sides(0)

    def step(self, k):
        @pl.when(self.valid(1 + k))
        def _():
            self.line_arrival(1 + k).wait_recv()
            if 1 + k < self.depth:

                @pl.when(self.has_above())
                def _():
                    self.line_copy(1 + k, True).start()

            self.sides(1 + k)

        @pl.when(self.valid(self.depth + 1 + k))
        def _():
            self.line_arrival(self.depth + 1 + k).wait_recv()
            if 1 + k < self.depth:

                @pl.when(self.has_below())
                def _():
                    self.line_copy(self.depth + 1 + k, False).start()

            self.sides(self.depth + 1 + k)

    def side_step(self, j):
        @pl.when(self.valid(j))
        def _():
            self.far_copy(j).wait_recv()
            self.far_core_copy(j).start()

    def wait_blocks(self):
        for j in range(2 * self.depth + 1):

            @pl.when(self.valid(j))
            def _():
                self.core_arrival(j).wait_recv()
                if self.far is not None:
                    self.far_core_arrival(j).wait_recv()

    def wait_sends(self):
        for j in range(2 * self.depth + 1):

            @pl.when(self.valid(j))
            def _():
                self.core_copy(j).wait_send()
                if self.far is not None:
                    self.far_copy(j).wait_send()
                    self.far_core_copy(j).wait_send()

        for j in self.ups():

            @pl.when(self.valid(j) & self.has_above())
            def _():
                self.line_copy(j, True).wait_send()

        for j in self.downs():

            @pl.when(self.valid(j) & self.has_below())
            def _():
                self.line_copy(j, False).wait_send()


def forward_kernel(
    tokens, gains, weight_own, wout_own, expert_up, expert_down, share_up, share_down,
    cotangent, marks, bias, arrange, lengths,
    first_out, weight_out, wout_out, experts, share, share_far, grads, seconds, qkv, merged, log_total, middle,
    lowered, cosine, sine, layout,
    group, weight, wout, expert_raw, expert_pack, share_raw, share_pack, mask, outgoing, incoming,
    local, line_w, line_o, line_g, line_s, ring_a, ring_b, sc_a, sc_b, ex_a, ex_b, sh_a, sh_b,
):
    seq, head = lax.axis_index("seq"), lax.axis_index("head")
    n_seq = lax.axis_size("seq")
    near_x, near_y, near_core = plane_places()
    peers = ring_places()
    size = len(peers)
    rows, width = tokens.shape
    heads = qkv.shape[1] // (3 * HD)
    units = experts.shape[2]
    y = head // 2
    share_rows = share.shape[2]
    hidden = expert_down.shape[0]
    part = weight_own.shape[0]

    fetch = [
        pltpu.make_async_copy(
            weight_own, weight.at[pl.ds(pl.multiple_of(seq * part, 16), part)], local.at[0]
        ),
        pltpu.make_async_copy(wout_own, wout.at[seq], local.at[1]),
        pltpu.make_async_copy(expert_up, expert_raw, local.at[2]),
        pltpu.make_async_copy(expert_down, expert_pack.at[2], local.at[3]),
        pltpu.make_async_copy(share_up, share_raw, local.at[4]),
        pltpu.make_async_copy(share_down, share_pack.at[2], local.at[5]),
        pltpu.make_async_copy(cotangent, grads.at[0, seq, :, pl.ds(0, width)], local.at[6]),
        pltpu.make_async_copy(marks, grads.at[0, seq, :, pl.ds(width, marks.shape[1])], local.at[13]),
    ]
    for copy in fetch:
        copy.start()
    greet(
        [{"head": peer} for peer in peers[1:]]
        + [{"seq": (seq + k) % n_seq} for k in range(1, n_seq)]
    )

    gather_w = Line(lambda i: weight.at[pl.ds(pl.multiple_of(i * part, 16), part)], None, line_w)
    gather_o = Line(lambda i: wout.at[i], None, line_o)
    gather_g = Line(lambda i: grads.at[0, i], lambda i: grads.at[1, i], line_g)
    gather_s = Line(lambda i: seconds.at[0, i], lambda i: seconds.at[1, i], line_s)
    fetch[0].wait()
    gather_w.begin()
    fetch[1].wait()
    gather_o.begin()

    group[:rows] = norm_rows(tokens[...].astype(f32), gains[0:1, :].astype(f32))
    ring = [
        remote(
            group.at[pl.ds(0, rows)], group.at[pl.ds(r * rows, rows)],
            ring_a.at[r - 1], ring_b.at[r - 1], head=peers[size - r],
        )
        for r in range(1, size)
    ]
    for copy in ring:
        copy.start()

    fetch[2].wait()
    fetch[3].wait()
    mine = pl.ds(pl.multiple_of(y * units, 16), units)
    other = pl.ds(pl.multiple_of((1 - y) * units, 16), units)
    ups = [
        remote(expert_pack.at[m, other], experts.at[2, m], ex_a.at[m], ex_b.at[m], head=near_y)
        for m in range(3)
    ]
    sides = [
        remote(expert_pack.at[m, mine], experts.at[1, m], ex_a.at[3 + m], ex_b.at[3 + m], head=near_x)
        for m in range(3)
    ]
    ons = [
        remote(experts.at[2, m], experts.at[3, m], ex_a.at[6 + m], ex_b.at[6 + m], head=near_x)
        for m in range(3)
    ]
    order = (2, 0, 1)
    for m in order:
        if m < 2:
            expert_pack[m] = expert_raw[:, m * hidden : (m + 1) * hidden].T
        ups[m].start()
        sides[m].start()
    keep = [pltpu.make_async_copy(expert_pack.at[:, mine], experts.at[0], local.at[7])]
    keep[0].start()

    fetch[4].wait()
    fetch[5].wait()
    for m in range(2):
        share_pack[m] = share_raw[:, m * hidden : (m + 1) * hidden].T

    def share_block(i):
        return share_pack.at[:, pl.ds(pl.multiple_of(i * share_rows, 16), share_rows)]

    share_own = pltpu.make_async_copy(share_block(seq), share.at[seq], local.at[8])
    share_own.start()
    z, depth = seq // 2, n_seq // 2

    def share_send(distance, up, flip):
        to = (seq + 2 * distance if up else seq - 2 * distance) + flip * (near_core - seq)
        j = (2 * distance + up) * 2 + flip
        return remote(share_block(to), share.at[seq], sh_a.at[j], sh_b.at[j], seq=to)

    def share_source(distance, up, flip):
        return (seq - 2 * distance if up else seq + 2 * distance) + flip * (near_core - seq)

    def share_arrival(distance, up, flip):
        j = (2 * distance + up) * 2 + flip
        block = share.at[share_source(distance, up, flip)]
        return remote(block, block, sh_a.at[j], sh_b.at[j], seq=near_core)

    def share_cross(distance, up, flip):
        source = share_source(distance, up, flip)
        j = 4 * depth + (2 * distance + up) * 2 + flip
        return remote(
            share.at[source], share_far.at[source], sh_a.at[j], sh_b.at[j], head=near_x
        )

    def each_share(distance, arriving, act):
        if distance == 0:
            act(0, 1, 1)
            return
        for up in (0, 1):
            below = z >= distance
            above = z + distance < depth
            there = (below if up else above) if arriving else (above if up else below)

            @pl.when(there)
            def _():
                for flip in (0, 1):
                    act(distance, up, flip)

    def share_on(distance):
        def act(*at):
            share_arrival(*at).wait_recv()
            share_cross(*at).start()

        each_share(distance, True, act)

    total_rows = group.shape[0]
    row = lax.broadcasted_iota(jnp.int32, mask.shape, 0) + head * rows
    row = jnp.where(row >= total_rows, row - total_rows, row)
    at_place = lax.broadcasted_iota(jnp.int32, mask.shape, 1).astype(f32)
    place = jnp.sum(jnp.where(arrange[...] == row, at_place, 0.0), axis=1, keepdims=True)
    doc = jnp.zeros_like(place)
    start = jnp.zeros_like(place)
    end = jnp.float32(0)
    for k in range(lengths.shape[1]):
        length = lengths[0, k].astype(f32)
        end = end + length
        doc += jnp.where(place >= end, 1.0, 0.0)
        start += jnp.where(place >= end, length, 0.0)
    lane = lax.broadcasted_iota(jnp.int32, (total_rows, HD), 1)
    half = HD // 2
    exponent = jnp.where(lane < half, lane, lane - half).astype(f32) * (-2.0 / HD)
    angle = (place - start) * jnp.exp(exponent * math.log(THETA))
    sines = jnp.sin(angle)
    cosine[...] = jnp.cos(angle)
    sine[...] = jnp.where(lane < half, -sines, sines)
    layout[...] = jnp.where(lane == 0, doc, jnp.where(lane == 1, place, 0.0)).T[:2]
    same = (doc == layout[0:1, :]) & (layout[1:2, :] <= place)
    mask[...] = jnp.where(same, 0.0, NEGATIVE)
    gather_w.step(0)
    gather_o.step(0)
    gather_w.step(1)
    gather_o.step(1)
    ups[2].wait_recv()
    ons[2].start()
    fetch[6].wait()
    fetch[7].wait()
    gather_w.step(2)
    gather_o.step(2)
    gather_g.begin()
    for distance in range(depth):
        each_share(distance, False, lambda *at: share_send(*at).start())
    for copy in ring:
        copy.wait_recv()
    gather_w.wait_blocks()
    gather_o.wait_blocks()
    keep += [
        pltpu.make_async_copy(weight, weight_out, local.at[9]),
        pltpu.make_async_copy(wout, wout_out, local.at[10]),
        pltpu.make_async_copy(group, first_out, local.at[11]),
    ]
    for copy in keep[1:]:
        copy.start()

    step = 3 * HD
    cos, sin = cosine[...], sine[...]
    every_bias = bias[...].astype(f32)
    bias_row = lax.broadcasted_iota(jnp.int32, every_bias.shape, 0)
    for n in range(heads):
        shift_row = jnp.where(bias_row == head * heads + n, every_bias, 0.0)
        linear = dot(group[...], weight[:, n * step : (n + 1) * step], 1, 0)
        linear = linear + jnp.sum(shift_row, axis=0, keepdims=True)
        parts, output, log_sum = head_forward(linear, cos, sin, mask[...])
        for k in range(3):
            qkv[:, n * step + k * HD : n * step + (k + 1) * HD] = parts[k]
        merged[:, n * HD : (n + 1) * HD] = output
        log_total[n] = jnp.broadcast_to(log_sum, log_total.shape[1:])
        if n == 2:
            gather_g.step(0)
            gather_g.side_step(0)
    copies, own = scatter_start(merged, wout, outgoing, incoming, sc_a, sc_b, rows, peers)
    ups[0].wait_recv()
    ons[0].start()
    block = wout.shape[2]
    for b in range(len(own)):
        cols = slice(b * block, (b + 1) * block)
        middle[:, cols] = tokens[:, cols].astype(f32) + own[b]
    gather_g.step(1)
    for copy in copies:
        copy.wait_recv()
    total = middle[...]
    for r in range(size - 1):
        total += incoming[r].astype(f32)
    middle[...] = total
    lowered[...] = norm_rows(total, gains[1:2, :].astype(f32))
    last = pltpu.make_async_copy(lowered, seconds.at[0, seq], local.at[12])
    last.start()
    last.wait()
    gather_s.begin()
    ups[1].wait_recv()
    ons[1].start()

    share_own.wait()
    cross_own = remote(share.at[seq], share_far.at[seq], sh_a.at[0], sh_b.at[0], head=near_x)
    cross_own.start()
    gather_g.step(2)
    share_on(0)
    share_on(1)
    for j in (1, 1 + gather_g.depth, 2, 2 + gather_g.depth):
        gather_g.side_step(j)
    gather_s.step(0)
    share_on(2)
    for j in (3, 3 + gather_g.depth):
        gather_g.side_step(j)
    gather_s.side_step(0)
    gather_s.step(1)
    for j in (1, 1 + gather_g.depth):
        gather_s.side_step(j)
    gather_s.step(2)
    share_on(3)
    for j in (2, 2 + gather_g.depth, 3, 3 + gather_g.depth):
        gather_s.side_step(j)

    gather_g.wait_blocks()
    gather_s.wait_blocks()
    for copy in sides + ons + [cross_own]:
        copy.wait()
    for distance in range(depth):
        each_share(distance, True, lambda *at: share_cross(*at).wait())
        each_share(distance, False, lambda *at: share_send(*at).wait_send())
    for copy in ups + ring + copies:
        copy.wait_send()
    for copy in keep:
        copy.wait()
    for line in (gather_w, gather_o, gather_g, gather_s):
        line.wait_sends()


def forward(
    tokens, gains, weight_own, wout_own, expert_up, expert_down, share_up, share_down,
    cotangent, marks, bias, arrange, lengths,
):
    n_seq, n_head = lax.axis_size("seq"), lax.axis_size("head")
    rows, width = tokens.shape
    group_tok = rows * n_head
    wide = wout_own.shape[0]
    heads = wide // HD
    part = weight_own.shape[0]
    hidden, head_part = expert_down.shape
    units = hidden // 2
    share_all, seq_part = share_down.shape
    share_rows = share_all // n_seq
    ext = width + marks.shape[1]
    anywhere = pl.BlockSpec(memory_space=pl.ANY)
    vmem = pl.BlockSpec(memory_space=pltpu.VMEM)
    dma = pltpu.SemaphoreType.DMA
    lines = n_seq - 1

    def hbm(*shape):
        return (anywhere, jax.ShapeDtypeStruct(shape, bf16))

    outs = [
        hbm(group_tok, width),
        hbm(width, 3 * wide),
        hbm(n_seq, wide, part),
        hbm(4, 3, units, head_part),
        hbm(n_seq, 3, share_rows, seq_part),
        hbm(n_seq, 3, share_rows, seq_part),
        hbm(2, n_seq, rows, ext),
        hbm(2, n_seq, rows, width),
        (vmem, jax.ShapeDtypeStruct((group_tok, 3 * wide), bf16)),
        (vmem, jax.ShapeDtypeStruct((group_tok, wide), bf16)),
        (vmem, jax.ShapeDtypeStruct((heads, group_tok, LANES), f32)),
        (vmem, jax.ShapeDtypeStruct((rows, width), f32)),
        (vmem, jax.ShapeDtypeStruct((rows, width), bf16)),
        (vmem, jax.ShapeDtypeStruct((group_tok, HD), f32)),
        (vmem, jax.ShapeDtypeStruct((group_tok, HD), f32)),
        (vmem, jax.ShapeDtypeStruct((2, group_tok), f32)),
    ]
    return pl.pallas_call(
        forward_kernel,
        in_specs=[vmem] * 2 + [anywhere] * 8 + [vmem] * 2 + [pl.BlockSpec(memory_space=pltpu.SMEM)],
        out_specs=[spec for spec, _ in outs],
        out_shape=[shape for _, shape in outs],
        scratch_shapes=[
            pltpu.VMEM((group_tok, width), bf16),
            pltpu.VMEM((width, 3 * wide), bf16),
            pltpu.VMEM((n_seq, wide, part), bf16),
            pltpu.VMEM(expert_up.shape, bf16),
            pltpu.VMEM((3, hidden, head_part), bf16),
            pltpu.VMEM(share_up.shape, bf16),
            pltpu.VMEM((3, share_all, seq_part), bf16),
            pltpu.VMEM((group_tok, group_tok), f32),
            pltpu.VMEM((n_head - 1, rows, width), bf16),
            pltpu.VMEM((n_head - 1, rows, width), bf16),
            dma((14,)),
            dma((4, lines)),
            dma((4, lines)),
            dma((8, lines)),
            dma((8, lines)),
            dma((n_head - 1,)),
            dma((n_head - 1,)),
            dma((n_head - 1,)),
            dma((n_head - 1,)),
            dma((9,)),
            dma((9,)),
            dma((4 * n_seq,)),
            dma((4 * n_seq,)),
        ],
        compiler_params=pltpu.CompilerParams(
            collective_id=0, has_side_effects=True, vmem_limit_bytes=VMEM_BYTES
        ),
        cost_estimate=pl.CostEstimate(
            flops=2 * group_tok * width * 4 * wide, bytes_accessed=1 << 29, transcendentals=0
        ),
        name="forward",
    )(
        tokens, gains, weight_own, wout_own, expert_up, expert_down, share_up,
        share_down, cotangent, marks, bias, arrange, lengths,
    )


def mesh_part():
    return lax.axis_index("head") // 2


def token_bits():
    return bits_of(lax.axis_size("head"))[1:]


def token_gather(block):
    order = token_bits()
    column = lax.all_gather(block, "seq", axis=0, tiled=True)
    share = column.shape[0] // 2
    half = share // 2
    core = lax.rem(lax.axis_index("seq"), 2)
    own = lax.dynamic_slice_in_dim(column, core * share, share, 0)
    upper = spread(own[:half], order)
    lower = spread(own[half:], order[::-1])
    chunks = [column]
    for r in sorted(upper)[1:]:
        for piece in (upper[r], lower[r]):
            chunks.append(jnp.concatenate([piece, swap(piece, "seq", 1)], axis=0))
    return chunks


def token_scatter(chunks):
    order = token_bits()
    column = chunks[0]
    share = column.shape[0] // 2
    half = share // 2
    core = lax.rem(lax.axis_index("seq"), 2)
    own = lax.dynamic_slice_in_dim(column, core * share, share, 0)
    sides = [{0: own[:half]}, {0: own[half:]}]
    for i, chunk in enumerate(chunks[1:]):
        sides[i % 2][2 * (i // 2 + 1)] = chunk[:half] + swap(chunk[half:], "seq", 1)
    total = jnp.concatenate([collect(sides[0], order), collect(sides[1], order[::-1])], axis=0)
    column = lax.dynamic_update_slice_in_dim(column, total, core * share, 0)
    return lax.psum_scatter(column, "seq", scatter_dimension=0, tiled=True)


def total_over_all(values):
    for axis in ("head", "seq"):
        for bit in bits_of(lax.axis_size(axis)):
            values = values + swap(values, axis, bit)
    return values


def turn(values, cosine, sine):
    return values * cosine + pltpu.roll(values, HD // 2, 1) * sine


def mask_of(layout):
    rows = layout.shape[1]
    cols = jnp.concatenate([layout, jnp.zeros((6, rows), f32)], axis=0).T
    same = cols[:, 0:1] == layout[0:1, :]
    return jnp.where(same & (layout[1:2, :] <= cols[:, 1:2]), 0.0, NEGATIVE)


def wide_tables(cosine, sine):
    return (
        jnp.concatenate([cosine, cosine], axis=1),
        jnp.concatenate([-sine, sine], axis=1),
    )


def head_forward(linear, cos, sin, mask):
    queries = turn(linear[:, :HD], cos, sin).astype(bf16)
    keys = turn(linear[:, HD : 2 * HD], cos, sin).astype(bf16)
    values = linear[:, 2 * HD :].astype(bf16)
    scores = dot(queries, keys, 1, 1) * HD ** (-0.5) + mask
    largest = jnp.max(scores, axis=1, keepdims=True)
    weights = jnp.exp(scores - largest)
    total = jnp.sum(weights, axis=1, keepdims=True)
    probs = (weights / total).astype(bf16)
    output = dot(probs, values, 1, 0).astype(bf16)
    return (queries, keys, values), output, largest + jnp.log(total)


def norm_rows(rows, gain):
    square = jnp.mean(rows * rows, axis=1, keepdims=True)
    return (rows * lax.rsqrt(square + EPS) * gain).astype(bf16)


def scatter_start(merged, wout, outgoing, incoming, sems_a, sems_b, rows, peers):
    blocks, _, size = wout.shape
    copies = []
    for r in range(len(peers) - 1, 0, -1):
        for b in range(blocks):
            outgoing[r - 1, :, b * size : (b + 1) * size] = dot(
                merged[r * rows : (r + 1) * rows, :], wout[b], 1, 0
            ).astype(bf16)
        copies.append(
            remote(
                outgoing.at[r - 1], incoming.at[r - 1], sems_a.at[r - 1], sems_b.at[r - 1],
                head=peers[r],
            )
        )
        copies[-1].start()
    return copies, [dot(merged[:rows, :], wout[b], 1, 0) for b in range(blocks)]


def attend_kernel(
    first, weight, wout, bias, cosine, sine, layout, tokens, gain,
    qkv, merged, log_total, middle, lowered, mask, outgoing, incoming, sems_a, sems_b,
):
    n = pl.program_id(0)
    heads = pl.num_programs(0)
    peers = ring_places()

    @pl.when(n == 0)
    def _():
        greet([{"head": peer} for peer in peers[1:]])
        mask[...] = mask_of(layout[...])

    linear = dot(first[...], weight[...], 1, 0) + bias[0]
    cos, sin = wide_tables(cosine[...], sine[...])
    parts, output, log_sum = head_forward(linear, cos, sin, mask[...])
    for k in range(3):
        qkv[:, k * HD : (k + 1) * HD] = parts[k]
    merged[:, pl.ds(pl.multiple_of(n * HD, HD), HD)] = output
    log_total[0] = jnp.broadcast_to(log_sum, log_total.shape[1:])

    @pl.when(n == heads - 1)
    def _():
        copies, own = scatter_start(
            merged, wout, outgoing, incoming, sems_a, sems_b, tokens.shape[0], peers
        )
        size = wout.shape[2]
        for b, block in enumerate(own):
            cols = slice(b * size, (b + 1) * size)
            middle[:, cols] = tokens[:, cols].astype(f32) + block
        for copy in copies:
            copy.wait()
        total = middle[...]
        for r in range(len(peers) - 1):
            total += incoming[r].astype(f32)
        middle[...] = total
        lowered[...] = norm_rows(total, gain[...])


def attend(first, weight, wout, bias, cosine, sine, layout, tokens, gain):
    rows, width = first.shape
    heads = bias.shape[0]
    own = tokens.shape[0]
    others = lax.axis_size("head") - 1
    step = 3 * HD
    wide = heads * HD

    def whole(shape):
        return pl.BlockSpec(shape, lambda n: (0,) * len(shape))

    return pl.pallas_call(
        attend_kernel,
        grid=(heads,),
        in_specs=[
            whole((rows, width)),
            pl.BlockSpec((width, step), lambda n: (0, n)),
            whole(wout.shape),
            pl.BlockSpec((1, 1, step), lambda n: (n, 0, 0)),
            whole((rows, HD // 2)),
            whole((rows, HD // 2)),
            whole((2, rows)),
            whole((own, width)),
            whole((1, width)),
        ],
        out_specs=[
            pl.BlockSpec((rows, step), lambda n: (0, n)),
            whole((rows, wide)),
            pl.BlockSpec((1, rows, LANES), lambda n: (n, 0, 0)),
            whole((own, width)),
            whole((own, width)),
        ],
        out_shape=[
            jax.ShapeDtypeStruct((rows, heads * step), bf16),
            jax.ShapeDtypeStruct((rows, wide), bf16),
            jax.ShapeDtypeStruct((heads, rows, LANES), f32),
            jax.ShapeDtypeStruct((own, width), f32),
            jax.ShapeDtypeStruct((own, width), bf16),
        ],
        scratch_shapes=[
            pltpu.VMEM((rows, rows), f32),
            pltpu.VMEM((others, own, width), bf16),
            pltpu.VMEM((others, own, width), bf16),
            pltpu.SemaphoreType.DMA((others,)),
            pltpu.SemaphoreType.DMA((others,)),
        ],
        compiler_params=pltpu.CompilerParams(
            collective_id=2, has_side_effects=True, vmem_limit_bytes=VMEM_BYTES
        ),
        cost_estimate=pl.CostEstimate(
            flops=2 * rows * width * 4 * wide, bytes_accessed=8 * width * wide, transcendentals=0
        ),
        name="attend",
    )(first, weight, wout, bias, cosine, sine, layout, tokens, gain)


def attend_back_kernel(
    plane, grad_own, first, weight, wout, qkv, merged, log_total, cosine, sine, layout,
    *refs,
):
    if plane:
        experts, grad_first, grad_weight, grad_bias, expert_in, x_a, x_b = refs[:5] + refs[-2:]
        refs = refs[5:-2]
    else:
        grad_first, grad_weight, grad_bias = refs[:3]
        refs = refs[3:]
    mask, grad_merged, acc, grad, sems_a, sems_b = refs
    n = pl.program_id(0)
    peers = ring_places()
    own = grad_own.shape[0]
    heads = pl.num_programs(0)
    if plane:
        near_x = plane_places()[0]
        cross = [remote(experts.at[3, 0], expert_in, x_a, x_b, head=near_x)]
    scale = HD ** (-0.5)
    blocks, _, size = grad_weight.shape
    wide = wout.shape[1]

    @pl.when(n == 0)
    def _():
        greet([{"head": peer} for peer in peers[1:]])
        copies = [
            remote(
                grad_own, grad.at[pl.ds(r * own, own)], sems_a.at[r - 1], sems_b.at[r - 1],
                head=peers[len(peers) - r],
            )
            for r in range(1, len(peers))
        ]
        for copy in copies:
            copy.start()
        grad[:own] = grad_own[...]
        mask[...] = mask_of(layout[...])
        acc[...] = jnp.zeros_like(acc)
        for copy in copies:
            copy.wait()
        if plane:
            for copy in cross:
                copy.start()
        total = jnp.zeros((grad.shape[0], wide), f32)
        for s in range(blocks):
            total += dot(grad[:, s * size : (s + 1) * size], wout[s], 1, 1)
        grad_merged[...] = total.astype(bf16)
        for s in range(blocks):
            grad_weight[s, 3 * wide :, :] = dot(
                merged[...], grad[:, s * size : (s + 1) * size], 0, 0
            ).astype(bf16)

    if plane:
        cos, sin = cosine[...], -sine[...]
    else:
        cos, sin = wide_tables(cosine[...], -sine[...])
    queries, keys, values = qkv[:, :HD], qkv[:, HD : 2 * HD], qkv[:, 2 * HD :]
    grad_out = grad_merged[:, pl.ds(pl.multiple_of(n * HD, HD), HD)]
    scores = dot(queries, keys, 1, 1) * scale + mask[...]
    probs = jnp.exp(scores - log_total[0][:, 0:1])
    grad_values = dot(probs.astype(bf16), grad_out, 0, 0).astype(bf16)
    grad_probs = dot(grad_out, values, 1, 1)
    centre = jnp.sum(probs * grad_probs, axis=1, keepdims=True)
    grad_scores = (probs * (grad_probs - centre)).astype(bf16)
    grad_queries = (dot(grad_scores, keys, 1, 0) * scale).astype(bf16).astype(f32)
    grad_keys = (dot(grad_scores, queries, 0, 0) * scale).astype(bf16).astype(f32)
    grad_linear = jnp.concatenate(
        [turn(grad_queries, cos, sin).astype(bf16), turn(grad_keys, cos, sin).astype(bf16), grad_values],
        axis=1,
    )
    grad_bias[0] = jnp.sum(grad_linear.astype(f32), axis=0, keepdims=True)
    acc[...] += dot(grad_linear, weight[...], 1, 1)
    step = 3 * HD
    for s in range(blocks):
        grad_weight[s, pl.ds(pl.multiple_of(n * step, HD), step), :] = dot(
            grad_linear, first[:, s * size : (s + 1) * size], 0, 0
        ).astype(bf16)

    @pl.when(n == heads - 1)
    def _():
        grad_first[...] = acc[...].astype(bf16)
        if plane:
            for copy in cross:
                copy.wait()


def attend_back(
    grad, first, weight, wout, qkv, merged, log_total, cosine, sine, layout, extra=()
):
    rows, width = first.shape
    heads = log_total.shape[0]
    step = 3 * HD
    wide = heads * HD
    n_seq = lax.axis_size("seq")
    size = width // n_seq
    own = grad.shape[0]
    others = lax.axis_size("head") - 1

    anywhere = pl.BlockSpec(memory_space=pl.ANY)
    more_outs, more_scratch = [], []
    if extra:
        more_outs = [jax.ShapeDtypeStruct(extra[0].shape[2:], bf16)]
        more_scratch = [pltpu.SemaphoreType.DMA] * 2

    def whole(shape):
        return pl.BlockSpec(shape, lambda n: (0,) * len(shape))

    return pl.pallas_call(
        functools.partial(attend_back_kernel, bool(extra)),
        grid=(heads,),
        in_specs=[
            whole((own, width)),
            whole((rows, width)),
            pl.BlockSpec((width, step), lambda n: (0, n)),
            whole(wout.shape),
            pl.BlockSpec((rows, step), lambda n: (0, n)),
            whole((rows, wide)),
            pl.BlockSpec((1, rows, LANES), lambda n: (n, 0, 0)),
            whole(cosine.shape),
            whole(sine.shape),
            whole((2, rows)),
        ]
        + [anywhere] * len(extra),
        out_specs=[
            whole((rows, width)),
            whole((n_seq, 4 * wide, size)),
            pl.BlockSpec((1, 1, step), lambda n: (n, 0, 0)),
        ]
        + [anywhere] * len(more_outs),
        out_shape=[
            jax.ShapeDtypeStruct((rows, width), bf16),
            jax.ShapeDtypeStruct((n_seq, 4 * wide, size), bf16),
            jax.ShapeDtypeStruct((heads, 1, step), f32),
        ]
        + more_outs,
        scratch_shapes=[
            pltpu.VMEM((rows, rows), f32),
            pltpu.VMEM((rows, wide), bf16),
            pltpu.VMEM((rows, width), f32),
            pltpu.VMEM((rows, width), bf16),
            pltpu.SemaphoreType.DMA((others,)),
            pltpu.SemaphoreType.DMA((others,)),
        ]
        + more_scratch,
        compiler_params=pltpu.CompilerParams(
            collective_id=3, has_side_effects=True, vmem_limit_bytes=VMEM_BYTES
        ),
        cost_estimate=pl.CostEstimate(
            flops=4 * rows * width * 4 * wide, bytes_accessed=16 * width * wide, transcendentals=0
        ),
        name="attend_back",
    )(grad, first, weight, wout, qkv, merged, log_total, cosine, sine, layout, *extra)


def pack_kernel(exp_units, share_units, at, *refs):
    stacked, shares = refs[0], refs[-5:-3]
    experts = [stacked.at[r] for r in range(stacked.shape[0])]
    rest, full, sems = refs[-3:]
    head = at[0]
    copies = []
    for r, block in enumerate(experts):
        size = block.shape[2]
        start = pl.multiple_of(jnp.bitwise_xor(head, r) * size, size)
        copies.append(
            pltpu.make_async_copy(
                block, full.at[:, pl.ds(0, exp_units), pl.ds(start, size)], sems.at[len(copies)]
            )
        )
    for r, block in enumerate(shares):
        size = block.shape[3]
        for s in range(block.shape[0]):
            copies.append(
                pltpu.make_async_copy(
                    block.at[s],
                    full.at[:, pl.ds(exp_units + r * share_units, share_units), pl.ds(s * size, size)],
                    sems.at[len(copies)],
                )
            )
    base = exp_units + 2 * share_units
    copies.append(
        pltpu.make_async_copy(rest, full.at[:, pl.ds(base, rest.shape[1]), :], sems.at[len(copies)])
    )
    for copy in copies:
        copy.start()
    for copy in copies:
        copy.wait()


def pack(at, experts, shares, rest, unit_rows):
    exp_units, share_units = experts.shape[2], shares[0].shape[2]
    count = experts.shape[0] + 2 * shares[0].shape[0] + 1
    anywhere = pl.BlockSpec(memory_space=pl.ANY)
    return pl.pallas_call(
        functools.partial(pack_kernel, exp_units, share_units),
        in_specs=[pl.BlockSpec(memory_space=pltpu.SMEM)] + [anywhere] * 4,
        out_specs=anywhere,
        out_shape=jax.ShapeDtypeStruct((3, unit_rows, rest.shape[2]), bf16),
        scratch_shapes=[pltpu.SemaphoreType.DMA((count,))],
        compiler_params=pltpu.CompilerParams(vmem_limit_bytes=1 << 20),
        cost_estimate=pl.CostEstimate(
            flops=0, bytes_accessed=12 * unit_rows * rest.shape[2], transcendentals=0
        ),
        name="pack",
    )(at, experts, *shares, rest)


def mix_rows(exp_units, base, n_exp, x, grad_ext, w, units, wait=None):
    rows, width = x.shape
    unit_rows = w.shape[1]
    seq = lax.axis_index("seq")
    block = base // LANES * LANES
    chunks = [(block, unit_rows)] + [(a, min(a + 512, block)) for a in range(0, block, 512)]
    lane = lax.broadcasted_iota(jnp.int32, (rows, LANES), 1)
    marks = grad_ext[:, width:].astype(f32)
    mark = jnp.sum(jnp.where(lane == seq, marks, 0.0), axis=1, keepdims=True)
    exp_sum = share_sum = gate_here = share_gate = 0.0
    for i, (a, b) in enumerate(chunks):
        if wait is not None and i < 2:
            wait(i)
        gate = dot(x, w[0, a:b], 1, 1)
        up = dot(x, w[1, a:b], 1, 1)
        raw = dot(grad_ext[:, :width], w[2, a:b], 1, 1)
        if i == 0:
            logits = gate[:, :LANES]
            from_base = lane - (base - block)
            is_logit = (from_base >= 0) & (from_base < n_exp)
            largest = jnp.max(jnp.where(is_logit, logits, NEGATIVE), axis=1, keepdims=True)
            powers = jnp.where(is_logit, jnp.exp(jnp.where(is_logit, logits - largest, 0.0)), 0.0)
            chosen = jnp.sum(jnp.where(from_base == seq, powers, 0.0), axis=1, keepdims=True)
            gate_here = mark * chosen / jnp.sum(powers, axis=1, keepdims=True)
            share_gate = jax.nn.sigmoid(
                jnp.sum(jnp.where(from_base == n_exp, logits, 0.0), axis=1, keepdims=True)
            )
        sigma = 0.5 * jnp.tanh(0.5 * gate) + 0.5
        silu = gate * sigma
        hidden = silu * up
        both = hidden * raw
        if b <= exp_units:
            factor = gate_here
            exp_sum += jnp.sum(both, axis=1, keepdims=True)
        elif a >= exp_units:
            factor = share_gate
            share_sum += jnp.sum(both, axis=1, keepdims=True)
        else:
            is_expert = lax.broadcasted_iota(jnp.int32, both.shape, 1) < exp_units - a
            factor = jnp.where(is_expert, gate_here, share_gate)
            part = jnp.sum(jnp.where(is_expert, both, 0.0), axis=1, keepdims=True)
            exp_sum += part
            share_sum += jnp.sum(both, axis=1, keepdims=True) - part
        grad_hidden = raw * factor
        units[0][:, a:b] = (grad_hidden * (sigma * up + hidden * (1.0 - sigma))).astype(bf16)
        units[1][:, a:b] = (grad_hidden * silu).astype(bf16)
        units[2][:, a:b] = (hidden * factor).astype(bf16)
    back = dot(units[0][...], w[0], 1, 0) + dot(units[1][...], w[1], 1, 0)
    extra = jnp.where(lane == seq, exp_sum * mark, jnp.where(lane == n_exp, share_sum, 0.0))
    return back.astype(bf16), extra.astype(bf16)


def mix_local_kernel(exp_units, base, n_exp, second, grad_ext, w_hbm, back, unit_out, w, sems):
    copies = [pltpu.make_async_copy(w_hbm.at[m], w.at[m], sems.at[m]) for m in range(3)]
    width = second.shape[1]

    @pl.when(pl.program_id(0) == 0)
    def _():
        for copy in copies:
            copy.start()
        for copy in copies:
            copy.wait()

    units = [unit_out.at[m] for m in range(3)]
    rows_back, extra = mix_rows(exp_units, base, n_exp, second[...], grad_ext, w, units)
    back[:, :width] = rows_back
    back[:, width:] = extra


def mix_local(second, grad_ext, full, exp_units, base, n_exp):
    rows, width = second.shape
    unit_rows = full.shape[1]
    wide = grad_ext.shape[1]
    return pl.pallas_call(
        functools.partial(mix_local_kernel, exp_units, base, n_exp),
        grid=(rows // TILE,),
        in_specs=[
            pl.BlockSpec((TILE, width), lambda i: (i, 0)),
            pl.BlockSpec((TILE, wide), lambda i: (i, 0)),
            pl.BlockSpec(memory_space=pl.ANY),
        ],
        out_specs=[
            pl.BlockSpec((TILE, wide), lambda i: (i, 0)),
            pl.BlockSpec((3, TILE, unit_rows), lambda i: (0, i, 0)),
        ],
        out_shape=[
            jax.ShapeDtypeStruct((rows, wide), bf16),
            jax.ShapeDtypeStruct((3, rows, unit_rows), bf16),
        ],
        scratch_shapes=[
            pltpu.VMEM((3, unit_rows, width), bf16),
            pltpu.SemaphoreType.DMA((3,)),
        ],
        compiler_params=pltpu.CompilerParams(vmem_limit_bytes=VMEM_BYTES),
        cost_estimate=pl.CostEstimate(
            flops=10 * rows * width * unit_rows,
            bytes_accessed=6 * unit_rows * width + 8 * rows * width,
            transcendentals=0,
        ),
        name="mix_local",
    )(second, grad_ext, full)


def mix_kernel(
    exp_units, base, n_exp, second, grad_ext, experts, share_own, share_far, rest, unit_out, back, down_out,
    w, held, core_in, home, e_sem, s_sem, r_sem, b_a, b_b, h_a, h_b, o_sem, d_sem,
):
    i = pl.program_id(0)
    _, near_y, near_core = plane_places()
    core = lax.axis_index("seq") % 2
    rows, width = second.shape[2:]
    at = [pl.ds(j * rows, rows) for j in range(2)]
    loads = [[], []]
    for m in range(3):
        for r, owner in enumerate(plane_owners()):
            size = experts.shape[3]
            start = pl.multiple_of(owner * size, size)
            loads[1].append(
                pltpu.make_async_copy(
                    experts.at[r, m], w.at[m, pl.ds(0, exp_units), pl.ds(start, size)], e_sem.at[m, r]
                )
            )
    share_rows, size = share_own.shape[2:]
    for r, share in enumerate((share_own, share_far)):
        for place in range(share.shape[0]):
            loads[0].append(
                pltpu.make_async_copy(
                    share.at[place],
                    w.at[
                        :,
                        pl.ds(exp_units + r * share_rows, share_rows),
                        pl.ds(place * size, size),
                    ],
                    s_sem.at[r, place],
                )
            )
    loads[0].append(
        pltpu.make_async_copy(rest, w.at[:, pl.ds(base, rest.shape[1])], r_sem)
    )
    keep = pltpu.make_async_copy(w.at[2], down_out, d_sem)
    back_c = [
        remote(held.at[j, 1 - core], core_in.at[j], b_a.at[j], b_b.at[j], seq=near_core)
        for j in range(2)
    ]
    back_y = [
        remote(held.at[j, core], home.at[j], h_a.at[j], h_b.at[j], head=near_y) for j in range(2)
    ]

    def wait_weights(m):
        @pl.when(i == 0)
        def _():
            for copy in loads[m]:
                copy.wait()

    @pl.when(i == 0)
    def _():
        for group in loads:
            for copy in group:
                copy.start()
        greet([{"head": near_y}, {"seq": near_core}])

    for c in range(2):
        units = [unit_out.at[m, 0, c] for m in range(3)]
        rows_back, extra = mix_rows(
            exp_units, base, n_exp, second[0, c], grad_ext.at[0, c], w, units,
            wait_weights if c == 0 else None,
        )
        held[i, c, :, :width] = rows_back
        held[i, c, :, width:] = extra
        if c == 0:
            for j in range(2):

                @pl.when(i == 1 + j)
                def _():
                    back_c[j].wait_recv()
                    held[j, core] = (held[j, core].astype(f32) + core_in[j].astype(f32)).astype(bf16)
                    back_y[j].start()

    for j in range(2):

        @pl.when(i == j)
        def _():
            back_c[j].start()
            if j == 0:
                keep.start()

    @pl.when(i == 3)
    def _():
        out = [
            [
                pltpu.make_async_copy(held.at[2 + j, c], back.at[c, at[j]], o_sem.at[j, k])
                for k, c in enumerate((1 - core, core))
            ]
            for j in range(2)
        ]
        for j in range(2):
            out[j][0].start()
        for j in range(2):
            back_y[j].wait_recv()
            held[2 + j, core] = (held[2 + j, core].astype(f32) + home[j].astype(f32)).astype(bf16)
            out[j][1].start()
        for j in range(2):
            out[j][0].wait()
            out[j][1].wait()
            back_c[j].wait_send()
            back_y[j].wait_send()
        keep.wait()


def mix(seconds, grads, experts, share_own, share_far, rest, exp_units, base, n_exp, unit_rows):
    rows, width = seconds.shape[1:]
    wide = grads.shape[2]
    half = rows // 2
    piece = half // 2
    anywhere = pl.BlockSpec(memory_space=pl.ANY)
    units, back, down_rows = pl.pallas_call(
        functools.partial(mix_kernel, exp_units, base, n_exp),
        grid=(4,),
        in_specs=[
            pl.BlockSpec((1, 2, piece, width), lambda i: (1 - i // 2, 0, i % 2, 0)),
            pl.BlockSpec((1, 2, piece, wide), lambda i: (1 - i // 2, 0, i % 2, 0)),
            anywhere,
            anywhere,
            anywhere,
            anywhere,
        ],
        out_specs=[
            pl.BlockSpec((3, 1, 2, piece, unit_rows), lambda i: (0, 1 - i // 2, 0, i % 2, 0)),
            anywhere,
            anywhere,
        ],
        out_shape=[
            jax.ShapeDtypeStruct((3, 2, 2, half, unit_rows), bf16),
            jax.ShapeDtypeStruct((2, half, wide), bf16),
            jax.ShapeDtypeStruct((unit_rows, width), bf16),
        ],
        scratch_shapes=[
            pltpu.VMEM((3, unit_rows, width), bf16),
            pltpu.VMEM((4, 2, piece, wide), bf16),
            pltpu.VMEM((2, piece, wide), bf16),
            pltpu.VMEM((2, piece, wide), bf16),
            pltpu.SemaphoreType.DMA((3, 4)),
            pltpu.SemaphoreType.DMA((2, share_own.shape[0])),
            pltpu.SemaphoreType.DMA,
            *[pltpu.SemaphoreType.DMA((2,))] * 4,
            pltpu.SemaphoreType.DMA((2, 2)),
            pltpu.SemaphoreType.DMA,
        ],
        compiler_params=pltpu.CompilerParams(
            collective_id=4, has_side_effects=True, vmem_limit_bytes=VMEM_BYTES
        ),
        cost_estimate=pl.CostEstimate(
            flops=20 * rows * width * unit_rows,
            bytes_accessed=6 * unit_rows * width + 16 * rows * width,
            transcendentals=0,
        ),
        name="mix",
    )(
        seconds.reshape(2, 2, half, width), grads.reshape(2, 2, half, wide), experts, share_own, share_far, rest
    )
    return units.reshape(3, 2, rows, unit_rows), back.reshape(rows, wide), down_rows


def unit_grads_kernel(count, exp_units, share_rows, at, *refs):
    units, seconds, grads = refs[:count], refs[count : 2 * count], refs[2 * count : 3 * count]
    experts, share_own, share_far = refs[3 * count :]
    m = pl.program_id(0)

    def run(rights):
        acc = dot(units[0][...], rights[0][...], 0, 0)
        for left, right in zip(units[1:], rights[1:]):
            acc += dot(left[...], right[...], 0, 0)
        experts[0, 0] = acc[:exp_units].astype(bf16)
        size = share_own.shape[3]
        for s in range(share_own.shape[0]):
            piece = acc[exp_units : exp_units + 2 * share_rows, s * size : (s + 1) * size].astype(bf16)
            share_own[s, 0] = piece[:share_rows]
            share_far[s, 0] = piece[share_rows:]

    @pl.when(m < 2)
    def _():
        run(seconds)

    @pl.when(m == 2)
    def _():
        run(grads)


def unit_grads(at, units, seconds, grads, exp_units, share_rows):
    n_head, n_seq = lax.axis_size("head"), lax.axis_size("seq")
    width = seconds[0][0].shape[2]
    unit_rows = units[0][0].shape[3]
    head_part, seq_part = width // n_head, width // n_seq
    near = n_seq // n_head
    rows = sum(block.shape[1] for block, _ in seconds)

    def far(r, at):
        return jnp.bitwise_xor(at[0], r)

    def place(q, m, r, at):
        return (m, q, 0, 0)

    def second_place(q, m, r, at):
        return (q, 0, jnp.where(m < 2, far(r, at), far(n_head - 1, at)))

    def grad_place(q, m, r, at):
        return (q, 0, jnp.where(m < 2, far(0, at), far(r, at)))

    in_specs = [
        pl.BlockSpec((None, None, block.shape[2], unit_rows), functools.partial(place, q))
        for block, q in units
    ]
    in_specs += [
        pl.BlockSpec((None, block.shape[1], head_part), functools.partial(second_place, q))
        for block, q in seconds
    ]
    in_specs += [
        pl.BlockSpec((None, block.shape[1], head_part), functools.partial(grad_place, q))
        for block, q in grads
    ]
    share_spec = pl.BlockSpec((near, 1, share_rows, seq_part), lambda m, r, at: (far(r, at), m, 0, 0))
    share_shape = jax.ShapeDtypeStruct((n_seq, 3, share_rows, seq_part), bf16)
    return pl.pallas_call(
        functools.partial(unit_grads_kernel, len(units), exp_units, share_rows),
        grid_spec=pltpu.PrefetchScalarGridSpec(
            num_scalar_prefetch=1,
            grid=(3, n_head),
            in_specs=in_specs,
            out_specs=[
                pl.BlockSpec((1, 1, exp_units, head_part), lambda m, r, at: (r, m, 0, 0)),
                share_spec,
                share_spec,
            ],
        ),
        out_shape=[
            jax.ShapeDtypeStruct((n_head, 3, exp_units, head_part), bf16),
            share_shape,
            share_shape,
        ],
        compiler_params=pltpu.CompilerParams(vmem_limit_bytes=VMEM_BYTES),
        cost_estimate=pl.CostEstimate(
            flops=6 * rows * width * unit_rows,
            bytes_accessed=6 * rows * unit_rows + 8 * rows * width + 6 * width * unit_rows,
            transcendentals=0,
        ),
        name="unit_grads",
    )(at, *(block for block, _ in units + seconds + grads))


def products_kernel(
    units, seconds, grads, down_rows, out, experts, expert_in_down, share_all,
    u, sides, right, far_half, column, core_in, home, share, share_in, stage,
    u_sem, r_sem, d_sem, c_a, c_b, y_a, y_b, x_a, x_b, z_a, z_b, e_sem, o_sem,
):
    seq, n_seq = lax.axis_index("seq"), lax.axis_size("seq")
    near_x, near_y, near_core = plane_places()
    core = seq % 2
    width = right.shape[2]
    rows = column.shape[0]
    piece = rows // 2
    exp_units = experts.shape[2]
    share_rows, seq_part = share_all.shape[2:]
    head_part = experts.shape[3]
    n_head = width // head_part
    edge = exp_units // LANES * LANES
    tail = exp_units - edge
    slot = {2: 1, 0: 2, 1: 0}

    def load_units(m):
        return [
            pltpu.make_async_copy(
                units.at[m, q], u.at[pl.ds(q * 2 * rows, 2 * rows)], u_sem.at[m, q]
            )
            for q in range(2)
        ]

    def load_right(k):
        source = grads if k else seconds
        return [
            pltpu.make_async_copy(
                source.at[q, :, pl.ds(f * head_part, head_part)],
                right.at[k, pl.ds(q * 2 * rows, 2 * rows), pl.ds(f * head_part, head_part)],
                r_sem.at[k, q, f],
            )
            for q in range(2)
            for f in range(n_head)
        ]

    down = sides.at[0]
    load_down = pltpu.make_async_copy(down_rows, down, d_sem)
    rights = [load_right(0), load_right(1)]
    first = load_units(2)
    first[1].start()
    load_down.start()
    first[0].start()
    for copy in rights[1] + rights[0]:
        copy.start()
    greet(
        [{"head": near_x}, {"head": near_y}] + [{"seq": (seq + k) % n_seq} for k in range(1, n_seq)]
    )

    pieces = [pl.ds(j * piece, piece) for j in range(2)]
    to_core = [
        remote(far_half.at[0, at], core_in.at[at], c_a.at[j], c_b.at[j], seq=near_core)
        for j, at in enumerate(pieces)
    ]
    to_y = [
        remote(far_half.at[1, at], home.at[at], y_a.at[j], y_b.at[j], head=near_y)
        for j, at in enumerate(pieces)
    ]
    to_x = [
        remote(share.at[1, :, m], share_in.at[:, m], x_a.at[m], x_b.at[m], head=near_x)
        for m in range(3)
    ]
    cross = remote(experts.at[3, 2], expert_in_down, x_a.at[3], x_b.at[3], head=near_x)
    spread_out = [[] for _ in range(3)]
    spread_in = []
    spread_own = []
    for m in range(3):
        for k in range(1, n_seq):
            to, source = (seq + k) % n_seq, (seq + n_seq - k) % n_seq
            spread_out[m].append(
                remote(
                    share.at[0, to, m], share_all.at[seq, m], z_a.at[m, k], z_b.at[m, k], seq=to
                )
            )
            block = share_all.at[source, m]
            spread_in.append(remote(block, block, z_a.at[m, k], z_b.at[m, k], seq=to))
        spread_own.append(
            pltpu.make_async_copy(share.at[0, seq, m], share_all.at[seq, m], z_a.at[m, 0])
        )

    def spread_share(m):
        to_x[m].wait_recv()
        for place in range(n_seq):
            total = share[0, place, m].astype(f32) + share_in[place, m].astype(f32)
            share[0, place, m] = total.astype(bf16)
        for copy in spread_out[m]:
            copy.start()
        spread_own[m].start()

    def out_rows(start):
        return dot(u[pl.ds(pl.multiple_of(start, 16), piece), :], down[...], 1, 0)

    def turn_units(m):
        block = 2 * piece
        for k in range(u.shape[0] // block):
            at = slice(k * block, (k + 1) * block)
            sides[slot[m], :, at] = u[at, :].T

    def share_part(m):
        for f in range(n_head):
            for copy in rights[1 if m == 2 else 0][f::n_head] if m < 3 else []:
                if m != 1:
                    copy.wait()
            block = right[1 if m == 2 else 0, :, f * head_part : (f + 1) * head_part]
            acc = dot(sides[slot[m], edge:], block, 1, 0)
            for b in range(head_part // seq_part):
                part = acc[tail : tail + 2 * share_rows, b * seq_part : (b + 1) * seq_part]
                place = f * (head_part // seq_part) + b
                share[0, place, m] = part[:share_rows].astype(bf16)
                share[1, place, m] = part[share_rows:].astype(bf16)
        to_x[m].start()

    owners = plane_owners()
    writes = []

    def expert_part(r, m):
        n = len(writes)
        if n >= 2:
            writes[n - 2].wait()
        start = pl.multiple_of(owners[r] * head_part, head_part)
        acc = dot(
            sides[slot[m], :exp_units],
            right[1 if m == 2 else 0, :, pl.ds(start, head_part)],
            1,
            0,
        )
        stage[n % 2] = acc.astype(bf16)
        writes.append(pltpu.make_async_copy(stage.at[n % 2], experts.at[r, m], e_sem.at[n % 2]))
        writes[-1].start()

    def pass_on(j):
        to_core[j].wait_recv()
        total = far_half[1, pieces[j]].astype(f32) + core_in[pieces[j]].astype(f32)
        far_half[1, pieces[j]] = total.astype(bf16)
        to_y[j].start()

    first[1].wait()
    load_down.wait()
    for k, half in ((0, 1 - core), (1, core)):
        for j in range(2):
            far_half[k, pieces[j]] = out_rows(2 * rows + half * rows + j * piece).astype(bf16)
            if k == 0:
                to_core[j].start()
            else:
                pass_on(j)
    first[0].wait()
    turn_units(2)
    share_part(2)
    for copy in to_core:
        copy.wait_send()
    for j in range(2):
        far_half[0, pieces[j]] = out_rows((1 - core) * rows + j * piece).astype(bf16)
    write = [
        pltpu.make_async_copy(far_half.at[0], out.at[1 - core], o_sem.at[0]),
        pltpu.make_async_copy(column, out.at[core], o_sem.at[1]),
    ]
    write[0].start()
    for j in range(2):
        column[pieces[j]] = out_rows(core * rows + j * piece).astype(bf16)
    for i, m in enumerate((0, 1)):
        load = load_units(m)
        for copy in load:
            copy.start()
        expert_part(3, 0 if i else 2)
        for copy in load:
            copy.wait()
        turn_units(m)
        share_part(m)
        spread_share(0 if i else 2)
    expert_part(3, 1)
    cross.start()
    for m in (2, 0, 1):
        expert_part(1, m)
    for m in (2, 0, 1):
        expert_part(2, m)
    spread_share(1)
    for m in (2, 0, 1):
        expert_part(0, m)

    for j in range(2):
        to_y[j].wait_recv()
        column[pieces[j]] = (column[pieces[j]].astype(f32) + home[pieces[j]].astype(f32)).astype(bf16)
    write[1].start()
    for copy in to_x + to_y:
        copy.wait_send()
    cross.wait()
    for group in spread_out:
        for copy in group:
            copy.wait_send()
    for copy in spread_in:
        copy.wait_recv()
    for copy in writes[-2:] + write + spread_own:
        copy.wait()


def products(units, seconds, grads, down_rows, exp_units, share_rows):
    n_head, n_seq = lax.axis_size("head"), lax.axis_size("seq")
    _, rows, width = seconds.shape
    unit_rows = units.shape[3]
    half = rows // 2
    head_part, seq_part = width // n_head, width // n_seq
    anywhere = pl.BlockSpec(memory_space=pl.ANY)
    dma = pltpu.SemaphoreType.DMA
    share_shape = (n_seq, 3, share_rows, seq_part)
    return pl.pallas_call(
        products_kernel,
        in_specs=[anywhere] * 4,
        out_specs=[anywhere] * 4,
        out_shape=[
            jax.ShapeDtypeStruct((2, half, width), bf16),
            jax.ShapeDtypeStruct((n_head, 3, exp_units, head_part), bf16),
            jax.ShapeDtypeStruct((exp_units, head_part), bf16),
            jax.ShapeDtypeStruct(share_shape, bf16),
        ],
        scratch_shapes=[
            pltpu.VMEM((2 * rows, unit_rows), bf16),
            pltpu.VMEM((3, unit_rows, 2 * rows), bf16),
            pltpu.VMEM((2, 2 * rows, width), bf16),
            pltpu.VMEM((2, half, width), bf16),
            pltpu.VMEM((half, width), bf16),
            pltpu.VMEM((half, width), bf16),
            pltpu.VMEM((half, width), bf16),
            pltpu.VMEM((2, *share_shape), bf16),
            pltpu.VMEM(share_shape, bf16),
            pltpu.VMEM((2, exp_units, head_part), bf16),
            dma((3, 2)),
            dma((2, 2, n_head)),
            dma,
            *[dma((2,))] * 4,
            *[dma((4,))] * 2,
            *[dma((3, n_seq))] * 2,
            *[dma((2,))] * 2,
        ],
        compiler_params=pltpu.CompilerParams(
            collective_id=5, has_side_effects=True, vmem_limit_bytes=VMEM_BYTES
        ),
        cost_estimate=pl.CostEstimate(
            flops=16 * rows * width * unit_rows,
            bytes_accessed=40 * rows * width,
            transcendentals=0,
        ),
        name="products",
    )(units, seconds, grads, down_rows)


def finish_kernel(
    experts, expert_in, expert_in_down, share_all, partial, grad_middle, tokens, gains, small,
    grad_up, grad_down, grad_share_up, grad_share_down, input_grad, totals,
    near, far, far_in, near_in, last_in, pack, share_pack, incoming, slots,
    l_sem, x_a, x_b, y_a, y_b, s_a, s_b, t_a, t_b, p_sem,
):
    seq, head = lax.axis_index("seq"), lax.axis_index("head")
    near_x, near_y, near_core = plane_places()
    peers = ring_places()
    y = head // 2
    rows, width = grad_middle.shape
    units = near.shape[1]
    share_rows = share_all.shape[2]
    hidden = pack.shape[1]
    steps = [{"seq": near_core}]
    for bit in (2, 4):
        steps.append({"seq": seq + bit - 2 * bit * ((seq // bit) % 2)})
    steps += [{"head": near_x}, {"head": near_y}]

    loads = [
        [pltpu.make_async_copy(experts.at[2, m], far.at[m], l_sem.at[m]) for m in range(3)],
        [
            pltpu.make_async_copy(block, far_in.at[k], l_sem.at[3 + k])
            for k, block in enumerate((expert_in, expert_in_down))
        ],
        [pltpu.make_async_copy(experts.at[0, m], near.at[m], l_sem.at[5 + m]) for m in range(3)],
    ]
    for group in loads:
        for copy in group:
            copy.start()
    share_loads = [
        pltpu.make_async_copy(
            share_all.at[i], share_pack.at[:, pl.ds(i * share_rows, share_rows)], p_sem.at[i]
        )
        for i in range(share_all.shape[0])
    ]
    for copy in share_loads:
        copy.start()
    greet(steps + [{"head": peers[2] + 1 - 2 * (head % 2)}])
    scatter = [
        remote(
            partial.at[pl.ds(r * rows, rows)], incoming.at[r - 1], s_a.at[r - 1], s_b.at[r - 1],
            head=peers[r],
        )
        for r in range(1, len(peers))
    ]
    last = remote(experts.at[3, 1], last_in, x_a.at[3], x_b.at[3], head=near_x)
    sides = [
        remote(experts.at[1, m], near_in.at[m], x_a.at[m], x_b.at[m], head=near_x) for m in range(3)
    ]
    for copy in scatter + [last] + sides[:2]:
        copy.start()
    here = pl.ds(pl.multiple_of(y * units, 16), units)
    there = pl.ds(pl.multiple_of((1 - y) * units, 16), units)
    across = [
        remote(far.at[m], pack.at[m, here], y_a.at[m], y_b.at[m], head=near_y) for m in range(3)
    ]
    across_in = [
        remote(far.at[m], pack.at[m, there], y_a.at[m], y_b.at[m], head=near_y) for m in range(3)
    ]
    for k, m in enumerate((0, 2)):
        loads[0][m].wait()
        loads[1][k].wait()
        far[m] = (far[m].astype(f32) + far_in[k].astype(f32)).astype(bf16)
        across[m].start()
    loads[0][1].wait()
    for copy in loads[2]:
        copy.wait()

    for copy in scatter:
        copy.wait_recv()
    total = partial[:rows].astype(f32)
    for r in range(len(peers) - 1):
        total += incoming[r].astype(f32)
    x = tokens[...].astype(f32)
    inverse = lax.rsqrt(jnp.mean(x * x, axis=1, keepdims=True) + EPS)
    normed = x * inverse
    slots[0] = small[...]
    slots[0, 10:11] = jnp.sum(total * normed, axis=0, keepdims=True)
    grad_normed = total * gains[0:1, :].astype(f32)
    mean = jnp.mean(grad_normed * normed, axis=1, keepdims=True)
    input_grad[...] = grad_middle[...] + inverse * (grad_normed - normed * mean)

    exchanges = [
        remote(slots.at[2 * k], slots.at[2 * k + 1], t_a.at[k], t_b.at[k], **place)
        for k, place in enumerate(steps)
    ]

    def exchange(k):
        exchanges[k].wait_recv()
        slots[2 * k + 2] = slots[2 * k] + slots[2 * k + 1]
        if k + 1 < len(steps):
            exchanges[k + 1].start()

    exchanges[0].start()

    for copy in share_loads:
        copy.wait()
    grad_share_down[...] = share_pack[2]
    exchange(0)
    grad_share_up[:, :hidden] = share_pack[0].T
    exchange(1)
    grad_share_up[:, hidden:] = share_pack[1].T
    last.wait_recv()
    far[1] = (far[1].astype(f32) + last_in[...].astype(f32)).astype(bf16)
    across[1].start()
    exchange(2)
    sides[2].start()

    def place_block(m):
        sides[m].wait_recv()
        pack[m, here] = (near[m].astype(f32) + near_in[m].astype(f32)).astype(bf16)
        across_in[m].wait_recv()
        if m < 2:
            grad_up[:, m * hidden : (m + 1) * hidden] = pack[m].T
        else:
            grad_down[...] = pack[m]

    place_block(0)
    exchange(3)
    place_block(1)
    exchange(4)
    totals[...] = slots[2 * len(steps)]
    place_block(2)
    for copy in scatter + exchanges + sides + across + [last]:
        copy.wait_send()


def finish(experts, expert_in, expert_in_down, share_all, partial, grad_middle, tokens, gain, small):
    n_head, n_seq = lax.axis_size("head"), lax.axis_size("seq")
    rows, width = tokens.shape
    _, _, units, head_part = experts.shape
    share_rows, seq_part = share_all.shape[2:]
    hidden, share_units = 2 * units, n_seq * share_rows
    anywhere = pl.BlockSpec(memory_space=pl.ANY)
    vmem = pl.BlockSpec(memory_space=pltpu.VMEM)
    dma = pltpu.SemaphoreType.DMA
    return pl.pallas_call(
        finish_kernel,
        in_specs=[anywhere] * 4 + [vmem] * 5,
        out_specs=[vmem] * 6,
        out_shape=[
            jax.ShapeDtypeStruct((head_part, 2 * hidden), bf16),
            jax.ShapeDtypeStruct((hidden, head_part), bf16),
            jax.ShapeDtypeStruct((seq_part, 2 * share_units), bf16),
            jax.ShapeDtypeStruct((share_units, seq_part), bf16),
            jax.ShapeDtypeStruct((rows, width), f32),
            jax.ShapeDtypeStruct(small.shape, f32),
        ],
        scratch_shapes=[
            pltpu.VMEM((3, units, head_part), bf16),
            pltpu.VMEM((3, units, head_part), bf16),
            pltpu.VMEM((2, units, head_part), bf16),
            pltpu.VMEM((3, units, head_part), bf16),
            pltpu.VMEM((units, head_part), bf16),
            pltpu.VMEM((3, hidden, head_part), bf16),
            pltpu.VMEM((3, share_units, seq_part), bf16),
            pltpu.VMEM((n_head - 1, rows, width), bf16),
            pltpu.VMEM((11, *small.shape), f32),
            dma((8,)),
            *[dma((4,))] * 2,
            *[dma((3,))] * 2,
            *[dma((n_head - 1,))] * 2,
            *[dma((5,))] * 2,
            dma((n_seq,)),
        ],
        compiler_params=pltpu.CompilerParams(
            collective_id=6, has_side_effects=True, vmem_limit_bytes=VMEM_BYTES
        ),
        cost_estimate=pl.CostEstimate(flops=0, bytes_accessed=1 << 27, transcendentals=0),
        name="finish",
    )(experts, expert_in, expert_in_down, share_all, partial, grad_middle, tokens, gain, small)


def after(value, *others):
    return lax.optimization_barrier((value, *others))[0]


def shards(
    tokens,
    cotangent,
    arrange,
    doc_lengths,
    routes,
    norm1_gain,
    qkv_weight,
    qkv_bias,
    out_weight,
    norm2_gain,
    router_weight,
    shared_gate_vec,
    shared_gate_up,
    shared_down,
    expert_gate_up,
    expert_down,
):
    highest = lax.Precision.HIGHEST
    tok_rows, width = tokens.shape
    n_seq = lax.axis_size("seq")
    n_head = lax.axis_size("head")
    seq = lax.axis_index("seq")
    head = lax.axis_index("head")
    group_tok = tok_rows * n_head
    heads_here = qkv_weight.shape[1]
    n_exp = router_weight.shape[1]
    hidden_all = expert_down.shape[1]
    parts = n_head // 2
    part = mesh_part()
    exp_units = hidden_all // parts
    share_all = shared_down.shape[0]
    share_units = share_all // n_seq
    share_rows = -(-share_units // 16) * 16
    base = exp_units + 2 * share_rows
    unit_rows = -(-(base + n_exp + 1) // LANES) * LANES
    seq_part = width // n_seq
    head_part = width // n_head

    wide = heads_here * HD
    plane = parts == 2 and n_seq == 8 and 2 * n_seq * tok_rows == width
    expert_up = expert_gate_up[0]
    at = jnp.stack([head, seq]).astype(jnp.int32)
    gate_rows = jnp.concatenate([router_weight.T, shared_gate_vec[None, :]], axis=0)
    rest = jnp.zeros((3, unit_rows - base, width), bf16).at[0, : n_exp + 1].set(gate_rows)

    expert_ids = jnp.arange(n_exp, dtype=jnp.int32)
    chosen = jnp.any(routes[:, :, None] == expert_ids[None, None, :], axis=1)
    marks = jnp.concatenate(
        [chosen.astype(bf16), jnp.zeros((tok_rows, LANES - n_exp), bf16)], axis=1
    )

    stream = tokens.astype(f32)
    gain_first = norm1_gain.astype(f32)
    scale_first = rms_scale(stream)
    normed_first = stream * scale_first
    gain_second = norm2_gain.astype(f32)
    weight_own = qkv_weight.reshape(seq_part, 3 * wide)
    if plane:
        gains = jnp.stack([norm1_gain, norm2_gain])
        (
            first_group, weight, wout, experts, share_own, share_far, grad_both, seconds,
            qkv, merged, log_total, middle, lowered_second, cosine, sine, layout,
        ) = forward(
            tokens, gains, weight_own, out_weight, expert_up,
            expert_down[0], shared_gate_up.reshape(seq_part, 2 * share_all), shared_down, cotangent,
            marks, qkv_bias, arrange, doc_lengths,
        )
        grad_both = grad_both.reshape(2, n_seq * tok_rows, width + LANES)
        seconds = seconds.reshape(2, n_seq * tok_rows, width)
        units, back_column, down_rows = mix(
            seconds,
            grad_both,
            experts,
            share_own,
            share_far,
            rest,
            exp_units,
            base,
            n_exp,
            unit_rows,
        )
        out_column, grad_experts, expert_in_down, share_parts = products(
            units, seconds, grad_both, down_rows, exp_units, share_rows
        )
        back_own = lax.psum_scatter(back_column, "seq", scatter_dimension=0, tiled=True)
    else:
        place, doc_index, position = layout_of(arrange[0], doc_lengths[0], group_tok)
        blocks = (head + jnp.arange(n_head, dtype=jnp.int32)) % n_head
        table = jnp.stack([place, doc_index, position]).reshape(3, n_head, tok_rows)
        place, doc_index, position = jnp.take(table, blocks, axis=1).reshape(3, group_tok)
        layout = jnp.stack([doc_index, place]).astype(f32)
        cosine, sine = rope_tables(position.astype(f32))
        grad_ext = jnp.concatenate([cotangent, marks], axis=1)
        bias_here = lax.dynamic_slice_in_dim(qkv_bias, head * heads_here, heads_here, 0)
        bias_here = bias_here.astype(f32)[:, None, :]
        weight = lax.all_gather(weight_own, "seq", axis=0, tiled=True)
        wout = lax.all_gather(out_weight, "seq", axis=0)
        first_group = group_gather((normed_first * gain_first).astype(bf16))
        send = jnp.stack([expert_up[:, :hidden_all].T, expert_up[:, hidden_all:].T, expert_down[0]])
        near = []
        for t in range(parts):
            there = jnp.bitwise_xor(part, t)
            block = lax.dynamic_slice_in_dim(send, there * exp_units, exp_units, 1)
            near.append(swap(block, "head", 2 * t) if t else block)
        experts = jnp.stack([block for own in near for block in (own, swap(own, "head", 1))])
        send = jnp.stack([shared_gate_up[:, 0].T, shared_gate_up[:, 1].T, shared_down])
        send = jnp.transpose(send.reshape(3, n_seq, share_units, seq_part), (1, 0, 2, 3))
        if share_rows > share_units:
            send = jnp.pad(send, ((0, 0), (0, 0), (0, share_rows - share_units), (0, 0)))
        share_own = lax.all_to_all(send, "seq", split_axis=0, concat_axis=0)
        full = pack(at, experts, [share_own, swap(share_own, "head", 1)], rest, unit_rows)
        qkv, merged, log_total, middle, lowered_second = attend(
            first_group, weight, wout, bias_here, cosine, sine, layout, tokens,
            gain_second[None, :],
        )
        grad_chunks = token_gather(grad_ext)
        second_chunks = token_gather(lowered_second)
        back_chunks = []
        unit_chunks = []
        for second, grad in zip(second_chunks, grad_chunks):
            back, units = mix_local(second, grad, full, exp_units, base, n_exp)
            back_chunks.append(back)
            unit_chunks.append(units)
        grad_experts, grad_share, grad_share_far = unit_grads(
            at,
            [(units[:, None], 0) for units in unit_chunks],
            [(second[None], 0) for second in second_chunks],
            [(grad[None], 0) for grad in grad_chunks],
            exp_units,
            share_rows,
        )
        out_chunks = [dot(units[2], full[2], 1, 0).astype(bf16) for units in unit_chunks]
        back_own = token_scatter(back_chunks)
        out_own = token_scatter(out_chunks)
    scale_second = rms_scale(middle)
    normed_second = middle * scale_second

    back_own = after(back_own, grad_experts).astype(f32)

    logits = dot(lowered_second, gate_rows, 1, 1)
    probs = jax.nn.softmax(logits[:, :n_exp], axis=-1)
    share_gate = jax.nn.sigmoid(logits[:, n_exp:])
    grad_probs = back_own[:, width : width + n_exp]
    grad_logits = probs * (grad_probs - jnp.sum(probs * grad_probs, axis=1, keepdims=True))
    grad_gate_logit = (
        back_own[:, width + n_exp : width + n_exp + 1] * share_gate * (1.0 - share_gate)
    )
    grad_gates = jnp.concatenate([grad_logits, grad_gate_logit], axis=1)
    grad_second = back_own[:, :width] + jnp.dot(
        grad_gates, gate_rows.astype(f32), precision=highest
    )
    grad_gate_cols = jnp.dot(grad_gates.T, lowered_second.astype(f32), precision=highest)
    grad_gain_second = jnp.sum(grad_second * normed_second, axis=0)
    grad_normed = grad_second * gain_second
    grad_middle = cotangent.astype(f32) + scale_second * (
        grad_normed - normed_second * jnp.mean(grad_normed * normed_second, axis=1, keepdims=True)
    )
    grad_attn = grad_middle.astype(bf16)
    if plane:
        out_own = lax.psum_scatter(
            after(out_column, grad_attn).reshape(n_seq * tok_rows, width),
            "seq",
            scatter_dimension=0,
            tiled=True,
        )
    mixed = (middle + out_own.astype(f32)).astype(bf16)
    back_args = (
        grad_attn, first_group, weight, wout, qkv, merged, log_total, cosine, sine, layout
    )
    if plane:
        grad_first, grad_weight, grad_bias_here, expert_in = attend_back(
            *back_args, extra=(grad_experts,)
        )
    else:
        grad_first, grad_weight, grad_bias_here = attend_back(*back_args)
    grad_weight = lax.psum_scatter(grad_weight, "seq", scatter_dimension=0, tiled=False)
    grad_bias = lax.dynamic_update_slice_in_dim(
        jnp.zeros(qkv_bias.shape, f32), grad_bias_here[:, 0], head * heads_here, 0
    )
    small = jnp.concatenate(
        [grad_gate_cols, grad_gain_second[None, :], jnp.zeros((1, width), f32), grad_bias.reshape(-1, width)],
        axis=0,
    )
    if plane:
        small = jnp.pad(small, ((0, 16 - small.shape[0]), (0, 0)))
        own_up, own_down, grad_share_up, grad_share_down, input_grad, totals = finish(
            grad_experts, expert_in, expert_in_down, share_parts, grad_first, grad_middle, tokens, gains,
            small,
        )
    else:
        grad_first = group_scatter(grad_first)
        small = small.at[n_exp + 2].set(jnp.sum(grad_first * normed_first, axis=0))
        grad_normed_first = grad_first * gain_first
        input_grad = grad_middle + scale_first * (
            grad_normed_first
            - normed_first * jnp.mean(grad_normed_first * normed_first, axis=1, keepdims=True)
        )
        totals = total_over_all(small)
        grad_share = grad_share + swap(grad_share_far, "head", 1)
        grad_share = lax.all_to_all(grad_share[:, :, :share_units], "seq", split_axis=0, concat_axis=0)
        grad_share = jnp.transpose(grad_share, (1, 0, 2, 3)).reshape(3, share_all, seq_part)
        own = {}
        for t in range(parts)[::-1]:
            total = grad_experts[2 * t] + swap(grad_experts[2 * t + 1], "head", 1)
            own[t] = swap(total, "head", 2 * t) if t else total
        own = jnp.stack([own[t] for t in range(parts)])
        own = jnp.take(own, jnp.bitwise_xor(part, jnp.arange(parts, dtype=jnp.int32)), axis=0)
        own = jnp.transpose(own, (1, 0, 2, 3)).reshape(3, hidden_all, head_part)
        own_up, own_down = jnp.concatenate([own[0].T, own[1].T], axis=1), own[2]
        grad_share_up = jnp.concatenate([grad_share[0].T, grad_share[1].T], axis=1)
        grad_share_down = grad_share[2]
    return (
        mixed,
        input_grad,
        totals[n_exp + 2],
        grad_weight[: 3 * wide].astype(f32).T.reshape(qkv_weight.shape),
        totals[n_exp + 3 : n_exp + 3 + 3].reshape(qkv_bias.shape),
        grad_weight[3 * wide :].astype(f32),
        totals[n_exp + 1],
        totals[:n_exp].T,
        totals[n_exp],
        grad_share_up.reshape(shared_gate_up.shape).astype(f32),
        grad_share_down.astype(f32),
        own_up.astype(f32)[None],
        own_down.astype(f32)[None],
    )


def solution(mesh):
    return jax.shard_map(
        shards,
        mesh=mesh,
        in_specs=(
            P(("seq", "head"), None),
            P(("seq", "head"), None),
            P("seq", None),
            P("seq", None),
            P(("seq", "head"), None),
            P(),
            P("seq", "head", None),
            P(),
            P("head", "seq"),
            P(),
            P(),
            P(),
            P("seq", None, "head"),
            P("head", "seq"),
            P("seq", "head", None),
            P("seq", None, "head"),
        ),
        out_specs=(
            P(("seq", "head"), None),
            P(("seq", "head"), None),
            P(),
            P("seq", "head", None),
            P(),
            P("head", "seq"),
            P(),
            P(),
            P(),
            P("seq", None, "head"),
            P("head", "seq"),
            P("seq", "head", None),
            P("seq", None, "head"),
        ),
        check_vma=False,
    )
```

```python
import functools
import math

import jax
import jax.numpy as jnp
from jax import lax
from jax.experimental import pallas as pl
from jax.experimental.pallas import tpu as pltpu
from jax.sharding import PartitionSpec as P

HD = 128
EPS = 1e-06
THETA = 1000000.0
NEGATIVE = -1e30
LANES = 128
TILE = 256
MESH = pl.DeviceIdType.MESH
VMEM_BYTES = 61 * 1024 * 1024
bf16 = jnp.bfloat16
f32 = jnp.float32


def rms_scale(values):
    return lax.rsqrt(jnp.mean(values * values, axis=-1, keepdims=True) + EPS)


def rope_tables(position):
    half = HD // 2
    exponent = jnp.arange(half, dtype=f32) * (2.0 / HD)
    frequency = THETA ** (-exponent)
    angle = position[:, None] * frequency[None, :]
    return (jnp.cos(angle), jnp.sin(angle))


def layout_of(arrange_row, length_row, group_tok):
    counter = jnp.arange(group_tok, dtype=jnp.int32)
    place = jnp.sum(
        jnp.where(arrange_row[None, :] == counter[:, None], counter[None, :], 0),
        axis=1,
        dtype=jnp.int32,
    )
    doc_index = jnp.zeros_like(place)
    start = jnp.zeros_like(place)
    end = jnp.int32(0)
    for k in range(length_row.shape[0]):
        end = end + length_row[k]
        doc_index += (place >= end).astype(jnp.int32)
        start += jnp.where(place >= end, length_row[k], 0)
    return (place, doc_index, place - start)


def dot(left, right, left_dim, right_dim):
    return lax.dot_general(
        left, right, (((left_dim,), (right_dim,)), ((), ())), preferred_element_type=f32
    )


def swap(block, axis, bit):
    size = lax.axis_size(axis)
    return lax.ppermute(block, axis, [(i, i ^ bit) for i in range(size)])


def bits_of(size):
    bits = []
    bit = 1
    while bit < size:
        bits.append(bit)
        bit *= 2
    return bits


def spread(block, order):
    found = {0: block}
    for bit in order:
        for near in sorted(found):
            found[near ^ bit] = swap(found[near], "head", bit)
    return found


def collect(parts, order):
    parts = dict(parts)
    for bit in reversed(order):
        for far in sorted((r for r in parts if r & bit), reverse=True):
            parts[far ^ bit] = parts[far ^ bit] + swap(parts.pop(far), "head", bit)
    return parts[0]


def shift(block, axis, step):
    size = lax.axis_size(axis)
    return lax.ppermute(block, axis, [((i + step) % size, i) for i in range(size)])


def group_gather(block):
    size = lax.axis_size("head")
    return jnp.concatenate([block] + [shift(block, "head", r) for r in range(1, size)], axis=0)


def group_scatter(block):
    size = lax.axis_size("head")
    rows = block.shape[0] // size
    total = block[:rows].astype(f32)
    for r in range(1, size):
        total += shift(block[r * rows : (r + 1) * rows], "head", size - r).astype(f32)
    return total


def remote(src, dst, send_sem, recv_sem, **place):
    return pltpu.make_async_remote_copy(
        src_ref=src,
        dst_ref=dst,
        send_sem=send_sem,
        recv_sem=recv_sem,
        device_id=place,
        device_id_type=MESH,
    )


def greet(places):
    barrier = pltpu.get_barrier_semaphore()
    for place in places:
        pl.semaphore_signal(barrier, inc=1, device_id=place, device_id_type=MESH)
    pl.semaphore_wait(barrier, len(places))


def plane_places():
    head, seq = lax.axis_index("head"), lax.axis_index("seq")
    x, y = head % 2, head // 2
    return y * 2 + (1 - x), (1 - y) * 2 + x, seq + 1 - 2 * (seq % 2)


def plane_owners():
    head = lax.axis_index("head")
    near_x, near_y, _ = plane_places()
    return head, near_x, near_y, near_y + 1 - 2 * (head % 2)


def ring_places():
    size = lax.axis_size("head")
    head = lax.axis_index("head")
    return [(head + r) % size for r in range(size)]


class Line:
    def __init__(self, place, far, sems):
        self.seq = lax.axis_index("seq")
        self.count = lax.axis_size("seq") // 2
        self.depth = self.count - 1
        self.z = self.seq // 2
        _, self.near_y, self.near_core = plane_places()
        self.place, self.far = place, far
        self.sems = sems

    def index(self, j):
        if j == 0:
            return self.seq
        if j <= self.depth:
            return self.seq - 2 * j
        return self.seq + 2 * (j - self.depth)

    def valid(self, j):
        if j == 0:
            return self.z >= 0
        if j <= self.depth:
            return self.z - j >= 0
        return self.z + (j - self.depth) < self.count

    def line_copy(self, j, up):
        block = self.place(self.index(j))
        if up:
            to, k = self.seq + 2, j
        else:
            to, k = self.seq - 2, self.depth + (j - self.depth if j else 0)
        return remote(block, block, self.sems.at[0, k], self.sems.at[1, k], seq=to)

    def line_arrival(self, j):
        block = self.place(self.index(j))
        return remote(
            block, block, self.sems.at[0, j - 1], self.sems.at[1, j - 1], seq=self.near_core
        )

    def core_copy(self, j):
        block = self.place(self.index(j))
        return remote(block, block, self.sems.at[2, j], self.sems.at[3, j], seq=self.near_core)

    def core_arrival(self, j):
        block = self.place(self.index(j) + self.near_core - self.seq)
        return remote(block, block, self.sems.at[2, j], self.sems.at[3, j], seq=self.near_core)

    def far_copy(self, j):
        i = self.index(j)
        return remote(
            self.place(i), self.far(i), self.sems.at[4, j], self.sems.at[5, j], head=self.near_y
        )

    def far_core_copy(self, j):
        there = self.far(self.index(j))
        return remote(there, there, self.sems.at[6, j], self.sems.at[7, j], seq=self.near_core)

    def far_core_arrival(self, j):
        there = self.far(self.index(j) + self.near_core - self.seq)
        return remote(there, there, self.sems.at[6, j], self.sems.at[7, j], seq=self.near_core)

    def sides(self, j):
        self.core_copy(j).start()
        if self.far is not None:
            self.far_copy(j).start()

    def ups(self):
        return range(self.depth)

    def downs(self):
        return [0] + [self.depth + k for k in range(1, self.depth)]

    def has_above(self):
        return self.z + 1 < self.count

    def has_below(self):
        return self.z >= 1

    def begin(self):
        @pl.when(self.has_above())
        def _():
            self.line_copy(0, True).start()

        @pl.when(self.has_below())
        def _():
            self.line_copy(0, False).start()

        self.sides(0)

    def step(self, k):
        @pl.when(self.valid(1 + k))
        def _():
            self.line_arrival(1 + k).wait_recv()
            if 1 + k < self.depth:

                @pl.when(self.has_above())
                def _():
                    self.line_copy(1 + k, True).start()

            self.sides(1 + k)

        @pl.when(self.valid(self.depth + 1 + k))
        def _():
            self.line_arrival(self.depth + 1 + k).wait_recv()
            if 1 + k < self.depth:

                @pl.when(self.has_below())
                def _():
                    self.line_copy(self.depth + 1 + k, False).start()

            self.sides(self.depth + 1 + k)

    def side_step(self, j):
        @pl.when(self.valid(j))
        def _():
            self.far_copy(j).wait_recv()
            self.far_core_copy(j).start()

    def wait_blocks(self):
        for j in range(2 * self.depth + 1):

            @pl.when(self.valid(j))
            def _():
                self.core_arrival(j).wait_recv()
                if self.far is not None:
                    self.far_core_arrival(j).wait_recv()

    def wait_sends(self):
        for j in range(2 * self.depth + 1):

            @pl.when(self.valid(j))
            def _():
                self.core_copy(j).wait_send()
                if self.far is not None:
                    self.far_copy(j).wait_send()
                    self.far_core_copy(j).wait_send()

        for j in self.ups():

            @pl.when(self.valid(j) & self.has_above())
            def _():
                self.line_copy(j, True).wait_send()

        for j in self.downs():

            @pl.when(self.valid(j) & self.has_below())
            def _():
                self.line_copy(j, False).wait_send()


def forward_kernel(
    tokens, gains, weight_own, wout_own, expert_up, expert_down, share_up, share_down,
    cotangent, marks, bias, arrange, lengths,
    first_out, weight_out, wout_out, experts, share, share_far, grads, seconds, qkv, merged, log_total, middle,
    lowered, cosine, sine, layout,
    group, weight, wout, expert_raw, expert_pack, share_raw, share_pack, mask, outgoing, incoming,
    local, line_w, line_o, line_g, line_s, ring_a, ring_b, sc_a, sc_b, ex_a, ex_b, sh_a, sh_b,
):
    seq, head = lax.axis_index("seq"), lax.axis_index("head")
    n_seq = lax.axis_size("seq")
    near_x, near_y, near_core = plane_places()
    peers = ring_places()
    size = len(peers)
    rows, width = tokens.shape
    heads = qkv.shape[1] // (3 * HD)
    units = experts.shape[2]
    y = head // 2
    share_rows = share.shape[2]
    hidden = expert_down.shape[0]
    part = weight_own.shape[0]

    fetch = [
        pltpu.make_async_copy(
            weight_own, weight.at[pl.ds(pl.multiple_of(seq * part, 16), part)], local.at[0]
        ),
        pltpu.make_async_copy(wout_own, wout.at[seq], local.at[1]),
        pltpu.make_async_copy(expert_up, expert_raw, local.at[2]),
        pltpu.make_async_copy(expert_down, expert_pack.at[2], local.at[3]),
        pltpu.make_async_copy(share_up, share_raw, local.at[4]),
        pltpu.make_async_copy(share_down, share_pack.at[2], local.at[5]),
        pltpu.make_async_copy(cotangent, grads.at[0, seq, :, pl.ds(0, width)], local.at[6]),
        pltpu.make_async_copy(marks, grads.at[0, seq, :, pl.ds(width, marks.shape[1])], local.at[13]),
    ]
    for copy in fetch:
        copy.start()
    greet(
        [{"head": peer} for peer in peers[1:]]
        + [{"seq": (seq + k) % n_seq} for k in range(1, n_seq)]
    )

    gather_w = Line(lambda i: weight.at[pl.ds(pl.multiple_of(i * part, 16), part)], None, line_w)
    gather_o = Line(lambda i: wout.at[i], None, line_o)
    gather_g = Line(lambda i: grads.at[0, i], lambda i: grads.at[1, i], line_g)
    gather_s = Line(lambda i: seconds.at[0, i], lambda i: seconds.at[1, i], line_s)
    fetch[0].wait()
    gather_w.begin()
    fetch[1].wait()
    gather_o.begin()

    group[:rows] = norm_rows(tokens[...].astype(f32), gains[0:1, :].astype(f32))
    ring = [
        remote(
            group.at[pl.ds(0, rows)], group.at[pl.ds(r * rows, rows)],
            ring_a.at[r - 1], ring_b.at[r - 1], head=peers[size - r],
        )
        for r in range(1, size)
    ]
    for copy in ring:
        copy.start()

    fetch[2].wait()
    fetch[3].wait()
    mine = pl.ds(pl.multiple_of(y * units, 16), units)
    other = pl.ds(pl.multiple_of((1 - y) * units, 16), units)
    ups = [
        remote(expert_pack.at[m, other], experts.at[2, m], ex_a.at[m], ex_b.at[m], head=near_y)
        for m in range(3)
    ]
    sides = [
        remote(expert_pack.at[m, mine], experts.at[1, m], ex_a.at[3 + m], ex_b.at[3 + m], head=near_x)
        for m in range(3)
    ]
    ons = [
        remote(experts.at[2, m], experts.at[3, m], ex_a.at[6 + m], ex_b.at[6 + m], head=near_x)
        for m in range(3)
    ]
    order = (2, 0, 1)
    for m in order:
        if m < 2:
            expert_pack[m] = expert_raw[:, m * hidden : (m + 1) * hidden].T
        ups[m].start()
        sides[m].start()
    keep = [pltpu.make_async_copy(expert_pack.at[:, mine], experts.at[0], local.at[7])]
    keep[0].start()

    fetch[4].wait()
    fetch[5].wait()
    for m in range(2):
        share_pack[m] = share_raw[:, m * hidden : (m + 1) * hidden].T

    def share_block(i):
        return share_pack.at[:, pl.ds(pl.multiple_of(i * share_rows, 16), share_rows)]

    share_own = pltpu.make_async_copy(share_block(seq), share.at[seq], local.at[8])
    share_own.start()
    z, depth = seq // 2, n_seq // 2

    def share_send(distance, up, flip):
        to = (seq + 2 * distance if up else seq - 2 * distance) + flip * (near_core - seq)
        j = (2 * distance + up) * 2 + flip
        return remote(share_block(to), share.at[seq], sh_a.at[j], sh_b.at[j], seq=to)

    def share_source(distance, up, flip):
        return (seq - 2 * distance if up else seq + 2 * distance) + flip * (near_core - seq)

    def share_arrival(distance, up, flip):
        j = (2 * distance + up) * 2 + flip
        block = share.at[share_source(distance, up, flip)]
        return remote(block, block, sh_a.at[j], sh_b.at[j], seq=near_core)

    def share_cross(distance, up, flip):
        source = share_source(distance, up, flip)
        j = 4 * depth + (2 * distance + up) * 2 + flip
        return remote(
            share.at[source], share_far.at[source], sh_a.at[j], sh_b.at[j], head=near_x
        )

    def each_share(distance, arriving, act):
        if distance == 0:
            act(0, 1, 1)
            return
        for up in (0, 1):
            below = z >= distance
            above = z + distance < depth
            there = (below if up else above) if arriving else (above if up else below)

            @pl.when(there)
            def _():
                for flip in (0, 1):
                    act(distance, up, flip)

    def share_on(distance):
        def act(*at):
            share_arrival(*at).wait_recv()
            share_cross(*at).start()

        each_share(distance, True, act)

    total_rows = group.shape[0]
    row = lax.broadcasted_iota(jnp.int32, mask.shape, 0) + head * rows
    row = jnp.where(row >= total_rows, row - total_rows, row)
    at_place = lax.broadcasted_iota(jnp.int32, mask.shape, 1).astype(f32)
    place = jnp.sum(jnp.where(arrange[...] == row, at_place, 0.0), axis=1, keepdims=True)
    doc = jnp.zeros_like(place)
    start = jnp.zeros_like(place)
    end = jnp.float32(0)
    for k in range(lengths.shape[1]):
        length = lengths[0, k].astype(f32)
        end = end + length
        doc += jnp.where(place >= end, 1.0, 0.0)
        start += jnp.where(place >= end, length, 0.0)
    lane = lax.broadcasted_iota(jnp.int32, (total_rows, HD), 1)
    half = HD // 2
    exponent = jnp.where(lane < half, lane, lane - half).astype(f32) * (-2.0 / HD)
    angle = (place - start) * jnp.exp(exponent * math.log(THETA))
    sines = jnp.sin(angle)
    cosine[...] = jnp.cos(angle)
    sine[...] = jnp.where(lane < half, -sines, sines)
    layout[...] = jnp.where(lane == 0, doc, jnp.where(lane == 1, place, 0.0)).T[:2]
    same = (doc == layout[0:1, :]) & (layout[1:2, :] <= place)
    mask[...] = jnp.where(same, 0.0, NEGATIVE)
    gather_w.step(0)
    gather_o.step(0)
    gather_w.step(1)
    gather_o.step(1)
    ups[2].wait_recv()
    ons[2].start()
    fetch[6].wait()
    fetch[7].wait()
    gather_w.step(2)
    gather_o.step(2)
    gather_g.begin()
    for distance in range(depth):
        each_share(distance, False, lambda *at: share_send(*at).start())
    for copy in ring:
        copy.wait_recv()
    gather_w.wait_blocks()
    gather_o.wait_blocks()
    keep += [
        pltpu.make_async_copy(weight, weight_out, local.at[9]),
        pltpu.make_async_copy(wout, wout_out, local.at[10]),
        pltpu.make_async_copy(group, first_out, local.at[11]),
    ]
    for copy in keep[1:]:
        copy.start()

    step = 3 * HD
    cos, sin = cosine[...], sine[...]
    every_bias = bias[...].astype(f32)
    bias_row = lax.broadcasted_iota(jnp.int32, every_bias.shape, 0)
    for n in range(heads):
        shift_row = jnp.where(bias_row == head * heads + n, every_bias, 0.0)
        linear = dot(group[...], weight[:, n * step : (n + 1) * step], 1, 0)
        linear = linear + jnp.sum(shift_row, axis=0, keepdims=True)
        parts, output, log_sum = head_forward(linear, cos, sin, mask[...])
        for k in range(3):
            qkv[:, n * step + k * HD : n * step + (k + 1) * HD] = parts[k]
        merged[:, n * HD : (n + 1) * HD] = output
        log_total[n] = jnp.broadcast_to(log_sum, log_total.shape[1:])
        if n == 2:
            gather_g.step(0)
            gather_g.side_step(0)
    copies, own = scatter_start(merged, wout, outgoing, incoming, sc_a, sc_b, rows, peers)
    ups[0].wait_recv()
    ons[0].start()
    block = wout.shape[2]
    for b in range(len(own)):
        cols = slice(b * block, (b + 1) * block)
        middle[:, cols] = tokens[:, cols].astype(f32) + own[b]
    gather_g.step(1)
    for copy in copies:
        copy.wait_recv()
    total = middle[...]
    for r in range(size - 1):
        total += incoming[r].astype(f32)
    middle[...] = total
    lowered[...] = norm_rows(total, gains[1:2, :].astype(f32))
    last = pltpu.make_async_copy(lowered, seconds.at[0, seq], local.at[12])
    last.start()
    last.wait()
    gather_s.begin()
    ups[1].wait_recv()
    ons[1].start()

    share_own.wait()
    cross_own = remote(share.at[seq], share_far.at[seq], sh_a.at[0], sh_b.at[0], head=near_x)
    cross_own.start()
    gather_g.step(2)
    share_on(0)
    share_on(1)
    for j in (1, 1 + gather_g.depth, 2, 2 + gather_g.depth):
        gather_g.side_step(j)
    gather_s.step(0)
    share_on(2)
    for j in (3, 3 + gather_g.depth):
        gather_g.side_step(j)
    gather_s.side_step(0)
    gather_s.step(1)
    for j in (1, 1 + gather_g.depth):
        gather_s.side_step(j)
    gather_s.step(2)
    share_on(3)
    for j in (2, 2 + gather_g.depth, 3, 3 + gather_g.depth):
        gather_s.side_step(j)

    gather_g.wait_blocks()
    gather_s.wait_blocks()
    for copy in sides + ons + [cross_own]:
        copy.wait()
    for distance in range(depth):
        each_share(distance, True, lambda *at: share_cross(*at).wait())
        each_share(distance, False, lambda *at: share_send(*at).wait_send())
    for copy in ups + ring + copies:
        copy.wait_send()
    for copy in keep:
        copy.wait()
    for line in (gather_w, gather_o, gather_g, gather_s):
        line.wait_sends()


def forward(
    tokens, gains, weight_own, wout_own, expert_up, expert_down, share_up, share_down,
    cotangent, marks, bias, arrange, lengths,
):
    n_seq, n_head = lax.axis_size("seq"), lax.axis_size("head")
    rows, width = tokens.shape
    group_tok = rows * n_head
    wide = wout_own.shape[0]
    heads = wide // HD
    part = weight_own.shape[0]
    hidden, head_part = expert_down.shape
    units = hidden // 2
    share_all, seq_part = share_down.shape
    share_rows = share_all // n_seq
    ext = width + marks.shape[1]
    anywhere = pl.BlockSpec(memory_space=pl.ANY)
    vmem = pl.BlockSpec(memory_space=pltpu.VMEM)
    dma = pltpu.SemaphoreType.DMA
    lines = n_seq - 1

    def hbm(*shape):
        return (anywhere, jax.ShapeDtypeStruct(shape, bf16))

    outs = [
        hbm(group_tok, width),
        hbm(width, 3 * wide),
        hbm(n_seq, wide, part),
        hbm(4, 3, units, head_part),
        hbm(n_seq, 3, share_rows, seq_part),
        hbm(n_seq, 3, share_rows, seq_part),
        hbm(2, n_seq, rows, ext),
        hbm(2, n_seq, rows, width),
        (vmem, jax.ShapeDtypeStruct((group_tok, 3 * wide), bf16)),
        (vmem, jax.ShapeDtypeStruct((group_tok, wide), bf16)),
        (vmem, jax.ShapeDtypeStruct((heads, group_tok, LANES), f32)),
        (vmem, jax.ShapeDtypeStruct((rows, width), f32)),
        (vmem, jax.ShapeDtypeStruct((rows, width), bf16)),
        (vmem, jax.ShapeDtypeStruct((group_tok, HD), f32)),
        (vmem, jax.ShapeDtypeStruct((group_tok, HD), f32)),
        (vmem, jax.ShapeDtypeStruct((2, group_tok), f32)),
    ]
    return pl.pallas_call(
        forward_kernel,
        in_specs=[vmem] * 2 + [anywhere] * 8 + [vmem] * 2 + [pl.BlockSpec(memory_space=pltpu.SMEM)],
        out_specs=[spec for spec, _ in outs],
        out_shape=[shape for _, shape in outs],
        scratch_shapes=[
            pltpu.VMEM((group_tok, width), bf16),
            pltpu.VMEM((width, 3 * wide), bf16),
            pltpu.VMEM((n_seq, wide, part), bf16),
            pltpu.VMEM(expert_up.shape, bf16),
            pltpu.VMEM((3, hidden, head_part), bf16),
            pltpu.VMEM(share_up.shape, bf16),
            pltpu.VMEM((3, share_all, seq_part), bf16),
            pltpu.VMEM((group_tok, group_tok), f32),
            pltpu.VMEM((n_head - 1, rows, width), bf16),
            pltpu.VMEM((n_head - 1, rows, width), bf16),
            dma((14,)),
            dma((4, lines)),
            dma((4, lines)),
            dma((8, lines)),
            dma((8, lines)),
            dma((n_head - 1,)),
            dma((n_head - 1,)),
            dma((n_head - 1,)),
            dma((n_head - 1,)),
            dma((9,)),
            dma((9,)),
            dma((4 * n_seq,)),
            dma((4 * n_seq,)),
        ],
        compiler_params=pltpu.CompilerParams(
            collective_id=0, has_side_effects=True, vmem_limit_bytes=VMEM_BYTES
        ),
        cost_estimate=pl.CostEstimate(
            flops=2 * group_tok * width * 4 * wide, bytes_accessed=1 << 29, transcendentals=0
        ),
        name="forward",
    )(
        tokens, gains, weight_own, wout_own, expert_up, expert_down, share_up,
        share_down, cotangent, marks, bias, arrange, lengths,
    )


def mesh_part():
    return lax.axis_index("head") // 2


def token_bits():
    return bits_of(lax.axis_size("head"))[1:]


def token_gather(block):
    order = token_bits()
    column = lax.all_gather(block, "seq", axis=0, tiled=True)
    share = column.shape[0] // 2
    half = share // 2
    core = lax.rem(lax.axis_index("seq"), 2)
    own = lax.dynamic_slice_in_dim(column, core * share, share, 0)
    upper = spread(own[:half], order)
    lower = spread(own[half:], order[::-1])
    chunks = [column]
    for r in sorted(upper)[1:]:
        for piece in (upper[r], lower[r]):
            chunks.append(jnp.concatenate([piece, swap(piece, "seq", 1)], axis=0))
    return chunks


def token_scatter(chunks):
    order = token_bits()
    column = chunks[0]
    share = column.shape[0] // 2
    half = share // 2
    core = lax.rem(lax.axis_index("seq"), 2)
    own = lax.dynamic_slice_in_dim(column, core * share, share, 0)
    sides = [{0: own[:half]}, {0: own[half:]}]
    for i, chunk in enumerate(chunks[1:]):
        sides[i % 2][2 * (i // 2 + 1)] = chunk[:half] + swap(chunk[half:], "seq", 1)
    total = jnp.concatenate([collect(sides[0], order), collect(sides[1], order[::-1])], axis=0)
    column = lax.dynamic_update_slice_in_dim(column, total, core * share, 0)
    return lax.psum_scatter(column, "seq", scatter_dimension=0, tiled=True)


def total_over_all(values):
    for axis in ("head", "seq"):
        for bit in bits_of(lax.axis_size(axis)):
            values = values + swap(values, axis, bit)
    return values


def turn(values, cosine, sine):
    return values * cosine + pltpu.roll(values, HD // 2, 1) * sine


def mask_of(layout):
    rows = layout.shape[1]
    cols = jnp.concatenate([layout, jnp.zeros((6, rows), f32)], axis=0).T
    same = cols[:, 0:1] == layout[0:1, :]
    return jnp.where(same & (layout[1:2, :] <= cols[:, 1:2]), 0.0, NEGATIVE)


def wide_tables(cosine, sine):
    return (
        jnp.concatenate([cosine, cosine], axis=1),
        jnp.concatenate([-sine, sine], axis=1),
    )


def head_forward(linear, cos, sin, mask):
    queries = turn(linear[:, :HD], cos, sin).astype(bf16)
    keys = turn(linear[:, HD : 2 * HD], cos, sin).astype(bf16)
    values = linear[:, 2 * HD :].astype(bf16)
    scores = dot(queries, keys, 1, 1) * HD ** (-0.5) + mask
    largest = jnp.max(scores, axis=1, keepdims=True)
    weights = jnp.exp(scores - largest)
    total = jnp.sum(weights, axis=1, keepdims=True)
    probs = (weights / total).astype(bf16)
    output = dot(probs, values, 1, 0).astype(bf16)
    return (queries, keys, values), output, largest + jnp.log(total)


def norm_rows(rows, gain):
    square = jnp.mean(rows * rows, axis=1, keepdims=True)
    return (rows * lax.rsqrt(square + EPS) * gain).astype(bf16)


def scatter_start(merged, wout, outgoing, incoming, sems_a, sems_b, rows, peers):
    blocks, _, size = wout.shape
    copies = []
    for r in range(len(peers) - 1, 0, -1):
        for b in range(blocks):
            outgoing[r - 1, :, b * size : (b + 1) * size] = dot(
                merged[r * rows : (r + 1) * rows, :], wout[b], 1, 0
            ).astype(bf16)
        copies.append(
            remote(
                outgoing.at[r - 1], incoming.at[r - 1], sems_a.at[r - 1], sems_b.at[r - 1],
                head=peers[r],
            )
        )
        copies[-1].start()
    return copies, [dot(merged[:rows, :], wout[b], 1, 0) for b in range(blocks)]


def attend_kernel(
    first, weight, wout, bias, cosine, sine, layout, tokens, gain,
    qkv, merged, log_total, middle, lowered, mask, outgoing, incoming, sems_a, sems_b,
):
    n = pl.program_id(0)
    heads = pl.num_programs(0)
    peers = ring_places()

    @pl.when(n == 0)
    def _():
        greet([{"head": peer} for peer in peers[1:]])
        mask[...] = mask_of(layout[...])

    linear = dot(first[...], weight[...], 1, 0) + bias[0]
    cos, sin = wide_tables(cosine[...], sine[...])
    parts, output, log_sum = head_forward(linear, cos, sin, mask[...])
    for k in range(3):
        qkv[:, k * HD : (k + 1) * HD] = parts[k]
    merged[:, pl.ds(pl.multiple_of(n * HD, HD), HD)] = output
    log_total[0] = jnp.broadcast_to(log_sum, log_total.shape[1:])

    @pl.when(n == heads - 1)
    def _():
        copies, own = scatter_start(
            merged, wout, outgoing, incoming, sems_a, sems_b, tokens.shape[0], peers
        )
        size = wout.shape[2]
        for b, block in enumerate(own):
            cols = slice(b * size, (b + 1) * size)
            middle[:, cols] = tokens[:, cols].astype(f32) + block
        for copy in copies:
            copy.wait()
        total = middle[...]
        for r in range(len(peers) - 1):
            total += incoming[r].astype(f32)
        middle[...] = total
        lowered[...] = norm_rows(total, gain[...])


def attend(first, weight, wout, bias, cosine, sine, layout, tokens, gain):
    rows, width = first.shape
    heads = bias.shape[0]
    own = tokens.shape[0]
    others = lax.axis_size("head") - 1
    step = 3 * HD
    wide = heads * HD

    def whole(shape):
        return pl.BlockSpec(shape, lambda n: (0,) * len(shape))

    return pl.pallas_call(
        attend_kernel,
        grid=(heads,),
        in_specs=[
            whole((rows, width)),
            pl.BlockSpec((width, step), lambda n: (0, n)),
            whole(wout.shape),
            pl.BlockSpec((1, 1, step), lambda n: (n, 0, 0)),
            whole((rows, HD // 2)),
            whole((rows, HD // 2)),
            whole((2, rows)),
            whole((own, width)),
            whole((1, width)),
        ],
        out_specs=[
            pl.BlockSpec((rows, step), lambda n: (0, n)),
            whole((rows, wide)),
            pl.BlockSpec((1, rows, LANES), lambda n: (n, 0, 0)),
            whole((own, width)),
            whole((own, width)),
        ],
        out_shape=[
            jax.ShapeDtypeStruct((rows, heads * step), bf16),
            jax.ShapeDtypeStruct((rows, wide), bf16),
            jax.ShapeDtypeStruct((heads, rows, LANES), f32),
            jax.ShapeDtypeStruct((own, width), f32),
            jax.ShapeDtypeStruct((own, width), bf16),
        ],
        scratch_shapes=[
            pltpu.VMEM((rows, rows), f32),
            pltpu.VMEM((others, own, width), bf16),
            pltpu.VMEM((others, own, width), bf16),
            pltpu.SemaphoreType.DMA((others,)),
            pltpu.SemaphoreType.DMA((others,)),
        ],
        compiler_params=pltpu.CompilerParams(
            collective_id=2, has_side_effects=True, vmem_limit_bytes=VMEM_BYTES
        ),
        cost_estimate=pl.CostEstimate(
            flops=2 * rows * width * 4 * wide, bytes_accessed=8 * width * wide, transcendentals=0
        ),
        name="attend",
    )(first, weight, wout, bias, cosine, sine, layout, tokens, gain)


def attend_back_kernel(
    plane, grad_own, first, weight, wout, qkv, merged, log_total, cosine, sine, layout,
    *refs,
):
    if plane:
        experts, grad_first, grad_weight, grad_bias, expert_in, x_a, x_b = refs[:5] + refs[-2:]
        refs = refs[5:-2]
    else:
        grad_first, grad_weight, grad_bias = refs[:3]
        refs = refs[3:]
    mask, grad_merged, acc, grad, sems_a, sems_b = refs
    n = pl.program_id(0)
    peers = ring_places()
    own = grad_own.shape[0]
    heads = pl.num_programs(0)
    if plane:
        near_x = plane_places()[0]
        cross = [remote(experts.at[3, 0], expert_in, x_a, x_b, head=near_x)]
    scale = HD ** (-0.5)
    blocks, _, size = grad_weight.shape
    wide = wout.shape[1]

    @pl.when(n == 0)
    def _():
        greet([{"head": peer} for peer in peers[1:]])
        copies = [
            remote(
                grad_own, grad.at[pl.ds(r * own, own)], sems_a.at[r - 1], sems_b.at[r - 1],
                head=peers[len(peers) - r],
            )
            for r in range(1, len(peers))
        ]
        for copy in copies:
            copy.start()
        grad[:own] = grad_own[...]
        mask[...] = mask_of(layout[...])
        acc[...] = jnp.zeros_like(acc)
        for copy in copies:
            copy.wait()
        if plane:
            for copy in cross:
                copy.start()
        total = jnp.zeros((grad.shape[0], wide), f32)
        for s in range(blocks):
            total += dot(grad[:, s * size : (s + 1) * size], wout[s], 1, 1)
        grad_merged[...] = total.astype(bf16)
        for s in range(blocks):
            grad_weight[s, 3 * wide :, :] = dot(
                merged[...], grad[:, s * size : (s + 1) * size], 0, 0
            ).astype(bf16)

    if plane:
        cos, sin = cosine[...], -sine[...]
    else:
        cos, sin = wide_tables(cosine[...], -sine[...])
    queries, keys, values = qkv[:, :HD], qkv[:, HD : 2 * HD], qkv[:, 2 * HD :]
    grad_out = grad_merged[:, pl.ds(pl.multiple_of(n * HD, HD), HD)]
    scores = dot(queries, keys, 1, 1) * scale + mask[...]
    probs = jnp.exp(scores - log_total[0][:, 0:1])
    grad_values = dot(probs.astype(bf16), grad_out, 0, 0).astype(bf16)
    grad_probs = dot(grad_out, values, 1, 1)
    centre = jnp.sum(probs * grad_probs, axis=1, keepdims=True)
    grad_scores = (probs * (grad_probs - centre)).astype(bf16)
    grad_queries = (dot(grad_scores, keys, 1, 0) * scale).astype(bf16).astype(f32)
    grad_keys = (dot(grad_scores, queries, 0, 0) * scale).astype(bf16).astype(f32)
    grad_linear = jnp.concatenate(
        [turn(grad_queries, cos, sin).astype(bf16), turn(grad_keys, cos, sin).astype(bf16), grad_values],
        axis=1,
    )
    grad_bias[0] = jnp.sum(grad_linear.astype(f32), axis=0, keepdims=True)
    acc[...] += dot(grad_linear, weight[...], 1, 1)
    step = 3 * HD
    for s in range(blocks):
        grad_weight[s, pl.ds(pl.multiple_of(n * step, HD), step), :] = dot(
            grad_linear, first[:, s * size : (s + 1) * size], 0, 0
        ).astype(bf16)

    @pl.when(n == heads - 1)
    def _():
        grad_first[...] = acc[...].astype(bf16)
        if plane:
            for copy in cross:
                copy.wait()


def attend_back(
    grad, first, weight, wout, qkv, merged, log_total, cosine, sine, layout, extra=()
):
    rows, width = first.shape
    heads = log_total.shape[0]
    step = 3 * HD
    wide = heads * HD
    n_seq = lax.axis_size("seq")
    size = width // n_seq
    own = grad.shape[0]
    others = lax.axis_size("head") - 1

    anywhere = pl.BlockSpec(memory_space=pl.ANY)
    more_outs, more_scratch = [], []
    if extra:
        more_outs = [jax.ShapeDtypeStruct(extra[0].shape[2:], bf16)]
        more_scratch = [pltpu.SemaphoreType.DMA] * 2

    def whole(shape):
        return pl.BlockSpec(shape, lambda n: (0,) * len(shape))

    return pl.pallas_call(
        functools.partial(attend_back_kernel, bool(extra)),
        grid=(heads,),
        in_specs=[
            whole((own, width)),
            whole((rows, width)),
            pl.BlockSpec((width, step), lambda n: (0, n)),
            whole(wout.shape),
            pl.BlockSpec((rows, step), lambda n: (0, n)),
            whole((rows, wide)),
            pl.BlockSpec((1, rows, LANES), lambda n: (n, 0, 0)),
            whole(cosine.shape),
            whole(sine.shape),
            whole((2, rows)),
        ]
        + [anywhere] * len(extra),
        out_specs=[
            whole((rows, width)),
            whole((n_seq, 4 * wide, size)),
            pl.BlockSpec((1, 1, step), lambda n: (n, 0, 0)),
        ]
        + [anywhere] * len(more_outs),
        out_shape=[
            jax.ShapeDtypeStruct((rows, width), bf16),
            jax.ShapeDtypeStruct((n_seq, 4 * wide, size), bf16),
            jax.ShapeDtypeStruct((heads, 1, step), f32),
        ]
        + more_outs,
        scratch_shapes=[
            pltpu.VMEM((rows, rows), f32),
            pltpu.VMEM((rows, wide), bf16),
            pltpu.VMEM((rows, width), f32),
            pltpu.VMEM((rows, width), bf16),
            pltpu.SemaphoreType.DMA((others,)),
            pltpu.SemaphoreType.DMA((others,)),
        ]
        + more_scratch,
        compiler_params=pltpu.CompilerParams(
            collective_id=3, has_side_effects=True, vmem_limit_bytes=VMEM_BYTES
        ),
        cost_estimate=pl.CostEstimate(
            flops=4 * rows * width * 4 * wide, bytes_accessed=16 * width * wide, transcendentals=0
        ),
        name="attend_back",
    )(grad, first, weight, wout, qkv, merged, log_total, cosine, sine, layout, *extra)


def pack_kernel(exp_units, share_units, at, *refs):
    stacked, shares = refs[0], refs[-5:-3]
    experts = [stacked.at[r] for r in range(stacked.shape[0])]
    rest, full, sems = refs[-3:]
    head = at[0]
    copies = []
    for r, block in enumerate(experts):
        size = block.shape[2]
        start = pl.multiple_of(jnp.bitwise_xor(head, r) * size, size)
        copies.append(
            pltpu.make_async_copy(
                block, full.at[:, pl.ds(0, exp_units), pl.ds(start, size)], sems.at[len(copies)]
            )
        )
    for r, block in enumerate(shares):
        size = block.shape[3]
        for s in range(block.shape[0]):
            copies.append(
                pltpu.make_async_copy(
                    block.at[s],
                    full.at[:, pl.ds(exp_units + r * share_units, share_units), pl.ds(s * size, size)],
                    sems.at[len(copies)],
                )
            )
    base = exp_units + 2 * share_units
    copies.append(
        pltpu.make_async_copy(rest, full.at[:, pl.ds(base, rest.shape[1]), :], sems.at[len(copies)])
    )
    for copy in copies:
        copy.start()
    for copy in copies:
        copy.wait()


def pack(at, experts, shares, rest, unit_rows):
    exp_units, share_units = experts.shape[2], shares[0].shape[2]
    count = experts.shape[0] + 2 * shares[0].shape[0] + 1
    anywhere = pl.BlockSpec(memory_space=pl.ANY)
    return pl.pallas_call(
        functools.partial(pack_kernel, exp_units, share_units),
        in_specs=[pl.BlockSpec(memory_space=pltpu.SMEM)] + [anywhere] * 4,
        out_specs=anywhere,
        out_shape=jax.ShapeDtypeStruct((3, unit_rows, rest.shape[2]), bf16),
        scratch_shapes=[pltpu.SemaphoreType.DMA((count,))],
        compiler_params=pltpu.CompilerParams(vmem_limit_bytes=1 << 20),
        cost_estimate=pl.CostEstimate(
            flops=0, bytes_accessed=12 * unit_rows * rest.shape[2], transcendentals=0
        ),
        name="pack",
    )(at, experts, *shares, rest)


def mix_rows(exp_units, base, n_exp, x, grad_ext, w, units, wait=None):
    rows, width = x.shape
    unit_rows = w.shape[1]
    seq = lax.axis_index("seq")
    block = base // LANES * LANES
    chunks = [(block, unit_rows)] + [(a, min(a + 512, block)) for a in range(0, block, 512)]
    lane = lax.broadcasted_iota(jnp.int32, (rows, LANES), 1)
    marks = grad_ext[:, width:].astype(f32)
    mark = jnp.sum(jnp.where(lane == seq, marks, 0.0), axis=1, keepdims=True)
    exp_sum = share_sum = gate_here = share_gate = 0.0
    for i, (a, b) in enumerate(chunks):
        if wait is not None and i < 2:
            wait(i)
        gate = dot(x, w[0, a:b], 1, 1)
        up = dot(x, w[1, a:b], 1, 1)
        raw = dot(grad_ext[:, :width], w[2, a:b], 1, 1)
        if i == 0:
            logits = gate[:, :LANES]
            from_base = lane - (base - block)
            is_logit = (from_base >= 0) & (from_base < n_exp)
            largest = jnp.max(jnp.where(is_logit, logits, NEGATIVE), axis=1, keepdims=True)
            powers = jnp.where(is_logit, jnp.exp(jnp.where(is_logit, logits - largest, 0.0)), 0.0)
            chosen = jnp.sum(jnp.where(from_base == seq, powers, 0.0), axis=1, keepdims=True)
            gate_here = mark * chosen / jnp.sum(powers, axis=1, keepdims=True)
            share_gate = jax.nn.sigmoid(
                jnp.sum(jnp.where(from_base == n_exp, logits, 0.0), axis=1, keepdims=True)
            )
        sigma = 0.5 * jnp.tanh(0.5 * gate) + 0.5
        silu = gate * sigma
        hidden = silu * up
        both = hidden * raw
        if b <= exp_units:
            factor = gate_here
            exp_sum += jnp.sum(both, axis=1, keepdims=True)
        elif a >= exp_units:
            factor = share_gate
            share_sum += jnp.sum(both, axis=1, keepdims=True)
        else:
            is_expert = lax.broadcasted_iota(jnp.int32, both.shape, 1) < exp_units - a
            factor = jnp.where(is_expert, gate_here, share_gate)
            part = jnp.sum(jnp.where(is_expert, both, 0.0), axis=1, keepdims=True)
            exp_sum += part
            share_sum += jnp.sum(both, axis=1, keepdims=True) - part
        grad_hidden = raw * factor
        units[0][:, a:b] = (grad_hidden * (sigma * up + hidden * (1.0 - sigma))).astype(bf16)
        units[1][:, a:b] = (grad_hidden * silu).astype(bf16)
        units[2][:, a:b] = (hidden * factor).astype(bf16)
    back = dot(units[0][...], w[0], 1, 0) + dot(units[1][...], w[1], 1, 0)
    extra = jnp.where(lane == seq, exp_sum * mark, jnp.where(lane == n_exp, share_sum, 0.0))
    return back.astype(bf16), extra.astype(bf16)


def mix_local_kernel(exp_units, base, n_exp, second, grad_ext, w_hbm, back, unit_out, w, sems):
    copies = [pltpu.make_async_copy(w_hbm.at[m], w.at[m], sems.at[m]) for m in range(3)]
    width = second.shape[1]

    @pl.when(pl.program_id(0) == 0)
    def _():
        for copy in copies:
            copy.start()
        for copy in copies:
            copy.wait()

    units = [unit_out.at[m] for m in range(3)]
    rows_back, extra = mix_rows(exp_units, base, n_exp, second[...], grad_ext, w, units)
    back[:, :width] = rows_back
    back[:, width:] = extra


def mix_local(second, grad_ext, full, exp_units, base, n_exp):
    rows, width = second.shape
    unit_rows = full.shape[1]
    wide = grad_ext.shape[1]
    return pl.pallas_call(
        functools.partial(mix_local_kernel, exp_units, base, n_exp),
        grid=(rows // TILE,),
        in_specs=[
            pl.BlockSpec((TILE, width), lambda i: (i, 0)),
            pl.BlockSpec((TILE, wide), lambda i: (i, 0)),
            pl.BlockSpec(memory_space=pl.ANY),
        ],
        out_specs=[
            pl.BlockSpec((TILE, wide), lambda i: (i, 0)),
            pl.BlockSpec((3, TILE, unit_rows), lambda i: (0, i, 0)),
        ],
        out_shape=[
            jax.ShapeDtypeStruct((rows, wide), bf16),
            jax.ShapeDtypeStruct((3, rows, unit_rows), bf16),
        ],
        scratch_shapes=[
            pltpu.VMEM((3, unit_rows, width), bf16),
            pltpu.SemaphoreType.DMA((3,)),
        ],
        compiler_params=pltpu.CompilerParams(vmem_limit_bytes=VMEM_BYTES),
        cost_estimate=pl.CostEstimate(
            flops=10 * rows * width * unit_rows,
            bytes_accessed=6 * unit_rows * width + 8 * rows * width,
            transcendentals=0,
        ),
        name="mix_local",
    )(second, grad_ext, full)


def mix_kernel(
    exp_units, base, n_exp, second, grad_ext, experts, share_own, share_far, rest, unit_out, back, down_out,
    w, held, core_in, home, e_sem, s_sem, r_sem, b_a, b_b, h_a, h_b, o_sem, d_sem,
):
    i = pl.program_id(0)
    _, near_y, near_core = plane_places()
    core = lax.axis_index("seq") % 2
    rows, width = second.shape[2:]
    at = [pl.ds(j * rows, rows) for j in range(2)]
    loads = [[], []]
    for m in range(3):
        for r, owner in enumerate(plane_owners()):
            size = experts.shape[3]
            start = pl.multiple_of(owner * size, size)
            loads[1].append(
                pltpu.make_async_copy(
                    experts.at[r, m], w.at[m, pl.ds(0, exp_units), pl.ds(start, size)], e_sem.at[m, r]
                )
            )
    share_rows, size = share_own.shape[2:]
    for r, share in enumerate((share_own, share_far)):
        for place in range(share.shape[0]):
            loads[0].append(
                pltpu.make_async_copy(
                    share.at[place],
                    w.at[
                        :,
                        pl.ds(exp_units + r * share_rows, share_rows),
                        pl.ds(place * size, size),
                    ],
                    s_sem.at[r, place],
                )
            )
    loads[0].append(
        pltpu.make_async_copy(rest, w.at[:, pl.ds(base, rest.shape[1])], r_sem)
    )
    keep = pltpu.make_async_copy(w.at[2], down_out, d_sem)
    back_c = [
        remote(held.at[j, 1 - core], core_in.at[j], b_a.at[j], b_b.at[j], seq=near_core)
        for j in range(2)
    ]
    back_y = [
        remote(held.at[j, core], home.at[j], h_a.at[j], h_b.at[j], head=near_y) for j in range(2)
    ]

    def wait_weights(m):
        @pl.when(i == 0)
        def _():
            for copy in loads[m]:
                copy.wait()

    @pl.when(i == 0)
    def _():
        for group in loads:
            for copy in group:
                copy.start()
        greet([{"head": near_y}, {"seq": near_core}])

    for c in range(2):
        units = [unit_out.at[m, 0, c] for m in range(3)]
        rows_back, extra = mix_rows(
            exp_units, base, n_exp, second[0, c], grad_ext.at[0, c], w, units,
            wait_weights if c == 0 else None,
        )
        held[i, c, :, :width] = rows_back
        held[i, c, :, width:] = extra
        if c == 0:
            for j in range(2):

                @pl.when(i == 1 + j)
                def _():
                    back_c[j].wait_recv()
                    held[j, core] = (held[j, core].astype(f32) + core_in[j].astype(f32)).astype(bf16)
                    back_y[j].start()

    for j in range(2):

        @pl.when(i == j)
        def _():
            back_c[j].start()
            if j == 0:
                keep.start()

    @pl.when(i == 3)
    def _():
        out = [
            [
                pltpu.make_async_copy(held.at[2 + j, c], back.at[c, at[j]], o_sem.at[j, k])
                for k, c in enumerate((1 - core, core))
            ]
            for j in range(2)
        ]
        for j in range(2):
            out[j][0].start()
        for j in range(2):
            back_y[j].wait_recv()
            held[2 + j, core] = (held[2 + j, core].astype(f32) + home[j].astype(f32)).astype(bf16)
            out[j][1].start()
        for j in range(2):
            out[j][0].wait()
            out[j][1].wait()
            back_c[j].wait_send()
            back_y[j].wait_send()
        keep.wait()


def mix(seconds, grads, experts, share_own, share_far, rest, exp_units, base, n_exp, unit_rows):
    rows, width = seconds.shape[1:]
    wide = grads.shape[2]
    half = rows // 2
    piece = half // 2
    anywhere = pl.BlockSpec(memory_space=pl.ANY)
    units, back, down_rows = pl.pallas_call(
        functools.partial(mix_kernel, exp_units, base, n_exp),
        grid=(4,),
        in_specs=[
            pl.BlockSpec((1, 2, piece, width), lambda i: (1 - i // 2, 0, i % 2, 0)),
            pl.BlockSpec((1, 2, piece, wide), lambda i: (1 - i // 2, 0, i % 2, 0)),
            anywhere,
            anywhere,
            anywhere,
            anywhere,
        ],
        out_specs=[
            pl.BlockSpec((3, 1, 2, piece, unit_rows), lambda i: (0, 1 - i // 2, 0, i % 2, 0)),
            anywhere,
            anywhere,
        ],
        out_shape=[
            jax.ShapeDtypeStruct((3, 2, 2, half, unit_rows), bf16),
            jax.ShapeDtypeStruct((2, half, wide), bf16),
            jax.ShapeDtypeStruct((unit_rows, width), bf16),
        ],
        scratch_shapes=[
            pltpu.VMEM((3, unit_rows, width), bf16),
            pltpu.VMEM((4, 2, piece, wide), bf16),
            pltpu.VMEM((2, piece, wide), bf16),
            pltpu.VMEM((2, piece, wide), bf16),
            pltpu.SemaphoreType.DMA((3, 4)),
            pltpu.SemaphoreType.DMA((2, share_own.shape[0])),
            pltpu.SemaphoreType.DMA,
            *[pltpu.SemaphoreType.DMA((2,))] * 4,
            pltpu.SemaphoreType.DMA((2, 2)),
            pltpu.SemaphoreType.DMA,
        ],
        compiler_params=pltpu.CompilerParams(
            collective_id=4, has_side_effects=True, vmem_limit_bytes=VMEM_BYTES
        ),
        cost_estimate=pl.CostEstimate(
            flops=20 * rows * width * unit_rows,
            bytes_accessed=6 * unit_rows * width + 16 * rows * width,
            transcendentals=0,
        ),
        name="mix",
    )(
        seconds.reshape(2, 2, half, width), grads.reshape(2, 2, half, wide), experts, share_own, share_far, rest
    )
    return units.reshape(3, 2, rows, unit_rows), back.reshape(rows, wide), down_rows


def unit_grads_kernel(count, exp_units, share_rows, at, *refs):
    units, seconds, grads = refs[:count], refs[count : 2 * count], refs[2 * count : 3 * count]
    experts, share_own, share_far = refs[3 * count :]
    m = pl.program_id(0)

    def run(rights):
        acc = dot(units[0][...], rights[0][...], 0, 0)
        for left, right in zip(units[1:], rights[1:]):
            acc += dot(left[...], right[...], 0, 0)
        experts[0, 0] = acc[:exp_units].astype(bf16)
        size = share_own.shape[3]
        for s in range(share_own.shape[0]):
            piece = acc[exp_units : exp_units + 2 * share_rows, s * size : (s + 1) * size].astype(bf16)
            share_own[s, 0] = piece[:share_rows]
            share_far[s, 0] = piece[share_rows:]

    @pl.when(m < 2)
    def _():
        run(seconds)

    @pl.when(m == 2)
    def _():
        run(grads)


def unit_grads(at, units, seconds, grads, exp_units, share_rows):
    n_head, n_seq = lax.axis_size("head"), lax.axis_size("seq")
    width = seconds[0][0].shape[2]
    unit_rows = units[0][0].shape[3]
    head_part, seq_part = width // n_head, width // n_seq
    near = n_seq // n_head
    rows = sum(block.shape[1] for block, _ in seconds)

    def far(r, at):
        return jnp.bitwise_xor(at[0], r)

    def place(q, m, r, at):
        return (m, q, 0, 0)

    def second_place(q, m, r, at):
        return (q, 0, jnp.where(m < 2, far(r, at), far(n_head - 1, at)))

    def grad_place(q, m, r, at):
        return (q, 0, jnp.where(m < 2, far(0, at), far(r, at)))

    in_specs = [
        pl.BlockSpec((None, None, block.shape[2], unit_rows), functools.partial(place, q))
        for block, q in units
    ]
    in_specs += [
        pl.BlockSpec((None, block.shape[1], head_part), functools.partial(second_place, q))
        for block, q in seconds
    ]
    in_specs += [
        pl.BlockSpec((None, block.shape[1], head_part), functools.partial(grad_place, q))
        for block, q in grads
    ]
    share_spec = pl.BlockSpec((near, 1, share_rows, seq_part), lambda m, r, at: (far(r, at), m, 0, 0))
    share_shape = jax.ShapeDtypeStruct((n_seq, 3, share_rows, seq_part), bf16)
    return pl.pallas_call(
        functools.partial(unit_grads_kernel, len(units), exp_units, share_rows),
        grid_spec=pltpu.PrefetchScalarGridSpec(
            num_scalar_prefetch=1,
            grid=(3, n_head),
            in_specs=in_specs,
            out_specs=[
                pl.BlockSpec((1, 1, exp_units, head_part), lambda m, r, at: (r, m, 0, 0)),
                share_spec,
                share_spec,
            ],
        ),
        out_shape=[
            jax.ShapeDtypeStruct((n_head, 3, exp_units, head_part), bf16),
            share_shape,
            share_shape,
        ],
        compiler_params=pltpu.CompilerParams(vmem_limit_bytes=VMEM_BYTES),
        cost_estimate=pl.CostEstimate(
            flops=6 * rows * width * unit_rows,
            bytes_accessed=6 * rows * unit_rows + 8 * rows * width + 6 * width * unit_rows,
            transcendentals=0,
        ),
        name="unit_grads",
    )(at, *(block for block, _ in units + seconds + grads))


def products_kernel(
    units, seconds, grads, down_rows, out, experts, expert_in_down, share_all,
    u, sides, right, far_half, column, core_in, home, share, share_in, stage,
    u_sem, r_sem, d_sem, c_a, c_b, y_a, y_b, x_a, x_b, z_a, z_b, e_sem, o_sem,
):
    seq, n_seq = lax.axis_index("seq"), lax.axis_size("seq")
    near_x, near_y, near_core = plane_places()
    core = seq % 2
    width = right.shape[2]
    rows = column.shape[0]
    piece = rows // 2
    exp_units = experts.shape[2]
    share_rows, seq_part = share_all.shape[2:]
    head_part = experts.shape[3]
    n_head = width // head_part
    edge = exp_units // LANES * LANES
    tail = exp_units - edge
    slot = {2: 1, 0: 2, 1: 0}

    def load_units(m):
        return [
            pltpu.make_async_copy(
                units.at[m, q], u.at[pl.ds(q * 2 * rows, 2 * rows)], u_sem.at[m, q]
            )
            for q in range(2)
        ]

    def load_right(k):
        source = grads if k else seconds
        return [
            pltpu.make_async_copy(
                source.at[q, :, pl.ds(f * head_part, head_part)],
                right.at[k, pl.ds(q * 2 * rows, 2 * rows), pl.ds(f * head_part, head_part)],
                r_sem.at[k, q, f],
            )
            for q in range(2)
            for f in range(n_head)
        ]

    down = sides.at[0]
    load_down = pltpu.make_async_copy(down_rows, down, d_sem)
    rights = [load_right(0), load_right(1)]
    first = load_units(2)
    first[1].start()
    load_down.start()
    first[0].start()
    for copy in rights[1] + rights[0]:
        copy.start()
    greet(
        [{"head": near_x}, {"head": near_y}] + [{"seq": (seq + k) % n_seq} for k in range(1, n_seq)]
    )

    pieces = [pl.ds(j * piece, piece) for j in range(2)]
    to_core = [
        remote(far_half.at[0, at], core_in.at[at], c_a.at[j], c_b.at[j], seq=near_core)
        for j, at in enumerate(pieces)
    ]
    to_y = [
        remote(far_half.at[1, at], home.at[at], y_a.at[j], y_b.at[j], head=near_y)
        for j, at in enumerate(pieces)
    ]
    to_x = [
        remote(share.at[1, :, m], share_in.at[:, m], x_a.at[m], x_b.at[m], head=near_x)
        for m in range(3)
    ]
    cross = remote(experts.at[3, 2], expert_in_down, x_a.at[3], x_b.at[3], head=near_x)
    spread_out = [[] for _ in range(3)]
    spread_in = []
    spread_own = []
    for m in range(3):
        for k in range(1, n_seq):
            to, source = (seq + k) % n_seq, (seq + n_seq - k) % n_seq
            spread_out[m].append(
                remote(
                    share.at[0, to, m], share_all.at[seq, m], z_a.at[m, k], z_b.at[m, k], seq=to
                )
            )
            block = share_all.at[source, m]
            spread_in.append(remote(block, block, z_a.at[m, k], z_b.at[m, k], seq=to))
        spread_own.append(
            pltpu.make_async_copy(share.at[0, seq, m], share_all.at[seq, m], z_a.at[m, 0])
        )

    def spread_share(m):
        to_x[m].wait_recv()
        for place in range(n_seq):
            total = share[0, place, m].astype(f32) + share_in[place, m].astype(f32)
            share[0, place, m] = total.astype(bf16)
        for copy in spread_out[m]:
            copy.start()
        spread_own[m].start()

    def out_rows(start):
        return dot(u[pl.ds(pl.multiple_of(start, 16), piece), :], down[...], 1, 0)

    def turn_units(m):
        block = 2 * piece
        for k in range(u.shape[0] // block):
            at = slice(k * block, (k + 1) * block)
            sides[slot[m], :, at] = u[at, :].T

    def share_part(m):
        for f in range(n_head):
            for copy in rights[1 if m == 2 else 0][f::n_head] if m < 3 else []:
                if m != 1:
                    copy.wait()
            block = right[1 if m == 2 else 0, :, f * head_part : (f + 1) * head_part]
            acc = dot(sides[slot[m], edge:], block, 1, 0)
            for b in range(head_part // seq_part):
                part = acc[tail : tail + 2 * share_rows, b * seq_part : (b + 1) * seq_part]
                place = f * (head_part // seq_part) + b
                share[0, place, m] = part[:share_rows].astype(bf16)
                share[1, place, m] = part[share_rows:].astype(bf16)
        to_x[m].start()

    owners = plane_owners()
    writes = []

    def expert_part(r, m):
        n = len(writes)
        if n >= 2:
            writes[n - 2].wait()
        start = pl.multiple_of(owners[r] * head_part, head_part)
        acc = dot(
            sides[slot[m], :exp_units],
            right[1 if m == 2 else 0, :, pl.ds(start, head_part)],
            1,
            0,
        )
        stage[n % 2] = acc.astype(bf16)
        writes.append(pltpu.make_async_copy(stage.at[n % 2], experts.at[r, m], e_sem.at[n % 2]))
        writes[-1].start()

    def pass_on(j):
        to_core[j].wait_recv()
        total = far_half[1, pieces[j]].astype(f32) + core_in[pieces[j]].astype(f32)
        far_half[1, pieces[j]] = total.astype(bf16)
        to_y[j].start()

    first[1].wait()
    load_down.wait()
    for k, half in ((0, 1 - core), (1, core)):
        for j in range(2):
            far_half[k, pieces[j]] = out_rows(2 * rows + half * rows + j * piece).astype(bf16)
            if k == 0:
                to_core[j].start()
            else:
                pass_on(j)
    first[0].wait()
    turn_units(2)
    share_part(2)
    for copy in to_core:
        copy.wait_send()
    for j in range(2):
        far_half[0, pieces[j]] = out_rows((1 - core) * rows + j * piece).astype(bf16)
    write = [
        pltpu.make_async_copy(far_half.at[0], out.at[1 - core], o_sem.at[0]),
        pltpu.make_async_copy(column, out.at[core], o_sem.at[1]),
    ]
    write[0].start()
    for j in range(2):
        column[pieces[j]] = out_rows(core * rows + j * piece).astype(bf16)
    for i, m in enumerate((0, 1)):
        load = load_units(m)
        for copy in load:
            copy.start()
        expert_part(3, 0 if i else 2)
        for copy in load:
            copy.wait()
        turn_units(m)
        share_part(m)
        spread_share(0 if i else 2)
    expert_part(3, 1)
    cross.start()
    for m in (2, 0, 1):
        expert_part(1, m)
    for m in (2, 0, 1):
        expert_part(2, m)
    spread_share(1)
    for m in (2, 0, 1):
        expert_part(0, m)

    for j in range(2):
        to_y[j].wait_recv()
        column[pieces[j]] = (column[pieces[j]].astype(f32) + home[pieces[j]].astype(f32)).astype(bf16)
    write[1].start()
    for copy in to_x + to_y:
        copy.wait_send()
    cross.wait()
    for group in spread_out:
        for copy in group:
            copy.wait_send()
    for copy in spread_in:
        copy.wait_recv()
    for copy in writes[-2:] + write + spread_own:
        copy.wait()


def products(units, seconds, grads, down_rows, exp_units, share_rows):
    n_head, n_seq = lax.axis_size("head"), lax.axis_size("seq")
    _, rows, width = seconds.shape
    unit_rows = units.shape[3]
    half = rows // 2
    head_part, seq_part = width // n_head, width // n_seq
    anywhere = pl.BlockSpec(memory_space=pl.ANY)
    dma = pltpu.SemaphoreType.DMA
    share_shape = (n_seq, 3, share_rows, seq_part)
    return pl.pallas_call(
        products_kernel,
        in_specs=[anywhere] * 4,
        out_specs=[anywhere] * 4,
        out_shape=[
            jax.ShapeDtypeStruct((2, half, width), bf16),
            jax.ShapeDtypeStruct((n_head, 3, exp_units, head_part), bf16),
            jax.ShapeDtypeStruct((exp_units, head_part), bf16),
            jax.ShapeDtypeStruct(share_shape, bf16),
        ],
        scratch_shapes=[
            pltpu.VMEM((2 * rows, unit_rows), bf16),
            pltpu.VMEM((3, unit_rows, 2 * rows), bf16),
            pltpu.VMEM((2, 2 * rows, width), bf16),
            pltpu.VMEM((2, half, width), bf16),
            pltpu.VMEM((half, width), bf16),
            pltpu.VMEM((half, width), bf16),
            pltpu.VMEM((half, width), bf16),
            pltpu.VMEM((2, *share_shape), bf16),
            pltpu.VMEM(share_shape, bf16),
            pltpu.VMEM((2, exp_units, head_part), bf16),
            dma((3, 2)),
            dma((2, 2, n_head)),
            dma,
            *[dma((2,))] * 4,
            *[dma((4,))] * 2,
            *[dma((3, n_seq))] * 2,
            *[dma((2,))] * 2,
        ],
        compiler_params=pltpu.CompilerParams(
            collective_id=5, has_side_effects=True, vmem_limit_bytes=VMEM_BYTES
        ),
        cost_estimate=pl.CostEstimate(
            flops=16 * rows * width * unit_rows,
            bytes_accessed=40 * rows * width,
            transcendentals=0,
        ),
        name="products",
    )(units, seconds, grads, down_rows)


def finish_kernel(
    experts, expert_in, expert_in_down, share_all, partial, grad_middle, tokens, gains, small,
    grad_up, grad_down, grad_share_up, grad_share_down, input_grad, totals,
    near, far, far_in, near_in, last_in, pack, share_pack, incoming, outgoing, slots,
    l_sem, x_a, x_b, y_a, y_b, s_a, s_b, t_a, t_b, p_sem,
):
    seq, head = lax.axis_index("seq"), lax.axis_index("head")
    near_x, near_y, near_core = plane_places()
    y = head // 2
    rows, width = grad_middle.shape
    units = near.shape[1]
    share_rows = share_all.shape[2]
    hidden = pack.shape[1]
    steps = [{"seq": near_core}]
    for bit in (2, 4):
        steps.append({"seq": seq + bit - 2 * bit * ((seq // bit) % 2)})
    steps += [{"head": near_y}, {"head": near_x}]

    loads = [
        [pltpu.make_async_copy(experts.at[2, m], far.at[m], l_sem.at[m]) for m in range(3)],
        [
            pltpu.make_async_copy(block, far_in.at[k], l_sem.at[3 + k])
            for k, block in enumerate((expert_in, expert_in_down))
        ],
        [pltpu.make_async_copy(experts.at[0, m], near.at[m], l_sem.at[5 + m]) for m in range(3)],
    ]
    for group in loads:
        for copy in group:
            copy.start()
    share_loads = [
        pltpu.make_async_copy(
            share_all.at[i], share_pack.at[:, pl.ds(i * share_rows, share_rows)], p_sem.at[i]
        )
        for i in range(share_all.shape[0])
    ]
    for copy in share_loads:
        copy.start()
    greet(steps)
    to_side = pl.ds(pl.multiple_of((1 + 2 * (head % 2)) * rows, 16), rows)
    to_far = pl.ds(pl.multiple_of((3 - 2 * (head % 2)) * rows, 16), rows)
    scatter = [
        remote(source, incoming.at[k], s_a.at[k], s_b.at[k], head=near_y)
        for k, source in enumerate((partial.at[pl.ds(2 * rows, rows)], partial.at[to_far]))
    ]
    scatter_side = remote(outgoing, incoming.at[2], s_a.at[2], s_b.at[2], head=near_x)
    last = remote(experts.at[3, 1], last_in, x_a.at[3], x_b.at[3], head=near_x)
    sides = [
        remote(experts.at[1, m], near_in.at[m], x_a.at[m], x_b.at[m], head=near_x) for m in range(3)
    ]
    for copy in scatter + [last] + sides[:1]:
        copy.start()
    here = pl.ds(pl.multiple_of(y * units, 16), units)
    there = pl.ds(pl.multiple_of((1 - y) * units, 16), units)
    across = [
        remote(far.at[m], pack.at[m, here], y_a.at[m], y_b.at[m], head=near_y) for m in range(3)
    ]
    across_in = [
        remote(far.at[m], pack.at[m, there], y_a.at[m], y_b.at[m], head=near_y) for m in range(3)
    ]
    for k, m in enumerate((0, 2)):
        loads[0][m].wait()
        loads[1][k].wait()
        far[m] = (far[m].astype(f32) + far_in[k].astype(f32)).astype(bf16)
        across[m].start()
    loads[0][1].wait()
    for copy in loads[2]:
        copy.wait()

    for copy in scatter:
        copy.wait_recv()
    outgoing[...] = (partial[to_side].astype(f32) + incoming[1].astype(f32)).astype(bf16)
    scatter_side.start()
    for copy in sides[1:]:
        copy.start()
    total = partial[:rows].astype(f32) + incoming[0].astype(f32)
    scatter_side.wait_recv()
    total += incoming[2].astype(f32)
    x = tokens[...].astype(f32)
    inverse = lax.rsqrt(jnp.mean(x * x, axis=1, keepdims=True) + EPS)
    normed = x * inverse
    slots[0] = small[...]
    slots[0, 10:11] = jnp.sum(total * normed, axis=0, keepdims=True)
    grad_normed = total * gains[0:1, :].astype(f32)
    mean = jnp.mean(grad_normed * normed, axis=1, keepdims=True)
    input_grad[...] = grad_middle[...] + inverse * (grad_normed - normed * mean)

    exchanges = [
        remote(slots.at[2 * k], slots.at[2 * k + 1], t_a.at[k], t_b.at[k], **place)
        for k, place in enumerate(steps)
    ]

    def exchange(k):
        exchanges[k].wait_recv()
        slots[2 * k + 2] = slots[2 * k] + slots[2 * k + 1]
        if k + 1 < len(steps):
            exchanges[k + 1].start()

    exchanges[0].start()

    for copy in share_loads:
        copy.wait()
    grad_share_down[...] = share_pack[2]
    exchange(0)
    grad_share_up[:, :hidden] = share_pack[0].T
    exchange(1)
    grad_share_up[:, hidden:] = share_pack[1].T
    last.wait_recv()
    far[1] = (far[1].astype(f32) + last_in[...].astype(f32)).astype(bf16)
    across[1].start()
    exchange(2)

    def place_block(m):
        sides[m].wait_recv()
        pack[m, here] = (near[m].astype(f32) + near_in[m].astype(f32)).astype(bf16)
        across_in[m].wait_recv()
        if m < 2:
            grad_up[:, m * hidden : (m + 1) * hidden] = pack[m].T
        else:
            grad_down[...] = pack[m]

    place_block(0)
    exchange(3)
    place_block(1)
    place_block(2)
    exchange(4)
    totals[...] = slots[2 * len(steps)]
    for copy in scatter + exchanges + sides + across + [last, scatter_side]:
        copy.wait_send()


def finish(experts, expert_in, expert_in_down, share_all, partial, grad_middle, tokens, gain, small):
    n_head, n_seq = lax.axis_size("head"), lax.axis_size("seq")
    rows, width = tokens.shape
    _, _, units, head_part = experts.shape
    share_rows, seq_part = share_all.shape[2:]
    hidden, share_units = 2 * units, n_seq * share_rows
    anywhere = pl.BlockSpec(memory_space=pl.ANY)
    vmem = pl.BlockSpec(memory_space=pltpu.VMEM)
    dma = pltpu.SemaphoreType.DMA
    return pl.pallas_call(
        finish_kernel,
        in_specs=[anywhere] * 4 + [vmem] * 5,
        out_specs=[vmem] * 6,
        out_shape=[
            jax.ShapeDtypeStruct((head_part, 2 * hidden), bf16),
            jax.ShapeDtypeStruct((hidden, head_part), bf16),
            jax.ShapeDtypeStruct((seq_part, 2 * share_units), bf16),
            jax.ShapeDtypeStruct((share_units, seq_part), bf16),
            jax.ShapeDtypeStruct((rows, width), f32),
            jax.ShapeDtypeStruct(small.shape, f32),
        ],
        scratch_shapes=[
            pltpu.VMEM((3, units, head_part), bf16),
            pltpu.VMEM((3, units, head_part), bf16),
            pltpu.VMEM((2, units, head_part), bf16),
            pltpu.VMEM((3, units, head_part), bf16),
            pltpu.VMEM((units, head_part), bf16),
            pltpu.VMEM((3, hidden, head_part), bf16),
            pltpu.VMEM((3, share_units, seq_part), bf16),
            pltpu.VMEM((n_head - 1, rows, width), bf16),
            pltpu.VMEM((rows, width), bf16),
            pltpu.VMEM((11, *small.shape), f32),
            dma((8,)),
            *[dma((4,))] * 2,
            *[dma((3,))] * 2,
            *[dma((n_head - 1,))] * 2,
            *[dma((5,))] * 2,
            dma((n_seq,)),
        ],
        compiler_params=pltpu.CompilerParams(
            collective_id=6, has_side_effects=True, vmem_limit_bytes=VMEM_BYTES
        ),
        cost_estimate=pl.CostEstimate(flops=0, bytes_accessed=1 << 27, transcendentals=0),
        name="finish",
    )(experts, expert_in, expert_in_down, share_all, partial, grad_middle, tokens, gain, small)


def after(value, *others):
    return lax.optimization_barrier((value, *others))[0]


def shards(
    tokens,
    cotangent,
    arrange,
    doc_lengths,
    routes,
    norm1_gain,
    qkv_weight,
    qkv_bias,
    out_weight,
    norm2_gain,
    router_weight,
    shared_gate_vec,
    shared_gate_up,
    shared_down,
    expert_gate_up,
    expert_down,
):
    highest = lax.Precision.HIGHEST
    tok_rows, width = tokens.shape
    n_seq = lax.axis_size("seq")
    n_head = lax.axis_size("head")
    seq = lax.axis_index("seq")
    head = lax.axis_index("head")
    group_tok = tok_rows * n_head
    heads_here = qkv_weight.shape[1]
    n_exp = router_weight.shape[1]
    hidden_all = expert_down.shape[1]
    parts = n_head // 2
    part = mesh_part()
    exp_units = hidden_all // parts
    share_all = shared_down.shape[0]
    share_units = share_all // n_seq
    share_rows = -(-share_units // 16) * 16
    base = exp_units + 2 * share_rows
    unit_rows = -(-(base + n_exp + 1) // LANES) * LANES
    seq_part = width // n_seq
    head_part = width // n_head

    wide = heads_here * HD
    plane = parts == 2 and n_seq == 8 and 2 * n_seq * tok_rows == width
    expert_up = expert_gate_up[0]
    at = jnp.stack([head, seq]).astype(jnp.int32)
    gate_rows = jnp.concatenate([router_weight.T, shared_gate_vec[None, :]], axis=0)
    rest = jnp.zeros((3, unit_rows - base, width), bf16).at[0, : n_exp + 1].set(gate_rows)

    expert_ids = jnp.arange(n_exp, dtype=jnp.int32)
    chosen = jnp.any(routes[:, :, None] == expert_ids[None, None, :], axis=1)
    marks = jnp.concatenate(
        [chosen.astype(bf16), jnp.zeros((tok_rows, LANES - n_exp), bf16)], axis=1
    )

    stream = tokens.astype(f32)
    gain_first = norm1_gain.astype(f32)
    scale_first = rms_scale(stream)
    normed_first = stream * scale_first
    gain_second = norm2_gain.astype(f32)
    weight_own = qkv_weight.reshape(seq_part, 3 * wide)
    if plane:
        gains = jnp.stack([norm1_gain, norm2_gain])
        (
            first_group, weight, wout, experts, share_own, share_far, grad_both, seconds,
            qkv, merged, log_total, middle, lowered_second, cosine, sine, layout,
        ) = forward(
            tokens, gains, weight_own, out_weight, expert_up,
            expert_down[0], shared_gate_up.reshape(seq_part, 2 * share_all), shared_down, cotangent,
            marks, qkv_bias, arrange, doc_lengths,
        )
        grad_both = grad_both.reshape(2, n_seq * tok_rows, width + LANES)
        seconds = seconds.reshape(2, n_seq * tok_rows, width)
        units, back_column, down_rows = mix(
            seconds,
            grad_both,
            experts,
            share_own,
            share_far,
            rest,
            exp_units,
            base,
            n_exp,
            unit_rows,
        )
        out_column, grad_experts, expert_in_down, share_parts = products(
            units, seconds, grad_both, down_rows, exp_units, share_rows
        )
        back_own = lax.psum_scatter(back_column, "seq", scatter_dimension=0, tiled=True)
    else:
        place, doc_index, position = layout_of(arrange[0], doc_lengths[0], group_tok)
        blocks = (head + jnp.arange(n_head, dtype=jnp.int32)) % n_head
        table = jnp.stack([place, doc_index, position]).reshape(3, n_head, tok_rows)
        place, doc_index, position = jnp.take(table, blocks, axis=1).reshape(3, group_tok)
        layout = jnp.stack([doc_index, place]).astype(f32)
        cosine, sine = rope_tables(position.astype(f32))
        grad_ext = jnp.concatenate([cotangent, marks], axis=1)
        bias_here = lax.dynamic_slice_in_dim(qkv_bias, head * heads_here, heads_here, 0)
        bias_here = bias_here.astype(f32)[:, None, :]
        weight = lax.all_gather(weight_own, "seq", axis=0, tiled=True)
        wout = lax.all_gather(out_weight, "seq", axis=0)
        first_group = group_gather((normed_first * gain_first).astype(bf16))
        send = jnp.stack([expert_up[:, :hidden_all].T, expert_up[:, hidden_all:].T, expert_down[0]])
        near = []
        for t in range(parts):
            there = jnp.bitwise_xor(part, t)
            block = lax.dynamic_slice_in_dim(send, there * exp_units, exp_units, 1)
            near.append(swap(block, "head", 2 * t) if t else block)
        experts = jnp.stack([block for own in near for block in (own, swap(own, "head", 1))])
        send = jnp.stack([shared_gate_up[:, 0].T, shared_gate_up[:, 1].T, shared_down])
        send = jnp.transpose(send.reshape(3, n_seq, share_units, seq_part), (1, 0, 2, 3))
        if share_rows > share_units:
            send = jnp.pad(send, ((0, 0), (0, 0), (0, share_rows - share_units), (0, 0)))
        share_own = lax.all_to_all(send, "seq", split_axis=0, concat_axis=0)
        full = pack(at, experts, [share_own, swap(share_own, "head", 1)], rest, unit_rows)
        qkv, merged, log_total, middle, lowered_second = attend(
            first_group, weight, wout, bias_here, cosine, sine, layout, tokens,
            gain_second[None, :],
        )
        grad_chunks = token_gather(grad_ext)
        second_chunks = token_gather(lowered_second)
        back_chunks = []
        unit_chunks = []
        for second, grad in zip(second_chunks, grad_chunks):
            back, units = mix_local(second, grad, full, exp_units, base, n_exp)
            back_chunks.append(back)
            unit_chunks.append(units)
        grad_experts, grad_share, grad_share_far = unit_grads(
            at,
            [(units[:, None], 0) for units in unit_chunks],
            [(second[None], 0) for second in second_chunks],
            [(grad[None], 0) for grad in grad_chunks],
            exp_units,
            share_rows,
        )
        out_chunks = [dot(units[2], full[2], 1, 0).astype(bf16) for units in unit_chunks]
        back_own = token_scatter(back_chunks)
        out_own = token_scatter(out_chunks)
    scale_second = rms_scale(middle)
    normed_second = middle * scale_second

    back_own = after(back_own, grad_experts).astype(f32)

    logits = dot(lowered_second, gate_rows, 1, 1)
    probs = jax.nn.softmax(logits[:, :n_exp], axis=-1)
    share_gate = jax.nn.sigmoid(logits[:, n_exp:])
    grad_probs = back_own[:, width : width + n_exp]
    grad_logits = probs * (grad_probs - jnp.sum(probs * grad_probs, axis=1, keepdims=True))
    grad_gate_logit = (
        back_own[:, width + n_exp : width + n_exp + 1] * share_gate * (1.0 - share_gate)
    )
    grad_gates = jnp.concatenate([grad_logits, grad_gate_logit], axis=1)
    grad_second = back_own[:, :width] + jnp.dot(
        grad_gates, gate_rows.astype(f32), precision=highest
    )
    grad_gate_cols = jnp.dot(grad_gates.T, lowered_second.astype(f32), precision=highest)
    grad_gain_second = jnp.sum(grad_second * normed_second, axis=0)
    grad_normed = grad_second * gain_second
    grad_middle = cotangent.astype(f32) + scale_second * (
        grad_normed - normed_second * jnp.mean(grad_normed * normed_second, axis=1, keepdims=True)
    )
    grad_attn = grad_middle.astype(bf16)
    if plane:
        out_own = lax.psum_scatter(
            after(out_column, grad_attn).reshape(n_seq * tok_rows, width),
            "seq",
            scatter_dimension=0,
            tiled=True,
        )
    mixed = (middle + out_own.astype(f32)).astype(bf16)
    back_args = (
        grad_attn, first_group, weight, wout, qkv, merged, log_total, cosine, sine, layout
    )
    if plane:
        grad_first, grad_weight, grad_bias_here, expert_in = attend_back(
            *back_args, extra=(grad_experts,)
        )
    else:
        grad_first, grad_weight, grad_bias_here = attend_back(*back_args)
    grad_weight = lax.psum_scatter(grad_weight, "seq", scatter_dimension=0, tiled=False)
    grad_bias = lax.dynamic_update_slice_in_dim(
        jnp.zeros(qkv_bias.shape, f32), grad_bias_here[:, 0], head * heads_here, 0
    )
    small = jnp.concatenate(
        [grad_gate_cols, grad_gain_second[None, :], jnp.zeros((1, width), f32), grad_bias.reshape(-1, width)],
        axis=0,
    )
    if plane:
        small = jnp.pad(small, ((0, 16 - small.shape[0]), (0, 0)))
        own_up, own_down, grad_share_up, grad_share_down, input_grad, totals = finish(
            grad_experts, expert_in, expert_in_down, share_parts, grad_first, grad_middle, tokens, gains,
            small,
        )
    else:
        grad_first = group_scatter(grad_first)
        small = small.at[n_exp + 2].set(jnp.sum(grad_first * normed_first, axis=0))
        grad_normed_first = grad_first * gain_first
        input_grad = grad_middle + scale_first * (
            grad_normed_first
            - normed_first * jnp.mean(grad_normed_first * normed_first, axis=1, keepdims=True)
        )
        totals = total_over_all(small)
        grad_share = grad_share + swap(grad_share_far, "head", 1)
        grad_share = lax.all_to_all(grad_share[:, :, :share_units], "seq", split_axis=0, concat_axis=0)
        grad_share = jnp.transpose(grad_share, (1, 0, 2, 3)).reshape(3, share_all, seq_part)
        own = {}
        for t in range(parts)[::-1]:
            total = grad_experts[2 * t] + swap(grad_experts[2 * t + 1], "head", 1)
            own[t] = swap(total, "head", 2 * t) if t else total
        own = jnp.stack([own[t] for t in range(parts)])
        own = jnp.take(own, jnp.bitwise_xor(part, jnp.arange(parts, dtype=jnp.int32)), axis=0)
        own = jnp.transpose(own, (1, 0, 2, 3)).reshape(3, hidden_all, head_part)
        own_up, own_down = jnp.concatenate([own[0].T, own[1].T], axis=1), own[2]
        grad_share_up = jnp.concatenate([grad_share[0].T, grad_share[1].T], axis=1)
        grad_share_down = grad_share[2]
    return (
        mixed,
        input_grad,
        totals[n_exp + 2],
        grad_weight[: 3 * wide].astype(f32).T.reshape(qkv_weight.shape),
        totals[n_exp + 3 : n_exp + 3 + 3].reshape(qkv_bias.shape),
        grad_weight[3 * wide :].astype(f32),
        totals[n_exp + 1],
        totals[:n_exp].T,
        totals[n_exp],
        grad_share_up.reshape(shared_gate_up.shape).astype(f32),
        grad_share_down.astype(f32),
        own_up.astype(f32)[None],
        own_down.astype(f32)[None],
    )


def solution(mesh):
    return jax.shard_map(
        shards,
        mesh=mesh,
        in_specs=(
            P(("seq", "head"), None),
            P(("seq", "head"), None),
            P("seq", None),
            P("seq", None),
            P(("seq", "head"), None),
            P(),
            P("seq", "head", None),
            P(),
            P("head", "seq"),
            P(),
            P(),
            P(),
            P("seq", None, "head"),
            P("head", "seq"),
            P("seq", "head", None),
            P("seq", None, "head"),
        ),
        out_specs=(
            P(("seq", "head"), None),
            P(("seq", "head"), None),
            P(),
            P("seq", "head", None),
            P(),
            P("head", "seq"),
            P(),
            P(),
            P(),
            P("seq", None, "head"),
            P("head", "seq"),
            P("seq", "head", None),
            P("seq", None, "head"),
        ),
        check_vma=False,
    )
```
